32 devices in a mesh: dp: 4 (over y, core), ctx: 8 (over z, x).
Axes of the slice: x: 2, y: 2, z: 4, core: 2. Of those that a mesh axis runs over, the one named last changes fastest.
Arguments:
- inputs: bfloat16 [2, 4, 1024, 1600], P(None, 'dp', 'ctx'), may hold values from -12 to 12
- grad_out: bfloat16 [2, 4, 1024, 1600], P(None, 'dp', 'ctx'), may hold values from -6 to 6
- w_qkv: bfloat16 [7680000], P(('dp', 'ctx')), may hold values from -1.5 to 1.5
- w_proj: bfloat16 [2560000], P(('dp', 'ctx')), may hold values from -2.5 to 2.5
- w_fc: bfloat16 [10240000], P(('dp', 'ctx')), may hold values from -0.15625 to 0.15625
- w_out: bfloat16 [10240000], P(('dp', 'ctx')), may hold values from -0.15625 to 0.15625
- smalls: bfloat16 [19200], P(('dp', 'ctx')), may hold values from -1.3 to 1.5
Outputs:
- outputs: bfloat16 [2, 4, 1024, 1600], P(None, 'dp', 'ctx')
- grad_in: float32 [2, 4, 1024, 1600], P(None, 'dp', 'ctx')
- grad_qkv: float32 [7680000], P(('dp', 'ctx'))
- grad_proj: float32 [2560000], P(('dp', 'ctx'))
- grad_fc: float32 [10240000], P(('dp', 'ctx'))
- grad_out_w: float32 [10240000], P(('dp', 'ctx'))
- grad_smalls: float32 [6400], P(('dp', 'ctx'))
- grad_rest: float32 [12800], P(('dp', 'ctx'))
The draws below stay inside these ranges and needn't reach their ends.
All inputs are finite; a program needn't handle non-finite values.
Results may differ from the reference program's by a relative error of at most 0.012.
Values may be sent and summed in bfloat16 or wider, within the bound.
A program may use at most 448 MiB of HBM per device.

```python
import math
import jax
import jax.numpy as jnp
from jax import lax

D = 1600
HEADS = 25
HEAD = 64
FF = 6400
LENGTH = 1024
MICRO = 2
BATCH = 4


def draw_inputs(key, part):
    key = jax.random.fold_in(key, 11)
    first, second = jax.random.split(key, 2)
    shape = (MICRO, BATCH, LENGTH, D)
    rows = jnp.exp(jax.random.uniform(second, (MICRO, BATCH, LENGTH, 1), jnp.float32, math.log(0.3), math.log(3.0)))
    base = jax.random.truncated_normal(first, -4.0, 4.0, shape, jnp.float32)
    return (base * rows).astype(jnp.bfloat16)


def draw_w_qkv(key, part):
    key = jax.random.fold_in(key, 23)
    first = jax.random.fold_in(key, 0)
    base = jax.random.truncated_normal(first, -4.0, 4.0, (D, 3 * D), jnp.float32) * D ** (-0.5)
    return base.reshape(-1).astype(jnp.bfloat16)


def draw_smalls(key, part):
    key = jax.random.fold_in(key, 37)
    first, second = jax.random.split(key)
    index = jnp.arange(8 * D + FF)
    is_gain = (index < D) | (index >= 5 * D) & (index < 6 * D)
    is_vbias = (index >= 3 * D) & (index < 4 * D)
    scale = jnp.where(is_vbias, 0.03, 0.3)
    gains = jax.random.uniform(first, (8 * D + FF,), jnp.float32, 0.5, 1.5)
    shifts = jax.random.truncated_normal(second, -4.0, 4.0, (8 * D + FF,), jnp.float32) * scale
    return jnp.where(is_gain, gains, shifts).astype(jnp.bfloat16)


def levels(key, dims, cuts, smallest, top_value):
    level, own = 1.0, jax.random.fold_in(key, 6)
    for dim, parts in cuts:
        heights = jnp.exp(jax.random.uniform(jax.random.fold_in(own, dim), (parts,), jnp.float32, smallest / len(cuts), top_value / len(cuts)))
        level = level * jnp.repeat(heights, dims[dim] // parts).reshape([-1 if axis == dim else 1 for axis in range(len(dims))])
    return level


def centred(key, dims, scale, most, pieces=(), kind=jnp.bfloat16):
    level = levels(key, dims, pieces, -0.22, 0.18) if pieces else 1.0
    drawn = jax.random.normal(key, dims, jnp.float32) * scale * level
    return jnp.minimum(jnp.maximum(drawn, -most), most).astype(kind)


def setup_inputs(seed: int = 0) -> dict:
    key_list = jax.random.split(jax.random.key(seed), 8)
    inputs = draw_inputs(jax.random.fold_in(key_list[7], 71), 0)
    grad_out = centred(key_list[1], (MICRO, BATCH, LENGTH, D), 1.0, 6.0, ((1, 4), (2, 8)))
    w_qkv = draw_w_qkv(jax.random.fold_in(key_list[7], 71), 0)
    w_proj = centred(key_list[3], (D * D,), (max(D // 256, 1)) ** -0.5, 2.5, ((0, 32),))
    w_fc = centred(key_list[4], (D * FF,), D ** -0.5, 0.15625, ((0, 32),))
    w_out = centred(key_list[5], (FF * D,), (FF // 4) ** -0.5, 0.15625, ((0, 32),))
    smalls = draw_smalls(jax.random.fold_in(key_list[7], 71), 0)
    return {"inputs": inputs, "grad_out": grad_out, "w_qkv": w_qkv, "w_proj": w_proj, "w_fc": w_fc, "w_out": w_out, "smalls": smalls}


EPS = 1e-05

@jax.custom_vjp
def low(v):
    return lax.optimization_barrier(v.astype(jnp.bfloat16)).astype(jnp.float32)

@jax.custom_vjp
def low_back(v):
    return v

def low_keep(v):
    return (low(v), None)

def low_pass(kept, grad):
    return (grad,)

def back_keep(v):
    return (v, None)

def back_low(kept, grad):
    return (low(grad),)
low.defvjp(low_keep, low_pass)
low_back.defvjp(back_keep, back_low)

def product(left, right):
    return jnp.dot(left, right, precision=lax.Precision.HIGHEST)

def layer_norm(values, gain, shift):
    center = values - lax.optimization_barrier(jnp.mean(values, axis=-1, keepdims=True))
    spread = lax.optimization_barrier(jnp.mean(center * center, axis=-1, keepdims=True))
    return center * lax.rsqrt(spread + EPS) * gain + shift

def block_forward(tokens, w_qkv, w_proj, w_fc, w_out, smalls):
    ln1_gain = smalls[0:D]
    ln1_shift = smalls[D:2 * D]
    q_bias = smalls[2 * D:3 * D]
    v_bias = smalls[3 * D:4 * D]
    proj_bias = smalls[4 * D:5 * D]
    ln2_gain = smalls[5 * D:6 * D]
    ln2_shift = smalls[6 * D:7 * D]
    fc_bias = smalls[7 * D:7 * D + FF]
    out_bias = smalls[7 * D + FF:]
    hidden_one = low(layer_norm(tokens, ln1_gain, ln1_shift))
    qkv_bias = jnp.concatenate([q_bias, jnp.zeros((D,), jnp.float32), v_bias])
    mixed = low(low_back(product(hidden_one, w_qkv) + qkv_bias))
    queries = mixed[:, :D].reshape(LENGTH, HEADS, HEAD)
    keys = mixed[:, D:2 * D].reshape(LENGTH, HEADS, HEAD)
    values = mixed[:, 2 * D:].reshape(LENGTH, HEADS, HEAD)
    scores = low_back(jnp.einsum('qhe,khe->hqk', queries, keys, precision=lax.Precision.HIGHEST) * 0.125)
    allowed = jnp.arange(LENGTH)[:, None] >= jnp.arange(LENGTH)[None, :]
    scores = jnp.where(allowed[None], scores, -1e+30)
    attn_prob = jax.nn.softmax(scores, axis=-1)
    context = jnp.einsum('hqk,khe->qhe', low(attn_prob), values, precision=lax.Precision.HIGHEST).reshape(LENGTH, D)
    context = low(low_back(context))
    branch = low_back(product(context, w_proj) + proj_bias)
    resid = tokens + branch
    hidden_two = low(layer_norm(resid, ln2_gain, ln2_shift))
    pre_act = low_back(product(hidden_two, w_fc) + fc_bias)
    activ = low(jax.nn.gelu(pre_act, approximate=True))
    return resid + product(activ, w_out) + out_bias

def reference(inputs, grad_out, w_qkv, w_proj, w_fc, w_out, smalls):
    weights = (w_qkv.astype(jnp.float32).reshape(D, 3 * D), w_proj.astype(jnp.float32).reshape(D, D), w_fc.astype(jnp.float32).reshape(D, FF), w_out.astype(jnp.float32).reshape(FF, D), smalls.astype(jnp.float32))
    seq_in = inputs.astype(jnp.float32).reshape(-1, LENGTH, D)
    seq_grad = grad_out.astype(jnp.float32).reshape(-1, LENGTH, D)

    def visit(carry, item):
        result, pull = jax.vjp(block_forward, item[0], *weights)
        grads = pull(item[1])
        summed = tuple((held + fresh for held, fresh in zip(carry, grads[1:])))
        return (summed, (result, grads[0]))
    start = tuple((jnp.zeros_like(weight) for weight in weights))
    totals, (results, in_grads) = lax.scan(visit, start, (seq_in, seq_grad))
    return (results.astype(jnp.bfloat16).reshape(inputs.shape), in_grads.reshape(inputs.shape), totals[0].reshape(-1), totals[1].reshape(-1), totals[2].reshape(-1), totals[3].reshape(-1), totals[4][:4 * D], totals[4][4 * D:])
```

```python
import jax
import jax.numpy as jnp
from jax import lax
from jax.sharding import PartitionSpec as P

D = 1600
HEADS = 25
HEAD = 64
FF = 6400
MICRO = 2


EPS = 1e-05


def layer_norm(values, gain, shift):
    center = values - jnp.mean(values, axis=-1, keepdims=True)
    spread = jnp.mean(center * center, axis=-1, keepdims=True)
    return center * lax.rsqrt(spread + EPS) * gain + shift


def gelu_tanh(values):
    return jax.nn.gelu(values, approximate=True)


def unpack(gathered):
    packed_qkv, packed_proj, packed_fc, packed_out, packed_small = gathered
    return (
        packed_qkv.reshape(D, 3 * D),
        packed_proj.reshape(D, D),
        packed_fc.reshape(D, FF),
        packed_out.reshape(FF, D),
        packed_small.astype(jnp.float32),
    )


def fetch(w_qkv, w_proj, w_fc, w_out, smalls):
    return unpack(
        (
            lax.all_gather(w_qkv, ("dp", "ctx"), axis=0, tiled=True),
            lax.all_gather(w_proj, ("dp", "ctx"), axis=0, tiled=True),
            lax.all_gather(w_fc, ("dp", "ctx"), axis=0, tiled=True),
            lax.all_gather(w_out, ("dp", "ctx"), axis=0, tiled=True),
            lax.all_gather(smalls, ("dp", "ctx"), axis=0, tiled=True),
        )
    )


def fetch_again(w_qkv, w_proj, w_fc, w_out, smalls):
    return unpack(
        (
            lax.all_gather(w_qkv, ("dp", "ctx"), axis=0, tiled=True),
            lax.all_gather(w_proj, ("dp", "ctx"), axis=0, tiled=True),
            lax.all_gather(w_fc, ("dp", "ctx"), axis=0, tiled=True),
            lax.all_gather(w_out, ("dp", "ctx"), axis=0, tiled=True),
            lax.all_gather(smalls, ("dp", "ctx"), axis=0, tiled=True),
        )
    )


def outer_sum(left, right):
    return lax.dot_general(
        left, right, (((0,), (0,)), ((), ())), preferred_element_type=jnp.float32
    )


def back_product(grad, weight):
    return lax.dot_general(
        grad, weight, (((1,), (1,)), ((), ())), preferred_element_type=jnp.float32
    )


def flat_term(left, right, start, count):
    width = right.shape[1]
    span = count // width + 2
    padded = jnp.pad(left, ((0, 0), (0, span)))
    first_row = start // width
    piece = lax.dynamic_slice_in_dim(padded, first_row, span, 1)
    block = outer_sum(piece, right).astype(jnp.bfloat16).reshape(-1)
    return lax.dynamic_slice_in_dim(block, start, count, 0)


def masked_scores(queries, keys, query_start, key_start):
    scores = (
        jnp.einsum("sqhe,skhe->shqk", queries, keys, preferred_element_type=jnp.float32) * 0.125
    )
    query_pos = query_start + jnp.arange(queries.shape[1])
    key_pos = key_start + jnp.arange(keys.shape[1])
    allowed = query_pos[:, None] >= key_pos[None, :]
    return jnp.where(allowed[None, None], scores, -1e30)


def segment(small_vals, which):
    return small_vals[which * D : (which + 1) * D]


def shards(inputs, grad_out, w_qkv, w_proj, w_fc, w_out, smalls):
    seqs = inputs.shape[1]
    local_len = inputs.shape[2]
    rows = seqs * local_len
    offset = lax.axis_index("ctx") * local_len
    acc_small = [jnp.zeros((D,), jnp.float32) for _ in range(7)]
    acc_fc_bias = jnp.zeros((FF,), jnp.float32)
    acc_out_bias = jnp.zeros((D,), jnp.float32)
    result_list = []
    grad_list = []
    kept_hidden_one = []
    kept_mixed_grad = []
    kept_context = []
    kept_branch_grad = []
    kept_hidden_two = []
    kept_pre_grad = []
    kept_activ = []
    kept_out_grad = []
    for batch_index in range(MICRO):
        params = fetch(w_qkv, w_proj, w_fc, w_out, smalls)
        mat_qkv, mat_proj, mat_fc, mat_out, small_vals = params
        tokens = inputs[batch_index].astype(jnp.float32).reshape(rows, D)
        hidden_one, ln1_pull = jax.vjp(
            layer_norm, tokens, segment(small_vals, 0), segment(small_vals, 1)
        )
        hidden_one = hidden_one.astype(jnp.bfloat16)
        qkv_bias = jnp.concatenate(
            [segment(small_vals, 2), jnp.zeros((D,), jnp.float32), segment(small_vals, 3)]
        )
        mixed = (
            jnp.dot(hidden_one, mat_qkv, preferred_element_type=jnp.float32) + qkv_bias
        ).astype(jnp.bfloat16)
        queries = mixed[:, :D].reshape(seqs, local_len, HEADS, HEAD)
        keys_local = mixed[:, D : 2 * D].reshape(seqs, local_len, D)
        values_local = mixed[:, 2 * D :].reshape(seqs, local_len, D)
        keys_all, values_all = (
            lax.all_gather(keys_local, "ctx", axis=1, tiled=True),
            lax.all_gather(values_local, "ctx", axis=1, tiled=True),
        )
        keys_all = keys_all.reshape(seqs, -1, HEADS, HEAD)
        values_all = values_all.reshape(seqs, -1, HEADS, HEAD)
        scores = masked_scores(queries, keys_all, offset, 0)
        row_peak = jnp.max(scores, axis=-1, keepdims=True)
        log_total = row_peak + jnp.log(jnp.sum(jnp.exp(scores - row_peak), axis=-1, keepdims=True))
        attn_low = jnp.exp(scores - log_total).astype(jnp.bfloat16)
        context = jnp.einsum(
            "shqk,skhe->sqhe", attn_low, values_all, preferred_element_type=jnp.float32
        )
        context = context.reshape(rows, D).astype(jnp.bfloat16)
        resid = (
            tokens
            + jnp.dot(context, mat_proj, preferred_element_type=jnp.float32)
            + segment(small_vals, 4)
        )
        hidden_two, ln2_pull = jax.vjp(
            layer_norm, resid, segment(small_vals, 5), segment(small_vals, 6)
        )
        hidden_two = hidden_two.astype(jnp.bfloat16)
        pre_act = (
            jnp.dot(hidden_two, mat_fc, preferred_element_type=jnp.float32)
            + small_vals[7 * D : 7 * D + FF]
        )
        activ, gelu_pull = jax.vjp(gelu_tanh, pre_act)
        activ = activ.astype(jnp.bfloat16)
        result = (
            resid
            + jnp.dot(activ, mat_out, preferred_element_type=jnp.float32)
            + small_vals[7 * D + FF :]
        )
        result_list.append(result.astype(jnp.bfloat16).reshape(seqs, local_len, D))
        back_params = fetch_again(w_qkv, w_proj, w_fc, w_out, smalls)
        mat_qkv, mat_proj, mat_fc, mat_out, small_vals = back_params
        grad_low = grad_out[batch_index].reshape(rows, D)
        grad_full = grad_low.astype(jnp.float32)
        acc_out_bias = acc_out_bias + jnp.sum(grad_full, axis=0)
        grad_act = back_product(grad_low, mat_out)
        (grad_pre,) = gelu_pull(grad_act)
        grad_pre = grad_pre.astype(jnp.bfloat16)
        acc_fc_bias = acc_fc_bias + jnp.sum(grad_pre.astype(jnp.float32), axis=0)
        grad_hidden_two = back_product(grad_pre, mat_fc)
        grad_ln_two, grad_gain_two, grad_shift_two = ln2_pull(grad_hidden_two)
        acc_small[5] = acc_small[5] + grad_gain_two
        acc_small[6] = acc_small[6] + grad_shift_two
        grad_resid = grad_full + grad_ln_two
        grad_branch = grad_resid.astype(jnp.bfloat16)
        acc_small[4] = acc_small[4] + jnp.sum(grad_branch.astype(jnp.float32), axis=0)
        grad_context = (
            back_product(grad_branch, mat_proj)
            .astype(jnp.bfloat16)
            .reshape(seqs, local_len, HEADS, HEAD)
        )
        scores = masked_scores(queries, keys_all, offset, 0)
        attn_prob = jnp.exp(scores - log_total)
        grad_attn = jnp.einsum(
            "sqhe,skhe->shqk", grad_context, values_all, preferred_element_type=jnp.float32
        )
        row_delta = jnp.sum(attn_prob * grad_attn, axis=-1, keepdims=True)
        grad_scores = (attn_prob * (grad_attn - row_delta)).astype(jnp.bfloat16)
        grad_queries = (
            jnp.einsum("shqk,skhe->sqhe", grad_scores, keys_all, preferred_element_type=jnp.float32)
            * 0.125
        )
        query_all, dctx_all = (
            lax.all_gather(queries.reshape(seqs, local_len, D), "ctx", axis=1, tiled=True),
            lax.all_gather(grad_context.reshape(seqs, local_len, D), "ctx", axis=1, tiled=True),
        )
        lse_all, delta_all = (
            lax.all_gather(jnp.transpose(log_total[..., 0], (0, 2, 1)), "ctx", axis=1, tiled=True),
            lax.all_gather(jnp.transpose(row_delta[..., 0], (0, 2, 1)), "ctx", axis=1, tiled=True),
        )
        query_all = query_all.reshape(seqs, -1, HEADS, HEAD)
        dctx_all = dctx_all.reshape(seqs, -1, HEADS, HEAD)
        lse_all = jnp.transpose(lse_all, (0, 2, 1))[..., None]
        delta_all = jnp.transpose(delta_all, (0, 2, 1))[..., None]
        own_keys = keys_local.reshape(seqs, local_len, HEADS, HEAD)
        own_values = values_local.reshape(seqs, local_len, HEADS, HEAD)
        col_scores = masked_scores(query_all, own_keys, 0, offset)
        col_prob = jnp.exp(col_scores - lse_all)
        col_dattn = jnp.einsum(
            "sqhe,skhe->shqk", dctx_all, own_values, preferred_element_type=jnp.float32
        )
        col_ds = (col_prob * (col_dattn - delta_all)).astype(jnp.bfloat16)
        grad_keys = (
            jnp.einsum("shqk,sqhe->skhe", col_ds, query_all, preferred_element_type=jnp.float32)
            * 0.125
        )
        grad_values = jnp.einsum(
            "shqk,sqhe->skhe",
            col_prob.astype(jnp.bfloat16),
            dctx_all,
            preferred_element_type=jnp.float32,
        )
        grad_mixed = jnp.concatenate(
            [
                grad_queries.reshape(rows, D),
                grad_keys.reshape(rows, D),
                grad_values.reshape(rows, D),
            ],
            axis=1,
        ).astype(jnp.bfloat16)
        bias_terms = jnp.sum(grad_mixed.astype(jnp.float32), axis=0)
        acc_small[2] = acc_small[2] + bias_terms[:D]
        acc_small[3] = acc_small[3] + bias_terms[2 * D :]
        grad_hidden_one = back_product(grad_mixed, mat_qkv)
        grad_ln_one, grad_gain_one, grad_shift_one = ln1_pull(grad_hidden_one)
        acc_small[0] = acc_small[0] + grad_gain_one
        acc_small[1] = acc_small[1] + grad_shift_one
        grad_list.append((grad_resid + grad_ln_one).reshape(seqs, local_len, D))
        kept_hidden_one.append(hidden_one)
        kept_mixed_grad.append(grad_mixed)
        kept_context.append(context)
        kept_branch_grad.append(grad_branch)
        kept_hidden_two.append(hidden_two)
        kept_pre_grad.append(grad_pre)
        kept_activ.append(activ)
        kept_out_grad.append(grad_low)
    front_grads = jnp.concatenate(acc_small[0:4])
    tail_grads = jnp.concatenate(acc_small[4:7] + [acc_fc_bias, acc_out_bias])
    grad_qkv = lax.psum_scatter(
        flat_term(
            jnp.concatenate(kept_hidden_one),
            jnp.concatenate(kept_mixed_grad),
            jnp.int32(0),
            lax.axis_size(("dp", "ctx")) * w_qkv.shape[0],
        ),
        ("dp", "ctx"),
        scatter_dimension=0,
        tiled=True,
    ).astype(jnp.float32)
    grad_proj = lax.psum_scatter(
        flat_term(
            jnp.concatenate(kept_context),
            jnp.concatenate(kept_branch_grad),
            jnp.int32(0),
            lax.axis_size(("dp", "ctx")) * w_proj.shape[0],
        ),
        ("dp", "ctx"),
        scatter_dimension=0,
        tiled=True,
    ).astype(jnp.float32)
    grad_fc = lax.psum_scatter(
        flat_term(
            jnp.concatenate(kept_hidden_two),
            jnp.concatenate(kept_pre_grad),
            jnp.int32(0),
            lax.axis_size(("dp", "ctx")) * w_fc.shape[0],
        ),
        ("dp", "ctx"),
        scatter_dimension=0,
        tiled=True,
    ).astype(jnp.float32)
    grad_out_w = lax.psum_scatter(
        flat_term(
            jnp.concatenate(kept_activ),
            jnp.concatenate(kept_out_grad),
            jnp.int32(0),
            lax.axis_size(("dp", "ctx")) * w_out.shape[0],
        ),
        ("dp", "ctx"),
        scatter_dimension=0,
        tiled=True,
    ).astype(jnp.float32)
    grad_front, grad_tail = (
        lax.psum_scatter(front_grads, ("dp", "ctx"), scatter_dimension=0, tiled=True),
        lax.psum_scatter(tail_grads, ("dp", "ctx"), scatter_dimension=0, tiled=True),
    )
    return (
        jnp.stack(result_list),
        jnp.stack(grad_list),
        grad_qkv,
        grad_proj,
        grad_fc,
        grad_out_w,
        grad_front,
        grad_tail,
    )


DP, CTX = 4, 8
ZN, XN, YN, CN = 4, 2, 2, 2
NDEV = 32
AXES = ("dp", "ctx")
SLOTS = 7
HW = SLOTS * HEAD
STARTS = (0, 7, 13, 19)
COUNTS = (7, 6, 6, 6)
BLK = 128


def place(index):
    dp, ctx = divmod(index, CTX)
    y, c = divmod(dp, CN)
    z, x = divmod(ctx, XN)
    return y, c, z, x


def number(y, c, z, x):
    return (y * CN + c) * CTX + z * XN + x


def pairs(target):
    found = []
    for index in range(NDEV):
        where = target(*place(index))
        if where is not None:
            found.append((index, number(*where)))
    return found


def send(values, target):
    return lax.ppermute(values, AXES, pairs(target))


def swap_x(values):
    return send(values, lambda y, c, z, x: (y, c, z, 1 - x))


def swap_core(values):
    return send(values, lambda y, c, z, x: (y, 1 - c, z, x))


def swap_y(values):
    return send(values, lambda y, c, z, x: (1 - y, c, z, x))


def pick(values, index):
    return lax.dynamic_index_in_dim(values, index, 0, keepdims=False)


def ordered(own, other, position, axis):
    first = jnp.where(position == 0, own, other)
    second = jnp.where(position == 0, other, own)
    return jnp.stack([first, second], axis=axis)


def line_gather(piece, z):
    right = left = piece
    rights, lefts = [], []
    for turn in range(1, ZN):
        right = send(right, lambda y, c, z, x: (y, c, z + 1, x) if turn - 1 <= z < ZN - 1 else None)
        left = send(left, lambda y, c, z, x: (y, c, z - 1, x) if 0 < z <= ZN - turn else None)
        rights.append(right)
        lefts.append(left)
    band = jnp.stack(rights[::-1] + [piece] + lefts)
    return lax.dynamic_slice_in_dim(band, ZN - 1 - z, ZN, 0)


def line_scatter(parts, z):
    right = left = None
    for turn in range(1, ZN):
        up = pick(parts, jnp.clip(z + ZN - turn, 0, ZN - 1))
        down = pick(parts, jnp.clip(z - ZN + turn, 0, ZN - 1))
        if right is not None:
            up, down = up + right, down + left
        right = send(up, lambda y, c, z, x: (y, c, z + 1, x) if z <= turn - 1 and z < ZN - 1 else None)
        left = send(down, lambda y, c, z, x: (y, c, z - 1, x) if z >= ZN - turn and z > 0 else None)
    return pick(parts, z) + right + left


def gather_zy(piece, y, z):
    column = line_gather(piece, z)
    return ordered(column, swap_y(column), y, 0)


def scatter_zy(parts, y, z):
    mine = pick(parts, y)
    theirs = pick(parts, 1 - y)
    return line_scatter(mine + swap_y(theirs), z)


def team_swap(parts, c, x):
    by_x = jnp.moveaxis(parts, 1, 0)
    got = swap_x(pick(by_x, 1 - x))
    both = ordered(pick(by_x, x), got, x, 1)
    got = swap_core(pick(both, 1 - c))
    return ordered(pick(both, c), got, c, 0)


def team_gather(values, c, x):
    mine = values.reshape(2, BLK, -1)
    row = ordered(mine, swap_x(mine), x, 1)
    return ordered(row, swap_core(row), c, 0).reshape(8 * BLK, -1)


def team_scatter(values, c, x):
    parts = values.reshape(2, 2, 2, BLK, -1)
    got = swap_core(pick(parts, 1 - c).astype(jnp.bfloat16))
    mine = jnp.moveaxis(pick(parts, c) + got.astype(jnp.float32), 1, 0)
    got = swap_x(pick(mine, 1 - x).astype(jnp.bfloat16))
    return (pick(mine, x) + got.astype(jnp.float32)).reshape(2 * BLK, -1)


def to_teams(values, z, c):
    half = z // 2
    got = []
    for k in range(2):
        block = pick(values, (z + k) % 2)[0]
        got.append(
            send(block, lambda y, c, z, x: (y, z // 2, 2 * ((z + k) % 2) + c, x))
        )
    return jnp.concatenate(
        [jnp.where(half == 0, got[0], got[1]), jnp.where(half == 0, got[1], got[0])]
    )


def from_teams(values, z, c):
    half = z // 2
    parts = values.reshape(2, BLK, -1)
    back = []
    for k in range(2):
        block = pick(parts, (half + k) % 2)

        def target(y, c, z, x, k=k):
            m, core = z // 2, z % 2
            return (y, core, 2 * c + (m + k) % 2, x)

        back.append(send(block, target))
    first = jnp.where(z % 2 == 0, back[0], back[1])
    second = jnp.where(z % 2 == 0, back[1], back[0])
    return jnp.stack([first, second])[:, None]


def head_parts(columns):
    found = []
    for start, count in zip(STARTS, COUNTS):
        part = columns[:, start * HEAD : (start + count) * HEAD]
        found.append(jnp.pad(part, ((0, 0), (0, (SLOTS - count) * HEAD))))
    return jnp.stack(found)


def head_join(parts):
    return jnp.concatenate(
        [parts[r][:, : COUNTS[r] * HEAD] for r in range(4)], axis=1
    )


def fast_shards(inputs, grad_out, w_qkv, w_proj, w_fc, w_out, smalls):
    dp, ctx = lax.axis_index("dp"), lax.axis_index("ctx")
    y, c, z, x = dp // CN, dp % CN, ctx // XN, ctx % XN
    rank = c * XN + x
    low = jnp.bfloat16
    small = lax.all_gather(smalls, AXES, axis=0, tiled=True).astype(jnp.float32)
    gain1, shift1, bias_q, bias_v, bias_proj, gain2, shift2 = [segment(small, i) for i in range(7)]
    bias_fc = small[7 * D : 7 * D + FF].reshape(YN, CN, ZN, XN, 200)
    bias_fc = lax.dynamic_index_in_dim(bias_fc, c, 1, keepdims=False)
    bias_fc = lax.dynamic_index_in_dim(bias_fc, x, 2, keepdims=False).reshape(-1)
    bias_out = small[7 * D + FF :]
    bias_qkv = jnp.stack(
        [head_parts(bias_q[None]), jnp.zeros((4, 1, HW)), head_parts(bias_v[None])], axis=1
    )
    bias_qkv = pick(bias_qkv, rank).reshape(3 * HW)

    tokens = to_teams(inputs, z, c).astype(jnp.float32)
    cotangent = to_teams(grad_out, z, c)

    rows = w_qkv.reshape(50, 3, D)
    parts = jnp.stack([head_parts(rows[:, i]) for i in range(3)], axis=2)
    parts = parts.reshape(CN, XN, 50, 3 * HW)
    piece = team_swap(parts, c, x)
    gathered = gather_zy(piece, y, z)
    mat_qkv = gathered.transpose(0, 2, 1, 3, 4, 5).reshape(D, 3 * HW)

    piece = w_proj.reshape(50, D)
    gathered = gather_zy(piece, y, z)
    both = ordered(gathered, swap_x(gathered), x, 2)
    full = ordered(both, swap_core(both), c, 1)
    mat_proj = full.reshape(D, D)

    parts = w_fc.reshape(50, YN, CN, ZN, XN, 200).transpose(2, 4, 0, 1, 3, 5)
    parts = parts.reshape(CN, XN, 50, D)
    piece = team_swap(parts, c, x)
    gathered = gather_zy(piece, y, z)
    mat_fc = gathered.transpose(0, 2, 1, 3, 4, 5).reshape(D, D)

    mat_out = gather_zy(w_out.reshape(200, D), y, z).reshape(D, D)

    hidden_one, ln1_pull = jax.vjp(layer_norm, tokens, gain1, shift1)
    hidden_one = team_gather(hidden_one.astype(low), c, x)
    mixed = (jnp.dot(hidden_one, mat_qkv, preferred_element_type=jnp.float32) + bias_qkv).astype(low)
    queries, keys, values = [
        mixed[:, i * HW : (i + 1) * HW].reshape(1, 8 * BLK, SLOTS, HEAD) for i in range(3)
    ]
    scores = masked_scores(queries, keys, 0, 0)
    peak = jnp.max(scores, axis=-1, keepdims=True)
    log_total = peak + jnp.log(jnp.sum(jnp.exp(scores - peak), axis=-1, keepdims=True))
    attn = jnp.exp(scores - log_total)
    attn_low = attn.astype(low)
    context = jnp.einsum("shqk,skhe->sqhe", attn_low, values, preferred_element_type=jnp.float32)
    context = context.astype(low).reshape(2, 2, 2, BLK, HW)
    context = team_swap(jnp.moveaxis(context, 2, 1), c, x).reshape(4, 2 * BLK, HW)
    context = head_join(context)
    resid = tokens + jnp.dot(context, mat_proj, preferred_element_type=jnp.float32) + bias_proj
    hidden_two, ln2_pull = jax.vjp(layer_norm, resid, gain2, shift2)
    hidden_two = team_gather(hidden_two.astype(low), c, x)
    pre_act = jnp.dot(hidden_two, mat_fc, preferred_element_type=jnp.float32) + bias_fc
    activ, gelu_pull = jax.vjp(gelu_tanh, pre_act)
    activ = activ.astype(low)
    result = team_scatter(jnp.dot(activ, mat_out, preferred_element_type=jnp.float32), c, x)
    result = (resid + result + bias_out).astype(low)
    outputs = from_teams(result, z, c)

    grad_full = cotangent.astype(jnp.float32)
    grad_all = team_gather(cotangent, c, x)
    (grad_pre,) = gelu_pull(back_product(grad_all, mat_out))
    grad_pre = grad_pre.astype(low)
    grad_hidden_two = team_scatter(back_product(grad_pre, mat_fc), c, x)
    grad_ln_two, grad_gain_two, grad_shift_two = ln2_pull(grad_hidden_two)
    grad_resid = grad_full + grad_ln_two
    grad_branch = grad_resid.astype(low)
    grad_context = back_product(grad_branch, mat_proj).astype(low)
    grad_context = team_swap(head_parts(grad_context).reshape(CN, XN, 2, BLK, HW), c, x)
    grad_context = jnp.moveaxis(grad_context, 1, 2).reshape(1, 8 * BLK, SLOTS, HEAD)
    grad_attn = jnp.einsum("sqhe,skhe->shqk", grad_context, values, preferred_element_type=jnp.float32)
    delta = jnp.sum(attn * grad_attn, axis=-1, keepdims=True)
    grad_scores = (attn * (grad_attn - delta)).astype(low)
    grad_q = jnp.einsum("shqk,skhe->sqhe", grad_scores, keys, preferred_element_type=jnp.float32) * 0.125
    grad_k = jnp.einsum("shqk,sqhe->skhe", grad_scores, queries, preferred_element_type=jnp.float32) * 0.125
    grad_v = jnp.einsum("shqk,sqhe->skhe", attn_low, grad_context, preferred_element_type=jnp.float32)
    grad_mixed = jnp.concatenate(
        [g.reshape(8 * BLK, HW) for g in (grad_q, grad_k, grad_v)], axis=1
    ).astype(low)
    grad_hidden_one = team_scatter(back_product(grad_mixed, mat_qkv), c, x)
    grad_ln_one, grad_gain_one, grad_shift_one = ln1_pull(grad_hidden_one)
    grad_in = from_teams((grad_resid + grad_ln_one).astype(low), z, c).astype(jnp.float32)

    total = outer_sum(activ, grad_all).astype(low)
    grad_out_w = scatter_zy(total.reshape(YN, ZN, 200, D), y, z)
    grad_out_w = grad_out_w.astype(jnp.float32).reshape(-1)

    total = outer_sum(hidden_two, grad_pre).astype(low)
    total = total.reshape(YN, CN, ZN, XN, 50, D).transpose(0, 2, 1, 3, 4, 5)
    part = team_swap(scatter_zy(total, y, z), c, x)
    grad_fc = part.reshape(CN, XN, 50, YN, ZN, 200).transpose(2, 3, 0, 4, 1, 5)
    grad_fc = grad_fc.astype(jnp.float32).reshape(-1)

    total = outer_sum(context, grad_branch).astype(low)
    total = total.reshape(YN, CN, ZN, XN, 50, D).transpose(1, 3, 0, 2, 4, 5)
    total = pick(total, c) + swap_core(pick(total, 1 - c))
    total = pick(total, x) + swap_x(pick(total, 1 - x))
    grad_proj = scatter_zy(total, y, z).astype(jnp.float32).reshape(-1)

    total = outer_sum(hidden_one, grad_mixed).astype(low)
    total = total.reshape(YN, CN, ZN, XN, 50, 3 * HW).transpose(0, 2, 1, 3, 4, 5)
    part = team_swap(scatter_zy(total, y, z), c, x).reshape(4, 50, 3, HW)
    grad_qkv = jnp.stack([head_join(part[:, :, i]) for i in range(3)], axis=1)
    grad_qkv = grad_qkv.astype(jnp.float32).reshape(-1)

    terms = jnp.sum(grad_mixed.astype(jnp.float32), axis=0).reshape(3, HW)
    here = (jnp.arange(4) == rank).astype(jnp.float32)[:, None, None]
    grad_bq = head_join(here * terms[0][None, None])[0]
    grad_bv = head_join(here * terms[2][None, None])[0]
    fc_terms = jnp.sum(grad_pre.astype(jnp.float32), axis=0).reshape(YN, 1, ZN, 1, 200)
    spot = (jnp.arange(CN) == c)[None, :, None, None, None] & (jnp.arange(XN) == x)[None, None, None, :, None]
    grad_fc_bias = jnp.where(spot, fc_terms, 0.0).reshape(-1)
    front = jnp.concatenate([grad_gain_one, grad_shift_one, grad_bq, grad_bv])
    tail = jnp.concatenate(
        [
            jnp.sum(grad_branch.astype(jnp.float32), axis=0),
            grad_gain_two,
            grad_shift_two,
            grad_fc_bias,
            jnp.sum(grad_full, axis=0),
        ]
    )
    grad_front = lax.psum_scatter(front, AXES, scatter_dimension=0, tiled=True)
    grad_tail = lax.psum_scatter(tail, AXES, scatter_dimension=0, tiled=True)
    return (outputs, grad_in, grad_qkv, grad_proj, grad_fc, grad_out_w, grad_front, grad_tail)


def solution(mesh):
    placed = (
        P(None, "dp", "ctx", None),
        P(None, "dp", "ctx", None),
        P(("dp", "ctx")),
        P(("dp", "ctx")),
        P(("dp", "ctx")),
        P(("dp", "ctx")),
        P(("dp", "ctx")),
    )
    fast = dict(mesh.shape) == {"dp": DP, "ctx": CTX}
    return jax.shard_map(
        fast_shards if fast else shards,
        mesh=mesh,
        in_specs=placed,
        out_specs=(
            P(None, "dp", "ctx", None),
            P(None, "dp", "ctx", None),
            P(("dp", "ctx")),
            P(("dp", "ctx")),
            P(("dp", "ctx")),
            P(("dp", "ctx")),
            P(("dp", "ctx")),
            P(("dp", "ctx")),
        ),
        check_vma=False,
    )
```

```python
import functools

import jax
import jax.numpy as jnp
import numpy as np
from jax import lax
from jax.experimental import pallas as pl
from jax.experimental.pallas import tpu as pltpu
from jax.sharding import PartitionSpec as P

D = 1600
HEADS = 25
HEAD = 64
FF = 6400
MICRO = 2


EPS = 1e-05


def layer_norm(values, gain, shift):
    center = values - jnp.mean(values, axis=-1, keepdims=True)
    spread = jnp.mean(center * center, axis=-1, keepdims=True)
    return center * lax.rsqrt(spread + EPS) * gain + shift


def gelu_tanh(values):
    return jax.nn.gelu(values, approximate=True)


def unpack(gathered):
    packed_qkv, packed_proj, packed_fc, packed_out, packed_small = gathered
    return (
        packed_qkv.reshape(D, 3 * D),
        packed_proj.reshape(D, D),
        packed_fc.reshape(D, FF),
        packed_out.reshape(FF, D),
        packed_small.astype(jnp.float32),
    )


def fetch(w_qkv, w_proj, w_fc, w_out, smalls):
    return unpack(
        (
            lax.all_gather(w_qkv, ("dp", "ctx"), axis=0, tiled=True),
            lax.all_gather(w_proj, ("dp", "ctx"), axis=0, tiled=True),
            lax.all_gather(w_fc, ("dp", "ctx"), axis=0, tiled=True),
            lax.all_gather(w_out, ("dp", "ctx"), axis=0, tiled=True),
            lax.all_gather(smalls, ("dp", "ctx"), axis=0, tiled=True),
        )
    )


def fetch_again(w_qkv, w_proj, w_fc, w_out, smalls):
    return unpack(
        (
            lax.all_gather(w_qkv, ("dp", "ctx"), axis=0, tiled=True),
            lax.all_gather(w_proj, ("dp", "ctx"), axis=0, tiled=True),
            lax.all_gather(w_fc, ("dp", "ctx"), axis=0, tiled=True),
            lax.all_gather(w_out, ("dp", "ctx"), axis=0, tiled=True),
            lax.all_gather(smalls, ("dp", "ctx"), axis=0, tiled=True),
        )
    )


def outer_sum(left, right):
    return lax.dot_general(
        left, right, (((0,), (0,)), ((), ())), preferred_element_type=jnp.float32
    )


def back_product(grad, weight):
    return lax.dot_general(
        grad, weight, (((1,), (1,)), ((), ())), preferred_element_type=jnp.float32
    )


def flat_term(left, right, start, count):
    width = right.shape[1]
    span = count // width + 2
    padded = jnp.pad(left, ((0, 0), (0, span)))
    first_row = start // width
    piece = lax.dynamic_slice_in_dim(padded, first_row, span, 1)
    block = outer_sum(piece, right).astype(jnp.bfloat16).reshape(-1)
    return lax.dynamic_slice_in_dim(block, start, count, 0)


def masked_scores(queries, keys, query_start, key_start):
    scores = (
        jnp.einsum("sqhe,skhe->shqk", queries, keys, preferred_element_type=jnp.float32) * 0.125
    )
    query_pos = query_start + jnp.arange(queries.shape[1])
    key_pos = key_start + jnp.arange(keys.shape[1])
    allowed = query_pos[:, None] >= key_pos[None, :]
    return jnp.where(allowed[None, None], scores, -1e30)


def segment(small_vals, which):
    return small_vals[which * D : (which + 1) * D]


def shards(inputs, grad_out, w_qkv, w_proj, w_fc, w_out, smalls):
    seqs = inputs.shape[1]
    local_len = inputs.shape[2]
    rows = seqs * local_len
    offset = lax.axis_index("ctx") * local_len
    acc_small = [jnp.zeros((D,), jnp.float32) for _ in range(7)]
    acc_fc_bias = jnp.zeros((FF,), jnp.float32)
    acc_out_bias = jnp.zeros((D,), jnp.float32)
    result_list = []
    grad_list = []
    kept_hidden_one = []
    kept_mixed_grad = []
    kept_context = []
    kept_branch_grad = []
    kept_hidden_two = []
    kept_pre_grad = []
    kept_activ = []
    kept_out_grad = []
    for batch_index in range(MICRO):
        params = fetch(w_qkv, w_proj, w_fc, w_out, smalls)
        mat_qkv, mat_proj, mat_fc, mat_out, small_vals = params
        tokens = inputs[batch_index].astype(jnp.float32).reshape(rows, D)
        hidden_one, ln1_pull = jax.vjp(
            layer_norm, tokens, segment(small_vals, 0), segment(small_vals, 1)
        )
        hidden_one = hidden_one.astype(jnp.bfloat16)
        qkv_bias = jnp.concatenate(
            [segment(small_vals, 2), jnp.zeros((D,), jnp.float32), segment(small_vals, 3)]
        )
        mixed = (
            jnp.dot(hidden_one, mat_qkv, preferred_element_type=jnp.float32) + qkv_bias
        ).astype(jnp.bfloat16)
        queries = mixed[:, :D].reshape(seqs, local_len, HEADS, HEAD)
        keys_local = mixed[:, D : 2 * D].reshape(seqs, local_len, D)
        values_local = mixed[:, 2 * D :].reshape(seqs, local_len, D)
        keys_all, values_all = (
            lax.all_gather(keys_local, "ctx", axis=1, tiled=True),
            lax.all_gather(values_local, "ctx", axis=1, tiled=True),
        )
        keys_all = keys_all.reshape(seqs, -1, HEADS, HEAD)
        values_all = values_all.reshape(seqs, -1, HEADS, HEAD)
        scores = masked_scores(queries, keys_all, offset, 0)
        row_peak = jnp.max(scores, axis=-1, keepdims=True)
        log_total = row_peak + jnp.log(jnp.sum(jnp.exp(scores - row_peak), axis=-1, keepdims=True))
        attn_low = jnp.exp(scores - log_total).astype(jnp.bfloat16)
        context = jnp.einsum(
            "shqk,skhe->sqhe", attn_low, values_all, preferred_element_type=jnp.float32
        )
        context = context.reshape(rows, D).astype(jnp.bfloat16)
        resid = (
            tokens
            + jnp.dot(context, mat_proj, preferred_element_type=jnp.float32)
            + segment(small_vals, 4)
        )
        hidden_two, ln2_pull = jax.vjp(
            layer_norm, resid, segment(small_vals, 5), segment(small_vals, 6)
        )
        hidden_two = hidden_two.astype(jnp.bfloat16)
        pre_act = (
            jnp.dot(hidden_two, mat_fc, preferred_element_type=jnp.float32)
            + small_vals[7 * D : 7 * D + FF]
        )
        activ, gelu_pull = jax.vjp(gelu_tanh, pre_act)
        activ = activ.astype(jnp.bfloat16)
        result = (
            resid
            + jnp.dot(activ, mat_out, preferred_element_type=jnp.float32)
            + small_vals[7 * D + FF :]
        )
        result_list.append(result.astype(jnp.bfloat16).reshape(seqs, local_len, D))
        back_params = fetch_again(w_qkv, w_proj, w_fc, w_out, smalls)
        mat_qkv, mat_proj, mat_fc, mat_out, small_vals = back_params
        grad_low = grad_out[batch_index].reshape(rows, D)
        grad_full = grad_low.astype(jnp.float32)
        acc_out_bias = acc_out_bias + jnp.sum(grad_full, axis=0)
        grad_act = back_product(grad_low, mat_out)
        (grad_pre,) = gelu_pull(grad_act)
        grad_pre = grad_pre.astype(jnp.bfloat16)
        acc_fc_bias = acc_fc_bias + jnp.sum(grad_pre.astype(jnp.float32), axis=0)
        grad_hidden_two = back_product(grad_pre, mat_fc)
        grad_ln_two, grad_gain_two, grad_shift_two = ln2_pull(grad_hidden_two)
        acc_small[5] = acc_small[5] + grad_gain_two
        acc_small[6] = acc_small[6] + grad_shift_two
        grad_resid = grad_full + grad_ln_two
        grad_branch = grad_resid.astype(jnp.bfloat16)
        acc_small[4] = acc_small[4] + jnp.sum(grad_branch.astype(jnp.float32), axis=0)
        grad_context = (
            back_product(grad_branch, mat_proj)
            .astype(jnp.bfloat16)
            .reshape(seqs, local_len, HEADS, HEAD)
        )
        scores = masked_scores(queries, keys_all, offset, 0)
        attn_prob = jnp.exp(scores - log_total)
        grad_attn = jnp.einsum(
            "sqhe,skhe->shqk", grad_context, values_all, preferred_element_type=jnp.float32
        )
        row_delta = jnp.sum(attn_prob * grad_attn, axis=-1, keepdims=True)
        grad_scores = (attn_prob * (grad_attn - row_delta)).astype(jnp.bfloat16)
        grad_queries = (
            jnp.einsum("shqk,skhe->sqhe", grad_scores, keys_all, preferred_element_type=jnp.float32)
            * 0.125
        )
        query_all, dctx_all = (
            lax.all_gather(queries.reshape(seqs, local_len, D), "ctx", axis=1, tiled=True),
            lax.all_gather(grad_context.reshape(seqs, local_len, D), "ctx", axis=1, tiled=True),
        )
        lse_all, delta_all = (
            lax.all_gather(jnp.transpose(log_total[..., 0], (0, 2, 1)), "ctx", axis=1, tiled=True),
            lax.all_gather(jnp.transpose(row_delta[..., 0], (0, 2, 1)), "ctx", axis=1, tiled=True),
        )
        query_all = query_all.reshape(seqs, -1, HEADS, HEAD)
        dctx_all = dctx_all.reshape(seqs, -1, HEADS, HEAD)
        lse_all = jnp.transpose(lse_all, (0, 2, 1))[..., None]
        delta_all = jnp.transpose(delta_all, (0, 2, 1))[..., None]
        own_keys = keys_local.reshape(seqs, local_len, HEADS, HEAD)
        own_values = values_local.reshape(seqs, local_len, HEADS, HEAD)
        col_scores = masked_scores(query_all, own_keys, 0, offset)
        col_prob = jnp.exp(col_scores - lse_all)
        col_dattn = jnp.einsum(
            "sqhe,skhe->shqk", dctx_all, own_values, preferred_element_type=jnp.float32
        )
        col_ds = (col_prob * (col_dattn - delta_all)).astype(jnp.bfloat16)
        grad_keys = (
            jnp.einsum("shqk,sqhe->skhe", col_ds, query_all, preferred_element_type=jnp.float32)
            * 0.125
        )
        grad_values = jnp.einsum(
            "shqk,sqhe->skhe",
            col_prob.astype(jnp.bfloat16),
            dctx_all,
            preferred_element_type=jnp.float32,
        )
        grad_mixed = jnp.concatenate(
            [
                grad_queries.reshape(rows, D),
                grad_keys.reshape(rows, D),
                grad_values.reshape(rows, D),
            ],
            axis=1,
        ).astype(jnp.bfloat16)
        bias_terms = jnp.sum(grad_mixed.astype(jnp.float32), axis=0)
        acc_small[2] = acc_small[2] + bias_terms[:D]
        acc_small[3] = acc_small[3] + bias_terms[2 * D :]
        grad_hidden_one = back_product(grad_mixed, mat_qkv)
        grad_ln_one, grad_gain_one, grad_shift_one = ln1_pull(grad_hidden_one)
        acc_small[0] = acc_small[0] + grad_gain_one
        acc_small[1] = acc_small[1] + grad_shift_one
        grad_list.append((grad_resid + grad_ln_one).reshape(seqs, local_len, D))
        kept_hidden_one.append(hidden_one)
        kept_mixed_grad.append(grad_mixed)
        kept_context.append(context)
        kept_branch_grad.append(grad_branch)
        kept_hidden_two.append(hidden_two)
        kept_pre_grad.append(grad_pre)
        kept_activ.append(activ)
        kept_out_grad.append(grad_low)
    front_grads = jnp.concatenate(acc_small[0:4])
    tail_grads = jnp.concatenate(acc_small[4:7] + [acc_fc_bias, acc_out_bias])
    grad_qkv = lax.psum_scatter(
        flat_term(
            jnp.concatenate(kept_hidden_one),
            jnp.concatenate(kept_mixed_grad),
            jnp.int32(0),
            lax.axis_size(("dp", "ctx")) * w_qkv.shape[0],
        ),
        ("dp", "ctx"),
        scatter_dimension=0,
        tiled=True,
    ).astype(jnp.float32)
    grad_proj = lax.psum_scatter(
        flat_term(
            jnp.concatenate(kept_context),
            jnp.concatenate(kept_branch_grad),
            jnp.int32(0),
            lax.axis_size(("dp", "ctx")) * w_proj.shape[0],
        ),
        ("dp", "ctx"),
        scatter_dimension=0,
        tiled=True,
    ).astype(jnp.float32)
    grad_fc = lax.psum_scatter(
        flat_term(
            jnp.concatenate(kept_hidden_two),
            jnp.concatenate(kept_pre_grad),
            jnp.int32(0),
            lax.axis_size(("dp", "ctx")) * w_fc.shape[0],
        ),
        ("dp", "ctx"),
        scatter_dimension=0,
        tiled=True,
    ).astype(jnp.float32)
    grad_out_w = lax.psum_scatter(
        flat_term(
            jnp.concatenate(kept_activ),
            jnp.concatenate(kept_out_grad),
            jnp.int32(0),
            lax.axis_size(("dp", "ctx")) * w_out.shape[0],
        ),
        ("dp", "ctx"),
        scatter_dimension=0,
        tiled=True,
    ).astype(jnp.float32)
    grad_front, grad_tail = (
        lax.psum_scatter(front_grads, ("dp", "ctx"), scatter_dimension=0, tiled=True),
        lax.psum_scatter(tail_grads, ("dp", "ctx"), scatter_dimension=0, tiled=True),
    )
    return (
        jnp.stack(result_list),
        jnp.stack(grad_list),
        grad_qkv,
        grad_proj,
        grad_fc,
        grad_out_w,
        grad_front,
        grad_tail,
    )


DP, CTX = 4, 8
YN, CN, ZN, XN = 2, 2, 4, 2
SLOTS = 7
HW = SLOTS * HEAD
QW = 3 * HW
STARTS = (0, 7, 13, 19)
COUNTS = (7, 6, 6, 6)
BLK = 128
SEQ = 8 * BLK
PIECE = 208
WIDE = 8 * PIECE
PB = 64
PROJ = 32 * PB
LOW = jnp.bfloat16
F32 = jnp.float32
VMEM_BYTES = 60 * 1024 * 1024
ANY = pl.BlockSpec(memory_space=pl.ANY)
VM = pl.BlockSpec(memory_space=pltpu.VMEM)


def here():
    dp, ctx = lax.axis_index("dp"), lax.axis_index("ctx")
    return dp // CN, dp % CN, ctx // XN, ctx % XN


def device(y, c, z, x):
    return (y * CN + c, z * XN + x)


class Wires:
    def __init__(self, sems):
        self.sems, self.used = sems, 0

    def one(self):
        self.used += 1
        return self.sems.at[self.used - 1]

    def far(self, source, target, where):
        return pltpu.make_async_remote_copy(
            src_ref=source,
            dst_ref=target,
            send_sem=self.one(),
            recv_sem=self.one(),
            device_id=where,
            device_id_type=pl.DeviceIdType.MESH,
        )

    def near(self, source, target):
        return pltpu.make_async_copy(source, target, self.one())


def signal(where):
    pl.semaphore_signal(
        pltpu.get_barrier_semaphore(), inc=1, device_id=where, device_id_type=pl.DeviceIdType.MESH
    )


def team_peers(y, c, z, x):
    return [device(y, 1 - c, z, x), device(y, c, z, 1 - x), device(y, 1 - c, z, 1 - x)]


def grid_peers(y, c, z, x):
    ring = [device(y, c, lax.rem(z + k, ZN), x) for k in range(1, ZN)]
    return ring + [device(1 - y, c, z, x)]


def meet(peers):
    for peer in peers:
        signal(peer)
    pl.semaphore_wait(pltpu.get_barrier_semaphore(), len(peers))


def call(body, name, ident, ins, outs, in_specs, out_specs, scratch, sems, cost=None):
    return pl.pallas_call(
        body,
        out_shape=[jax.ShapeDtypeStruct(s, d) for s, d in outs],
        in_specs=in_specs,
        out_specs=out_specs,
        scratch_shapes=list(scratch) + [pltpu.SemaphoreType.DMA((sems,))],
        compiler_params=pltpu.CompilerParams(
            collective_id=ident, has_side_effects=True, vmem_limit_bytes=VMEM_BYTES
        ),
        name=name,
    )(*ins)


class Gather:
    def __init__(self, wires, piece, whole, spot):
        y, c, z, x = self.spot = spot
        self.z = z
        self.across = device(1 - y, c, z, x)
        up = device(y, c, lax.min(z + 1, ZN - 1), x)
        down = device(y, c, lax.max(z - 1, 0), x)
        self.local = wires.near(piece, whole.at[y, z])
        self.mine = wires.far(piece, whole.at[y, z], self.across)
        self.ups, self.downs, self.from_low, self.from_high = [], [], [], []
        for turn in range(1, ZN):
            low = lax.max(z - (turn - 1), 0)
            high = lax.min(z + (turn - 1), ZN - 1)
            source = piece if turn == 1 else whole.at[y, low]
            self.ups.append(wires.far(source, whole.at[y, low], up))
            source = piece if turn == 1 else whole.at[y, high]
            self.downs.append(wires.far(source, whole.at[y, high], down))
            low = lax.max(z - turn, 0)
            high = lax.min(z + turn, ZN - 1)
            self.from_low.append(wires.far(whole.at[y, low], whole.at[y, low], self.across))
            self.from_high.append(wires.far(whole.at[y, high], whole.at[y, high], self.across))

    def send_up(self, turn):
        return (self.z >= turn - 1) & (self.z < ZN - 1)

    def send_down(self, turn):
        return (self.z <= ZN - turn) & (self.z > 0)

    def start(self):
        self.local.start()
        self.mine.start()
        pl.when(self.send_up(1))(self.ups[0].start)
        pl.when(self.send_down(1))(self.downs[0].start)

    def step(self, turn):
        @pl.when(self.z >= turn)
        def _():
            self.ups[turn - 1].wait_recv()
            if turn < ZN - 1:
                pl.when(self.send_up(turn + 1))(self.ups[turn].start)
            self.from_low[turn - 1].start()

        @pl.when(self.z + turn <= ZN - 1)
        def _():
            self.downs[turn - 1].wait_recv()
            if turn < ZN - 1:
                pl.when(self.send_down(turn + 1))(self.downs[turn].start)
            self.from_high[turn - 1].start()

    def finish(self):
        self.local.wait()
        self.mine.wait()
        for turn in range(1, ZN):
            pl.when(self.send_up(turn))(self.ups[turn - 1].wait_send)
            pl.when(self.send_down(turn))(self.downs[turn - 1].wait_send)
            pl.when(self.z >= turn)(self.from_low[turn - 1].wait)
            pl.when(self.z + turn <= ZN - 1)(self.from_high[turn - 1].wait)


GATHER_SEMS = 1 + 2 + 2 * 4 * 3


class Scatter:
    def __init__(self, wires, parts, landed, arrived, spot):
        y, c, z, x = spot
        self.y, self.z = y, z
        self.parts, self.landed, self.arrived = parts, landed, arrived
        across = device(1 - y, c, z, x)
        self.order = [lax.rem(z + k, ZN) for k in (1, 2, 3, 0)]
        self.over = [wires.far(parts.at[1 - y, o], landed.at[o], across) for o in self.order]
        self.along = [
            wires.far(landed.at[o], arrived.at[k], device(y, c, o, x))
            for k, o in enumerate(self.order[:3])
        ]

    def start(self):
        for copy in self.over:
            copy.start()

    def step(self, k):
        o = self.order[k]
        self.over[k].wait_recv()
        self.landed[o] = (self.landed[o].astype(F32) + self.parts[self.y, o].astype(F32)).astype(LOW)
        self.along[k].start()

    def finish(self, total):
        self.over[3].wait_recv()
        summed = self.landed[self.z].astype(F32) + self.parts[self.y, self.z].astype(F32)
        for k in range(3):
            self.along[k].wait_recv()
            summed = summed + self.arrived[k].astype(F32)
        total[...] = summed.astype(total.dtype)
        for copy in self.over + self.along:
            copy.wait_send()


SCATTER_SEMS = 2 * 7


class TeamGather:
    def __init__(self, wires, block, whole, spot):
        y, c, z, x = spot
        mate, beside = device(y, 1 - c, z, x), device(y, c, z, 1 - x)
        self.local = [wires.near(block.at[s], whole.at[c, s, x]) for s in range(2)]
        self.to_mate = [wires.far(block.at[s], whole.at[c, s, x], mate) for s in range(2)]
        self.to_side = [wires.far(block.at[s], whole.at[c, s, x], beside) for s in range(2)]
        self.relay = [
            wires.far(whole.at[c, s, 1 - x], whole.at[c, s, 1 - x], mate) for s in range(2)
        ]

    def start(self):
        for copy in self.to_side + self.to_mate + self.local:
            copy.start()

    def step(self, s):
        self.to_side[s].wait_recv()
        self.relay[s].start()

    def finish(self):
        for copy in self.local + self.to_mate + self.relay:
            copy.wait()
        for copy in self.to_side:
            copy.wait_send()


TEAM_GATHER_SEMS = 2 + 2 * 6


class TeamSwap:
    def __init__(self, wires, source, target, spot):
        y, c, z, x = spot
        self.local = wires.near(source(c, x), target(c, x))
        self.copies = [
            wires.far(source(p, q), target(c, x), device(y, p, z, q))
            for p, q in ((c, 1 - x), (1 - c, 1 - x), (1 - c, x))
        ]

    def start(self):
        for copy in self.copies + [self.local]:
            copy.start()

    def finish(self):
        for copy in self.copies + [self.local]:
            copy.wait()


TEAM_SWAP_SEMS = 1 + 2 * 3


class TeamScatter:
    def __init__(self, wires, parts, landed, leaving, arrived, spot):
        y, c, z, x = spot
        self.c, self.x = c, x
        self.parts, self.landed, self.leaving, self.arrived = parts, landed, leaving, arrived
        mate, beside = device(y, 1 - c, z, x), device(y, c, z, 1 - x)
        self.to_mate = [wires.far(parts.at[1 - c, s], landed.at[s], mate) for s in range(2)]
        self.to_side = [wires.far(leaving.at[s], arrived.at[s], beside) for s in range(2)]

    def start(self):
        for copy in self.to_mate:
            copy.start()

    def step(self, s):
        self.to_mate[s].wait_recv()
        far = 1 - self.x
        self.leaving[s] = (
            self.landed[s, far].astype(F32) + self.parts[self.c, s, far].astype(F32)
        ).astype(LOW)
        self.to_side[s].start()

    def finish(self, total):
        for s in range(2):
            self.to_side[s].wait_recv()
            total[s] = (
                self.landed[s, self.x].astype(F32)
                + self.parts[self.c, s, self.x].astype(F32)
                + self.arrived[s].astype(F32)
            )
        for copy in self.to_mate + self.to_side:
            copy.wait_send()


TEAM_SCATTER_SEMS = 2 * 4


def team_scatter_scratch(width):
    return [
        pltpu.VMEM((2, 2, BLK, width), LOW),
        pltpu.VMEM((2, BLK, width), LOW),
        pltpu.VMEM((2, BLK, width), LOW),
    ]


def scatter_scratch(rows, width):
    return [pltpu.VMEM((ZN, rows, width), LOW), pltpu.VMEM((ZN - 1, rows, width), LOW)]


class Tokens:
    def __init__(self, wires, source, target, spot, back):
        y, c, z, x = spot
        self.own, self.local, self.copies, self.peers = [], [], [], []
        for k in range(2):
            if not back:
                m = lax.rem(z + k, 2)
                goal_c, goal_z = z // 2, 2 * m + c
                block, landing = source.at[m], target.at[lax.rem(z, 2)]
            else:
                m = z // 2
                s = lax.rem(m + k, 2)
                goal_c, goal_z = lax.rem(z, 2), 2 * c + s
                block, landing = source.at[s], target.at[m]
            goal = device(y, goal_c, goal_z, x)
            stays = (goal_c == c) & (goal_z == z)
            self.own.append(stays)
            self.peers.append(goal)
            self.local.append(wires.near(block, landing))
            self.copies.append(wires.far(block, landing, goal))

    def start(self):
        for stays, local, copy in zip(self.own, self.local, self.copies):
            pl.when(stays)(local.start)
            pl.when(jnp.logical_not(stays))(copy.start)

    def finish(self):
        for stays, local, copy in zip(self.own, self.local, self.copies):
            pl.when(stays)(local.wait)
            pl.when(jnp.logical_not(stays))(copy.wait)


TOKENS_SEMS = 2 * 3


def token_sources(spot, back):
    y, c, z, x = spot
    found = []
    for k in range(2):
        if back:
            m = lax.rem(z + k, 2)
            goal = (z // 2, 2 * m + c)
        else:
            s = lax.rem(z // 2 + k, 2)
            goal = (lax.rem(z, 2), 2 * c + s)
        found.append((device(y, goal[0], goal[1], x), (goal[0] == c) & (goal[1] == z)))
    return found


def meet_tokens(peers, spot, back):
    for peer in peers:
        signal(peer)
    for source, stays in token_sources(spot, back):
        pl.when(jnp.logical_not(stays))(functools.partial(signal, source))
    leaving = sum(jnp.where(stays, 0, 1) for _, stays in token_sources(spot, not back))
    pl.semaphore_wait(pltpu.get_barrier_semaphore(), len(peers) + leaving)


def prologue(inputs, units_qkv, units_fc, small, tokens, got_qkv, got_fc, smalls, sems):
    spot = y, c, z, x = here()
    wires = Wires(sems)
    meet_tokens(team_peers(*spot) + grid_peers(*spot), spot, False)
    first = TeamSwap(
        wires, lambda p, q: small, lambda p, q: smalls.at[y, z, p * XN + q], spot
    )
    qkv = TeamSwap(
        wires, lambda p, q: units_qkv.at[p * XN + q], lambda p, q: got_qkv.at[p * XN + q], spot
    )
    fc = TeamSwap(
        wires, lambda p, q: units_fc.at[p * XN + q], lambda p, q: got_fc.at[p * XN + q], spot
    )
    move = Tokens(wires, inputs, tokens, spot, False)
    first.start()
    move.start()
    qkv.start()
    fc.start()
    first.finish()
    column = [
        wires.far(smalls.at[y, z], smalls.at[y, z], device(y, c, lax.rem(z + k, ZN), x))
        for k in range(1, ZN)
    ]
    for copy in column:
        copy.start()
    for copy in column:
        copy.wait()
    over = wires.far(smalls.at[y], smalls.at[y], device(1 - y, c, z, x))
    over.start()
    over.wait()
    qkv.finish()
    fc.finish()
    move.finish()


def gather_all(
    hidden, grads, piece_qkv, piece_fc, piece_out, piece_proj,
    hidden_all, cotangent, all_qkv, all_fc, all_out, all_proj, sems,
):
    spot = y, c, z, x = here()
    wires = Wires(sems)
    rank = c * XN + x
    meet_tokens(team_peers(*spot) + grid_peers(*spot), spot, False)
    team = TeamGather(wires, hidden, hidden_all, spot)
    qkv = Gather(wires, piece_qkv, all_qkv, spot)
    proj = Gather(wires, piece_proj, all_proj.at[rank], spot)
    fc = Gather(wires, piece_fc, all_fc, spot)
    out = Gather(wires, piece_out, all_out, spot)
    move = Tokens(wires, grads, cotangent, spot, False)
    side = wires.far(all_proj.at[rank], all_proj.at[rank], device(y, c, z, 1 - x))
    other = c * XN + 1 - x
    mate = device(y, 1 - c, z, x)
    relay = [
        wires.far(all_proj.at[r], all_proj.at[r], mate) for r in (rank, other)
    ]
    team.start()
    jobs = [qkv, proj, fc, out]
    for job in jobs:
        job.start()
        if job is qkv:
            team.step(0)
            team.step(1)
        for turn in range(1, ZN):
            job.step(turn)
        if job is fc:
            proj.finish()
            side.start()
            relay[0].start()
    move.start()
    side.wait_recv()
    relay[1].start()
    for job in (qkv, fc, out):
        job.finish()
    team.finish()
    move.finish()
    side.wait_send()
    for copy in relay:
        copy.wait()


def swap_context(context, got, sems):
    spot = y, c, z, x = here()
    wires = Wires(sems)
    meet(team_peers(*spot))
    copies = [
        TeamSwap(wires, lambda p, q: context.at[p, s, q], lambda p, q: got.at[p * XN + q, s], spot)
        for s in range(2)
    ]
    for copy in copies:
        copy.start()
    for copy in copies:
        copy.finish()


def gather_two(left, right, left_all, right_all, sems):
    spot = here()
    wires = Wires(sems)
    meet(team_peers(*spot))
    one = TeamGather(wires, left, left_all, spot)
    two = TeamGather(wires, right, right_all, spot)
    one.start()
    one.step(0)
    one.step(1)
    two.start()
    two.step(0)
    two.step(1)
    one.finish()
    two.finish()


def middle(
    result_part, hidden_part, grad_out_part, grad_fc_part,
    result, hidden, grad_out_w, grad_fc,
    l1, s1, a1, l2, s2, a2, l3, a3, l4, a4, sems,
):
    spot = here()
    wires = Wires(sems)
    meet(team_peers(*spot) + grid_peers(*spot))
    second = TeamScatter(wires, hidden_part, l2, s2, a2, spot)
    first = TeamScatter(wires, result_part, l1, s1, a1, spot)
    out = Scatter(wires, grad_out_part, l3, a3, spot)
    fc = Scatter(wires, grad_fc_part, l4, a4, spot)
    out.start()
    second.start()
    second.step(0)
    second.step(1)
    out.step(0)
    first.start()
    out.step(1)
    first.step(0)
    first.step(1)
    second.finish(hidden)
    out.step(2)
    fc.start()
    first.finish(result)
    out.finish(grad_out_w)
    fc.step(0)
    fc.step(1)
    fc.step(2)
    fc.finish(grad_fc)


def swap_grad_context(parts, whole, sems):
    spot = y, c, z, x = here()
    wires = Wires(sems)
    meet(team_peers(*spot))
    copies = [
        TeamSwap(wires, lambda p, q: parts.at[p * XN + q, s], lambda p, q: whole.at[p, s, q], spot)
        for s in range(2)
    ]
    for copy in copies:
        copy.start()
    for copy in copies:
        copy.finish()


def last(
    hidden_part, grad_qkv_part, grad_proj_part, result,
    hidden, grad_qkv, grad_proj, outputs,
    l1, s1, a1, l2, a2, l3, a3, pm, pk, px, sems,
):
    spot = y, c, z, x = here()
    wires = Wires(sems)
    meet_tokens(team_peers(*spot) + grid_peers(*spot), spot, True)
    first = TeamScatter(wires, hidden_part, l1, s1, a1, spot)
    qkv = Scatter(wires, grad_qkv_part, l2, a2, spot)
    to_mate = wires.far(grad_proj_part.at[1 - c], pm, device(y, 1 - c, z, x))
    to_side = wires.far(pm.at[1 - x], px, device(y, c, z, 1 - x))
    proj = Scatter(wires, pk, l3, a3, spot)
    move = Tokens(wires, result, outputs, spot, True)
    qkv.start()
    to_mate.start()
    first.start()
    to_mate.wait_recv()
    pm[1 - x] = (pm[1 - x].astype(F32) + grad_proj_part[c, 1 - x].astype(F32)).astype(LOW)
    to_side.start()
    first.step(0)
    first.step(1)
    qkv.step(0)
    qkv.step(1)
    qkv.step(2)
    to_side.wait_recv()
    pk[...] = (pm[x].astype(F32) + grad_proj_part[c, x].astype(F32) + px[...].astype(F32)).astype(LOW)
    proj.start()
    move.start()
    first.finish(hidden)
    qkv.finish(grad_qkv)
    proj.step(0)
    proj.step(1)
    proj.step(2)
    proj.finish(grad_proj)
    move.finish()
    to_mate.wait_send()
    to_side.wait_send()


def epilogue(
    grads, units_qkv, units_fc, small, grad_in, got_qkv, got_fc, total, by_y, by_z, by_team, sems
):
    spot = y, c, z, x = here()
    wires = Wires(sems)
    meet_tokens(team_peers(*spot) + grid_peers(*spot), spot, True)
    move = Tokens(wires, grads, grad_in, spot, True)
    qkv = TeamSwap(
        wires, lambda p, q: units_qkv.at[p * XN + q], lambda p, q: got_qkv.at[p * XN + q], spot
    )
    fc = TeamSwap(
        wires, lambda p, q: units_fc.at[p * XN + q], lambda p, q: got_fc.at[p * XN + q], spot
    )
    over = wires.far(small.at[1 - y], by_y, device(1 - y, c, z, x))
    over.start()
    move.start()
    qkv.start()
    fc.start()
    over.wait()
    by_y[...] = by_y[...] + small[y]
    column = [
        wires.far(by_y.at[lax.rem(z + k, ZN)], by_z.at[k - 1], device(y, c, lax.rem(z + k, ZN), x))
        for k in range(1, ZN)
    ]
    for copy in column:
        copy.start()
    for copy in column:
        copy.wait()
    by_z[3] = by_y[z] + by_z[0] + by_z[1] + by_z[2]
    team = [
        wires.far(by_z.at[3, p * XN + q], by_team.at[i], device(y, p, z, q))
        for i, (p, q) in enumerate(((c, 1 - x), (1 - c, 1 - x), (1 - c, x)))
    ]
    for copy in team:
        copy.start()
    for copy in team:
        copy.wait()
    total[...] = by_z[3, c * XN + x] + by_team[0] + by_team[1] + by_team[2]
    qkv.finish()
    fc.finish()
    move.finish()


QB = 256


def attend(mixed, context, totals):
    for head in range(SLOTS):
        lanes = slice(head * HEAD, (head + 1) * HEAD)
        keys = mixed[:, HW + head * HEAD : HW + (head + 1) * HEAD]
        values = mixed[:, 2 * HW + head * HEAD : 2 * HW + (head + 1) * HEAD]
        for block in range(SEQ // QB):
            rows = slice(block * QB, (block + 1) * QB)
            upto = (block + 1) * QB
            scores = (
                lax.dot_general(
                    mixed[rows, lanes], keys[:upto], (((1,), (1,)), ((), ())), preferred_element_type=F32
                )
                * 0.125
            )
            row = lax.broadcasted_iota(jnp.int32, (QB, upto), 0) + block * QB
            col = lax.broadcasted_iota(jnp.int32, (QB, upto), 1)
            scores = jnp.where(row >= col, scores, -1e30)
            peak = jnp.max(scores, axis=1, keepdims=True)
            weights = jnp.exp(scores - peak)
            total = jnp.sum(weights, axis=1, keepdims=True)
            prob = (weights * (1.0 / total)).astype(LOW)
            context[rows, lanes] = jnp.dot(
                prob, values[:upto], preferred_element_type=F32
            ).astype(LOW)
            totals[rows, head : head + 1] = peak + jnp.log(total)


def attend_back(mixed, totals, grads, out, acc_k, acc_v):
    for head in range(SLOTS):
        lanes = slice(head * HEAD, (head + 1) * HEAD)
        lanes_k = slice(HW + head * HEAD, HW + (head + 1) * HEAD)
        lanes_v = slice(2 * HW + head * HEAD, 2 * HW + (head + 1) * HEAD)
        keys = mixed[:, lanes_k]
        values = mixed[:, lanes_v]
        acc_k[...] = jnp.zeros_like(acc_k)
        acc_v[...] = jnp.zeros_like(acc_v)
        for block in range(SEQ // QB):
            rows = slice(block * QB, (block + 1) * QB)
            upto = (block + 1) * QB
            queries = mixed[rows, lanes]
            outer = grads[rows, lanes]
            scores = (
                lax.dot_general(
                    queries, keys[:upto], (((1,), (1,)), ((), ())), preferred_element_type=F32
                )
                * 0.125
            )
            row = lax.broadcasted_iota(jnp.int32, (QB, upto), 0) + block * QB
            col = lax.broadcasted_iota(jnp.int32, (QB, upto), 1)
            scores = jnp.where(row >= col, scores, -1e30)
            prob = jnp.exp(scores - totals[rows, head : head + 1])
            dprob = lax.dot_general(
                outer, values[:upto], (((1,), (1,)), ((), ())), preferred_element_type=F32
            )
            delta = jnp.sum(prob * dprob, axis=1, keepdims=True)
            ds = (prob * (dprob - delta)).astype(LOW)
            out[rows, lanes] = (
                jnp.dot(ds, keys[:upto], preferred_element_type=F32) * 0.125
            ).astype(LOW)
            acc_k[:upto] += outer_sum(ds, queries)
            acc_v[:upto] += outer_sum(prob.astype(LOW), outer)
        out[:, lanes_k] = (acc_k[...] * 0.125).astype(LOW)
        out[:, lanes_v] = acc_v[...].astype(LOW)


def plain(body, name, ins, outs, scratch=()):
    return pl.pallas_call(
        body,
        out_shape=[jax.ShapeDtypeStruct(s, d) for s, d in outs],
        in_specs=[VM] * len(ins),
        out_specs=[VM] * len(outs),
        scratch_shapes=list(scratch),
        compiler_params=pltpu.CompilerParams(vmem_limit_bytes=VMEM_BYTES),
        name=name,
    )(*ins)


def pick(values, index):
    return lax.dynamic_index_in_dim(values, index, 0, keepdims=False)


def pad_to(values, axis, size):
    widths = [(0, 0)] * values.ndim
    widths[axis] = (0, size - values.shape[axis])
    return jnp.pad(values, widths)


def head_parts(columns):
    return jnp.stack(
        [
            pad_to(columns[:, start * HEAD : (start + count) * HEAD], 1, HW)
            for start, count in zip(STARTS, COUNTS)
        ]
    )


def head_join(parts):
    return jnp.concatenate([parts[r][:, : COUNTS[r] * HEAD] for r in range(4)], axis=1)


def feature_order():
    order = -np.ones((YN, ZN, PIECE), np.int32)
    grid = np.arange(D).reshape(YN, CN, ZN, XN, 50).transpose(0, 2, 1, 3, 4)
    order[:, :, :200] = grid.reshape(YN, ZN, 200)
    return order.reshape(-1)


def context_order():
    natural = -np.ones(D, np.int32)
    grid = np.arange(D).reshape(YN, CN, ZN, XN, 50).transpose(1, 3, 0, 2, 4).reshape(32, 50)
    for block in range(32):
        natural[grid[block]] = block * PB + np.arange(50)
    order = -np.ones((4, HW), np.int32)
    for r in range(4):
        width = COUNTS[r] * HEAD
        order[r, :width] = natural[STARTS[r] * HEAD : STARTS[r] * HEAD + width]
    return order.reshape(-1)


def one_hot(order, size):
    rows = lax.broadcasted_iota(jnp.int32, (size, order.shape[0]), 0)
    return (rows == jnp.asarray(order)[None, :]).astype(LOW)


def dot(left, right):
    return jnp.dot(left, right, preferred_element_type=F32)


def ones_row(values):
    return jnp.sum(values.astype(F32), axis=0)


def fast_shards(inputs, grad_out, w_qkv, w_proj, w_fc, w_out, smalls):
    y, c, z, x = here()
    rank = c * XN + x
    to_wide = one_hot(feature_order(), D)
    to_heads = one_hot(context_order(), PROJ)

    rows = w_qkv.reshape(50, 3, D)
    units_qkv = jnp.stack([head_parts(rows[:, i]) for i in range(3)], axis=2).reshape(4, 50, QW)
    units_qkv = pad_to(units_qkv, 1, 64)
    units_fc = w_fc.reshape(50, YN, CN, ZN, XN, 200).transpose(2, 4, 0, 1, 3, 5)
    units_fc = pad_to(pad_to(units_fc, 5, PIECE).reshape(4, 50, WIDE), 1, 64)
    small = pad_to(smalls, 0, 2048).reshape(16, 128)
    tokens, got_qkv, got_fc, smalls_all = call(
        prologue, "prologue", 1,
        (inputs.reshape(MICRO, BLK, D), units_qkv, units_fc, small),
        [((2, BLK, D), LOW), ((4, 64, QW), LOW), ((4, 64, WIDE), LOW), ((YN, ZN, 4, 16, 128), LOW)],
        [ANY] * 4, [ANY] * 4, [], 3 * TEAM_SWAP_SEMS + TOKENS_SEMS + 8,
    )
    small = smalls_all.reshape(YN, ZN, CN, XN, 2048)[..., :600].transpose(0, 2, 1, 3, 4)
    small = small.reshape(-1).astype(F32)
    gain1, shift1, bias_q, bias_v, bias_proj, gain2, shift2 = [segment(small, i) for i in range(7)]
    bias_fc = small[7 * D : 7 * D + FF].reshape(YN, CN, ZN, XN, 200)
    bias_fc = lax.dynamic_index_in_dim(bias_fc, c, 1, keepdims=False)
    bias_fc = lax.dynamic_index_in_dim(bias_fc, x, 2, keepdims=False)
    bias_fc = pad_to(bias_fc, 2, PIECE).reshape(WIDE)
    bias_out = small[7 * D + FF :]
    bias_qkv = jnp.stack(
        [head_parts(bias_q[None]), jnp.zeros((4, 1, HW)), head_parts(bias_v[None])], axis=1
    )
    bias_qkv = pick(bias_qkv, rank).reshape(QW)

    tokens = tokens.reshape(2 * BLK, D).astype(F32)
    hidden_one, ln1_pull = jax.vjp(layer_norm, tokens, gain1, shift1)
    hidden_one = dot(hidden_one.astype(LOW), to_wide).astype(LOW)
    piece_qkv = pad_to(got_qkv[:, :50].reshape(200, QW), 0, PIECE)
    piece_fc = pad_to(got_fc[:, :50].reshape(200, WIDE), 0, PIECE)
    piece_out = pad_to(w_out.reshape(200, D), 0, PIECE)
    piece_proj = pad_to(w_proj.reshape(50, D), 0, PB)
    hidden_one, cotangent, mat_qkv, mat_fc, mat_out, mat_proj = call(
        gather_all, "gather_all", 2,
        (
            hidden_one.reshape(2, BLK, WIDE), grad_out.reshape(MICRO, BLK, D),
            piece_qkv, piece_fc, piece_out, piece_proj,
        ),
        [
            ((2, 2, 2, BLK, WIDE), LOW), ((2, BLK, D), LOW), ((YN, ZN, PIECE, QW), LOW),
            ((YN, ZN, PIECE, WIDE), LOW), ((YN, ZN, PIECE, D), LOW), ((4, YN, ZN, PB, D), LOW),
        ],
        [ANY] * 6, [ANY] * 6, [], TEAM_GATHER_SEMS + TOKENS_SEMS + 4 * GATHER_SEMS + 6,
    )
    hidden_one = hidden_one.reshape(SEQ, WIDE)
    mat_qkv = mat_qkv.reshape(WIDE, QW)
    mat_fc = mat_fc.reshape(WIDE, WIDE)
    mat_out = mat_out.reshape(WIDE, D)
    mat_proj = mat_proj.reshape(PROJ, D)

    mixed = (dot(hidden_one, mat_qkv) + bias_qkv).astype(LOW)
    context, totals = plain(
        attend, "attend", (mixed,), [((SEQ, HW), LOW), ((SEQ, SLOTS), F32)]
    )
    (got,) = call(
        swap_context, "swap_context", 3, (context.reshape(2, 2, 2, BLK, HW),),
        [((4, 2, BLK, HW), LOW)], [ANY], [ANY], [], 2 * TEAM_SWAP_SEMS,
    )
    got = got.reshape(4, 2 * BLK, HW)
    context = jnp.concatenate([got[r] for r in range(4)], axis=1)
    context = back_product(context, to_heads).astype(LOW)
    resid = tokens + dot(context, mat_proj) + bias_proj
    hidden_two, ln2_pull = jax.vjp(layer_norm, resid, gain2, shift2)
    hidden_two = dot(hidden_two.astype(LOW), to_wide).astype(LOW)
    hidden_two, grad_all = call(
        gather_two, "gather_two", 4, (hidden_two.reshape(2, BLK, WIDE), cotangent),
        [((2, 2, 2, BLK, WIDE), LOW), ((2, 2, 2, BLK, D), LOW)],
        [ANY] * 2, [ANY] * 2, [], 2 * TEAM_GATHER_SEMS,
    )
    hidden_two = hidden_two.reshape(SEQ, WIDE)
    grad_all = grad_all.reshape(SEQ, D)
    pre_act = dot(hidden_two, mat_fc) + bias_fc
    activ, gelu_pull = jax.vjp(gelu_tanh, pre_act)
    activ = activ.astype(LOW)
    result_part = dot(activ, mat_out).astype(LOW)
    (grad_pre,) = gelu_pull(back_product(grad_all, mat_out))
    grad_pre = grad_pre.astype(LOW)
    hidden_part = back_product(grad_pre, mat_fc).astype(LOW)
    grad_out_part = outer_sum(activ, grad_all).astype(LOW)
    grad_fc_part = outer_sum(hidden_two, grad_pre).astype(LOW)
    result, grad_hidden_two, grad_out_w, grad_fc = call(
        middle, "middle", 5,
        (
            result_part.reshape(2, 2, 2, BLK, D), hidden_part.reshape(2, 2, 2, BLK, WIDE),
            grad_out_part.reshape(YN, ZN, PIECE, D), grad_fc_part.reshape(YN, ZN, PIECE, WIDE),
        ),
        [((2, BLK, D), F32), ((2, BLK, WIDE), F32), ((PIECE, D), F32), ((PIECE, WIDE), LOW)],
        [VM] * 4, [VM] * 4,
        team_scatter_scratch(D) + team_scatter_scratch(WIDE)
        + scatter_scratch(PIECE, D) + scatter_scratch(PIECE, WIDE),
        2 * TEAM_SCATTER_SEMS + 2 * SCATTER_SEMS,
    )
    result = (resid + result.reshape(2 * BLK, D) + bias_out).astype(LOW)
    grad_out_w = grad_out_w[:200].reshape(-1)

    grad_full = cotangent.reshape(2 * BLK, D).astype(F32)
    grad_hidden_two = back_product(grad_hidden_two.reshape(2 * BLK, WIDE).astype(LOW), to_wide)
    grad_ln_two, grad_gain_two, grad_shift_two = ln2_pull(grad_hidden_two)
    grad_resid = grad_full + grad_ln_two
    grad_branch = grad_resid.astype(LOW)
    grad_context = back_product(grad_branch, mat_proj).astype(LOW)
    grad_context = dot(grad_context, to_heads).astype(LOW)
    grad_context = jnp.stack(
        [grad_context[:, r * HW : (r + 1) * HW] for r in range(4)]
    ).reshape(4, 2, BLK, HW)
    (grad_context,) = call(
        swap_grad_context, "swap_grad_context", 6, (grad_context,),
        [((2, 2, 2, BLK, HW), LOW)], [ANY], [ANY], [], 2 * TEAM_SWAP_SEMS,
    )
    (grad_mixed,) = plain(
        attend_back, "attend_back", (mixed, totals, grad_context.reshape(SEQ, HW)),
        [((SEQ, QW), LOW)], [pltpu.VMEM((SEQ, HEAD), F32)] * 2,
    )
    hidden_part = back_product(grad_mixed, mat_qkv).astype(LOW)
    grad_qkv_part = outer_sum(hidden_one, grad_mixed).astype(LOW)
    grad_proj_part = outer_sum(context, grad_branch).astype(LOW)
    grad_hidden_one, grad_qkv, grad_proj, outputs = call(
        last, "last", 7,
        (
            hidden_part.reshape(2, 2, 2, BLK, WIDE), grad_qkv_part.reshape(YN, ZN, PIECE, QW),
            grad_proj_part.reshape(CN, XN, YN, ZN, PB, D), result.reshape(2, BLK, D),
        ),
        [((2, BLK, WIDE), F32), ((PIECE, QW), LOW), ((PB, D), F32), ((2, BLK, D), LOW)],
        [VM, VM, VM, ANY], [VM, VM, VM, ANY],
        team_scatter_scratch(WIDE) + scatter_scratch(PIECE, QW) + scatter_scratch(PB, D)
        + [
            pltpu.VMEM((XN, YN, ZN, PB, D), LOW),
            pltpu.VMEM((YN, ZN, PB, D), LOW),
            pltpu.VMEM((YN, ZN, PB, D), LOW),
        ],
        TEAM_SCATTER_SEMS + 2 * SCATTER_SEMS + TOKENS_SEMS + 4,
    )
    grad_hidden_one = back_product(grad_hidden_one.reshape(2 * BLK, WIDE).astype(LOW), to_wide)
    grad_ln_one, grad_gain_one, grad_shift_one = ln1_pull(grad_hidden_one)
    grad_in = (grad_resid + grad_ln_one).astype(LOW)
    grad_proj = grad_proj[:50].reshape(-1)

    terms = ones_row(grad_mixed).reshape(3, HW)
    mine = (jnp.arange(4) == rank).astype(F32)[:, None, None]
    grad_bq = head_join(mine * terms[0][None, None])[0]
    grad_bv = head_join(mine * terms[2][None, None])[0]
    fc_terms = ones_row(grad_pre).reshape(YN, 1, ZN, 1, PIECE)[..., :200]
    spot = (jnp.arange(CN) == c)[None, :, None, None, None] & (jnp.arange(XN) == x)[
        None, None, None, :, None
    ]
    grad_fc_bias = jnp.where(spot, fc_terms, 0.0).reshape(-1)
    front = jnp.concatenate([grad_gain_one, grad_shift_one, grad_bq, grad_bv])
    tail = jnp.concatenate(
        [
            ones_row(grad_branch), grad_gain_two, grad_shift_two, grad_fc_bias,
            jnp.sum(grad_full, axis=0),
        ]
    )
    small = jnp.concatenate([front.reshape(32, 200), tail.reshape(32, 400)], axis=1)
    small = pad_to(small, 1, 1024).reshape(YN, CN, ZN, XN, 8, 128).transpose(0, 2, 1, 3, 4, 5)
    units_qkv = pad_to(grad_qkv[:200].reshape(4, 50, QW), 1, 64)
    units_fc = pad_to(grad_fc[:200].reshape(4, 50, WIDE), 1, 64)
    grad_in, got_qkv, got_fc, total = call(
        epilogue, "epilogue", 8,
        (grad_in.reshape(2, BLK, D), units_qkv, units_fc, small.reshape(YN, ZN, 4, 8, 128)),
        [((MICRO, BLK, D), LOW), ((4, 64, QW), LOW), ((4, 64, WIDE), LOW), ((8, 128), F32)],
        [ANY, ANY, ANY, VM], [ANY, ANY, ANY, VM],
        [pltpu.VMEM((ZN, 4, 8, 128), F32), pltpu.VMEM((4, 4, 8, 128), F32), pltpu.VMEM((3, 8, 128), F32)],
        2 * TEAM_SWAP_SEMS + TOKENS_SEMS + 14,
    )
    parts = got_qkv[:, :50].reshape(4, 50, 3, HW)
    grad_qkv = jnp.stack([head_join(parts[:, :, i]) for i in range(3)], axis=1)
    grad_qkv = grad_qkv.astype(F32).reshape(-1)
    grad_fc = got_fc[:, :50].reshape(CN, XN, 50, YN, ZN, PIECE)[..., :200]
    grad_fc = grad_fc.transpose(2, 3, 0, 4, 1, 5).astype(F32).reshape(-1)
    total = total.reshape(-1)
    return (
        outputs[:, None],
        grad_in.astype(F32)[:, None],
        grad_qkv,
        grad_proj,
        grad_fc,
        grad_out_w,
        total[:200],
        total[200:600],
    )


def solution(mesh):
    placed = (
        P(None, "dp", "ctx", None),
        P(None, "dp", "ctx", None),
        P(("dp", "ctx")),
        P(("dp", "ctx")),
        P(("dp", "ctx")),
        P(("dp", "ctx")),
        P(("dp", "ctx")),
    )
    fast = dict(mesh.shape) == {"dp": DP, "ctx": CTX}
    return jax.shard_map(
        fast_shards if fast else shards,
        mesh=mesh,
        in_specs=placed,
        out_specs=(
            P(None, "dp", "ctx", None),
            P(None, "dp", "ctx", None),
            P(("dp", "ctx")),
            P(("dp", "ctx")),
            P(("dp", "ctx")),
            P(("dp", "ctx")),
            P(("dp", "ctx")),
            P(("dp", "ctx")),
        ),
        check_vma=False,
    )
```

```python
import functools

import jax
import jax.numpy as jnp
import numpy as np
from jax import lax
from jax.experimental import pallas as pl
from jax.experimental.pallas import tpu as pltpu
from jax.sharding import PartitionSpec as P

D = 1600
HEADS = 25
HEAD = 64
FF = 6400
MICRO = 2


EPS = 1e-05


def layer_norm(values, gain, shift):
    center = values - jnp.mean(values, axis=-1, keepdims=True)
    spread = jnp.mean(center * center, axis=-1, keepdims=True)
    return center * lax.rsqrt(spread + EPS) * gain + shift


def gelu_tanh(values):
    return jax.nn.gelu(values, approximate=True)


def unpack(gathered):
    packed_qkv, packed_proj, packed_fc, packed_out, packed_small = gathered
    return (
        packed_qkv.reshape(D, 3 * D),
        packed_proj.reshape(D, D),
        packed_fc.reshape(D, FF),
        packed_out.reshape(FF, D),
        packed_small.astype(jnp.float32),
    )


def fetch(w_qkv, w_proj, w_fc, w_out, smalls):
    return unpack(
        (
            lax.all_gather(w_qkv, ("dp", "ctx"), axis=0, tiled=True),
            lax.all_gather(w_proj, ("dp", "ctx"), axis=0, tiled=True),
            lax.all_gather(w_fc, ("dp", "ctx"), axis=0, tiled=True),
            lax.all_gather(w_out, ("dp", "ctx"), axis=0, tiled=True),
            lax.all_gather(smalls, ("dp", "ctx"), axis=0, tiled=True),
        )
    )


def fetch_again(w_qkv, w_proj, w_fc, w_out, smalls):
    return unpack(
        (
            lax.all_gather(w_qkv, ("dp", "ctx"), axis=0, tiled=True),
            lax.all_gather(w_proj, ("dp", "ctx"), axis=0, tiled=True),
            lax.all_gather(w_fc, ("dp", "ctx"), axis=0, tiled=True),
            lax.all_gather(w_out, ("dp", "ctx"), axis=0, tiled=True),
            lax.all_gather(smalls, ("dp", "ctx"), axis=0, tiled=True),
        )
    )


def outer_sum(left, right):
    return lax.dot_general(
        left, right, (((0,), (0,)), ((), ())), preferred_element_type=jnp.float32
    )


def back_product(grad, weight):
    return lax.dot_general(
        grad, weight, (((1,), (1,)), ((), ())), preferred_element_type=jnp.float32
    )


def flat_term(left, right, start, count):
    width = right.shape[1]
    span = count // width + 2
    padded = jnp.pad(left, ((0, 0), (0, span)))
    first_row = start // width
    piece = lax.dynamic_slice_in_dim(padded, first_row, span, 1)
    block = outer_sum(piece, right).astype(jnp.bfloat16).reshape(-1)
    return lax.dynamic_slice_in_dim(block, start, count, 0)


def masked_scores(queries, keys, query_start, key_start):
    scores = (
        jnp.einsum("sqhe,skhe->shqk", queries, keys, preferred_element_type=jnp.float32) * 0.125
    )
    query_pos = query_start + jnp.arange(queries.shape[1])
    key_pos = key_start + jnp.arange(keys.shape[1])
    allowed = query_pos[:, None] >= key_pos[None, :]
    return jnp.where(allowed[None, None], scores, -1e30)


def segment(small_vals, which):
    return small_vals[which * D : (which + 1) * D]


def shards(inputs, grad_out, w_qkv, w_proj, w_fc, w_out, smalls):
    seqs = inputs.shape[1]
    local_len = inputs.shape[2]
    rows = seqs * local_len
    offset = lax.axis_index("ctx") * local_len
    acc_small = [jnp.zeros((D,), jnp.float32) for _ in range(7)]
    acc_fc_bias = jnp.zeros((FF,), jnp.float32)
    acc_out_bias = jnp.zeros((D,), jnp.float32)
    result_list = []
    grad_list = []
    kept_hidden_one = []
    kept_mixed_grad = []
    kept_context = []
    kept_branch_grad = []
    kept_hidden_two = []
    kept_pre_grad = []
    kept_activ = []
    kept_out_grad = []
    for batch_index in range(MICRO):
        params = fetch(w_qkv, w_proj, w_fc, w_out, smalls)
        mat_qkv, mat_proj, mat_fc, mat_out, small_vals = params
        tokens = inputs[batch_index].astype(jnp.float32).reshape(rows, D)
        hidden_one, ln1_pull = jax.vjp(
            layer_norm, tokens, segment(small_vals, 0), segment(small_vals, 1)
        )
        hidden_one = hidden_one.astype(jnp.bfloat16)
        qkv_bias = jnp.concatenate(
            [segment(small_vals, 2), jnp.zeros((D,), jnp.float32), segment(small_vals, 3)]
        )
        mixed = (
            jnp.dot(hidden_one, mat_qkv, preferred_element_type=jnp.float32) + qkv_bias
        ).astype(jnp.bfloat16)
        queries = mixed[:, :D].reshape(seqs, local_len, HEADS, HEAD)
        keys_local = mixed[:, D : 2 * D].reshape(seqs, local_len, D)
        values_local = mixed[:, 2 * D :].reshape(seqs, local_len, D)
        keys_all, values_all = (
            lax.all_gather(keys_local, "ctx", axis=1, tiled=True),
            lax.all_gather(values_local, "ctx", axis=1, tiled=True),
        )
        keys_all = keys_all.reshape(seqs, -1, HEADS, HEAD)
        values_all = values_all.reshape(seqs, -1, HEADS, HEAD)
        scores = masked_scores(queries, keys_all, offset, 0)
        row_peak = jnp.max(scores, axis=-1, keepdims=True)
        log_total = row_peak + jnp.log(jnp.sum(jnp.exp(scores - row_peak), axis=-1, keepdims=True))
        attn_low = jnp.exp(scores - log_total).astype(jnp.bfloat16)
        context = jnp.einsum(
            "shqk,skhe->sqhe", attn_low, values_all, preferred_element_type=jnp.float32
        )
        context = context.reshape(rows, D).astype(jnp.bfloat16)
        resid = (
            tokens
            + jnp.dot(context, mat_proj, preferred_element_type=jnp.float32)
            + segment(small_vals, 4)
        )
        hidden_two, ln2_pull = jax.vjp(
            layer_norm, resid, segment(small_vals, 5), segment(small_vals, 6)
        )
        hidden_two = hidden_two.astype(jnp.bfloat16)
        pre_act = (
            jnp.dot(hidden_two, mat_fc, preferred_element_type=jnp.float32)
            + small_vals[7 * D : 7 * D + FF]
        )
        activ, gelu_pull = jax.vjp(gelu_tanh, pre_act)
        activ = activ.astype(jnp.bfloat16)
        result = (
            resid
            + jnp.dot(activ, mat_out, preferred_element_type=jnp.float32)
            + small_vals[7 * D + FF :]
        )
        result_list.append(result.astype(jnp.bfloat16).reshape(seqs, local_len, D))
        back_params = fetch_again(w_qkv, w_proj, w_fc, w_out, smalls)
        mat_qkv, mat_proj, mat_fc, mat_out, small_vals = back_params
        grad_low = grad_out[batch_index].reshape(rows, D)
        grad_full = grad_low.astype(jnp.float32)
        acc_out_bias = acc_out_bias + jnp.sum(grad_full, axis=0)
        grad_act = back_product(grad_low, mat_out)
        (grad_pre,) = gelu_pull(grad_act)
        grad_pre = grad_pre.astype(jnp.bfloat16)
        acc_fc_bias = acc_fc_bias + jnp.sum(grad_pre.astype(jnp.float32), axis=0)
        grad_hidden_two = back_product(grad_pre, mat_fc)
        grad_ln_two, grad_gain_two, grad_shift_two = ln2_pull(grad_hidden_two)
        acc_small[5] = acc_small[5] + grad_gain_two
        acc_small[6] = acc_small[6] + grad_shift_two
        grad_resid = grad_full + grad_ln_two
        grad_branch = grad_resid.astype(jnp.bfloat16)
        acc_small[4] = acc_small[4] + jnp.sum(grad_branch.astype(jnp.float32), axis=0)
        grad_context = (
            back_product(grad_branch, mat_proj)
            .astype(jnp.bfloat16)
            .reshape(seqs, local_len, HEADS, HEAD)
        )
        scores = masked_scores(queries, keys_all, offset, 0)
        attn_prob = jnp.exp(scores - log_total)
        grad_attn = jnp.einsum(
            "sqhe,skhe->shqk", grad_context, values_all, preferred_element_type=jnp.float32
        )
        row_delta = jnp.sum(attn_prob * grad_attn, axis=-1, keepdims=True)
        grad_scores = (attn_prob * (grad_attn - row_delta)).astype(jnp.bfloat16)
        grad_queries = (
            jnp.einsum("shqk,skhe->sqhe", grad_scores, keys_all, preferred_element_type=jnp.float32)
            * 0.125
        )
        query_all, dctx_all = (
            lax.all_gather(queries.reshape(seqs, local_len, D), "ctx", axis=1, tiled=True),
            lax.all_gather(grad_context.reshape(seqs, local_len, D), "ctx", axis=1, tiled=True),
        )
        lse_all, delta_all = (
            lax.all_gather(jnp.transpose(log_total[..., 0], (0, 2, 1)), "ctx", axis=1, tiled=True),
            lax.all_gather(jnp.transpose(row_delta[..., 0], (0, 2, 1)), "ctx", axis=1, tiled=True),
        )
        query_all = query_all.reshape(seqs, -1, HEADS, HEAD)
        dctx_all = dctx_all.reshape(seqs, -1, HEADS, HEAD)
        lse_all = jnp.transpose(lse_all, (0, 2, 1))[..., None]
        delta_all = jnp.transpose(delta_all, (0, 2, 1))[..., None]
        own_keys = keys_local.reshape(seqs, local_len, HEADS, HEAD)
        own_values = values_local.reshape(seqs, local_len, HEADS, HEAD)
        col_scores = masked_scores(query_all, own_keys, 0, offset)
        col_prob = jnp.exp(col_scores - lse_all)
        col_dattn = jnp.einsum(
            "sqhe,skhe->shqk", dctx_all, own_values, preferred_element_type=jnp.float32
        )
        col_ds = (col_prob * (col_dattn - delta_all)).astype(jnp.bfloat16)
        grad_keys = (
            jnp.einsum("shqk,sqhe->skhe", col_ds, query_all, preferred_element_type=jnp.float32)
            * 0.125
        )
        grad_values = jnp.einsum(
            "shqk,sqhe->skhe",
            col_prob.astype(jnp.bfloat16),
            dctx_all,
            preferred_element_type=jnp.float32,
        )
        grad_mixed = jnp.concatenate(
            [
                grad_queries.reshape(rows, D),
                grad_keys.reshape(rows, D),
                grad_values.reshape(rows, D),
            ],
            axis=1,
        ).astype(jnp.bfloat16)
        bias_terms = jnp.sum(grad_mixed.astype(jnp.float32), axis=0)
        acc_small[2] = acc_small[2] + bias_terms[:D]
        acc_small[3] = acc_small[3] + bias_terms[2 * D :]
        grad_hidden_one = back_product(grad_mixed, mat_qkv)
        grad_ln_one, grad_gain_one, grad_shift_one = ln1_pull(grad_hidden_one)
        acc_small[0] = acc_small[0] + grad_gain_one
        acc_small[1] = acc_small[1] + grad_shift_one
        grad_list.append((grad_resid + grad_ln_one).reshape(seqs, local_len, D))
        kept_hidden_one.append(hidden_one)
        kept_mixed_grad.append(grad_mixed)
        kept_context.append(context)
        kept_branch_grad.append(grad_branch)
        kept_hidden_two.append(hidden_two)
        kept_pre_grad.append(grad_pre)
        kept_activ.append(activ)
        kept_out_grad.append(grad_low)
    front_grads = jnp.concatenate(acc_small[0:4])
    tail_grads = jnp.concatenate(acc_small[4:7] + [acc_fc_bias, acc_out_bias])
    grad_qkv = lax.psum_scatter(
        flat_term(
            jnp.concatenate(kept_hidden_one),
            jnp.concatenate(kept_mixed_grad),
            jnp.int32(0),
            lax.axis_size(("dp", "ctx")) * w_qkv.shape[0],
        ),
        ("dp", "ctx"),
        scatter_dimension=0,
        tiled=True,
    ).astype(jnp.float32)
    grad_proj = lax.psum_scatter(
        flat_term(
            jnp.concatenate(kept_context),
            jnp.concatenate(kept_branch_grad),
            jnp.int32(0),
            lax.axis_size(("dp", "ctx")) * w_proj.shape[0],
        ),
        ("dp", "ctx"),
        scatter_dimension=0,
        tiled=True,
    ).astype(jnp.float32)
    grad_fc = lax.psum_scatter(
        flat_term(
            jnp.concatenate(kept_hidden_two),
            jnp.concatenate(kept_pre_grad),
            jnp.int32(0),
            lax.axis_size(("dp", "ctx")) * w_fc.shape[0],
        ),
        ("dp", "ctx"),
        scatter_dimension=0,
        tiled=True,
    ).astype(jnp.float32)
    grad_out_w = lax.psum_scatter(
        flat_term(
            jnp.concatenate(kept_activ),
            jnp.concatenate(kept_out_grad),
            jnp.int32(0),
            lax.axis_size(("dp", "ctx")) * w_out.shape[0],
        ),
        ("dp", "ctx"),
        scatter_dimension=0,
        tiled=True,
    ).astype(jnp.float32)
    grad_front, grad_tail = (
        lax.psum_scatter(front_grads, ("dp", "ctx"), scatter_dimension=0, tiled=True),
        lax.psum_scatter(tail_grads, ("dp", "ctx"), scatter_dimension=0, tiled=True),
    )
    return (
        jnp.stack(result_list),
        jnp.stack(grad_list),
        grad_qkv,
        grad_proj,
        grad_fc,
        grad_out_w,
        grad_front,
        grad_tail,
    )


DP, CTX = 4, 8
YN, CN, ZN, XN = 2, 2, 4, 2
SLOTS = 7
HW = SLOTS * HEAD
QW = 3 * HW
STARTS = (0, 7, 13, 19)
COUNTS = (7, 6, 6, 6)
BLK = 128
SEQ = 8 * BLK
PIECE = 208
WIDE = 8 * PIECE
PB = 64
PROJ = 32 * PB
LOW = jnp.bfloat16
F32 = jnp.float32
VMEM_BYTES = 60 * 1024 * 1024
ANY = pl.BlockSpec(memory_space=pl.ANY)
VM = pl.BlockSpec(memory_space=pltpu.VMEM)


def here():
    dp, ctx = lax.axis_index("dp"), lax.axis_index("ctx")
    return dp // CN, dp % CN, ctx // XN, ctx % XN


def device(y, c, z, x):
    return (y * CN + c, z * XN + x)


class Wires:
    def __init__(self, sems):
        self.sems, self.used = sems, 0

    def one(self):
        self.used += 1
        return self.sems.at[self.used - 1]

    def far(self, source, target, where):
        return pltpu.make_async_remote_copy(
            src_ref=source,
            dst_ref=target,
            send_sem=self.one(),
            recv_sem=self.one(),
            device_id=where,
            device_id_type=pl.DeviceIdType.MESH,
        )

    def near(self, source, target):
        return pltpu.make_async_copy(source, target, self.one())


def signal(where):
    pl.semaphore_signal(
        pltpu.get_barrier_semaphore(), inc=1, device_id=where, device_id_type=pl.DeviceIdType.MESH
    )


def team_peers(y, c, z, x):
    return [device(y, 1 - c, z, x), device(y, c, z, 1 - x), device(y, 1 - c, z, 1 - x)]


def grid_peers(y, c, z, x):
    ring = [device(y, c, lax.rem(z + k, ZN), x) for k in range(1, ZN)]
    return ring + [device(1 - y, c, z, x)]


def meet(peers):
    for peer in peers:
        signal(peer)
    pl.semaphore_wait(pltpu.get_barrier_semaphore(), len(peers))


def call(body, name, ident, ins, outs, in_specs, out_specs, scratch, sems, cost=None):
    return pl.pallas_call(
        body,
        out_shape=[jax.ShapeDtypeStruct(s, d) for s, d in outs],
        in_specs=in_specs,
        out_specs=out_specs,
        scratch_shapes=list(scratch) + [pltpu.SemaphoreType.DMA((sems,))],
        compiler_params=pltpu.CompilerParams(
            collective_id=ident, has_side_effects=True, vmem_limit_bytes=VMEM_BYTES
        ),
        name=name,
    )(*ins)


class Gather:
    def __init__(self, wires, piece, whole, spot):
        y, c, z, x = self.spot = spot
        self.z = z
        self.across = device(1 - y, c, z, x)
        up = device(y, c, lax.min(z + 1, ZN - 1), x)
        down = device(y, c, lax.max(z - 1, 0), x)
        self.local = wires.near(piece, whole.at[y, z])
        self.mine = wires.far(piece, whole.at[y, z], self.across)
        self.ups, self.downs, self.from_low, self.from_high = [], [], [], []
        for turn in range(1, ZN):
            low = lax.max(z - (turn - 1), 0)
            high = lax.min(z + (turn - 1), ZN - 1)
            source = piece if turn == 1 else whole.at[y, low]
            self.ups.append(wires.far(source, whole.at[y, low], up))
            source = piece if turn == 1 else whole.at[y, high]
            self.downs.append(wires.far(source, whole.at[y, high], down))
            low = lax.max(z - turn, 0)
            high = lax.min(z + turn, ZN - 1)
            self.from_low.append(wires.far(whole.at[y, low], whole.at[y, low], self.across))
            self.from_high.append(wires.far(whole.at[y, high], whole.at[y, high], self.across))

    def send_up(self, turn):
        return (self.z >= turn - 1) & (self.z < ZN - 1)

    def send_down(self, turn):
        return (self.z <= ZN - turn) & (self.z > 0)

    def start(self):
        self.local.start()
        self.mine.start()
        pl.when(self.send_up(1))(self.ups[0].start)
        pl.when(self.send_down(1))(self.downs[0].start)

    def step(self, turn):
        @pl.when(self.z >= turn)
        def _():
            self.ups[turn - 1].wait_recv()
            if turn < ZN - 1:
                pl.when(self.send_up(turn + 1))(self.ups[turn].start)
            self.from_low[turn - 1].start()

        @pl.when(self.z + turn <= ZN - 1)
        def _():
            self.downs[turn - 1].wait_recv()
            if turn < ZN - 1:
                pl.when(self.send_down(turn + 1))(self.downs[turn].start)
            self.from_high[turn - 1].start()

    def finish(self):
        self.local.wait()
        self.mine.wait()
        for turn in range(1, ZN):
            pl.when(self.send_up(turn))(self.ups[turn - 1].wait_send)
            pl.when(self.send_down(turn))(self.downs[turn - 1].wait_send)
            pl.when(self.z >= turn)(self.from_low[turn - 1].wait)
            pl.when(self.z + turn <= ZN - 1)(self.from_high[turn - 1].wait)


GATHER_SEMS = 1 + 2 + 2 * 4 * 3


class Scatter:
    def __init__(self, wires, parts, landed, arrived, spot):
        y, c, z, x = spot
        self.y, self.z, self.size = y, z, landed.shape[1]
        self.parts, self.landed, self.arrived = parts, landed, arrived
        across = device(1 - y, c, z, x)
        self.order = [lax.rem(z + k, ZN) for k in (1, 2, 3, 0)]
        self.over = [
            wires.far(parts.at[self.rows(1 - y, o)], landed.at[o], across) for o in self.order
        ]
        self.along = [
            wires.far(landed.at[o], arrived.at[k], device(y, c, o, x))
            for k, o in enumerate(self.order[:3])
        ]

    def rows(self, y, z):
        return pl.ds(pl.multiple_of((y * ZN + z) * self.size, 16), self.size)

    def start(self):
        for copy in self.over:
            copy.start()

    def step(self, k):
        o = self.order[k]
        self.over[k].wait_recv()
        self.landed[o] = (self.landed[o].astype(F32) + self.parts[self.rows(self.y, o), :].astype(F32)).astype(LOW)
        self.along[k].start()

    def finish(self, total):
        self.over[3].wait_recv()
        summed = self.landed[self.z].astype(F32) + self.parts[self.rows(self.y, self.z), :].astype(F32)
        for k in range(3):
            self.along[k].wait_recv()
            summed = summed + self.arrived[k].astype(F32)
        total[...] = summed.astype(total.dtype)
        for copy in self.over + self.along:
            copy.wait_send()


SCATTER_SEMS = 2 * 7


class TeamGather:
    def __init__(self, wires, block, whole, spot):
        y, c, z, x = spot
        mate, beside = device(y, 1 - c, z, x), device(y, c, z, 1 - x)
        self.local = [wires.near(block.at[s], whole.at[c, s, x]) for s in range(2)]
        self.to_mate = [wires.far(block.at[s], whole.at[c, s, x], mate) for s in range(2)]
        self.to_side = [wires.far(block.at[s], whole.at[c, s, x], beside) for s in range(2)]
        self.relay = [
            wires.far(whole.at[c, s, 1 - x], whole.at[c, s, 1 - x], mate) for s in range(2)
        ]

    def start(self):
        for copy in self.to_side + self.to_mate + self.local:
            copy.start()

    def step(self, s):
        self.to_side[s].wait_recv()
        self.relay[s].start()

    def finish(self):
        for copy in self.local + self.to_mate + self.relay:
            copy.wait()
        for copy in self.to_side:
            copy.wait_send()


TEAM_GATHER_SEMS = 2 + 2 * 6


class TeamSwap:
    def __init__(self, wires, source, target, spot):
        y, c, z, x = spot
        self.local = wires.near(source(c, x), target(c, x))
        self.copies = [
            wires.far(source(p, q), target(c, x), device(y, p, z, q))
            for p, q in ((c, 1 - x), (1 - c, 1 - x), (1 - c, x))
        ]

    def start(self):
        for copy in self.copies + [self.local]:
            copy.start()

    def finish(self):
        for copy in self.copies + [self.local]:
            copy.wait()


TEAM_SWAP_SEMS = 1 + 2 * 3


class TeamScatter:
    def __init__(self, wires, parts, landed, leaving, arrived, spot):
        y, c, z, x = spot
        self.c, self.x = c, x
        self.parts, self.landed, self.leaving, self.arrived = parts, landed, leaving, arrived
        mate, beside = device(y, 1 - c, z, x), device(y, c, z, 1 - x)
        self.to_mate = [wires.far(parts.at[half_rows(1 - c, s)], landed.at[s], mate) for s in range(2)]
        self.to_side = [wires.far(leaving.at[s], arrived.at[s], beside) for s in range(2)]

    def side(self, x):
        return pl.ds(pl.multiple_of(x * BLK, BLK), BLK)

    def start(self):
        for copy in self.to_mate:
            copy.start()

    def step(self, s):
        self.to_mate[s].wait_recv()
        far = 1 - self.x
        self.leaving[s] = (
            self.landed[s, self.side(far), :].astype(F32)
            + self.parts[block_rows(self.c, s, far), :].astype(F32)
        ).astype(LOW)
        self.to_side[s].start()

    def finish(self, total):
        for s in range(2):
            self.to_side[s].wait_recv()
            total[s] = (
                self.landed[s, self.side(self.x), :].astype(F32)
                + self.parts[block_rows(self.c, s, self.x), :].astype(F32)
                + self.arrived[s].astype(F32)
            )
        for copy in self.to_mate + self.to_side:
            copy.wait_send()


def block_rows(c, s, x):
    return pl.ds(pl.multiple_of((c * 4 + s * 2 + x) * BLK, BLK), BLK)


def half_rows(c, s):
    return pl.ds(pl.multiple_of((c * 2 + s) * 2 * BLK, 2 * BLK), 2 * BLK)


TEAM_SCATTER_SEMS = 2 * 4


def team_scatter_scratch(width):
    return [
        pltpu.VMEM((2, 2 * BLK, width), LOW),
        pltpu.VMEM((2, BLK, width), LOW),
        pltpu.VMEM((2, BLK, width), LOW),
    ]


def scatter_scratch(rows, width):
    return [pltpu.VMEM((ZN, rows, width), LOW), pltpu.VMEM((ZN - 1, rows, width), LOW)]


class Tokens:
    def __init__(self, wires, source, target, spot, back):
        y, c, z, x = spot
        self.own, self.local, self.copies, self.peers = [], [], [], []
        for k in range(2):
            if not back:
                m = lax.rem(z + k, 2)
                goal_c, goal_z = z // 2, 2 * m + c
                block, landing = source.at[m], target.at[lax.rem(z, 2)]
            else:
                m = z // 2
                s = lax.rem(m + k, 2)
                goal_c, goal_z = lax.rem(z, 2), 2 * c + s
                block, landing = source.at[s], target.at[m]
            goal = device(y, goal_c, goal_z, x)
            stays = (goal_c == c) & (goal_z == z)
            self.own.append(stays)
            self.peers.append(goal)
            self.local.append(wires.near(block, landing))
            self.copies.append(wires.far(block, landing, goal))

    def start(self):
        for stays, local, copy in zip(self.own, self.local, self.copies):
            pl.when(stays)(local.start)
            pl.when(jnp.logical_not(stays))(copy.start)

    def finish(self):
        for stays, local, copy in zip(self.own, self.local, self.copies):
            pl.when(stays)(local.wait)
            pl.when(jnp.logical_not(stays))(copy.wait)


TOKENS_SEMS = 2 * 3


def token_sources(spot, back):
    y, c, z, x = spot
    found = []
    for k in range(2):
        if back:
            m = lax.rem(z + k, 2)
            goal = (z // 2, 2 * m + c)
        else:
            s = lax.rem(z // 2 + k, 2)
            goal = (lax.rem(z, 2), 2 * c + s)
        found.append((device(y, goal[0], goal[1], x), (goal[0] == c) & (goal[1] == z)))
    return found


def meet_tokens(peers, spot, back):
    for peer in peers:
        signal(peer)
    for source, stays in token_sources(spot, back):
        pl.when(jnp.logical_not(stays))(functools.partial(signal, source))
    leaving = sum(jnp.where(stays, 0, 1) for _, stays in token_sources(spot, not back))
    pl.semaphore_wait(pltpu.get_barrier_semaphore(), len(peers) + leaving)


def prologue(
    inputs, units_qkv, units_fc, small, piece_out,
    tokens, got_qkv, got_fc, smalls, all_out, sems,
):
    spot = y, c, z, x = here()
    wires = Wires(sems)
    meet_tokens(team_peers(*spot) + grid_peers(*spot), spot, False)
    first = TeamSwap(
        wires, lambda p, q: small, lambda p, q: smalls.at[y, z, p * XN + q], spot
    )
    qkv = TeamSwap(
        wires, lambda p, q: units_qkv.at[p * XN + q], lambda p, q: got_qkv.at[p * XN + q], spot
    )
    fc = TeamSwap(
        wires, lambda p, q: units_fc.at[p * XN + q], lambda p, q: got_fc.at[p * XN + q], spot
    )
    move = Tokens(wires, inputs, tokens, spot, False)
    out = Gather(wires, piece_out, all_out, spot)
    column = [
        wires.far(smalls.at[y, z], smalls.at[y, z], device(y, c, lax.rem(z + k, ZN), x))
        for k in range(1, ZN)
    ]
    over = wires.far(smalls.at[y], smalls.at[y], device(1 - y, c, z, x))
    first.start()
    move.start()
    qkv.start()
    fc.start()
    first.finish()
    for copy in column:
        copy.start()
    out.start()
    for copy in column:
        copy.wait()
    over.start()
    over.wait()
    out.step(1)
    move.finish()
    qkv.finish()
    fc.finish()
    out.step(2)
    out.step(3)
    out.finish()


def gather_first(
    hidden, grads, piece_qkv, piece_proj, hidden_all, cotangent, all_qkv, all_proj, sems,
):
    spot = y, c, z, x = here()
    wires = Wires(sems)
    rank = c * XN + x
    meet_tokens(team_peers(*spot) + grid_peers(*spot), spot, False)
    team = TeamGather(wires, hidden, hidden_all, spot)
    bring = Tokens(wires, grads, cotangent, spot, False)
    qkv = Gather(wires, piece_qkv, all_qkv, spot)
    proj = Gather(wires, piece_proj, all_proj.at[rank], spot)
    side = wires.far(all_proj.at[rank], all_proj.at[rank], device(y, c, z, 1 - x))
    mate = device(y, 1 - c, z, x)
    relay = [
        wires.far(all_proj.at[r], all_proj.at[r], mate) for r in (rank, c * XN + 1 - x)
    ]
    proj.start()
    qkv.start()
    team.start()
    proj.step(1)
    proj.step(2)
    proj.step(3)
    qkv.step(1)
    team.step(0)
    team.step(1)
    proj.finish()
    side.start()
    relay[0].start()
    bring.start()
    qkv.step(2)
    qkv.step(3)
    side.wait_recv()
    relay[1].start()
    qkv.finish()
    team.finish()
    bring.finish()
    side.wait_send()
    for copy in relay:
        copy.wait()


def attention(
    hidden, mat_qkv, bias_qkv, piece_fc, cotangent, mixed, context, totals, got, all_fc, grad_all,
    hidden_in, mat_in, sems,
):
    spot = y, c, z, x = here()
    wires = Wires(sems)
    load = [wires.near(mat_qkv, mat_in), wires.near(hidden, hidden_in)]
    for copy in load:
        copy.start()
    meet(team_peers(*spot) + grid_peers(*spot))
    fc = Gather(wires, piece_fc, all_fc, spot)
    fc.start()
    team = TeamGather(wires, cotangent, grad_all, spot)
    team.start()
    swaps = [
        TeamSwap(
            wires,
            lambda p, q, s=s: context.at[block_rows(p, s, q)],
            lambda p, q, s=s: got.at[p * XN + q, s],
            spot,
        )
        for s in range(2)
    ]
    for copy in load:
        copy.wait()

    @pl.loop(0, SEQ // QB)
    def _(i):
        rows = pl.ds(pl.multiple_of(i * QB, QB), QB)
        mixed[rows, :] = (dot(hidden_in[rows, :], mat_in[...]) + bias_qkv[...]).astype(LOW)

    for head in range(SLOTS):
        attend(mixed, context, totals, head)
        if head == 2:
            fc.step(1)
        if head == 4:
            team.step(0)
            team.step(1)
    for copy in swaps:
        copy.start()
    fc.step(2)
    for copy in swaps:
        copy.finish()
    fc.step(3)
    team.finish()
    fc.finish()


def gather_second(block, whole, sems):
    spot = here()
    wires = Wires(sems)
    meet(team_peers(*spot))
    team = TeamGather(wires, block, whole, spot)
    team.start()
    team.step(0)
    team.step(1)
    team.finish()


def gelu_both(f):
    square = f * f
    t = jnp.tanh(0.7978845608028654 * f * (1.0 + 0.044715 * square))
    half = 0.5 * (1.0 + t)
    slope = half + f * (0.5 * 0.7978845608028654) * (1.0 - t * t) * (1.0 + 3 * 0.044715 * square)
    return f * half, slope


def chunks(total, step):
    return [(start, min(step, total - start)) for start in range(0, total, step)]


def outer_into(target, left, right):
    count = left.shape[1] // 256

    @pl.loop(0, count)
    def _(i):
        at = pl.ds(pl.multiple_of(i * 256, 256), 256)
        target[at, :] = outer_sum(left[:, at], right[...]).astype(LOW)

    rest = left.shape[1] - count * 256
    if rest:
        target[count * 256 :, :] = outer_sum(left[:, count * 256 :], right[...]).astype(LOW)


def feed_forward(
    hidden_two, grad_all, mat_fc, mat_out, bias_fc,
    result, hidden, grad_out_w, grad_pre, terms,
    h2, dy, wf, wo, activ, part_r, part_h, part_o, l1, s1, a1, l2, s2, a2, l3, a3, sems,
):
    spot = y, c, z, x = here()
    wires = Wires(sems)
    load = [
        wires.near(*both) for both in ((hidden_two, h2), (mat_fc, wf), (grad_all, dy), (mat_out, wo))
    ]
    for copy in load:
        copy.start()
    meet(team_peers(*spot) + grid_peers(*spot))
    second = TeamScatter(wires, part_h, l2, s2, a2, spot)
    first = TeamScatter(wires, part_r, l1, s1, a1, spot)
    out = Scatter(wires, part_o, l3, a3, spot)
    load[0].wait()
    load[1].wait()

    @pl.loop(0, SEQ // QB)
    def _(i):
        rows = pl.ds(pl.multiple_of(i * QB, QB), QB)
        f = dot(h2[rows, :], wf[...]) + bias_fc[...]
        value, slope = gelu_both(f)
        activ[rows, :] = value.astype(LOW)
        grad_pre[rows, :] = slope.astype(LOW)

    load[2].wait()
    outer_into(part_o, activ, dy)
    out.start()
    load[3].wait()
    terms[...] = jnp.zeros_like(terms)

    @pl.loop(0, SEQ // QB)
    def _(i):
        rows = pl.ds(pl.multiple_of(i * QB, QB), QB)
        df = (back_product(dy[rows, :], wo[...]) * grad_pre[rows, :].astype(F32)).astype(LOW)
        grad_pre[rows, :] = df
        terms[...] += jnp.sum(df.astype(F32), axis=0, keepdims=True)

    def into(target, make):
        def half(which):
            @pl.loop(0, 2)
            def _(s):
                rows = half_rows(which, s)
                target[rows, :] = make(rows).astype(LOW)

        return half

    half = into(part_h, lambda rows: back_product(grad_pre[rows, :], wf[...]))
    half(1 - c)
    second.start()
    half(c)
    out.step(0)
    second.step(0)
    second.step(1)
    half = into(part_r, lambda rows: dot(activ[rows, :], wo[...]))
    half(1 - c)
    first.start()
    half(c)
    out.step(1)
    first.step(0)
    first.step(1)
    second.finish(hidden)
    out.step(2)
    first.finish(result)
    out.finish(grad_out_w)


def backward(
    hidden_one, hidden_two, grad_pre, mat_qkv, mixed, totals, swap_parts, context, branch, result,
    hidden, grad_qkv, grad_fc, grad_proj, outputs, terms,
    ha, hb, wq, part_f, part_h, grads, grad_mixed, acc_k, acc_v,
    l1, s1, a1, l2, a2, l3, a3, l4, a4, pm, pk, px, sems,
):
    spot = y, c, z, x = here()
    wires = Wires(sems)
    load = [wires.near(*both) for both in ((hidden_two, ha), (grad_pre, hb), (mat_qkv, wq))]
    again = wires.near(hidden_one, ha)
    for copy in load:
        copy.start()
    meet_tokens(team_peers(*spot) + grid_peers(*spot), spot, True)
    swaps = [
        TeamSwap(
            wires,
            lambda p, q, s=s: swap_parts.at[p * XN + q, s],
            lambda p, q, s=s: grads.at[block_rows(p, s, q)],
            spot,
        )
        for s in range(2)
    ]
    for copy in swaps:
        copy.start()
    fc = Scatter(wires, part_f, l2, a2, spot)
    first = TeamScatter(wires, part_h, l1, s1, a1, spot)
    qkv = Scatter(wires, wq, l3, a3, spot)
    quarter = PROJ // 4
    to_mate = wires.far(hb, pm, device(y, 1 - c, z, x))

    def side(q):
        return pl.ds(pl.multiple_of(q * quarter, 16), quarter)

    def term(p, q):
        at = pl.ds(pl.multiple_of((p * 2 + q) * quarter, quarter), quarter)
        return outer_sum(context[:, at], branch[...])

    to_side = wires.far(pm.at[side(1 - x)], px, device(y, c, z, 1 - x))
    proj = Scatter(wires, pk, l4, a4, spot)
    move = Tokens(wires, result, outputs, spot, True)
    load[0].wait()
    load[1].wait()
    outer_into(part_f, ha, hb)
    fc.start()
    again.start()
    for q in range(2):
        hb[side(q), :D] = term(1 - c, q).astype(LOW)
    to_mate.start()
    for copy in swaps:
        copy.finish()
    for head in range(SLOTS):
        attend_back(mixed, totals, grads, grad_mixed, acc_k, acc_v, head)
        if head == 1:
            fc.step(0)
            to_mate.wait_recv()
            pm[side(1 - x), :D] = (pm[side(1 - x), :D].astype(F32) + term(c, 1 - x)).astype(LOW)
        if head == 5:
            fc.step(1)
    load[2].wait()

    def half(which):
        @pl.loop(0, 2)
        def _(s):
            rows = half_rows(which, s)
            part_h[rows, :] = back_product(grad_mixed[rows, :], wq[...]).astype(LOW)

    half(1 - c)
    first.start()
    half(c)
    again.wait()
    first.step(0)
    first.step(1)
    to_side.start()
    outer_into(wq, ha, grad_mixed)
    qkv.start()
    fc.step(2)
    terms[...] = jnp.sum(grad_mixed[...].astype(F32), axis=0, keepdims=True)
    move.start()
    first.finish(hidden)
    to_side.wait_recv()
    pk[...] = (
        pm[side(x), :D].astype(F32) + term(c, x) + px[:, :D].astype(F32)
    ).astype(LOW)
    proj.start()
    fc.finish(grad_fc)
    qkv.step(0)
    qkv.step(1)
    qkv.step(2)
    proj.step(0)
    proj.step(1)
    proj.step(2)
    qkv.finish(grad_qkv)
    proj.finish(grad_proj)
    move.finish()
    to_mate.wait_send()
    to_side.wait_send()


def epilogue(
    grads, units_qkv, units_fc, small, grad_in, got_qkv, got_fc, total, by_y, by_z, by_team, sems
):
    spot = y, c, z, x = here()
    wires = Wires(sems)
    meet_tokens(team_peers(*spot) + grid_peers(*spot), spot, True)
    move = Tokens(wires, grads, grad_in, spot, True)
    qkv = TeamSwap(
        wires, lambda p, q: units_qkv.at[p * XN + q], lambda p, q: got_qkv.at[p * XN + q], spot
    )
    fc = TeamSwap(
        wires, lambda p, q: units_fc.at[p * XN + q], lambda p, q: got_fc.at[p * XN + q], spot
    )
    over = wires.far(small.at[1 - y], by_y, device(1 - y, c, z, x))
    over.start()
    move.start()
    qkv.start()
    fc.start()
    over.wait()
    by_y[...] = by_y[...] + small[y]
    column = [
        wires.far(by_y.at[lax.rem(z + k, ZN)], by_z.at[k - 1], device(y, c, lax.rem(z + k, ZN), x))
        for k in range(1, ZN)
    ]
    for copy in column:
        copy.start()
    for copy in column:
        copy.wait()
    by_z[3] = by_y[z] + by_z[0] + by_z[1] + by_z[2]
    team = [
        wires.far(by_z.at[3, p * XN + q], by_team.at[i], device(y, p, z, q))
        for i, (p, q) in enumerate(((c, 1 - x), (1 - c, 1 - x), (1 - c, x)))
    ]
    for copy in team:
        copy.start()
    for copy in team:
        copy.wait()
    total[...] = by_z[3, c * XN + x] + by_team[0] + by_team[1] + by_team[2]
    qkv.finish()
    fc.finish()
    move.finish()


QB = 256


def attend(mixed, context, totals, head):
    lanes = slice(head * HEAD, (head + 1) * HEAD)
    keys = mixed[:, HW + head * HEAD : HW + (head + 1) * HEAD]
    values = mixed[:, 2 * HW + head * HEAD : 2 * HW + (head + 1) * HEAD]
    for block in range(SEQ // QB):
        rows = slice(block * QB, (block + 1) * QB)
        upto = (block + 1) * QB
        scores = (
            lax.dot_general(
                mixed[rows, lanes], keys[:upto], (((1,), (1,)), ((), ())), preferred_element_type=F32
            )
            * 0.125
        )
        row = lax.broadcasted_iota(jnp.int32, (QB, upto), 0) + block * QB
        col = lax.broadcasted_iota(jnp.int32, (QB, upto), 1)
        scores = jnp.where(row >= col, scores, -1e30)
        peak = jnp.max(scores, axis=1, keepdims=True)
        weights = jnp.exp(scores - peak)
        total = jnp.sum(weights, axis=1, keepdims=True)
        prob = (weights * (1.0 / total)).astype(LOW)
        found = jnp.dot(prob, values[:upto], preferred_element_type=F32).astype(LOW)
        context[rows, lanes] = found
        totals[rows, head : head + 1] = peak + jnp.log(total)


def attend_back(mixed, totals, grads, out, acc_k, acc_v, head):
    lanes = slice(head * HEAD, (head + 1) * HEAD)
    lanes_k = slice(HW + head * HEAD, HW + (head + 1) * HEAD)
    lanes_v = slice(2 * HW + head * HEAD, 2 * HW + (head + 1) * HEAD)
    keys = mixed[:, lanes_k]
    values = mixed[:, lanes_v]
    acc_k[...] = jnp.zeros_like(acc_k)
    acc_v[...] = jnp.zeros_like(acc_v)
    for block in range(SEQ // QB):
        rows = slice(block * QB, (block + 1) * QB)
        upto = (block + 1) * QB
        queries = mixed[rows, lanes]
        outer = grads[rows, lanes]
        scores = (
            lax.dot_general(
                queries, keys[:upto], (((1,), (1,)), ((), ())), preferred_element_type=F32
            )
            * 0.125
        )
        row = lax.broadcasted_iota(jnp.int32, (QB, upto), 0) + block * QB
        col = lax.broadcasted_iota(jnp.int32, (QB, upto), 1)
        scores = jnp.where(row >= col, scores, -1e30)
        prob = jnp.exp(scores - totals[rows, head : head + 1])
        dprob = lax.dot_general(
            outer, values[:upto], (((1,), (1,)), ((), ())), preferred_element_type=F32
        )
        delta = jnp.sum(prob * dprob, axis=1, keepdims=True)
        ds = (prob * (dprob - delta)).astype(LOW)
        out[rows, lanes] = (
            jnp.dot(ds, keys[:upto], preferred_element_type=F32) * 0.125
        ).astype(LOW)
        acc_k[:upto] += outer_sum(ds, queries)
        acc_v[:upto] += outer_sum(prob.astype(LOW), outer)
    out[:, lanes_k] = (acc_k[...] * 0.125).astype(LOW)
    out[:, lanes_v] = acc_v[...].astype(LOW)


def plain(body, name, ins, outs, scratch=()):
    return pl.pallas_call(
        body,
        out_shape=[jax.ShapeDtypeStruct(s, d) for s, d in outs],
        in_specs=[VM] * len(ins),
        out_specs=[VM] * len(outs),
        scratch_shapes=list(scratch),
        compiler_params=pltpu.CompilerParams(vmem_limit_bytes=VMEM_BYTES),
        name=name,
    )(*ins)


def pick(values, index):
    return lax.dynamic_index_in_dim(values, index, 0, keepdims=False)


def pad_to(values, axis, size):
    widths = [(0, 0)] * values.ndim
    widths[axis] = (0, size - values.shape[axis])
    return jnp.pad(values, widths)


def head_parts(columns):
    return jnp.stack(
        [
            pad_to(columns[:, start * HEAD : (start + count) * HEAD], 1, HW)
            for start, count in zip(STARTS, COUNTS)
        ]
    )


def head_join(parts):
    return jnp.concatenate([parts[r][:, : COUNTS[r] * HEAD] for r in range(4)], axis=1)


def feature_order():
    order = -np.ones((YN, ZN, PIECE), np.int32)
    grid = np.arange(D).reshape(YN, CN, ZN, XN, 50).transpose(0, 2, 1, 3, 4)
    order[:, :, :200] = grid.reshape(YN, ZN, 200)
    return order.reshape(-1)


def context_order():
    natural = -np.ones(D, np.int32)
    grid = np.arange(D).reshape(YN, CN, ZN, XN, 50).transpose(1, 3, 0, 2, 4).reshape(32, 50)
    for block in range(32):
        natural[grid[block]] = block * PB + np.arange(50)
    order = -np.ones((4, HW), np.int32)
    for r in range(4):
        width = COUNTS[r] * HEAD
        order[r, :width] = natural[STARTS[r] * HEAD : STARTS[r] * HEAD + width]
    return order.reshape(-1)


def one_hot(order, size):
    rows = lax.broadcasted_iota(jnp.int32, (size, order.shape[0]), 0)
    return (rows == jnp.asarray(order)[None, :]).astype(LOW)


def dot(left, right):
    return jnp.dot(left, right, preferred_element_type=F32)


def ones_row(values):
    return jnp.sum(values.astype(F32), axis=0)


def fast_shards(inputs, grad_out, w_qkv, w_proj, w_fc, w_out, smalls):
    y, c, z, x = here()
    rank = c * XN + x
    to_wide = one_hot(feature_order(), D)
    to_heads = one_hot(context_order(), PROJ)

    rows = w_qkv.reshape(50, 3, D)
    units_qkv = jnp.stack([head_parts(rows[:, i]) for i in range(3)], axis=2).reshape(4, 50, QW)
    units_qkv = pad_to(units_qkv, 1, 64)
    units_fc = w_fc.reshape(50, YN, CN, ZN, XN, 200).transpose(2, 4, 0, 1, 3, 5)
    units_fc = pad_to(pad_to(units_fc, 5, PIECE).reshape(4, 50, WIDE), 1, 64)
    small = pad_to(smalls, 0, 2048).reshape(16, 128)
    piece_out = pad_to(w_out.reshape(200, D), 0, PIECE)
    tokens, got_qkv, got_fc, smalls_all, mat_out = call(
        prologue, "prologue", 1,
        (inputs.reshape(MICRO, BLK, D), units_qkv, units_fc, small, piece_out),
        [
            ((2, BLK, D), LOW), ((4, 64, QW), LOW), ((4, 64, WIDE), LOW), ((YN, ZN, 4, 16, 128), LOW), ((YN, ZN, PIECE, D), LOW),
        ],
        [ANY] * 5, [ANY] * 5, [], 3 * TEAM_SWAP_SEMS + TOKENS_SEMS + GATHER_SEMS + 8,
    )
    small = smalls_all.reshape(YN, ZN, CN, XN, 2048)[..., :600].transpose(0, 2, 1, 3, 4)
    small = small.reshape(-1).astype(F32)
    gain1, shift1, bias_q, bias_v, bias_proj, gain2, shift2 = [segment(small, i) for i in range(7)]
    bias_fc = small[7 * D : 7 * D + FF].reshape(YN, CN, ZN, XN, 200)
    bias_fc = lax.dynamic_index_in_dim(bias_fc, c, 1, keepdims=False)
    bias_fc = lax.dynamic_index_in_dim(bias_fc, x, 2, keepdims=False)
    bias_fc = pad_to(bias_fc, 2, PIECE).reshape(WIDE)
    bias_out = small[7 * D + FF :]
    bias_qkv = jnp.stack(
        [head_parts(bias_q[None]), jnp.zeros((4, 1, HW)), head_parts(bias_v[None])], axis=1
    )
    bias_qkv = pick(bias_qkv, rank).reshape(QW)

    tokens = tokens.reshape(2 * BLK, D).astype(F32)
    hidden_one, ln1_pull = jax.vjp(layer_norm, tokens, gain1, shift1)
    hidden_one = dot(hidden_one.astype(LOW), to_wide).astype(LOW)
    piece_qkv = pad_to(got_qkv[:, :50].reshape(200, QW), 0, PIECE)
    piece_fc = pad_to(got_fc[:, :50].reshape(200, WIDE), 0, PIECE)
    piece_proj = pad_to(w_proj.reshape(50, D), 0, PB)
    hidden_one, cotangent, mat_qkv, mat_proj = call(
        gather_first, "gather_first", 2,
        (
            hidden_one.reshape(2, BLK, WIDE), grad_out.reshape(MICRO, BLK, D),
            piece_qkv, piece_proj,
        ),
        [
            ((2, 2, 2, BLK, WIDE), LOW), ((2, BLK, D), LOW), ((YN, ZN, PIECE, QW), LOW),
            ((4, YN, ZN, PB, D), LOW),
        ],
        [ANY] * 4, [ANY] * 4, [], TEAM_GATHER_SEMS + TOKENS_SEMS + 2 * GATHER_SEMS + 6,
    )
    hidden_one = hidden_one.reshape(SEQ, WIDE)
    mat_qkv = mat_qkv.reshape(WIDE, QW)
    mat_out = mat_out.reshape(WIDE, D)
    mat_proj = mat_proj.reshape(PROJ, D)

    mixed, context, totals, got, mat_fc, grad_all = call(
        attention, "attention", 3,
        (hidden_one, mat_qkv, bias_qkv.reshape(1, QW), piece_fc, cotangent),
        [
            ((SEQ, QW), LOW), ((SEQ, HW), LOW), ((SEQ, SLOTS), F32), ((4, 2, BLK, HW), LOW),
            ((YN, ZN, PIECE, WIDE), LOW), ((2, 2, 2, BLK, D), LOW),
        ],
        [ANY, ANY, VM, ANY, ANY], [VM, VM, VM, VM, ANY, ANY],
        [pltpu.VMEM((SEQ, WIDE), LOW), pltpu.VMEM((WIDE, QW), LOW)],
        2 * TEAM_SWAP_SEMS + GATHER_SEMS + TEAM_GATHER_SEMS + 2,
    )
    mat_fc = mat_fc.reshape(WIDE, WIDE)
    grad_all = grad_all.reshape(SEQ, D)
    got = got.reshape(4, 2 * BLK, HW)
    context = jnp.concatenate([got[r] for r in range(4)], axis=1)
    context = back_product(context, to_heads).astype(LOW)
    resid = tokens + dot(context, mat_proj) + bias_proj
    hidden_two, ln2_pull = jax.vjp(layer_norm, resid, gain2, shift2)
    hidden_two = dot(hidden_two.astype(LOW), to_wide).astype(LOW)
    (hidden_two,) = call(
        gather_second, "gather_second", 4, (hidden_two.reshape(2, BLK, WIDE),),
        [((2, 2, 2, BLK, WIDE), LOW)], [ANY], [ANY], [], TEAM_GATHER_SEMS,
    )
    hidden_two = hidden_two.reshape(SEQ, WIDE)
    result, grad_hidden_two, grad_out_w, grad_pre, fc_terms = call(
        feed_forward, "feed_forward", 5,
        (hidden_two, grad_all, mat_fc, mat_out, bias_fc.reshape(1, WIDE)),
        [
            ((2, BLK, D), F32), ((2, BLK, WIDE), F32), ((PIECE, D), F32), ((SEQ, WIDE), LOW),
            ((1, WIDE), F32),
        ],
        [ANY] * 4 + [VM], [VM] * 5,
        [
            pltpu.VMEM((SEQ, WIDE), LOW), pltpu.VMEM((SEQ, D), LOW), pltpu.VMEM((WIDE, WIDE), LOW),
            pltpu.VMEM((WIDE, D), LOW), pltpu.VMEM((SEQ, WIDE), LOW), pltpu.VMEM((SEQ, D), LOW),
            pltpu.VMEM((SEQ, WIDE), LOW), pltpu.VMEM((WIDE, D), LOW),
        ]
        + team_scatter_scratch(D) + team_scatter_scratch(WIDE) + scatter_scratch(PIECE, D),
        2 * TEAM_SCATTER_SEMS + SCATTER_SEMS + 4,
    )
    result = (resid + result.reshape(2 * BLK, D) + bias_out).astype(LOW)
    grad_out_w = grad_out_w[:200].reshape(-1)

    grad_full = cotangent.reshape(2 * BLK, D).astype(F32)
    grad_hidden_two = back_product(grad_hidden_two.reshape(2 * BLK, WIDE).astype(LOW), to_wide)
    grad_ln_two, grad_gain_two, grad_shift_two = ln2_pull(grad_hidden_two)
    grad_resid = grad_full + grad_ln_two
    grad_branch = grad_resid.astype(LOW)
    grad_context = back_product(grad_branch, mat_proj).astype(LOW)
    grad_context = dot(grad_context, to_heads).astype(LOW)
    grad_context = jnp.stack(
        [grad_context[:, r * HW : (r + 1) * HW] for r in range(4)]
    ).reshape(4, 2, BLK, HW)
    grad_hidden_one, grad_qkv, grad_fc, grad_proj, outputs, terms = call(
        backward, "backward", 7,
        (
            hidden_one, hidden_two, grad_pre, mat_qkv, mixed, totals, grad_context, context,
            grad_branch, result.reshape(2, BLK, D),
        ),
        [
            ((2, BLK, WIDE), F32), ((PIECE, QW), LOW), ((PIECE, WIDE), LOW), ((PB, D), F32),
            ((2, BLK, D), LOW), ((1, QW), F32),
        ],
        [ANY] * 4 + [VM, VM, ANY, VM, VM, ANY], [VM, VM, VM, VM, ANY, VM],
        [
            pltpu.VMEM((SEQ, WIDE), LOW), pltpu.VMEM((SEQ, WIDE), LOW), pltpu.VMEM((WIDE, QW), LOW),
            pltpu.VMEM((WIDE, WIDE), LOW), pltpu.VMEM((SEQ, WIDE), LOW), pltpu.VMEM((SEQ, HW), LOW), pltpu.VMEM((SEQ, QW), LOW),
            pltpu.VMEM((SEQ, HEAD), F32), pltpu.VMEM((SEQ, HEAD), F32),
        ]
        + team_scatter_scratch(WIDE) + scatter_scratch(PIECE, WIDE) + scatter_scratch(PIECE, QW)
        + scatter_scratch(PB, D)
        + [
            pltpu.VMEM((PROJ // 2, WIDE), LOW), pltpu.VMEM((PROJ // 4, D), LOW),
            pltpu.VMEM((PROJ // 4, WIDE), LOW),
        ],
        TEAM_SCATTER_SEMS + 3 * SCATTER_SEMS + TOKENS_SEMS + 2 * TEAM_SWAP_SEMS + 8,
    )
    grad_hidden_one = back_product(grad_hidden_one.reshape(2 * BLK, WIDE).astype(LOW), to_wide)
    grad_ln_one, grad_gain_one, grad_shift_one = ln1_pull(grad_hidden_one)
    grad_in = (grad_resid + grad_ln_one).astype(LOW)
    grad_proj = grad_proj[:50].reshape(-1)

    terms = terms.reshape(3, HW)
    mine = (jnp.arange(4) == rank).astype(F32)[:, None, None]
    grad_bq = head_join(mine * terms[0][None, None])[0]
    grad_bv = head_join(mine * terms[2][None, None])[0]
    fc_terms = fc_terms.reshape(YN, 1, ZN, 1, PIECE)[..., :200]
    spot = (jnp.arange(CN) == c)[None, :, None, None, None] & (jnp.arange(XN) == x)[
        None, None, None, :, None
    ]
    grad_fc_bias = jnp.where(spot, fc_terms, 0.0).reshape(-1)
    front = jnp.concatenate([grad_gain_one, grad_shift_one, grad_bq, grad_bv])
    tail = jnp.concatenate(
        [
            ones_row(grad_branch), grad_gain_two, grad_shift_two, grad_fc_bias,
            jnp.sum(grad_full, axis=0),
        ]
    )
    small = jnp.concatenate([front.reshape(32, 200), tail.reshape(32, 400)], axis=1)
    small = pad_to(small, 1, 1024).reshape(YN, CN, ZN, XN, 8, 128).transpose(0, 2, 1, 3, 4, 5)
    units_qkv = pad_to(grad_qkv[:200].reshape(4, 50, QW), 1, 64)
    units_fc = pad_to(grad_fc[:200].reshape(4, 50, WIDE), 1, 64)
    grad_in, got_qkv, got_fc, total = call(
        epilogue, "epilogue", 8,
        (grad_in.reshape(2, BLK, D), units_qkv, units_fc, small.reshape(YN, ZN, 4, 8, 128)),
        [((MICRO, BLK, D), LOW), ((4, 64, QW), LOW), ((4, 64, WIDE), LOW), ((8, 128), F32)],
        [ANY, ANY, ANY, VM], [ANY, ANY, ANY, VM],
        [pltpu.VMEM((ZN, 4, 8, 128), F32), pltpu.VMEM((4, 4, 8, 128), F32), pltpu.VMEM((3, 8, 128), F32)],
        2 * TEAM_SWAP_SEMS + TOKENS_SEMS + 14,
    )
    parts = got_qkv[:, :50].reshape(4, 50, 3, HW)
    grad_qkv = jnp.stack([head_join(parts[:, :, i]) for i in range(3)], axis=1)
    grad_qkv = grad_qkv.astype(F32).reshape(-1)
    grad_fc = got_fc[:, :50].reshape(CN, XN, 50, YN, ZN, PIECE)[..., :200]
    grad_fc = grad_fc.transpose(2, 3, 0, 4, 1, 5).astype(F32).reshape(-1)
    total = total.reshape(-1)
    return (
        outputs[:, None],
        grad_in.astype(F32)[:, None],
        grad_qkv,
        grad_proj,
        grad_fc,
        grad_out_w,
        total[:200],
        total[200:600],
    )


def solution(mesh):
    placed = (
        P(None, "dp", "ctx", None),
        P(None, "dp", "ctx", None),
        P(("dp", "ctx")),
        P(("dp", "ctx")),
        P(("dp", "ctx")),
        P(("dp", "ctx")),
        P(("dp", "ctx")),
    )
    fast = dict(mesh.shape) == {"dp": DP, "ctx": CTX}
    return jax.shard_map(
        fast_shards if fast else shards,
        mesh=mesh,
        in_specs=placed,
        out_specs=(
            P(None, "dp", "ctx", None),
            P(None, "dp", "ctx", None),
            P(("dp", "ctx")),
            P(("dp", "ctx")),
            P(("dp", "ctx")),
            P(("dp", "ctx")),
            P(("dp", "ctx")),
            P(("dp", "ctx")),
        ),
        check_vma=False,
    )
```

```python
import functools

import jax
import jax.numpy as jnp
import numpy as np
from jax import lax
from jax.experimental import pallas as pl
from jax.experimental.pallas import tpu as pltpu
from jax.sharding import PartitionSpec as P

D = 1600
HEADS = 25
HEAD = 64
FF = 6400
MICRO = 2


EPS = 1e-05


def layer_norm(values, gain, shift):
    center = values - jnp.mean(values, axis=-1, keepdims=True)
    spread = jnp.mean(center * center, axis=-1, keepdims=True)
    return center * lax.rsqrt(spread + EPS) * gain + shift


def gelu_tanh(values):
    return jax.nn.gelu(values, approximate=True)


def unpack(gathered):
    packed_qkv, packed_proj, packed_fc, packed_out, packed_small = gathered
    return (
        packed_qkv.reshape(D, 3 * D),
        packed_proj.reshape(D, D),
        packed_fc.reshape(D, FF),
        packed_out.reshape(FF, D),
        packed_small.astype(jnp.float32),
    )


def fetch(w_qkv, w_proj, w_fc, w_out, smalls):
    return unpack(
        (
            lax.all_gather(w_qkv, ("dp", "ctx"), axis=0, tiled=True),
            lax.all_gather(w_proj, ("dp", "ctx"), axis=0, tiled=True),
            lax.all_gather(w_fc, ("dp", "ctx"), axis=0, tiled=True),
            lax.all_gather(w_out, ("dp", "ctx"), axis=0, tiled=True),
            lax.all_gather(smalls, ("dp", "ctx"), axis=0, tiled=True),
        )
    )


def fetch_again(w_qkv, w_proj, w_fc, w_out, smalls):
    return unpack(
        (
            lax.all_gather(w_qkv, ("dp", "ctx"), axis=0, tiled=True),
            lax.all_gather(w_proj, ("dp", "ctx"), axis=0, tiled=True),
            lax.all_gather(w_fc, ("dp", "ctx"), axis=0, tiled=True),
            lax.all_gather(w_out, ("dp", "ctx"), axis=0, tiled=True),
            lax.all_gather(smalls, ("dp", "ctx"), axis=0, tiled=True),
        )
    )


def outer_sum(left, right):
    return lax.dot_general(
        left, right, (((0,), (0,)), ((), ())), preferred_element_type=jnp.float32
    )


def back_product(grad, weight):
    return lax.dot_general(
        grad, weight, (((1,), (1,)), ((), ())), preferred_element_type=jnp.float32
    )


def flat_term(left, right, start, count):
    width = right.shape[1]
    span = count // width + 2
    padded = jnp.pad(left, ((0, 0), (0, span)))
    first_row = start // width
    piece = lax.dynamic_slice_in_dim(padded, first_row, span, 1)
    block = outer_sum(piece, right).astype(jnp.bfloat16).reshape(-1)
    return lax.dynamic_slice_in_dim(block, start, count, 0)


def masked_scores(queries, keys, query_start, key_start):
    scores = (
        jnp.einsum("sqhe,skhe->shqk", queries, keys, preferred_element_type=jnp.float32) * 0.125
    )
    query_pos = query_start + jnp.arange(queries.shape[1])
    key_pos = key_start + jnp.arange(keys.shape[1])
    allowed = query_pos[:, None] >= key_pos[None, :]
    return jnp.where(allowed[None, None], scores, -1e30)


def segment(small_vals, which):
    return small_vals[which * D : (which + 1) * D]


def shards(inputs, grad_out, w_qkv, w_proj, w_fc, w_out, smalls):
    seqs = inputs.shape[1]
    local_len = inputs.shape[2]
    rows = seqs * local_len
    offset = lax.axis_index("ctx") * local_len
    acc_small = [jnp.zeros((D,), jnp.float32) for _ in range(7)]
    acc_fc_bias = jnp.zeros((FF,), jnp.float32)
    acc_out_bias = jnp.zeros((D,), jnp.float32)
    result_list = []
    grad_list = []
    kept_hidden_one = []
    kept_mixed_grad = []
    kept_context = []
    kept_branch_grad = []
    kept_hidden_two = []
    kept_pre_grad = []
    kept_activ = []
    kept_out_grad = []
    for batch_index in range(MICRO):
        params = fetch(w_qkv, w_proj, w_fc, w_out, smalls)
        mat_qkv, mat_proj, mat_fc, mat_out, small_vals = params
        tokens = inputs[batch_index].astype(jnp.float32).reshape(rows, D)
        hidden_one, ln1_pull = jax.vjp(
            layer_norm, tokens, segment(small_vals, 0), segment(small_vals, 1)
        )
        hidden_one = hidden_one.astype(jnp.bfloat16)
        qkv_bias = jnp.concatenate(
            [segment(small_vals, 2), jnp.zeros((D,), jnp.float32), segment(small_vals, 3)]
        )
        mixed = (
            jnp.dot(hidden_one, mat_qkv, preferred_element_type=jnp.float32) + qkv_bias
        ).astype(jnp.bfloat16)
        queries = mixed[:, :D].reshape(seqs, local_len, HEADS, HEAD)
        keys_local = mixed[:, D : 2 * D].reshape(seqs, local_len, D)
        values_local = mixed[:, 2 * D :].reshape(seqs, local_len, D)
        keys_all, values_all = (
            lax.all_gather(keys_local, "ctx", axis=1, tiled=True),
            lax.all_gather(values_local, "ctx", axis=1, tiled=True),
        )
        keys_all = keys_all.reshape(seqs, -1, HEADS, HEAD)
        values_all = values_all.reshape(seqs, -1, HEADS, HEAD)
        scores = masked_scores(queries, keys_all, offset, 0)
        row_peak = jnp.max(scores, axis=-1, keepdims=True)
        log_total = row_peak + jnp.log(jnp.sum(jnp.exp(scores - row_peak), axis=-1, keepdims=True))
        attn_low = jnp.exp(scores - log_total).astype(jnp.bfloat16)
        context = jnp.einsum(
            "shqk,skhe->sqhe", attn_low, values_all, preferred_element_type=jnp.float32
        )
        context = context.reshape(rows, D).astype(jnp.bfloat16)
        resid = (
            tokens
            + jnp.dot(context, mat_proj, preferred_element_type=jnp.float32)
            + segment(small_vals, 4)
        )
        hidden_two, ln2_pull = jax.vjp(
            layer_norm, resid, segment(small_vals, 5), segment(small_vals, 6)
        )
        hidden_two = hidden_two.astype(jnp.bfloat16)
        pre_act = (
            jnp.dot(hidden_two, mat_fc, preferred_element_type=jnp.float32)
            + small_vals[7 * D : 7 * D + FF]
        )
        activ, gelu_pull = jax.vjp(gelu_tanh, pre_act)
        activ = activ.astype(jnp.bfloat16)
        result = (
            resid
            + jnp.dot(activ, mat_out, preferred_element_type=jnp.float32)
            + small_vals[7 * D + FF :]
        )
        result_list.append(result.astype(jnp.bfloat16).reshape(seqs, local_len, D))
        back_params = fetch_again(w_qkv, w_proj, w_fc, w_out, smalls)
        mat_qkv, mat_proj, mat_fc, mat_out, small_vals = back_params
        grad_low = grad_out[batch_index].reshape(rows, D)
        grad_full = grad_low.astype(jnp.float32)
        acc_out_bias = acc_out_bias + jnp.sum(grad_full, axis=0)
        grad_act = back_product(grad_low, mat_out)
        (grad_pre,) = gelu_pull(grad_act)
        grad_pre = grad_pre.astype(jnp.bfloat16)
        acc_fc_bias = acc_fc_bias + jnp.sum(grad_pre.astype(jnp.float32), axis=0)
        grad_hidden_two = back_product(grad_pre, mat_fc)
        grad_ln_two, grad_gain_two, grad_shift_two = ln2_pull(grad_hidden_two)
        acc_small[5] = acc_small[5] + grad_gain_two
        acc_small[6] = acc_small[6] + grad_shift_two
        grad_resid = grad_full + grad_ln_two
        grad_branch = grad_resid.astype(jnp.bfloat16)
        acc_small[4] = acc_small[4] + jnp.sum(grad_branch.astype(jnp.float32), axis=0)
        grad_context = (
            back_product(grad_branch, mat_proj)
            .astype(jnp.bfloat16)
            .reshape(seqs, local_len, HEADS, HEAD)
        )
        scores = masked_scores(queries, keys_all, offset, 0)
        attn_prob = jnp.exp(scores - log_total)
        grad_attn = jnp.einsum(
            "sqhe,skhe->shqk", grad_context, values_all, preferred_element_type=jnp.float32
        )
        row_delta = jnp.sum(attn_prob * grad_attn, axis=-1, keepdims=True)
        grad_scores = (attn_prob * (grad_attn - row_delta)).astype(jnp.bfloat16)
        grad_queries = (
            jnp.einsum("shqk,skhe->sqhe", grad_scores, keys_all, preferred_element_type=jnp.float32)
            * 0.125
        )
        query_all, dctx_all = (
            lax.all_gather(queries.reshape(seqs, local_len, D), "ctx", axis=1, tiled=True),
            lax.all_gather(grad_context.reshape(seqs, local_len, D), "ctx", axis=1, tiled=True),
        )
        lse_all, delta_all = (
            lax.all_gather(jnp.transpose(log_total[..., 0], (0, 2, 1)), "ctx", axis=1, tiled=True),
            lax.all_gather(jnp.transpose(row_delta[..., 0], (0, 2, 1)), "ctx", axis=1, tiled=True),
        )
        query_all = query_all.reshape(seqs, -1, HEADS, HEAD)
        dctx_all = dctx_all.reshape(seqs, -1, HEADS, HEAD)
        lse_all = jnp.transpose(lse_all, (0, 2, 1))[..., None]
        delta_all = jnp.transpose(delta_all, (0, 2, 1))[..., None]
        own_keys = keys_local.reshape(seqs, local_len, HEADS, HEAD)
        own_values = values_local.reshape(seqs, local_len, HEADS, HEAD)
        col_scores = masked_scores(query_all, own_keys, 0, offset)
        col_prob = jnp.exp(col_scores - lse_all)
        col_dattn = jnp.einsum(
            "sqhe,skhe->shqk", dctx_all, own_values, preferred_element_type=jnp.float32
        )
        col_ds = (col_prob * (col_dattn - delta_all)).astype(jnp.bfloat16)
        grad_keys = (
            jnp.einsum("shqk,sqhe->skhe", col_ds, query_all, preferred_element_type=jnp.float32)
            * 0.125
        )
        grad_values = jnp.einsum(
            "shqk,sqhe->skhe",
            col_prob.astype(jnp.bfloat16),
            dctx_all,
            preferred_element_type=jnp.float32,
        )
        grad_mixed = jnp.concatenate(
            [
                grad_queries.reshape(rows, D),
                grad_keys.reshape(rows, D),
                grad_values.reshape(rows, D),
            ],
            axis=1,
        ).astype(jnp.bfloat16)
        bias_terms = jnp.sum(grad_mixed.astype(jnp.float32), axis=0)
        acc_small[2] = acc_small[2] + bias_terms[:D]
        acc_small[3] = acc_small[3] + bias_terms[2 * D :]
        grad_hidden_one = back_product(grad_mixed, mat_qkv)
        grad_ln_one, grad_gain_one, grad_shift_one = ln1_pull(grad_hidden_one)
        acc_small[0] = acc_small[0] + grad_gain_one
        acc_small[1] = acc_small[1] + grad_shift_one
        grad_list.append((grad_resid + grad_ln_one).reshape(seqs, local_len, D))
        kept_hidden_one.append(hidden_one)
        kept_mixed_grad.append(grad_mixed)
        kept_context.append(context)
        kept_branch_grad.append(grad_branch)
        kept_hidden_two.append(hidden_two)
        kept_pre_grad.append(grad_pre)
        kept_activ.append(activ)
        kept_out_grad.append(grad_low)
    front_grads = jnp.concatenate(acc_small[0:4])
    tail_grads = jnp.concatenate(acc_small[4:7] + [acc_fc_bias, acc_out_bias])
    grad_qkv = lax.psum_scatter(
        flat_term(
            jnp.concatenate(kept_hidden_one),
            jnp.concatenate(kept_mixed_grad),
            jnp.int32(0),
            lax.axis_size(("dp", "ctx")) * w_qkv.shape[0],
        ),
        ("dp", "ctx"),
        scatter_dimension=0,
        tiled=True,
    ).astype(jnp.float32)
    grad_proj = lax.psum_scatter(
        flat_term(
            jnp.concatenate(kept_context),
            jnp.concatenate(kept_branch_grad),
            jnp.int32(0),
            lax.axis_size(("dp", "ctx")) * w_proj.shape[0],
        ),
        ("dp", "ctx"),
        scatter_dimension=0,
        tiled=True,
    ).astype(jnp.float32)
    grad_fc = lax.psum_scatter(
        flat_term(
            jnp.concatenate(kept_hidden_two),
            jnp.concatenate(kept_pre_grad),
            jnp.int32(0),
            lax.axis_size(("dp", "ctx")) * w_fc.shape[0],
        ),
        ("dp", "ctx"),
        scatter_dimension=0,
        tiled=True,
    ).astype(jnp.float32)
    grad_out_w = lax.psum_scatter(
        flat_term(
            jnp.concatenate(kept_activ),
            jnp.concatenate(kept_out_grad),
            jnp.int32(0),
            lax.axis_size(("dp", "ctx")) * w_out.shape[0],
        ),
        ("dp", "ctx"),
        scatter_dimension=0,
        tiled=True,
    ).astype(jnp.float32)
    grad_front, grad_tail = (
        lax.psum_scatter(front_grads, ("dp", "ctx"), scatter_dimension=0, tiled=True),
        lax.psum_scatter(tail_grads, ("dp", "ctx"), scatter_dimension=0, tiled=True),
    )
    return (
        jnp.stack(result_list),
        jnp.stack(grad_list),
        grad_qkv,
        grad_proj,
        grad_fc,
        grad_out_w,
        grad_front,
        grad_tail,
    )


DP, CTX = 4, 8
YN, CN, ZN, XN = 2, 2, 4, 2
SLOTS = 7
HW = SLOTS * HEAD
QW = 3 * HW
STARTS = (0, 7, 13, 19)
COUNTS = (7, 6, 6, 6)
BLK = 128
SEQ = 8 * BLK
PIECE = 208
WIDE = 8 * PIECE
PB = 64
PROJ = 32 * PB
LOW = jnp.bfloat16
F32 = jnp.float32
VMEM_BYTES = 60 * 1024 * 1024
ANY = pl.BlockSpec(memory_space=pl.ANY)
VM = pl.BlockSpec(memory_space=pltpu.VMEM)


def here():
    dp, ctx = lax.axis_index("dp"), lax.axis_index("ctx")
    return dp // CN, dp % CN, ctx // XN, ctx % XN


def device(y, c, z, x):
    return (y * CN + c, z * XN + x)


class Wires:
    def __init__(self, sems):
        self.sems, self.used = sems, 0

    def one(self):
        self.used += 1
        assert self.used <= self.sems.shape[0]
        return self.sems.at[self.used - 1]

    def far(self, source, target, where):
        return pltpu.make_async_remote_copy(
            src_ref=source,
            dst_ref=target,
            send_sem=self.one(),
            recv_sem=self.one(),
            device_id=where,
            device_id_type=pl.DeviceIdType.MESH,
        )

    def near(self, source, target):
        return pltpu.make_async_copy(source, target, self.one())


def signal(where):
    pl.semaphore_signal(
        pltpu.get_barrier_semaphore(), inc=1, device_id=where, device_id_type=pl.DeviceIdType.MESH
    )


def team_peers(y, c, z, x):
    return [device(y, 1 - c, z, x), device(y, c, z, 1 - x), device(y, 1 - c, z, 1 - x)]


def grid_peers(y, c, z, x):
    ring = [device(y, c, lax.rem(z + k, ZN), x) for k in range(1, ZN)]
    return ring + [device(1 - y, c, z, x)]


def meet(peers):
    for peer in peers:
        signal(peer)
    pl.semaphore_wait(pltpu.get_barrier_semaphore(), len(peers))


def call(body, name, ident, ins, outs, in_specs, out_specs, scratch, sems, cost=None):
    return pl.pallas_call(
        body,
        out_shape=[jax.ShapeDtypeStruct(s, d) for s, d in outs],
        in_specs=in_specs,
        out_specs=out_specs,
        scratch_shapes=list(scratch) + [pltpu.SemaphoreType.DMA((sems,))],
        compiler_params=pltpu.CompilerParams(
            collective_id=ident, has_side_effects=True, vmem_limit_bytes=VMEM_BYTES
        ),
        name=name,
    )(*ins)


class Gather:
    def __init__(self, wires, piece, whole, spot):
        y, c, z, x = self.spot = spot
        self.z = z
        self.across = device(1 - y, c, z, x)
        up = device(y, c, lax.min(z + 1, ZN - 1), x)
        down = device(y, c, lax.max(z - 1, 0), x)
        self.local = wires.near(piece, whole.at[y, z])
        self.mine = wires.far(piece, whole.at[y, z], self.across)
        self.ups, self.downs, self.from_low, self.from_high = [], [], [], []
        for turn in range(1, ZN):
            low = lax.max(z - (turn - 1), 0)
            high = lax.min(z + (turn - 1), ZN - 1)
            source = piece if turn == 1 else whole.at[y, low]
            self.ups.append(wires.far(source, whole.at[y, low], up))
            source = piece if turn == 1 else whole.at[y, high]
            self.downs.append(wires.far(source, whole.at[y, high], down))
            low = lax.max(z - turn, 0)
            high = lax.min(z + turn, ZN - 1)
            self.from_low.append(wires.far(whole.at[y, low], whole.at[y, low], self.across))
            self.from_high.append(wires.far(whole.at[y, high], whole.at[y, high], self.across))

    def send_up(self, turn):
        return (self.z >= turn - 1) & (self.z < ZN - 1)

    def send_down(self, turn):
        return (self.z <= ZN - turn) & (self.z > 0)

    def start(self):
        self.local.start()
        self.mine.start()
        pl.when(self.send_up(1))(self.ups[0].start)
        pl.when(self.send_down(1))(self.downs[0].start)

    def step(self, turn):
        @pl.when(self.z >= turn)
        def _():
            self.ups[turn - 1].wait_recv()
            if turn < ZN - 1:
                pl.when(self.send_up(turn + 1))(self.ups[turn].start)
            self.from_low[turn - 1].start()

        @pl.when(self.z + turn <= ZN - 1)
        def _():
            self.downs[turn - 1].wait_recv()
            if turn < ZN - 1:
                pl.when(self.send_down(turn + 1))(self.downs[turn].start)
            self.from_high[turn - 1].start()

    def finish(self):
        self.local.wait()
        self.mine.wait()
        for turn in range(1, ZN):
            pl.when(self.send_up(turn))(self.ups[turn - 1].wait_send)
            pl.when(self.send_down(turn))(self.downs[turn - 1].wait_send)
            pl.when(self.z >= turn)(self.from_low[turn - 1].wait)
            pl.when(self.z + turn <= ZN - 1)(self.from_high[turn - 1].wait)


GATHER_SEMS = 1 + 2 + 2 * 4 * 3


class Scatter:
    def __init__(self, wires, parts, landed, arrived, spot):
        y, c, z, x = spot
        self.y, self.z, self.size = y, z, landed.shape[1]
        self.parts, self.landed, self.arrived = parts, landed, arrived
        across = device(1 - y, c, z, x)
        up = device(y, c, lax.min(z + 1, ZN - 1), x)
        down = device(y, c, lax.max(z - 1, 0), x)
        base = wires.used
        wires.used += 2 * ZN
        self.over = lambda o: pltpu.make_async_remote_copy(
            src_ref=parts.at[self.rows(1 - y, o)],
            dst_ref=landed.at[o],
            send_sem=wires.sems.at[base + o],
            recv_sem=wires.sems.at[base + ZN + o],
            device_id=across,
            device_id_type=pl.DeviceIdType.MESH,
        )
        self.ups, self.downs = [], []
        for turn in range(1, ZN):
            high = lax.min(z + ZN - turn, ZN - 1)
            low = lax.max(z - ZN + turn, 0)
            slot = self.slot(0, turn, z + 1)
            self.ups.append((high, wires.far(landed.at[high], arrived.at[slot], up)))
            slot = self.slot(1, turn, z - 1)
            self.downs.append((low, wires.far(landed.at[low], arrived.at[slot], down)))

    def rows(self, y, z):
        return pl.ds(pl.multiple_of((y * ZN + z) * self.size, 16), self.size)

    @staticmethod
    def slot(side, turn, z):
        return jnp.where(z == 1 + side, turn - 1, turn + 1)

    def start(self):
        z = self.z
        first = jnp.where(z < 2, 3, 0)
        second = jnp.where(z < 2, 2, 1)
        third = jnp.where(z == 0, 1, jnp.where(z == 1, 0, jnp.where(z == 2, 3, 2)))
        for o in (first, second, third, z):
            self.over(o).start()

    def goes_up(self, turn):
        return (self.z <= turn - 1) & (self.z < ZN - 1)

    def goes_down(self, turn):
        return (self.z >= ZN - turn) & (self.z > 0)

    def add(self, o, side, turn, more):
        total = self.landed[o].astype(F32) + self.parts[self.rows(self.y, o), :].astype(F32)
        if more:
            total = total + self.arrived[self.slot(side, turn - 1, self.z)].astype(F32)
        self.landed[o] = total.astype(LOW)

    def step(self, turn):
        for side, goes, jobs, inner in (
            (0, self.goes_up, self.ups, self.z > 0),
            (1, self.goes_down, self.downs, self.z < ZN - 1),
        ):
            o, copy = jobs[turn - 1]

            @pl.when(goes(turn))
            def _(side=side, jobs=jobs, inner=inner, o=o, copy=copy):
                self.over(o).wait_recv()
                if turn == 1:
                    self.add(o, side, turn, False)
                else:

                    @pl.when(inner)
                    def _():
                        jobs[turn - 2][1].wait_recv()
                        self.add(o, side, turn, True)

                    @pl.when(jnp.logical_not(inner))
                    def _():
                        self.add(o, side, turn, False)

                copy.start()

    def finish(self, total):
        self.over(self.z).wait_recv()
        total[...] = (
            self.landed[self.z].astype(F32) + self.parts[self.rows(self.y, self.z), :].astype(F32)
        ).astype(total.dtype)
        last = ZN - 1

        @pl.when(self.z > 0)
        def _():
            self.ups[last - 1][1].wait_recv()
            total[...] = (total[...].astype(F32) + self.arrived[self.slot(0, last, self.z)].astype(F32)).astype(total.dtype)

        @pl.when(self.z < ZN - 1)
        def _():
            self.downs[last - 1][1].wait_recv()
            total[...] = (total[...].astype(F32) + self.arrived[self.slot(1, last, self.z)].astype(F32)).astype(total.dtype)

        for o in range(ZN):
            self.over(o).wait_send()
        for turn in range(1, ZN):
            pl.when(self.goes_up(turn))(self.ups[turn - 1][1].wait_send)
            pl.when(self.goes_down(turn))(self.downs[turn - 1][1].wait_send)


SCATTER_SEMS = 2 * (ZN + 6)


class TeamGather:
    def __init__(self, wires, block, whole, spot):
        y, c, z, x = spot
        mate, beside = device(y, 1 - c, z, x), device(y, c, z, 1 - x)
        self.local = [wires.near(block.at[s], whole.at[c, s, x]) for s in range(2)]
        self.to_mate = [wires.far(block.at[s], whole.at[c, s, x], mate) for s in range(2)]
        self.to_side = [wires.far(block.at[s], whole.at[c, s, x], beside) for s in range(2)]
        self.relay = [
            wires.far(whole.at[c, s, 1 - x], whole.at[c, s, 1 - x], mate) for s in range(2)
        ]

    def start(self):
        for copy in self.to_side + self.to_mate + self.local:
            copy.start()

    def step(self, s):
        self.to_side[s].wait_recv()
        self.relay[s].start()

    def finish(self):
        for copy in self.local + self.to_mate + self.relay:
            copy.wait()
        for copy in self.to_side:
            copy.wait_send()


TEAM_GATHER_SEMS = 2 + 2 * 6


class TeamSwap:
    def __init__(self, wires, source, target, spot):
        y, c, z, x = spot
        self.local = wires.near(source(c, x), target(c, x))
        self.copies = [
            wires.far(source(p, q), target(c, x), device(y, p, z, q))
            for p, q in ((c, 1 - x), (1 - c, 1 - x), (1 - c, x))
        ]

    def start(self):
        for copy in self.copies + [self.local]:
            copy.start()

    def finish(self):
        for copy in self.copies + [self.local]:
            copy.wait()


TEAM_SWAP_SEMS = 1 + 2 * 3


class TeamScatter:
    def __init__(self, wires, parts, landed, leaving, arrived, spot):
        y, c, z, x = spot
        self.c, self.x = c, x
        self.parts, self.landed, self.leaving, self.arrived = parts, landed, leaving, arrived
        mate, beside = device(y, 1 - c, z, x), device(y, c, z, 1 - x)
        self.to_mate = [wires.far(parts.at[half_rows(1 - c, s)], landed.at[s], mate) for s in range(2)]
        self.to_side = [wires.far(leaving.at[s], arrived.at[s], beside) for s in range(2)]

    def side(self, x):
        return pl.ds(pl.multiple_of(x * BLK, BLK), BLK)

    def start(self):
        for copy in self.to_mate:
            copy.start()

    def step(self, s):
        self.to_mate[s].wait_recv()
        far = 1 - self.x
        self.leaving[s] = (
            self.landed[s, self.side(far), :].astype(F32)
            + self.parts[block_rows(self.c, s, far), :].astype(F32)
        ).astype(LOW)
        self.to_side[s].start()

    def finish(self, total):
        for s in range(2):
            self.to_side[s].wait_recv()
            total[s] = (
                self.landed[s, self.side(self.x), :].astype(F32)
                + self.parts[block_rows(self.c, s, self.x), :].astype(F32)
                + self.arrived[s].astype(F32)
            )
        for copy in self.to_mate + self.to_side:
            copy.wait_send()


def block_rows(c, s, x):
    return pl.ds(pl.multiple_of((c * 4 + s * 2 + x) * BLK, BLK), BLK)


def half_rows(c, s):
    return pl.ds(pl.multiple_of((c * 2 + s) * 2 * BLK, 2 * BLK), 2 * BLK)


TEAM_SCATTER_SEMS = 2 * 4


def team_scatter_scratch(width):
    return [
        pltpu.VMEM((2, 2 * BLK, width), LOW),
        pltpu.VMEM((2, BLK, width), LOW),
        pltpu.VMEM((2, BLK, width), LOW),
    ]


def scatter_scratch(rows, width):
    return [pltpu.VMEM((ZN, rows, width), LOW), pltpu.VMEM((5, rows, width), LOW)]


class Tokens:
    def __init__(self, wires, source, target, spot, back):
        y, c, z, x = spot
        self.own, self.local, self.copies, self.peers = [], [], [], []
        for k in range(2):
            if not back:
                m = lax.rem(z + k, 2)
                goal_c, goal_z = z // 2, 2 * m + c
                block, landing = source.at[m], target.at[lax.rem(z, 2)]
            else:
                m = z // 2
                s = lax.rem(m + k, 2)
                goal_c, goal_z = lax.rem(z, 2), 2 * c + s
                block, landing = source.at[s], target.at[m]
            goal = device(y, goal_c, goal_z, x)
            stays = (goal_c == c) & (goal_z == z)
            self.own.append(stays)
            self.peers.append(goal)
            self.local.append(wires.near(block, landing))
            self.copies.append(wires.far(block, landing, goal))

    def start(self):
        for stays, local, copy in zip(self.own, self.local, self.copies):
            pl.when(stays)(local.start)
            pl.when(jnp.logical_not(stays))(copy.start)

    def finish(self):
        for stays, local, copy in zip(self.own, self.local, self.copies):
            pl.when(stays)(local.wait)
            pl.when(jnp.logical_not(stays))(copy.wait)


TOKENS_SEMS = 2 * 3


def token_sources(spot, back):
    y, c, z, x = spot
    found = []
    for k in range(2):
        if back:
            m = lax.rem(z + k, 2)
            goal = (z // 2, 2 * m + c)
        else:
            s = lax.rem(z // 2 + k, 2)
            goal = (lax.rem(z, 2), 2 * c + s)
        found.append((device(y, goal[0], goal[1], x), (goal[0] == c) & (goal[1] == z)))
    return found


def meet_tokens(peers, spot, back):
    for peer in peers:
        signal(peer)
    for source, stays in token_sources(spot, back):
        pl.when(jnp.logical_not(stays))(functools.partial(signal, source))
    leaving = sum(jnp.where(stays, 0, 1) for _, stays in token_sources(spot, not back))
    pl.semaphore_wait(pltpu.get_barrier_semaphore(), len(peers) + leaving)


def prologue(
    inputs, units_qkv, units_fc, small, piece_out, piece_proj,
    tokens, got_qkv, got_fc, smalls, all_out, all_proj, sems,
):
    spot = y, c, z, x = here()
    wires = Wires(sems)
    meet_tokens(team_peers(*spot) + grid_peers(*spot), spot, False)
    first = TeamSwap(
        wires, lambda p, q: small, lambda p, q: smalls.at[y, z, p * XN + q], spot
    )
    qkv = TeamSwap(
        wires, lambda p, q: units_qkv.at[p * XN + q], lambda p, q: got_qkv.at[p * XN + q], spot
    )
    fc = TeamSwap(
        wires, lambda p, q: units_fc.at[p * XN + q], lambda p, q: got_fc.at[p * XN + q], spot
    )
    move = Tokens(wires, inputs, tokens, spot, False)
    out = Gather(wires, piece_out, all_out, spot)
    rank = c * XN + x
    proj = Gather(wires, piece_proj, all_proj.at[rank], spot)
    side = wires.far(all_proj.at[rank], all_proj.at[rank], device(y, c, z, 1 - x))
    mate = device(y, 1 - c, z, x)
    relay = [
        wires.far(all_proj.at[r], all_proj.at[r], mate) for r in (rank, c * XN + 1 - x)
    ]
    column = [
        wires.far(smalls.at[y, z], smalls.at[y, z], device(y, c, lax.rem(z + k, ZN), x))
        for k in range(1, ZN)
    ]
    over = wires.far(smalls.at[y], smalls.at[y], device(1 - y, c, z, x))
    first.start()
    move.start()
    qkv.start()
    fc.start()
    first.finish()
    for copy in column:
        copy.start()
    proj.start()
    out.start()
    for copy in column:
        copy.wait()
    over.start()
    proj.step(1)
    over.wait()
    proj.step(2)
    proj.step(3)
    out.step(1)
    proj.finish()
    side.start()
    relay[0].start()
    move.finish()
    qkv.finish()
    fc.finish()
    out.step(2)
    out.step(3)
    side.wait_recv()
    relay[1].start()
    out.finish()
    side.wait_send()
    for copy in relay:
        copy.wait()


def forward(
    hidden, grads, piece_qkv, piece_fc, mat_proj, to_proj, to_wide,
    tokens, bias_qkv, bias_proj, gain2, shift2,
    hidden_all, cotangent, grad_all, all_qkv, all_fc, second_all, mixed, totals, context_out, resid,
    hidden_in, mat_in, proj_in, to_proj_in, to_wide_in, context, got, second, sems,
):
    spot = y, c, z, x = here()
    wires = Wires(sems)
    load = [
        wires.near(*both)
        for both in ((mat_proj, proj_in), (to_proj, to_proj_in), (to_wide, to_wide_in))
    ]
    load_hidden, load_qkv = wires.near(hidden_all, hidden_in), wires.near(all_qkv, mat_in)
    meet_tokens(team_peers(*spot) + grid_peers(*spot), spot, False)
    team = TeamGather(wires, hidden, hidden_all, spot)
    qkv = Gather(wires, piece_qkv, all_qkv, spot)
    fc = Gather(wires, piece_fc, all_fc, spot)
    bring = Tokens(wires, grads, cotangent, spot, False)
    team_two = TeamGather(wires, cotangent, grad_all, spot)
    team_three = TeamGather(wires, second, second_all, spot)
    swaps = [
        TeamSwap(
            wires,
            lambda p, q, s=s: context.at[block_rows(p, s, q)],
            lambda p, q, s=s: got.at[p * XN + q, s],
            spot,
        )
        for s in range(2)
    ]
    qkv.start()
    team.start()
    qkv.step(1)
    team.step(0)
    team.step(1)
    qkv.step(2)
    qkv.step(3)
    fc.start()
    for copy in load:
        copy.start()
    team.finish()
    load_hidden.start()
    qkv.finish()
    load_qkv.start()
    bring.start()
    load_hidden.wait()
    load_qkv.wait()

    @pl.loop(0, SEQ // QB)
    def _(i):
        rows = pl.ds(pl.multiple_of(i * QB, QB), QB)
        flat = hidden_in[i // 2, i % 2].reshape(QB, WIDE)
        mixed[rows, :] = (dot(flat, mat_in[...].reshape(WIDE, QW)) + bias_qkv[...]).astype(LOW)

    fc.step(1)
    for head in range(SLOTS):
        attend(mixed, context, totals, head)
        if head == 2:
            fc.step(2)
    bring.finish()
    for copy in swaps:
        copy.start()
    team_two.start()
    fc.step(3)
    for copy in load:
        copy.wait()
    for copy in swaps:
        copy.finish()
    placed = 0.0
    for r in range(4):
        placed = placed + dot(
            got[r].reshape(2 * BLK, HW), to_proj_in[r * HW : (r + 1) * HW, :]
        )
    placed = placed.astype(LOW)
    context_out[...] = placed
    found = tokens[...].astype(F32) + dot(placed, proj_in[...]) + bias_proj[...]
    resid[...] = found
    normed = layer_norm(found, gain2[...], shift2[...]).astype(LOW)
    second[...] = dot(normed, to_wide_in[...]).astype(LOW).reshape(2, BLK, WIDE)
    team_three.start()
    team_two.step(0)
    team_two.step(1)
    team_three.step(0)
    team_three.step(1)
    team_two.finish()
    team_three.finish()
    fc.finish()


def gelu_both(f):
    square = f * f
    t = jnp.tanh(0.7978845608028654 * f * (1.0 + 0.044715 * square))
    half = 0.5 * (1.0 + t)
    slope = half + f * (0.5 * 0.7978845608028654) * (1.0 - t * t) * (1.0 + 3 * 0.044715 * square)
    return f * half, slope


def chunks(total, step):
    return [(start, min(step, total - start)) for start in range(0, total, step)]


def outer_into(target, left, right):
    count = left.shape[1] // 256

    @pl.loop(0, count)
    def _(i):
        at = pl.ds(pl.multiple_of(i * 256, 256), 256)
        target[at, :] = outer_sum(left[:, at], right[...]).astype(LOW)

    rest = left.shape[1] - count * 256
    if rest:
        target[count * 256 :, :] = outer_sum(left[:, count * 256 :], right[...]).astype(LOW)


def feed_forward(
    hidden_two, grad_all, mat_fc, mat_out, bias_fc,
    result, hidden, grad_out_w, grad_pre, terms,
    h2, dy, wf, wo, activ, part_r, part_h, part_o, l1, s1, a1, l2, s2, a2, l3, a3, sems,
):
    spot = y, c, z, x = here()
    wires = Wires(sems)
    load = [
        wires.near(*both) for both in ((hidden_two, h2), (mat_fc, wf), (grad_all, dy), (mat_out, wo))
    ]
    for copy in load:
        copy.start()
    meet(team_peers(*spot) + grid_peers(*spot))
    second = TeamScatter(wires, part_h, l2, s2, a2, spot)
    first = TeamScatter(wires, part_r, l1, s1, a1, spot)
    out = Scatter(wires, part_o, l3, a3, spot)
    load[0].wait()
    load[1].wait()

    @pl.loop(0, SEQ // QB)
    def _(i):
        rows = pl.ds(pl.multiple_of(i * QB, QB), QB)
        f = dot(h2[rows, :], wf[...]) + bias_fc[...]
        value, slope = gelu_both(f)
        activ[rows, :] = value.astype(LOW)
        grad_pre[rows, :] = slope.astype(LOW)

    load[2].wait()
    outer_into(part_o, activ, dy)
    out.start()
    load[3].wait()
    terms[...] = jnp.zeros_like(terms)

    @pl.loop(0, SEQ // QB)
    def _(i):
        rows = pl.ds(pl.multiple_of(i * QB, QB), QB)
        df = (back_product(dy[rows, :], wo[...]) * grad_pre[rows, :].astype(F32)).astype(LOW)
        grad_pre[rows, :] = df
        terms[...] += jnp.sum(df.astype(F32), axis=0, keepdims=True)

    def into(target, make):
        def half(which):
            @pl.loop(0, 2)
            def _(s):
                rows = half_rows(which, s)
                target[rows, :] = make(rows).astype(LOW)

        return half

    half = into(part_h, lambda rows: back_product(grad_pre[rows, :], wf[...]))
    half(1 - c)
    second.start()
    half(c)
    out.step(1)
    second.step(0)
    second.step(1)
    half = into(part_r, lambda rows: dot(activ[rows, :], wo[...]))
    half(1 - c)
    first.start()
    half(c)
    out.step(2)
    first.step(0)
    first.step(1)
    second.finish(hidden)
    out.step(3)
    first.finish(result)
    out.finish(grad_out_w)


def backward(
    hidden_one, hidden_two, grad_pre, mat_qkv, mixed_all, totals, swap_parts, context, branch, result,
    hidden, grad_qkv, grad_fc, grad_proj, outputs, terms,
    ha, hb, wq, part_f, part_h, grads, mixed, acc_k, acc_v,
    l1, s1, a1, l2, a2, l3, a3, l4, a4, pm, pk, px, sems,
):
    spot = y, c, z, x = here()
    wires = Wires(sems)
    load = [wires.near(*both) for both in ((hidden_two, ha), (grad_pre, hb), (mixed_all, mixed), (mat_qkv, wq))]
    again = wires.near(hidden_one, ha)
    for copy in load:
        copy.start()
    meet_tokens(team_peers(*spot) + grid_peers(*spot), spot, True)
    swaps = [
        TeamSwap(
            wires,
            lambda p, q, s=s: swap_parts.at[p * XN + q, s],
            lambda p, q, s=s: grads.at[block_rows(p, s, q)],
            spot,
        )
        for s in range(2)
    ]
    for copy in swaps:
        copy.start()
    fc = Scatter(wires, part_f, l2, a2, spot)
    first = TeamScatter(wires, part_h, l1, s1, a1, spot)
    qkv = Scatter(wires, wq, l3, a3, spot)
    quarter = PROJ // 4
    to_mate = wires.far(hb, pm, device(y, 1 - c, z, x))

    def side(q):
        return pl.ds(pl.multiple_of(q * quarter, 16), quarter)

    def term(p, q):
        at = pl.ds(pl.multiple_of((p * 2 + q) * quarter, quarter), quarter)
        return outer_sum(context[:, at], branch[...])

    to_side = wires.far(pm.at[side(1 - x)], px, device(y, c, z, 1 - x))
    proj = Scatter(wires, pk, l4, a4, spot)
    move = Tokens(wires, result, outputs, spot, True)
    load[0].wait()
    load[1].wait()
    outer_into(part_f, ha, hb)
    fc.start()
    again.start()
    for q in range(2):
        hb[side(q), :D] = term(1 - c, q).astype(LOW)
    to_mate.start()
    load[2].wait()
    for copy in swaps:
        copy.finish()
    for head in range(SLOTS):
        attend_back(mixed, totals, grads, acc_k, acc_v, head)
        if head == 1:
            fc.step(1)
            to_mate.wait_recv()
            pm[side(1 - x), :D] = (pm[side(1 - x), :D].astype(F32) + term(c, 1 - x)).astype(LOW)
        if head == 5:
            fc.step(2)
    load[3].wait()

    def half(which):
        @pl.loop(0, 2)
        def _(s):
            rows = half_rows(which, s)
            part_h[rows, :] = back_product(mixed[rows, :], wq[...]).astype(LOW)

    half(1 - c)
    first.start()
    half(c)
    again.wait()
    first.step(0)
    first.step(1)
    to_side.start()
    outer_into(wq, ha, mixed)
    qkv.start()
    fc.step(3)
    terms[...] = jnp.sum(mixed[...].astype(F32), axis=0, keepdims=True)
    move.start()
    first.finish(hidden)
    to_side.wait_recv()
    pk[...] = (
        pm[side(x), :D].astype(F32) + term(c, x) + px[:, :D].astype(F32)
    ).astype(LOW)
    proj.start()
    fc.finish(grad_fc)
    qkv.step(1)
    qkv.step(2)
    qkv.step(3)
    proj.step(1)
    proj.step(2)
    proj.step(3)
    qkv.finish(grad_qkv)
    proj.finish(grad_proj)
    move.finish()
    to_mate.wait_send()
    to_side.wait_send()


def epilogue(
    grads, units_qkv, units_fc, small, grad_in, got_qkv, got_fc, total, by_y, by_z, by_team, sems
):
    spot = y, c, z, x = here()
    wires = Wires(sems)
    meet_tokens(team_peers(*spot) + grid_peers(*spot), spot, True)
    move = Tokens(wires, grads, grad_in, spot, True)
    qkv = TeamSwap(
        wires, lambda p, q: units_qkv.at[p * XN + q], lambda p, q: got_qkv.at[p * XN + q], spot
    )
    fc = TeamSwap(
        wires, lambda p, q: units_fc.at[p * XN + q], lambda p, q: got_fc.at[p * XN + q], spot
    )
    over = wires.far(small.at[1 - y], by_y, device(1 - y, c, z, x))
    over.start()
    move.start()
    qkv.start()
    fc.start()
    over.wait()
    by_y[...] = by_y[...] + small[y]
    column = [
        wires.far(by_y.at[lax.rem(z + k, ZN)], by_z.at[k - 1], device(y, c, lax.rem(z + k, ZN), x))
        for k in range(1, ZN)
    ]
    for copy in column:
        copy.start()
    for copy in column:
        copy.wait()
    by_z[3] = by_y[z] + by_z[0] + by_z[1] + by_z[2]
    team = [
        wires.far(by_z.at[3, p * XN + q], by_team.at[i], device(y, p, z, q))
        for i, (p, q) in enumerate(((c, 1 - x), (1 - c, 1 - x), (1 - c, x)))
    ]
    for copy in team:
        copy.start()
    for copy in team:
        copy.wait()
    total[...] = by_z[3, c * XN + x] + by_team[0] + by_team[1] + by_team[2]
    qkv.finish()
    fc.finish()
    move.finish()


QB = 256


def attend(mixed, context, totals, head):
    lanes = slice(head * HEAD, (head + 1) * HEAD)
    keys = mixed[:, HW + head * HEAD : HW + (head + 1) * HEAD]
    values = mixed[:, 2 * HW + head * HEAD : 2 * HW + (head + 1) * HEAD]
    for block in range(SEQ // QB):
        rows = slice(block * QB, (block + 1) * QB)
        upto = (block + 1) * QB
        scores = (
            lax.dot_general(
                mixed[rows, lanes], keys[:upto], (((1,), (1,)), ((), ())), preferred_element_type=F32
            )
            * 0.125
        )
        row = lax.broadcasted_iota(jnp.int32, (QB, upto), 0) + block * QB
        col = lax.broadcasted_iota(jnp.int32, (QB, upto), 1)
        scores = jnp.where(row >= col, scores, -1e30)
        peak = jnp.max(scores, axis=1, keepdims=True)
        weights = jnp.exp(scores - peak)
        total = jnp.sum(weights, axis=1, keepdims=True)
        prob = (weights * (1.0 / total)).astype(LOW)
        found = jnp.dot(prob, values[:upto], preferred_element_type=F32).astype(LOW)
        context[rows, lanes] = found
        totals[rows, head : head + 1] = peak + jnp.log(total)


def attend_back(mixed, totals, grads, acc_k, acc_v, head):
    lanes = slice(head * HEAD, (head + 1) * HEAD)
    lanes_k = slice(HW + head * HEAD, HW + (head + 1) * HEAD)
    lanes_v = slice(2 * HW + head * HEAD, 2 * HW + (head + 1) * HEAD)
    keys = mixed[:, lanes_k]
    values = mixed[:, lanes_v]
    acc_k[...] = jnp.zeros_like(acc_k)
    acc_v[...] = jnp.zeros_like(acc_v)
    for block in range(SEQ // QB):
        rows = slice(block * QB, (block + 1) * QB)
        upto = (block + 1) * QB
        queries = mixed[rows, lanes]
        outer = grads[rows, lanes]
        scores = (
            lax.dot_general(
                queries, keys[:upto], (((1,), (1,)), ((), ())), preferred_element_type=F32
            )
            * 0.125
        )
        row = lax.broadcasted_iota(jnp.int32, (QB, upto), 0) + block * QB
        col = lax.broadcasted_iota(jnp.int32, (QB, upto), 1)
        scores = jnp.where(row >= col, scores, -1e30)
        prob = jnp.exp(scores - totals[rows, head : head + 1])
        dprob = lax.dot_general(
            outer, values[:upto], (((1,), (1,)), ((), ())), preferred_element_type=F32
        )
        delta = jnp.sum(prob * dprob, axis=1, keepdims=True)
        ds = (prob * (dprob - delta)).astype(LOW)
        mixed[rows, lanes] = (
            jnp.dot(ds, keys[:upto], preferred_element_type=F32) * 0.125
        ).astype(LOW)
        acc_k[:upto] += outer_sum(ds, queries)
        acc_v[:upto] += outer_sum(prob.astype(LOW), outer)
    mixed[:, lanes_k] = (acc_k[...] * 0.125).astype(LOW)
    mixed[:, lanes_v] = acc_v[...].astype(LOW)


def plain(body, name, ins, outs, scratch=()):
    return pl.pallas_call(
        body,
        out_shape=[jax.ShapeDtypeStruct(s, d) for s, d in outs],
        in_specs=[VM] * len(ins),
        out_specs=[VM] * len(outs),
        scratch_shapes=list(scratch),
        compiler_params=pltpu.CompilerParams(vmem_limit_bytes=VMEM_BYTES),
        name=name,
    )(*ins)


def pick(values, index):
    return lax.dynamic_index_in_dim(values, index, 0, keepdims=False)


def pad_to(values, axis, size):
    widths = [(0, 0)] * values.ndim
    widths[axis] = (0, size - values.shape[axis])
    return jnp.pad(values, widths)


def head_parts(columns):
    return jnp.stack(
        [
            pad_to(columns[:, start * HEAD : (start + count) * HEAD], 1, HW)
            for start, count in zip(STARTS, COUNTS)
        ]
    )


def head_join(parts):
    return jnp.concatenate([parts[r][:, : COUNTS[r] * HEAD] for r in range(4)], axis=1)


def feature_order():
    order = -np.ones((YN, ZN, PIECE), np.int32)
    grid = np.arange(D).reshape(YN, CN, ZN, XN, 50).transpose(0, 2, 1, 3, 4)
    order[:, :, :200] = grid.reshape(YN, ZN, 200)
    return order.reshape(-1)


def context_order():
    natural = -np.ones(D, np.int32)
    grid = np.arange(D).reshape(YN, CN, ZN, XN, 50).transpose(1, 3, 0, 2, 4).reshape(32, 50)
    for block in range(32):
        natural[grid[block]] = block * PB + np.arange(50)
    order = -np.ones((4, HW), np.int32)
    for r in range(4):
        width = COUNTS[r] * HEAD
        order[r, :width] = natural[STARTS[r] * HEAD : STARTS[r] * HEAD + width]
    return order.reshape(-1)


def one_hot(order, size):
    rows = lax.broadcasted_iota(jnp.int32, (size, order.shape[0]), 0)
    return (rows == jnp.asarray(order)[None, :]).astype(LOW)


def dot(left, right):
    return jnp.dot(left, right, preferred_element_type=F32)


def ones_row(values):
    return jnp.sum(values.astype(F32), axis=0)


def fast_shards(inputs, grad_out, w_qkv, w_proj, w_fc, w_out, smalls):
    y, c, z, x = here()
    rank = c * XN + x
    to_wide = one_hot(feature_order(), D)
    to_heads = one_hot(context_order(), PROJ)

    rows = w_qkv.reshape(50, 3, D)
    units_qkv = jnp.stack([head_parts(rows[:, i]) for i in range(3)], axis=2).reshape(4, 50, QW)
    units_qkv = pad_to(units_qkv, 1, 64)
    units_fc = w_fc.reshape(50, YN, CN, ZN, XN, 200).transpose(2, 4, 0, 1, 3, 5)
    units_fc = pad_to(pad_to(units_fc, 5, PIECE).reshape(4, 50, WIDE), 1, 64)
    small = pad_to(smalls, 0, 2048).reshape(16, 128)
    piece_out = pad_to(w_out.reshape(200, D), 0, PIECE)
    piece_proj = pad_to(w_proj.reshape(50, D), 0, PB)
    tokens, got_qkv, got_fc, smalls_all, mat_out, mat_proj = call(
        prologue, "prologue", 1,
        (inputs.reshape(MICRO, BLK, D), units_qkv, units_fc, small, piece_out, piece_proj),
        [
            ((2, BLK, D), LOW), ((4, 64, QW), LOW), ((4, 64, WIDE), LOW),
            ((YN, ZN, 4, 16, 128), LOW), ((YN, ZN, PIECE, D), LOW), ((4, YN, ZN, PB, D), LOW),
        ],
        [ANY] * 6, [ANY] * 6, [], 3 * TEAM_SWAP_SEMS + TOKENS_SEMS + 2 * GATHER_SEMS + 14,
    )
    mat_out = mat_out.reshape(WIDE, D)
    mat_proj = mat_proj.reshape(PROJ, D)
    small = smalls_all.reshape(YN, ZN, CN, XN, 2048)[..., :600].transpose(0, 2, 1, 3, 4)
    small = small.reshape(-1).astype(F32)
    gain1, shift1, bias_q, bias_v, bias_proj, gain2, shift2 = [segment(small, i) for i in range(7)]
    bias_fc = small[7 * D : 7 * D + FF].reshape(YN, CN, ZN, XN, 200)
    bias_fc = lax.dynamic_index_in_dim(bias_fc, c, 1, keepdims=False)
    bias_fc = lax.dynamic_index_in_dim(bias_fc, x, 2, keepdims=False)
    bias_fc = pad_to(bias_fc, 2, PIECE).reshape(WIDE)
    bias_out = small[7 * D + FF :]
    bias_qkv = jnp.stack(
        [head_parts(bias_q[None]), jnp.zeros((4, 1, HW)), head_parts(bias_v[None])], axis=1
    )
    bias_qkv = pick(bias_qkv, rank).reshape(QW)

    tokens_low = tokens.reshape(2 * BLK, D)
    tokens = tokens_low.astype(F32)
    hidden_one, ln1_pull = jax.vjp(layer_norm, tokens, gain1, shift1)
    hidden_one = dot(hidden_one.astype(LOW), to_wide).astype(LOW)
    piece_qkv = pad_to(got_qkv[:, :50].reshape(200, QW), 0, PIECE)
    piece_fc = pad_to(got_fc[:, :50].reshape(200, WIDE), 0, PIECE)
    (
        hidden_one, cotangent, grad_all, mat_qkv, mat_fc, hidden_two, mixed, totals, context, resid,
    ) = call(
        forward, "forward", 2,
        (
            hidden_one.reshape(2, BLK, WIDE), grad_out.reshape(MICRO, BLK, D), piece_qkv, piece_fc,
            mat_proj, to_heads.T, to_wide, tokens_low, bias_qkv.reshape(1, QW),
            bias_proj.reshape(1, D), gain2.reshape(1, D), shift2.reshape(1, D),
        ),
        [
            ((2, 2, 2, BLK, WIDE), LOW), ((2, BLK, D), LOW), ((2, 2, 2, BLK, D), LOW),
            ((YN, ZN, PIECE, QW), LOW), ((YN, ZN, PIECE, WIDE), LOW), ((2, 2, 2, BLK, WIDE), LOW),
            ((SEQ, QW), LOW), ((SEQ, SLOTS), F32), ((2 * BLK, PROJ), LOW), ((2 * BLK, D), F32),
        ],
        [ANY] * 7 + [VM] * 5, [ANY] * 6 + [VM] * 4,
        [
            pltpu.VMEM((2, 2, 2, BLK, WIDE), LOW), pltpu.VMEM((YN, ZN, PIECE, QW), LOW),
            pltpu.VMEM((PROJ, D), LOW), pltpu.VMEM((4 * HW, PROJ), LOW), pltpu.VMEM((D, WIDE), LOW),
            pltpu.VMEM((SEQ, HW), LOW), pltpu.VMEM((4, 2, BLK, HW), LOW), pltpu.VMEM((2, BLK, WIDE), LOW),
        ],
        3 * TEAM_GATHER_SEMS + TOKENS_SEMS + 2 * GATHER_SEMS + 2 * TEAM_SWAP_SEMS + 5,
    )
    hidden_one = hidden_one.reshape(SEQ, WIDE)
    hidden_two = hidden_two.reshape(SEQ, WIDE)
    grad_all = grad_all.reshape(SEQ, D)
    mat_qkv = mat_qkv.reshape(WIDE, QW)
    mat_fc = mat_fc.reshape(WIDE, WIDE)
    _, ln2_pull = jax.vjp(layer_norm, resid, gain2, shift2)
    result, grad_hidden_two, grad_out_w, grad_pre, fc_terms = call(
        feed_forward, "feed_forward", 5,
        (hidden_two, grad_all, mat_fc, mat_out, bias_fc.reshape(1, WIDE)),
        [
            ((2, BLK, D), F32), ((2, BLK, WIDE), F32), ((PIECE, D), F32), ((SEQ, WIDE), LOW),
            ((1, WIDE), F32),
        ],
        [ANY] * 4 + [VM], [VM] * 5,
        [
            pltpu.VMEM((SEQ, WIDE), LOW), pltpu.VMEM((SEQ, D), LOW), pltpu.VMEM((WIDE, WIDE), LOW),
            pltpu.VMEM((WIDE, D), LOW), pltpu.VMEM((SEQ, WIDE), LOW), pltpu.VMEM((SEQ, D), LOW),
            pltpu.VMEM((SEQ, WIDE), LOW), pltpu.VMEM((WIDE, D), LOW),
        ]
        + team_scatter_scratch(D) + team_scatter_scratch(WIDE) + scatter_scratch(PIECE, D),
        2 * TEAM_SCATTER_SEMS + SCATTER_SEMS + 4,
    )
    result = (resid + result.reshape(2 * BLK, D) + bias_out).astype(LOW)
    grad_out_w = grad_out_w[:200].reshape(-1)

    grad_full = cotangent.reshape(2 * BLK, D).astype(F32)
    grad_hidden_two = back_product(grad_hidden_two.reshape(2 * BLK, WIDE).astype(LOW), to_wide)
    grad_ln_two, grad_gain_two, grad_shift_two = ln2_pull(grad_hidden_two)
    grad_resid = grad_full + grad_ln_two
    grad_branch = grad_resid.astype(LOW)
    grad_context = back_product(grad_branch, mat_proj).astype(LOW)
    grad_context = dot(grad_context, to_heads).astype(LOW)
    grad_context = jnp.stack(
        [grad_context[:, r * HW : (r + 1) * HW] for r in range(4)]
    ).reshape(4, 2, BLK, HW)
    grad_hidden_one, grad_qkv, grad_fc, grad_proj, outputs, terms = call(
        backward, "backward", 7,
        (
            hidden_one, hidden_two, grad_pre, mat_qkv, mixed, totals, grad_context, context,
            grad_branch, result.reshape(2, BLK, D),
        ),
        [
            ((2, BLK, WIDE), F32), ((PIECE, QW), LOW), ((PIECE, WIDE), LOW), ((PB, D), F32),
            ((2, BLK, D), LOW), ((1, QW), F32),
        ],
        [ANY] * 5 + [VM, ANY, VM, VM, ANY], [VM, VM, VM, VM, ANY, VM],
        [
            pltpu.VMEM((SEQ, WIDE), LOW), pltpu.VMEM((SEQ, WIDE), LOW), pltpu.VMEM((WIDE, QW), LOW),
            pltpu.VMEM((WIDE, WIDE), LOW), pltpu.VMEM((SEQ, WIDE), LOW), pltpu.VMEM((SEQ, HW), LOW), pltpu.VMEM((SEQ, QW), LOW),
            pltpu.VMEM((SEQ, HEAD), F32), pltpu.VMEM((SEQ, HEAD), F32),
        ]
        + team_scatter_scratch(WIDE) + scatter_scratch(PIECE, WIDE) + scatter_scratch(PIECE, QW)
        + scatter_scratch(PB, D)
        + [
            pltpu.VMEM((PROJ // 2, WIDE), LOW), pltpu.VMEM((PROJ // 4, D), LOW),
            pltpu.VMEM((PROJ // 4, WIDE), LOW),
        ],
        TEAM_SCATTER_SEMS + 3 * SCATTER_SEMS + TOKENS_SEMS + 2 * TEAM_SWAP_SEMS + 9,
    )
    grad_hidden_one = back_product(grad_hidden_one.reshape(2 * BLK, WIDE).astype(LOW), to_wide)
    grad_ln_one, grad_gain_one, grad_shift_one = ln1_pull(grad_hidden_one)
    grad_in = (grad_resid + grad_ln_one).astype(LOW)
    grad_proj = grad_proj[:50].reshape(-1)

    terms = terms.reshape(3, HW)
    mine = (jnp.arange(4) == rank).astype(F32)[:, None, None]
    grad_bq = head_join(mine * terms[0][None, None])[0]
    grad_bv = head_join(mine * terms[2][None, None])[0]
    fc_terms = fc_terms.reshape(YN, 1, ZN, 1, PIECE)[..., :200]
    spot = (jnp.arange(CN) == c)[None, :, None, None, None] & (jnp.arange(XN) == x)[
        None, None, None, :, None
    ]
    grad_fc_bias = jnp.where(spot, fc_terms, 0.0).reshape(-1)
    front = jnp.concatenate([grad_gain_one, grad_shift_one, grad_bq, grad_bv])
    tail = jnp.concatenate(
        [
            ones_row(grad_branch), grad_gain_two, grad_shift_two, grad_fc_bias,
            jnp.sum(grad_full, axis=0),
        ]
    )
    small = jnp.concatenate([front.reshape(32, 200), tail.reshape(32, 400)], axis=1)
    small = pad_to(small, 1, 1024).reshape(YN, CN, ZN, XN, 8, 128).transpose(0, 2, 1, 3, 4, 5)
    units_qkv = pad_to(grad_qkv[:200].reshape(4, 50, QW), 1, 64)
    units_fc = pad_to(grad_fc[:200].reshape(4, 50, WIDE), 1, 64)
    grad_in, got_qkv, got_fc, total = call(
        epilogue, "epilogue", 8,
        (grad_in.reshape(2, BLK, D), units_qkv, units_fc, small.reshape(YN, ZN, 4, 8, 128)),
        [((MICRO, BLK, D), LOW), ((4, 64, QW), LOW), ((4, 64, WIDE), LOW), ((8, 128), F32)],
        [ANY, ANY, ANY, VM], [ANY, ANY, ANY, VM],
        [pltpu.VMEM((ZN, 4, 8, 128), F32), pltpu.VMEM((4, 4, 8, 128), F32), pltpu.VMEM((3, 8, 128), F32)],
        2 * TEAM_SWAP_SEMS + TOKENS_SEMS + 14,
    )
    parts = got_qkv[:, :50].reshape(4, 50, 3, HW)
    grad_qkv = jnp.stack([head_join(parts[:, :, i]) for i in range(3)], axis=1)
    grad_qkv = grad_qkv.astype(F32).reshape(-1)
    grad_fc = got_fc[:, :50].reshape(CN, XN, 50, YN, ZN, PIECE)[..., :200]
    grad_fc = grad_fc.transpose(2, 3, 0, 4, 1, 5).astype(F32).reshape(-1)
    total = total.reshape(-1)
    return (
        outputs[:, None],
        grad_in.astype(F32)[:, None],
        grad_qkv,
        grad_proj,
        grad_fc,
        grad_out_w,
        total[:200],
        total[200:600],
    )


def solution(mesh):
    placed = (
        P(None, "dp", "ctx", None),
        P(None, "dp", "ctx", None),
        P(("dp", "ctx")),
        P(("dp", "ctx")),
        P(("dp", "ctx")),
        P(("dp", "ctx")),
        P(("dp", "ctx")),
    )
    fast = dict(mesh.shape) == {"dp": DP, "ctx": CTX}
    return jax.shard_map(
        fast_shards if fast else shards,
        mesh=mesh,
        in_specs=placed,
        out_specs=(
            P(None, "dp", "ctx", None),
            P(None, "dp", "ctx", None),
            P(("dp", "ctx")),
            P(("dp", "ctx")),
            P(("dp", "ctx")),
            P(("dp", "ctx")),
            P(("dp", "ctx")),
            P(("dp", "ctx")),
        ),
        check_vma=False,
    )
```

```python
import functools

import jax
import jax.numpy as jnp
import numpy as np
from jax import lax
from jax.experimental import pallas as pl
from jax.experimental.pallas import tpu as pltpu
from jax.sharding import PartitionSpec as P

D = 1600
HEADS = 25
HEAD = 64
FF = 6400
MICRO = 2


EPS = 1e-05


def layer_norm(values, gain, shift):
    center = values - jnp.mean(values, axis=-1, keepdims=True)
    spread = jnp.mean(center * center, axis=-1, keepdims=True)
    return center * lax.rsqrt(spread + EPS) * gain + shift


def gelu_tanh(values):
    return jax.nn.gelu(values, approximate=True)


def unpack(gathered):
    packed_qkv, packed_proj, packed_fc, packed_out, packed_small = gathered
    return (
        packed_qkv.reshape(D, 3 * D),
        packed_proj.reshape(D, D),
        packed_fc.reshape(D, FF),
        packed_out.reshape(FF, D),
        packed_small.astype(jnp.float32),
    )


def fetch(w_qkv, w_proj, w_fc, w_out, smalls):
    return unpack(
        (
            lax.all_gather(w_qkv, ("dp", "ctx"), axis=0, tiled=True),
            lax.all_gather(w_proj, ("dp", "ctx"), axis=0, tiled=True),
            lax.all_gather(w_fc, ("dp", "ctx"), axis=0, tiled=True),
            lax.all_gather(w_out, ("dp", "ctx"), axis=0, tiled=True),
            lax.all_gather(smalls, ("dp", "ctx"), axis=0, tiled=True),
        )
    )


def fetch_again(w_qkv, w_proj, w_fc, w_out, smalls):
    return unpack(
        (
            lax.all_gather(w_qkv, ("dp", "ctx"), axis=0, tiled=True),
            lax.all_gather(w_proj, ("dp", "ctx"), axis=0, tiled=True),
            lax.all_gather(w_fc, ("dp", "ctx"), axis=0, tiled=True),
            lax.all_gather(w_out, ("dp", "ctx"), axis=0, tiled=True),
            lax.all_gather(smalls, ("dp", "ctx"), axis=0, tiled=True),
        )
    )


def outer_sum(left, right):
    return lax.dot_general(
        left, right, (((0,), (0,)), ((), ())), preferred_element_type=jnp.float32
    )


def back_product(grad, weight):
    return lax.dot_general(
        grad, weight, (((1,), (1,)), ((), ())), preferred_element_type=jnp.float32
    )


def flat_term(left, right, start, count):
    width = right.shape[1]
    span = count // width + 2
    padded = jnp.pad(left, ((0, 0), (0, span)))
    first_row = start // width
    piece = lax.dynamic_slice_in_dim(padded, first_row, span, 1)
    block = outer_sum(piece, right).astype(jnp.bfloat16).reshape(-1)
    return lax.dynamic_slice_in_dim(block, start, count, 0)


def masked_scores(queries, keys, query_start, key_start):
    scores = (
        jnp.einsum("sqhe,skhe->shqk", queries, keys, preferred_element_type=jnp.float32) * 0.125
    )
    query_pos = query_start + jnp.arange(queries.shape[1])
    key_pos = key_start + jnp.arange(keys.shape[1])
    allowed = query_pos[:, None] >= key_pos[None, :]
    return jnp.where(allowed[None, None], scores, -1e30)


def segment(small_vals, which):
    return small_vals[which * D : (which + 1) * D]


def shards(inputs, grad_out, w_qkv, w_proj, w_fc, w_out, smalls):
    seqs = inputs.shape[1]
    local_len = inputs.shape[2]
    rows = seqs * local_len
    offset = lax.axis_index("ctx") * local_len
    acc_small = [jnp.zeros((D,), jnp.float32) for _ in range(7)]
    acc_fc_bias = jnp.zeros((FF,), jnp.float32)
    acc_out_bias = jnp.zeros((D,), jnp.float32)
    result_list = []
    grad_list = []
    kept_hidden_one = []
    kept_mixed_grad = []
    kept_context = []
    kept_branch_grad = []
    kept_hidden_two = []
    kept_pre_grad = []
    kept_activ = []
    kept_out_grad = []
    for batch_index in range(MICRO):
        params = fetch(w_qkv, w_proj, w_fc, w_out, smalls)
        mat_qkv, mat_proj, mat_fc, mat_out, small_vals = params
        tokens = inputs[batch_index].astype(jnp.float32).reshape(rows, D)
        hidden_one, ln1_pull = jax.vjp(
            layer_norm, tokens, segment(small_vals, 0), segment(small_vals, 1)
        )
        hidden_one = hidden_one.astype(jnp.bfloat16)
        qkv_bias = jnp.concatenate(
            [segment(small_vals, 2), jnp.zeros((D,), jnp.float32), segment(small_vals, 3)]
        )
        mixed = (
            jnp.dot(hidden_one, mat_qkv, preferred_element_type=jnp.float32) + qkv_bias
        ).astype(jnp.bfloat16)
        queries = mixed[:, :D].reshape(seqs, local_len, HEADS, HEAD)
        keys_local = mixed[:, D : 2 * D].reshape(seqs, local_len, D)
        values_local = mixed[:, 2 * D :].reshape(seqs, local_len, D)
        keys_all, values_all = (
            lax.all_gather(keys_local, "ctx", axis=1, tiled=True),
            lax.all_gather(values_local, "ctx", axis=1, tiled=True),
        )
        keys_all = keys_all.reshape(seqs, -1, HEADS, HEAD)
        values_all = values_all.reshape(seqs, -1, HEADS, HEAD)
        scores = masked_scores(queries, keys_all, offset, 0)
        row_peak = jnp.max(scores, axis=-1, keepdims=True)
        log_total = row_peak + jnp.log(jnp.sum(jnp.exp(scores - row_peak), axis=-1, keepdims=True))
        attn_low = jnp.exp(scores - log_total).astype(jnp.bfloat16)
        context = jnp.einsum(
            "shqk,skhe->sqhe", attn_low, values_all, preferred_element_type=jnp.float32
        )
        context = context.reshape(rows, D).astype(jnp.bfloat16)
        resid = (
            tokens
            + jnp.dot(context, mat_proj, preferred_element_type=jnp.float32)
            + segment(small_vals, 4)
        )
        hidden_two, ln2_pull = jax.vjp(
            layer_norm, resid, segment(small_vals, 5), segment(small_vals, 6)
        )
        hidden_two = hidden_two.astype(jnp.bfloat16)
        pre_act = (
            jnp.dot(hidden_two, mat_fc, preferred_element_type=jnp.float32)
            + small_vals[7 * D : 7 * D + FF]
        )
        activ, gelu_pull = jax.vjp(gelu_tanh, pre_act)
        activ = activ.astype(jnp.bfloat16)
        result = (
            resid
            + jnp.dot(activ, mat_out, preferred_element_type=jnp.float32)
            + small_vals[7 * D + FF :]
        )
        result_list.append(result.astype(jnp.bfloat16).reshape(seqs, local_len, D))
        back_params = fetch_again(w_qkv, w_proj, w_fc, w_out, smalls)
        mat_qkv, mat_proj, mat_fc, mat_out, small_vals = back_params
        grad_low = grad_out[batch_index].reshape(rows, D)
        grad_full = grad_low.astype(jnp.float32)
        acc_out_bias = acc_out_bias + jnp.sum(grad_full, axis=0)
        grad_act = back_product(grad_low, mat_out)
        (grad_pre,) = gelu_pull(grad_act)
        grad_pre = grad_pre.astype(jnp.bfloat16)
        acc_fc_bias = acc_fc_bias + jnp.sum(grad_pre.astype(jnp.float32), axis=0)
        grad_hidden_two = back_product(grad_pre, mat_fc)
        grad_ln_two, grad_gain_two, grad_shift_two = ln2_pull(grad_hidden_two)
        acc_small[5] = acc_small[5] + grad_gain_two
        acc_small[6] = acc_small[6] + grad_shift_two
        grad_resid = grad_full + grad_ln_two
        grad_branch = grad_resid.astype(jnp.bfloat16)
        acc_small[4] = acc_small[4] + jnp.sum(grad_branch.astype(jnp.float32), axis=0)
        grad_context = (
            back_product(grad_branch, mat_proj)
            .astype(jnp.bfloat16)
            .reshape(seqs, local_len, HEADS, HEAD)
        )
        scores = masked_scores(queries, keys_all, offset, 0)
        attn_prob = jnp.exp(scores - log_total)
        grad_attn = jnp.einsum(
            "sqhe,skhe->shqk", grad_context, values_all, preferred_element_type=jnp.float32
        )
        row_delta = jnp.sum(attn_prob * grad_attn, axis=-1, keepdims=True)
        grad_scores = (attn_prob * (grad_attn - row_delta)).astype(jnp.bfloat16)
        grad_queries = (
            jnp.einsum("shqk,skhe->sqhe", grad_scores, keys_all, preferred_element_type=jnp.float32)
            * 0.125
        )
        query_all, dctx_all = (
            lax.all_gather(queries.reshape(seqs, local_len, D), "ctx", axis=1, tiled=True),
            lax.all_gather(grad_context.reshape(seqs, local_len, D), "ctx", axis=1, tiled=True),
        )
        lse_all, delta_all = (
            lax.all_gather(jnp.transpose(log_total[..., 0], (0, 2, 1)), "ctx", axis=1, tiled=True),
            lax.all_gather(jnp.transpose(row_delta[..., 0], (0, 2, 1)), "ctx", axis=1, tiled=True),
        )
        query_all = query_all.reshape(seqs, -1, HEADS, HEAD)
        dctx_all = dctx_all.reshape(seqs, -1, HEADS, HEAD)
        lse_all = jnp.transpose(lse_all, (0, 2, 1))[..., None]
        delta_all = jnp.transpose(delta_all, (0, 2, 1))[..., None]
        own_keys = keys_local.reshape(seqs, local_len, HEADS, HEAD)
        own_values = values_local.reshape(seqs, local_len, HEADS, HEAD)
        col_scores = masked_scores(query_all, own_keys, 0, offset)
        col_prob = jnp.exp(col_scores - lse_all)
        col_dattn = jnp.einsum(
            "sqhe,skhe->shqk", dctx_all, own_values, preferred_element_type=jnp.float32
        )
        col_ds = (col_prob * (col_dattn - delta_all)).astype(jnp.bfloat16)
        grad_keys = (
            jnp.einsum("shqk,sqhe->skhe", col_ds, query_all, preferred_element_type=jnp.float32)
            * 0.125
        )
        grad_values = jnp.einsum(
            "shqk,sqhe->skhe",
            col_prob.astype(jnp.bfloat16),
            dctx_all,
            preferred_element_type=jnp.float32,
        )
        grad_mixed = jnp.concatenate(
            [
                grad_queries.reshape(rows, D),
                grad_keys.reshape(rows, D),
                grad_values.reshape(rows, D),
            ],
            axis=1,
        ).astype(jnp.bfloat16)
        bias_terms = jnp.sum(grad_mixed.astype(jnp.float32), axis=0)
        acc_small[2] = acc_small[2] + bias_terms[:D]
        acc_small[3] = acc_small[3] + bias_terms[2 * D :]
        grad_hidden_one = back_product(grad_mixed, mat_qkv)
        grad_ln_one, grad_gain_one, grad_shift_one = ln1_pull(grad_hidden_one)
        acc_small[0] = acc_small[0] + grad_gain_one
        acc_small[1] = acc_small[1] + grad_shift_one
        grad_list.append((grad_resid + grad_ln_one).reshape(seqs, local_len, D))
        kept_hidden_one.append(hidden_one)
        kept_mixed_grad.append(grad_mixed)
        kept_context.append(context)
        kept_branch_grad.append(grad_branch)
        kept_hidden_two.append(hidden_two)
        kept_pre_grad.append(grad_pre)
        kept_activ.append(activ)
        kept_out_grad.append(grad_low)
    front_grads = jnp.concatenate(acc_small[0:4])
    tail_grads = jnp.concatenate(acc_small[4:7] + [acc_fc_bias, acc_out_bias])
    grad_qkv = lax.psum_scatter(
        flat_term(
            jnp.concatenate(kept_hidden_one),
            jnp.concatenate(kept_mixed_grad),
            jnp.int32(0),
            lax.axis_size(("dp", "ctx")) * w_qkv.shape[0],
        ),
        ("dp", "ctx"),
        scatter_dimension=0,
        tiled=True,
    ).astype(jnp.float32)
    grad_proj = lax.psum_scatter(
        flat_term(
            jnp.concatenate(kept_context),
            jnp.concatenate(kept_branch_grad),
            jnp.int32(0),
            lax.axis_size(("dp", "ctx")) * w_proj.shape[0],
        ),
        ("dp", "ctx"),
        scatter_dimension=0,
        tiled=True,
    ).astype(jnp.float32)
    grad_fc = lax.psum_scatter(
        flat_term(
            jnp.concatenate(kept_hidden_two),
            jnp.concatenate(kept_pre_grad),
            jnp.int32(0),
            lax.axis_size(("dp", "ctx")) * w_fc.shape[0],
        ),
        ("dp", "ctx"),
        scatter_dimension=0,
        tiled=True,
    ).astype(jnp.float32)
    grad_out_w = lax.psum_scatter(
        flat_term(
            jnp.concatenate(kept_activ),
            jnp.concatenate(kept_out_grad),
            jnp.int32(0),
            lax.axis_size(("dp", "ctx")) * w_out.shape[0],
        ),
        ("dp", "ctx"),
        scatter_dimension=0,
        tiled=True,
    ).astype(jnp.float32)
    grad_front, grad_tail = (
        lax.psum_scatter(front_grads, ("dp", "ctx"), scatter_dimension=0, tiled=True),
        lax.psum_scatter(tail_grads, ("dp", "ctx"), scatter_dimension=0, tiled=True),
    )
    return (
        jnp.stack(result_list),
        jnp.stack(grad_list),
        grad_qkv,
        grad_proj,
        grad_fc,
        grad_out_w,
        grad_front,
        grad_tail,
    )


DP, CTX = 4, 8
YN, CN, HN, LN, XN = 2, 2, 2, 2, 2
SLOTS = 7
HW = SLOTS * HEAD
QW = 3 * HW
STARTS = (0, 7, 13, 19)
COUNTS = (7, 6, 6, 6)
BLK = 128
SEQ = 8 * BLK
PIECE = 208
WIDE = 8 * PIECE
PB = 64
PROJ = 32 * PB
LOW = jnp.bfloat16
F32 = jnp.float32
VMEM_BYTES = 60 * 1024 * 1024
ANY = pl.BlockSpec(memory_space=pl.ANY)
VM = pl.BlockSpec(memory_space=pltpu.VMEM)


def here():
    dp, ctx = lax.axis_index("dp"), lax.axis_index("ctx")
    return dp // CN, dp % CN, ctx // 4, (ctx // XN) % LN, ctx % XN


def device(y, c, h, l, x):
    return (y * CN + c, (h * LN + l) * XN + x)


def team_number(y, h, x):
    return y * 4 + h * 2 + x


class Wires:
    def __init__(self, sems):
        self.sems, self.used = sems, 0

    def one(self):
        self.used += 1
        assert self.used <= self.sems.shape[0]
        return self.sems.at[self.used - 1]

    def far(self, source, target, where):
        return pltpu.make_async_remote_copy(
            src_ref=source,
            dst_ref=target,
            send_sem=self.one(),
            recv_sem=self.one(),
            device_id=where,
            device_id_type=pl.DeviceIdType.MESH,
        )

    def near(self, source, target):
        return pltpu.make_async_copy(source, target, self.one())


def signal(where):
    pl.semaphore_signal(
        pltpu.get_barrier_semaphore(), inc=1, device_id=where, device_id_type=pl.DeviceIdType.MESH
    )


def team_peers(y, c, h, l, x):
    return [
        device(y, 1 - c, h, l, x), device(y, c, h, 1 - l, x), device(y, 1 - c, h, 1 - l, x)
    ]


def grid_peers(y, c, h, l, x):
    return [
        device(1 - y, c, h, l, x), device(y, c, 1 - h, l, x), device(y, c, h, l, 1 - x)
    ]


def meet(peers):
    for peer in peers:
        signal(peer)
    pl.semaphore_wait(pltpu.get_barrier_semaphore(), len(peers))


def call(body, name, ident, ins, outs, in_specs, out_specs, scratch, sems, cost=None):
    return pl.pallas_call(
        body,
        out_shape=[jax.ShapeDtypeStruct(s, d) for s, d in outs],
        in_specs=in_specs,
        out_specs=out_specs,
        scratch_shapes=list(scratch) + [pltpu.SemaphoreType.DMA((sems,))],
        compiler_params=pltpu.CompilerParams(
            collective_id=ident, has_side_effects=True, vmem_limit_bytes=VMEM_BYTES
        ),
        name=name,
    )(*ins)


class Routes:
    def __init__(self, spot):
        y, c, h, l, x = spot
        self.place = (y, h, x)
        self.peers = {
            "y": device(1 - y, c, h, l, x),
            "h": device(y, c, 1 - h, l, x),
            "x": device(y, c, h, l, 1 - x),
        }

    def flipped(self, ways):
        y, h, x = self.place
        return team_number(
            1 - y if "y" in ways else y, 1 - h if "h" in ways else h, 1 - x if "x" in ways else x
        )


def halves(rows):
    cut = (rows // 2 + 15) // 16 * 16
    return ((0, cut, "hxy"), (cut, rows - cut, "hyx"))


class Gather:
    def __init__(self, wires, piece, whole, spot):
        routes = Routes(spot)
        self.local = wires.near(piece, whole.at[routes.flipped("")])
        self.parts = []
        for start, size, order in halves(piece.shape[0]):
            at = pl.ds(start, size)
            first, second, third = order

            def copy(ways, way):
                spot = whole.at[routes.flipped(ways), at]
                source = piece.at[at] if not ways else spot
                return wires.far(source, spot, routes.peers[way])

            self.parts.append(
                {
                    "first": copy("", first),
                    "second": [copy("", second), copy(first, second)],
                    "third": [
                        copy("", third), copy(second, third), copy(first, third),
                        copy(first + second, third),
                    ],
                }
            )

    def start(self):
        self.local.start()
        for part in self.parts:
            part["first"].start()
            part["second"][0].start()
            part["third"][0].start()

    def step(self, turn):
        for part in self.parts:
            if turn == 1:
                part["second"][0].wait_recv()
                part["third"][1].start()
            elif turn == 2:
                part["first"].wait_recv()
                part["second"][1].start()
                part["third"][2].start()
            else:
                part["second"][1].wait_recv()
                part["third"][3].start()

    def finish(self):
        self.local.wait()
        for part in self.parts:
            for copy in [part["first"]] + part["second"]:
                copy.wait_send()
            for copy in part["third"]:
                copy.wait()


GATHER_SEMS = 1 + 2 * 2 * 7


class Scatter:
    def __init__(self, wires, parts, landed, spot):
        routes = Routes(spot)
        self.rows = landed.shape[1]
        self.parts, self.landed = parts, landed
        self.jobs = []
        for start, size, order in halves(self.rows):
            first, second, third = order
            at = pl.ds(start, size)

            def term(ways):
                base = routes.flipped(ways) * self.rows + start
                return parts.at[pl.ds(pl.multiple_of(base, 16), size)]

            stay = [second + first, second, first, ""]
            job = {
                "terms": [term(ways) for ways in stay],
                "spots": [landed.at[k, at] for k in range(7)],
                "over": [
                    wires.far(term(third + ways), landed.at[k, at], routes.peers[third])
                    for k, ways in enumerate(stay)
                ],
                "along": [
                    wires.far(landed.at[k, at], landed.at[4 + k, at], routes.peers[second])
                    for k in range(2)
                ],
                "last": wires.far(landed.at[2, at], landed.at[6, at], routes.peers[first]),
                "at": slice(start, start + size),
            }
            self.jobs.append(job)

    def start(self):
        for k in (0, 2):
            for job in self.jobs:
                job["over"][k].start()

    def step(self, turn):
        k = (0, 2, 1)[turn - 1]
        for job in self.jobs:
            job["over"][k].wait_recv()
            if turn < 3:
                job["over"][2 * turn - 1].start()
            total = job["spots"][k][...].astype(F32) + job["terms"][k][...].astype(F32)
            if turn == 2:
                job["along"][0].wait_recv()
                total = total + job["spots"][4][...].astype(F32)
            job["spots"][k][...] = total.astype(LOW)
            (job["along"] + [job["last"]])[k].start()

    def finish(self, total):
        for job in self.jobs:
            job["over"][3].wait_recv()
            job["along"][1].wait_recv()
            job["last"].wait_recv()
            summed = job["terms"][3][...].astype(F32)
            for k in (3, 5, 6):
                summed = summed + job["spots"][k][...].astype(F32)
            total[job["at"], :] = summed.astype(total.dtype)
            for copy in job["over"] + job["along"] + [job["last"]]:
                copy.wait_send()


SCATTER_SEMS = 2 * 2 * 7


class TeamGather:
    def __init__(self, wires, block, whole, spot):
        y, c, h, l, x = spot
        mate, beside = device(y, 1 - c, h, l, x), device(y, c, h, 1 - l, x)

        def at(l, s):
            return whole.at[c * 4 + l * 2 + s]

        self.local = [wires.near(block.at[s], at(l, s)) for s in range(2)]
        self.to_mate = [wires.far(block.at[s], at(l, s), mate) for s in range(2)]
        self.to_side = [wires.far(block.at[s], at(l, s), beside) for s in range(2)]
        self.relay = [wires.far(at(1 - l, s), at(1 - l, s), mate) for s in range(2)]

    def start(self):
        for copy in self.to_side + self.to_mate + self.local:
            copy.start()

    def step(self, s):
        self.to_side[s].wait_recv()
        self.relay[s].start()

    def finish(self):
        for copy in self.local + self.to_mate + self.relay:
            copy.wait()
        for copy in self.to_side:
            copy.wait_send()


TEAM_GATHER_SEMS = 2 + 2 * 6


class TeamSwap:
    def __init__(self, wires, source, target, spot):
        y, c, h, l, x = spot
        self.local = wires.near(source(c, l), target(c, l))
        self.copies = [
            wires.far(source(p, q), target(c, l), device(y, p, h, q, x))
            for p, q in ((c, 1 - l), (1 - c, 1 - l), (1 - c, l))
        ]

    def start(self):
        for copy in self.copies + [self.local]:
            copy.start()

    def finish(self):
        for copy in self.copies + [self.local]:
            copy.wait()


TEAM_SWAP_SEMS = 1 + 2 * 3


def pair_rows(c, l):
    return pl.ds(pl.multiple_of((c * 2 + l) * 2 * BLK, 2 * BLK), 2 * BLK)


def block_rows(c, l, s):
    return pl.ds(pl.multiple_of((c * 4 + l * 2 + s) * BLK, BLK), BLK)


class TeamScatter:
    def __init__(self, wires, parts, landed, leaving, arrived, spot):
        y, c, h, l, x = spot
        self.c, self.l = c, l
        self.parts, self.landed, self.leaving, self.arrived = parts, landed, leaving, arrived
        mate, beside = device(y, 1 - c, h, l, x), device(y, c, h, 1 - l, x)
        self.to_mate = [
            wires.far(parts.at[pair_rows(1 - c, q)], landed.at[k], mate)
            for k, q in enumerate((1 - l, l))
        ]
        self.to_side = [wires.far(leaving.at[s], arrived.at[s], beside) for s in range(2)]

    def start(self):
        for copy in self.to_mate:
            copy.start()

    def step(self, s):
        if s == 0:
            self.to_mate[0].wait_recv()
        rows = slice(s * BLK, (s + 1) * BLK)
        self.leaving[s] = (
            self.landed[0, rows, :].astype(F32)
            + self.parts[block_rows(self.c, 1 - self.l, s), :].astype(F32)
        ).astype(LOW)
        self.to_side[s].start()

    def finish(self, total):
        self.to_mate[1].wait_recv()
        for s in range(2):
            self.to_side[s].wait_recv()
            total[s] = (
                self.landed[1, s * BLK : (s + 1) * BLK, :].astype(F32)
                + self.parts[block_rows(self.c, self.l, s), :].astype(F32)
                + self.arrived[s].astype(F32)
            )
        for copy in self.to_mate + self.to_side:
            copy.wait_send()


TEAM_SCATTER_SEMS = 2 * 4


def team_scatter_scratch(width):
    return [
        pltpu.VMEM((2, 2 * BLK, width), LOW),
        pltpu.VMEM((2, BLK, width), LOW),
        pltpu.VMEM((2, BLK, width), LOW),
    ]


def scatter_scratch(rows, width):
    return [pltpu.VMEM((7, rows, width), LOW)]


class Tokens:
    def __init__(self, wires, source, target, spot):
        y, c, h, l, x = spot
        self.stays = h == c
        goals = token_goals(spot)
        pairs = []
        for k in range(2):
            other = lax.rem(x + k, 2)
            pairs.append((source.at[other], target.at[x]))
        self.local = wires.near(*pairs[0])
        self.copies = [wires.far(*pair, goal) for pair, goal in zip(pairs, goals)]

    def start(self):
        pl.when(self.stays)(self.local.start)
        pl.when(jnp.logical_not(self.stays))(self.copies[0].start)
        self.copies[1].start()

    def finish(self):
        pl.when(self.stays)(self.local.wait)
        pl.when(jnp.logical_not(self.stays))(self.copies[0].wait)
        self.copies[1].wait()


TOKENS_SEMS = 1 + 2 * 2


def token_goals(spot):
    y, c, h, l, x = spot
    return [device(y, h, c, l, x), device(y, h, c, l, 1 - x)]


def meet_tokens(peers, spot):
    y, c, h, l, x = spot
    same, other = token_goals(spot)
    for peer in peers + [other]:
        signal(peer)
    pl.when(h != c)(functools.partial(signal, same))
    count = len(peers) + 1 + jnp.where(h == c, 0, 1)
    pl.semaphore_wait(pltpu.get_barrier_semaphore(), count)


class Smalls:
    def __init__(self, wires, small, smalls, spot):
        y, c, h, l, x = spot
        own = team_number(y, h, x)
        self.first = TeamSwap(
            wires, lambda p, q: small, lambda p, q: smalls.at[own, p * LN + q], spot
        )
        self.second = [
            wires.far(smalls.at[own], smalls.at[own], where) for where in team_twins(*spot)
        ]

    def start(self):
        self.first.start()

    def step(self):
        self.first.finish()
        for copy in self.second:
            copy.start()

    def finish(self):
        for copy in self.second:
            copy.wait()


SMALLS_SEMS = TEAM_SWAP_SEMS + 2 * 7


def team_twins(y, c, h, l, x):
    ways = ((0, 0, 1), (1, 0, 0), (0, 1, 0), (1, 0, 1), (0, 1, 1), (1, 1, 0), (1, 1, 1))
    return [
        device(1 - y if a else y, c, 1 - h if b else h, l, 1 - x if d else x) for a, b, d in ways
    ]


def join_units(units, wide, piece):
    for k in range(4):
        wide[k * 50 : (k + 1) * 50, :] = units[k, :50, :].astype(F32)
    wide[200:, :] = jnp.zeros((PIECE - 200, wide.shape[1]), F32)
    piece[...] = wide[...].astype(LOW)


def prologue(
    inputs, units_qkv, units_fc, small, piece_proj,
    tokens, smalls, all_qkv, all_proj, piece_fc,
    got_qkv, got_fc, wide_qkv, wide_fc, piece_qkv, beside_proj, sems,
):
    spot = y, c, h, l, x = here()
    wires = Wires(sems)
    rank = c * LN + l
    meet_tokens(team_peers(*spot) + team_twins(*spot), spot)
    values = Smalls(wires, small, smalls, spot)
    qkv_units = TeamSwap(
        wires, lambda p, q: units_qkv.at[p * LN + q], lambda p, q: got_qkv.at[p * LN + q], spot
    )
    fc_units = TeamSwap(
        wires, lambda p, q: units_fc.at[p * LN + q], lambda p, q: got_fc.at[p * LN + q], spot
    )
    move = Tokens(wires, inputs, tokens, spot)
    qkv = Gather(wires, piece_qkv, all_qkv, spot)
    other = c * LN + 1 - l
    proj = Gather(wires, piece_proj, all_proj.at[rank], spot)
    side = wires.far(piece_proj, beside_proj, device(y, c, h, 1 - l, x))
    beside = Gather(wires, beside_proj, all_proj.at[other], spot)
    mate = device(y, 1 - c, h, l, x)
    relay = [
        wires.far(all_proj.at[r], all_proj.at[r], mate) for r in (rank, other)
    ]
    values.start()
    qkv_units.start()
    values.step()
    side.start()
    proj.start()
    qkv_units.finish()
    join_units(got_qkv, wide_qkv, piece_qkv)
    qkv.start()
    fc_units.start()
    move.start()
    side.wait()
    beside.start()
    proj.step(1)
    proj.step(2)
    proj.step(3)
    values.finish()
    qkv.step(1)
    proj.finish()
    relay[0].start()
    beside.step(1)
    qkv.step(2)
    beside.step(2)
    fc_units.finish()
    join_units(got_fc, wide_fc, piece_fc)
    qkv.step(3)
    beside.step(3)
    beside.finish()
    relay[1].start()
    move.finish()
    qkv.finish()
    for copy in relay:
        copy.wait()


def forward(
    hidden, grads, piece_fc, piece_out, mat_qkv, mat_proj, to_proj, to_wide,
    tokens, bias_qkv, bias_proj, gain2, shift2,
    hidden_all, cotangent, grad_all, all_fc, all_out, second_all, mixed, totals, context_out, resid,
    mat_in, proj_in, to_proj_in, to_wide_in, context, got, second, sems,
):
    spot = y, c, h, l, x = here()
    wires = Wires(sems)
    load = [
        wires.near(*both)
        for both in (
            (mat_qkv, mat_in), (mat_proj, proj_in), (to_proj, to_proj_in), (to_wide, to_wide_in)
        )
    ]
    for copy in load:
        copy.start()
    meet_tokens(team_peers(*spot) + grid_peers(*spot), spot)
    team = TeamGather(wires, hidden, hidden_all, spot)
    fc = Gather(wires, piece_fc, all_fc, spot)
    out = Gather(wires, piece_out, all_out, spot)
    bring = Tokens(wires, grads, cotangent, spot)
    team_two = TeamGather(wires, cotangent, grad_all, spot)
    team_three = TeamGather(wires, second, second_all, spot)
    swaps = [
        TeamSwap(
            wires,
            lambda p, q, s=s: context.at[block_rows(p, q, s)],
            lambda p, q, s=s: got.at[p * LN + q, s],
            spot,
        )
        for s in range(2)
    ]
    team.start()
    fc.start()
    team.step(0)
    team.step(1)
    load[0].wait()
    team.finish()
    bring.start()
    fc.step(1)

    @pl.loop(0, SEQ // QB)
    def _(i):
        rows = pl.ds(pl.multiple_of(i * QB, QB), QB)
        flat = hidden_all[pl.ds(pl.multiple_of(i * 2, 2), 2)].reshape(QB, WIDE)
        mixed[rows, :] = (dot(flat, mat_in[...]) + bias_qkv[...]).astype(LOW)

    fc.step(2)
    for head in range(SLOTS):
        attend(mixed, context, totals, head)
        if head == 0:
            fc.step(3)
            out.start()
            bring.finish()
            team_two.start()
        if head == 3:
            team_two.step(0)
        if head == 4:
            out.step(1)
    team_two.step(1)
    for copy in swaps:
        copy.start()
    for copy in load[1:]:
        copy.wait()
    for copy in swaps:
        copy.finish()
    out.step(2)
    placed = 0.0
    for r in range(4):
        placed = placed + dot(
            got[r].reshape(2 * BLK, HW), to_proj_in[r * HW : (r + 1) * HW, :]
        )
    placed = placed.astype(LOW)
    context_out[...] = placed
    found = tokens[...].astype(F32) + dot(placed, proj_in[...]) + bias_proj[...]
    resid[...] = found
    normed = layer_norm(found, gain2[...], shift2[...]).astype(LOW)
    second[...] = dot(normed, to_wide_in[...]).astype(LOW).reshape(2, BLK, WIDE)
    team_three.start()
    fc.finish()
    team_three.step(0)
    out.step(3)
    team_three.step(1)
    team_two.finish()
    team_three.finish()
    out.finish()


def gelu_both(f):
    square = f * f
    t = jnp.tanh(0.7978845608028654 * f * (1.0 + 0.044715 * square))
    half = 0.5 * (1.0 + t)
    slope = half + f * (0.5 * 0.7978845608028654) * (1.0 - t * t) * (1.0 + 3 * 0.044715 * square)
    return f * half, slope


def chunks(total, step):
    return [(start, min(step, total - start)) for start in range(0, total, step)]


def outer_into(target, left, right):
    count = left.shape[1] // 256

    @pl.loop(0, count)
    def _(i):
        at = pl.ds(pl.multiple_of(i * 256, 256), 256)
        target[at, :] = outer_sum(left[:, at], right()).astype(LOW)

    rest = left.shape[1] - count * 256
    if rest:
        target[count * 256 :, :] = outer_sum(left[:, count * 256 :], right()).astype(LOW)


def feed_forward(
    hidden_two, grad_all, mat_fc, mat_out, bias_fc,
    result, hidden, grad_out_w, grad_pre, terms,
    h2, dy, wf, wo, activ, part_r, part_h, part_o, l1, s1, a1, l2, s2, a2, l3, sems,
):
    spot = y, c, h, l, x = here()
    wires = Wires(sems)
    load = [
        wires.near(*both) for both in ((hidden_two, h2), (mat_fc, wf), (grad_all, dy), (mat_out, wo))
    ]
    for copy in load:
        copy.start()
    meet(team_peers(*spot) + grid_peers(*spot))
    second = TeamScatter(wires, part_h, l2, s2, a2, spot)
    first = TeamScatter(wires, part_r, l1, s1, a1, spot)
    out = Scatter(wires, part_o, l3, spot)
    load[0].wait()
    load[1].wait()

    @pl.loop(0, SEQ // QB)
    def _(i):
        rows = pl.ds(pl.multiple_of(i * QB, QB), QB)
        f = dot(h2[rows, :], wf[...]) + bias_fc[...]
        value, slope = gelu_both(f)
        activ[rows, :] = value.astype(LOW)
        grad_pre[rows, :] = slope.astype(LOW)

    load[2].wait()
    outer_into(part_o, activ, lambda: dy[...].reshape(SEQ, D))
    out.start()
    load[3].wait()
    terms[...] = jnp.zeros_like(terms)

    @pl.loop(0, SEQ // QB)
    def _(i):
        rows = pl.ds(pl.multiple_of(i * QB, QB), QB)
        here_dy = dy[pl.ds(pl.multiple_of(i * 2, 2), 2)].reshape(QB, D)
        df = (back_product(here_dy, wo[...]) * grad_pre[rows, :].astype(F32)).astype(LOW)
        grad_pre[rows, :] = df
        terms[...] += jnp.sum(df.astype(F32), axis=0, keepdims=True)

    def into(target, make):
        def half(which):
            @pl.loop(0, 2)
            def _(s):
                rows = pair_rows(which, s)
                target[rows, :] = make(rows).astype(LOW)

        return half

    half = into(part_h, lambda rows: back_product(grad_pre[rows, :], wf[...]))
    half(1 - c)
    second.start()
    half(c)
    out.step(1)
    second.step(0)
    second.step(1)
    half = into(part_r, lambda rows: dot(activ[rows, :], wo[...]))
    half(1 - c)
    first.start()
    half(c)
    out.step(2)
    first.step(0)
    first.step(1)
    second.finish(hidden)
    out.step(3)
    first.finish(result)
    out.finish(grad_out_w)


def backward(
    hidden_one, hidden_two, grad_pre, mat_qkv, mixed_all, totals, swap_parts, context, branch, result,
    hidden, grad_qkv, grad_fc, grad_proj, outputs, terms,
    ha, hb, wq, part_f, part_h, grads, mixed, acc_k, acc_v,
    l1, s1, a1, l2, l3, l4, pm, pk, px, sems,
):
    spot = y, c, h, l, x = here()
    wires = Wires(sems)
    load = [wires.near(*both) for both in ((hidden_two, ha), (grad_pre, hb), (mixed_all, mixed), (mat_qkv, wq))]
    again = wires.near(hidden_one, ha)
    for copy in load:
        copy.start()
    meet_tokens(team_peers(*spot) + grid_peers(*spot), spot)
    swaps = [
        TeamSwap(
            wires,
            lambda p, q, s=s: swap_parts.at[p * LN + q, s],
            lambda p, q, s=s: grads.at[block_rows(p, q, s)],
            spot,
        )
        for s in range(2)
    ]
    for copy in swaps:
        copy.start()
    fc = Scatter(wires, part_f, l2, spot)
    first = TeamScatter(wires, part_h, l1, s1, a1, spot)
    qkv = Scatter(wires, wq, l3, spot)
    quarter = PROJ // 4
    to_mate = wires.far(hb, pm, device(y, 1 - c, h, l, x))

    def side(q):
        return pl.ds(pl.multiple_of(q * quarter, 16), quarter)

    def term(p, q):
        at = pl.ds(pl.multiple_of((p * 2 + q) * quarter, quarter), quarter)
        return outer_sum(context[:, at], branch[...])

    to_side = wires.far(pm.at[side(1 - l)], px, device(y, c, h, 1 - l, x))
    proj = Scatter(wires, pk, l4, spot)
    move = Tokens(wires, result, outputs, spot)
    load[0].wait()
    load[1].wait()
    outer_into(part_f, ha, lambda: hb[...])
    fc.start()
    again.start()
    for q in range(2):
        hb[side(q), :D] = term(1 - c, q).astype(LOW)
    to_mate.start()
    load[2].wait()
    for copy in swaps:
        copy.finish()
    for head in range(SLOTS):
        attend_back(mixed, totals, grads, acc_k, acc_v, head)
        if head == 0:
            fc.step(1)
            to_mate.wait_recv()
            pm[side(1 - l), :D] = (pm[side(1 - l), :D].astype(F32) + term(c, 1 - l)).astype(LOW)
        if head == 1:
            to_side.start()
        if head == 2:
            fc.step(2)
        if head == 4:
            fc.step(3)
            move.start()
    load[3].wait()

    def half(which):
        @pl.loop(0, 2)
        def _(s):
            rows = pair_rows(which, s)
            part_h[rows, :] = back_product(mixed[rows, :], wq[...]).astype(LOW)

    half(1 - c)
    first.start()
    half(c)
    again.wait()
    outer_into(wq, ha, lambda: mixed[...])
    qkv.start()
    first.step(0)
    first.step(1)
    fc.finish(grad_fc)
    to_side.wait_recv()
    pk[...] = (
        pm[side(l), :D].astype(F32) + term(c, l) + px[:, :D].astype(F32)
    ).astype(LOW)
    proj.start()
    qkv.step(1)
    terms[...] = jnp.sum(mixed[...].astype(F32), axis=0, keepdims=True)
    qkv.step(2)
    proj.step(1)
    qkv.step(3)
    proj.step(2)
    proj.step(3)
    first.finish(hidden)
    qkv.finish(grad_qkv)
    proj.finish(grad_proj)
    move.finish()
    to_mate.wait_send()
    to_side.wait_send()


def epilogue(
    grads, units_qkv, units_fc, small, grad_in, got_qkv, got_fc, total, by_team, own, by_rank, sems
):
    spot = y, c, h, l, x = here()
    wires = Wires(sems)
    meet_tokens(team_peers(*spot) + team_twins(*spot), spot)
    move = Tokens(wires, grads, grad_in, spot)
    qkv = TeamSwap(
        wires, lambda p, q: units_qkv.at[p * LN + q], lambda p, q: got_qkv.at[p * LN + q], spot
    )
    fc = TeamSwap(
        wires, lambda p, q: units_fc.at[p * LN + q], lambda p, q: got_fc.at[p * LN + q], spot
    )
    here_team = team_number(y, h, x)
    ways = ((0, 0, 1), (1, 0, 0), (0, 1, 0), (1, 0, 1), (0, 1, 1), (1, 1, 0), (1, 1, 1))
    twins = [
        wires.far(
            small.at[team_number(1 - y if a else y, 1 - h if b else h, 1 - x if d else x)],
            by_team.at[i],
            where,
        )
        for i, ((a, b, d), where) in enumerate(zip(ways, team_twins(*spot)))
    ]
    for copy in twins:
        copy.start()
    qkv.start()
    fc.start()
    move.start()
    for copy in twins:
        copy.wait()
    summed = small[here_team]
    for i in range(7):
        summed = summed + by_team[i]
    own[...] = summed
    team = [
        wires.far(own.at[p * LN + q], by_rank.at[i], device(y, p, h, q, x))
        for i, (p, q) in enumerate(((c, 1 - l), (1 - c, 1 - l), (1 - c, l)))
    ]
    for copy in team:
        copy.start()
    for copy in team:
        copy.wait()
    total[...] = own[c * LN + l] + by_rank[0] + by_rank[1] + by_rank[2]
    qkv.finish()
    fc.finish()
    move.finish()


QB = 256


def attend(mixed, context, totals, head):
    lanes = slice(head * HEAD, (head + 1) * HEAD)
    keys = mixed[:, HW + head * HEAD : HW + (head + 1) * HEAD]
    values = mixed[:, 2 * HW + head * HEAD : 2 * HW + (head + 1) * HEAD]
    for block in range(SEQ // QB):
        rows = slice(block * QB, (block + 1) * QB)
        upto = (block + 1) * QB
        scores = (
            lax.dot_general(
                mixed[rows, lanes], keys[:upto], (((1,), (1,)), ((), ())), preferred_element_type=F32
            )
            * 0.125
        )
        row = lax.broadcasted_iota(jnp.int32, (QB, upto), 0) + block * QB
        col = lax.broadcasted_iota(jnp.int32, (QB, upto), 1)
        scores = jnp.where(row >= col, scores, -1e30)
        peak = jnp.max(scores, axis=1, keepdims=True)
        weights = jnp.exp(scores - peak)
        total = jnp.sum(weights, axis=1, keepdims=True)
        prob = (weights * (1.0 / total)).astype(LOW)
        found = jnp.dot(prob, values[:upto], preferred_element_type=F32).astype(LOW)
        context[rows, lanes] = found
        totals[rows, head : head + 1] = peak + jnp.log(total)


def attend_back(mixed, totals, grads, acc_k, acc_v, head):
    lanes = slice(head * HEAD, (head + 1) * HEAD)
    lanes_k = slice(HW + head * HEAD, HW + (head + 1) * HEAD)
    lanes_v = slice(2 * HW + head * HEAD, 2 * HW + (head + 1) * HEAD)
    keys = mixed[:, lanes_k]
    values = mixed[:, lanes_v]
    acc_k[...] = jnp.zeros_like(acc_k)
    acc_v[...] = jnp.zeros_like(acc_v)
    for block in range(SEQ // QB):
        rows = slice(block * QB, (block + 1) * QB)
        upto = (block + 1) * QB
        queries = mixed[rows, lanes]
        outer = grads[rows, lanes]
        scores = (
            lax.dot_general(
                queries, keys[:upto], (((1,), (1,)), ((), ())), preferred_element_type=F32
            )
            * 0.125
        )
        row = lax.broadcasted_iota(jnp.int32, (QB, upto), 0) + block * QB
        col = lax.broadcasted_iota(jnp.int32, (QB, upto), 1)
        scores = jnp.where(row >= col, scores, -1e30)
        prob = jnp.exp(scores - totals[rows, head : head + 1])
        dprob = lax.dot_general(
            outer, values[:upto], (((1,), (1,)), ((), ())), preferred_element_type=F32
        )
        delta = jnp.sum(prob * dprob, axis=1, keepdims=True)
        ds = (prob * (dprob - delta)).astype(LOW)
        mixed[rows, lanes] = (
            jnp.dot(ds, keys[:upto], preferred_element_type=F32) * 0.125
        ).astype(LOW)
        acc_k[:upto] += outer_sum(ds, queries)
        acc_v[:upto] += outer_sum(prob.astype(LOW), outer)
    mixed[:, lanes_k] = (acc_k[...] * 0.125).astype(LOW)
    mixed[:, lanes_v] = acc_v[...].astype(LOW)


def plain(body, name, ins, outs, scratch=()):
    return pl.pallas_call(
        body,
        out_shape=[jax.ShapeDtypeStruct(s, d) for s, d in outs],
        in_specs=[VM] * len(ins),
        out_specs=[VM] * len(outs),
        scratch_shapes=list(scratch),
        compiler_params=pltpu.CompilerParams(vmem_limit_bytes=VMEM_BYTES),
        name=name,
    )(*ins)


def pick(values, index):
    return lax.dynamic_index_in_dim(values, index, 0, keepdims=False)


def pad_to(values, axis, size):
    widths = [(0, 0)] * values.ndim
    widths[axis] = (0, size - values.shape[axis])
    return jnp.pad(values, widths)


def head_parts(columns):
    return jnp.stack(
        [
            pad_to(columns[:, start * HEAD : (start + count) * HEAD], 1, HW)
            for start, count in zip(STARTS, COUNTS)
        ]
    )


def head_join(parts):
    return jnp.concatenate([parts[r][:, : COUNTS[r] * HEAD] for r in range(4)], axis=1)


def feature_order():
    order = -np.ones((8, PIECE), np.int32)
    grid = np.arange(D).reshape(YN, CN, HN, LN, XN, 50).transpose(0, 2, 4, 1, 3, 5)
    order[:, :200] = grid.reshape(8, 200)
    return order.reshape(-1)


def context_order():
    natural = -np.ones(D, np.int32)
    grid = np.arange(D).reshape(YN, CN, HN, LN, XN, 50).transpose(1, 3, 0, 2, 4, 5).reshape(32, 50)
    for block in range(32):
        natural[grid[block]] = block * PB + np.arange(50)
    order = -np.ones((4, HW), np.int32)
    for r in range(4):
        width = COUNTS[r] * HEAD
        order[r, :width] = natural[STARTS[r] * HEAD : STARTS[r] * HEAD + width]
    return order.reshape(-1)


def one_hot(order, size):
    return (np.arange(size)[:, None] == order[None, :]).astype(LOW)


def dot(left, right):
    return jnp.dot(left, right, preferred_element_type=F32)


def ones_row(values):
    return jnp.sum(values.astype(F32), axis=0)


def fast_shards(inputs, grad_out, w_qkv, w_proj, w_fc, w_out, smalls):
    y, c, h, l, x = here()
    rank = c * LN + l
    to_wide = jnp.asarray(one_hot(feature_order(), D))
    to_proj = jnp.asarray(one_hot(context_order(), PROJ).T.copy())

    rows = w_qkv.reshape(50, 3, D)
    units_qkv = jnp.stack([head_parts(rows[:, i]) for i in range(3)], axis=2).reshape(4, 50, QW)
    units_qkv = pad_to(units_qkv, 1, 64)
    units_fc = w_fc.reshape(50, YN, CN, HN, LN, XN, 200).transpose(2, 4, 0, 1, 3, 5, 6)
    units_fc = pad_to(pad_to(units_fc, 6, PIECE).reshape(4, 50, WIDE), 1, 64)
    small = pad_to(smalls, 0, 2048).reshape(16, 128)
    piece_out = pad_to(w_out.reshape(200, D), 0, PIECE)
    piece_proj = pad_to(w_proj.reshape(50, D), 0, PB)
    tokens, smalls_all, mat_qkv, mat_proj, piece_fc = call(
        prologue, "prologue", 1,
        (inputs.reshape(MICRO, BLK, D), units_qkv, units_fc, small, piece_proj),
        [
            ((2, BLK, D), LOW), ((8, 4, 16, 128), LOW), ((8, PIECE, QW), LOW), ((4, 8, PB, D), LOW),
            ((PIECE, WIDE), LOW),
        ],
        [VM] * 5, [ANY] * 4 + [VM],
        [
            pltpu.VMEM((4, 64, QW), LOW), pltpu.VMEM((4, 64, WIDE), LOW),
            pltpu.VMEM((PIECE, QW), F32), pltpu.VMEM((PIECE, WIDE), F32), pltpu.VMEM((PIECE, QW), LOW),
            pltpu.VMEM((PB, D), LOW),
        ],
        SMALLS_SEMS + 2 * TEAM_SWAP_SEMS + TOKENS_SEMS + 3 * GATHER_SEMS + 6,
    )
    mat_qkv = mat_qkv.reshape(WIDE, QW)
    mat_proj = mat_proj.reshape(PROJ, D)
    small = smalls_all.reshape(YN, HN, XN, CN, LN, 2048)[..., :600].transpose(0, 3, 1, 4, 2, 5)
    small = small.reshape(-1).astype(F32)
    gain1, shift1, bias_q, bias_v, bias_proj, gain2, shift2 = [segment(small, i) for i in range(7)]
    bias_fc = small[7 * D : 7 * D + FF].reshape(YN, CN, HN, LN, XN, 200)
    bias_fc = lax.dynamic_index_in_dim(bias_fc, c, 1, keepdims=False)
    bias_fc = lax.dynamic_index_in_dim(bias_fc, l, 2, keepdims=False)
    bias_fc = pad_to(bias_fc, 3, PIECE).reshape(WIDE)
    bias_out = small[7 * D + FF :]
    bias_qkv = jnp.stack(
        [head_parts(bias_q[None]), jnp.zeros((4, 1, HW)), head_parts(bias_v[None])], axis=1
    )
    bias_qkv = pick(bias_qkv, rank).reshape(QW)

    tokens_low = tokens.reshape(2 * BLK, D)
    tokens = tokens_low.astype(F32)
    hidden_one, ln1_pull = jax.vjp(layer_norm, tokens, gain1, shift1)
    hidden_one = dot(hidden_one.astype(LOW), to_wide).astype(LOW)
    (
        hidden_one, cotangent, grad_all, mat_fc, mat_out, hidden_two, mixed, totals, context, resid,
    ) = call(
        forward, "forward", 2,
        (
            hidden_one.reshape(2, BLK, WIDE), grad_out.reshape(MICRO, BLK, D), piece_fc, piece_out,
            mat_qkv, mat_proj, to_proj, to_wide, tokens_low, bias_qkv.reshape(1, QW),
            bias_proj.reshape(1, D), gain2.reshape(1, D), shift2.reshape(1, D),
        ),
        [
            ((8, BLK, WIDE), LOW), ((2, BLK, D), LOW), ((8, BLK, D), LOW),
            ((8, PIECE, WIDE), LOW), ((8, PIECE, D), LOW),
            ((8, BLK, WIDE), LOW), ((SEQ, QW), LOW), ((SEQ, SLOTS), F32), ((2 * BLK, PROJ), LOW),
            ((2 * BLK, D), F32),
        ],
        [VM] * 4 + [ANY] * 4 + [VM] * 5, [VM, VM] + [ANY] * 4 + [VM] * 4,
        [
            pltpu.VMEM((WIDE, QW), LOW), pltpu.VMEM((PROJ, D), LOW), pltpu.VMEM((4 * HW, PROJ), LOW),
            pltpu.VMEM((D, WIDE), LOW), pltpu.VMEM((SEQ, HW), LOW), pltpu.VMEM((4, 2, BLK, HW), LOW),
            pltpu.VMEM((2, BLK, WIDE), LOW),
        ],
        3 * TEAM_GATHER_SEMS + TOKENS_SEMS + 2 * GATHER_SEMS + 2 * TEAM_SWAP_SEMS + 4,
    )
    hidden_one = hidden_one.reshape(SEQ, WIDE)
    hidden_two = hidden_two.reshape(SEQ, WIDE)
    mat_out = mat_out.reshape(WIDE, D)
    mat_fc = mat_fc.reshape(WIDE, WIDE)
    _, ln2_pull = jax.vjp(layer_norm, resid, gain2, shift2)
    result, grad_hidden_two, grad_out_w, grad_pre, fc_terms = call(
        feed_forward, "feed_forward", 5,
        (hidden_two, grad_all, mat_fc, mat_out, bias_fc.reshape(1, WIDE)),
        [
            ((2, BLK, D), F32), ((2, BLK, WIDE), F32), ((PIECE, D), F32), ((SEQ, WIDE), LOW),
            ((1, WIDE), F32),
        ],
        [ANY] * 4 + [VM], [VM] * 5,
        [
            pltpu.VMEM((SEQ, WIDE), LOW), pltpu.VMEM((8, BLK, D), LOW), pltpu.VMEM((WIDE, WIDE), LOW),
            pltpu.VMEM((WIDE, D), LOW), pltpu.VMEM((SEQ, WIDE), LOW), pltpu.VMEM((SEQ, D), LOW),
            pltpu.VMEM((SEQ, WIDE), LOW), pltpu.VMEM((WIDE, D), LOW),
        ]
        + team_scatter_scratch(D) + team_scatter_scratch(WIDE) + scatter_scratch(PIECE, D),
        2 * TEAM_SCATTER_SEMS + SCATTER_SEMS + 4,
    )
    result = (resid + result.reshape(2 * BLK, D) + bias_out).astype(LOW)
    grad_out_w = grad_out_w[:200].reshape(-1)

    grad_full = cotangent.reshape(2 * BLK, D).astype(F32)
    grad_hidden_two = back_product(grad_hidden_two.reshape(2 * BLK, WIDE).astype(LOW), to_wide)
    grad_ln_two, grad_gain_two, grad_shift_two = ln2_pull(grad_hidden_two)
    grad_resid = grad_full + grad_ln_two
    grad_branch = grad_resid.astype(LOW)
    grad_context = back_product(grad_branch, mat_proj).astype(LOW)
    grad_context = back_product(grad_context, to_proj).astype(LOW)
    grad_context = jnp.stack(
        [grad_context[:, r * HW : (r + 1) * HW] for r in range(4)]
    ).reshape(4, 2, BLK, HW)
    grad_hidden_one, grad_qkv, grad_fc, grad_proj, outputs, terms = call(
        backward, "backward", 7,
        (
            hidden_one, hidden_two, grad_pre, mat_qkv, mixed, totals, grad_context, context,
            grad_branch, result.reshape(2, BLK, D),
        ),
        [
            ((2, BLK, WIDE), F32), ((PIECE, QW), LOW), ((PIECE, WIDE), LOW), ((PB, D), F32),
            ((2, BLK, D), LOW), ((1, QW), F32),
        ],
        [ANY] * 5 + [VM, ANY, VM, VM, VM], [VM, VM, VM, VM, ANY, VM],
        [
            pltpu.VMEM((SEQ, WIDE), LOW), pltpu.VMEM((SEQ, WIDE), LOW), pltpu.VMEM((WIDE, QW), LOW),
            pltpu.VMEM((WIDE, WIDE), LOW), pltpu.VMEM((SEQ, WIDE), LOW), pltpu.VMEM((SEQ, HW), LOW), pltpu.VMEM((SEQ, QW), LOW),
            pltpu.VMEM((SEQ, HEAD), F32), pltpu.VMEM((SEQ, HEAD), F32),
        ]
        + team_scatter_scratch(WIDE) + scatter_scratch(PIECE, WIDE) + scatter_scratch(PIECE, QW)
        + scatter_scratch(PB, D)
        + [
            pltpu.VMEM((PROJ // 2, WIDE), LOW), pltpu.VMEM((PROJ // 4, D), LOW),
            pltpu.VMEM((PROJ // 4, WIDE), LOW),
        ],
        TEAM_SCATTER_SEMS + 3 * SCATTER_SEMS + TOKENS_SEMS + 2 * TEAM_SWAP_SEMS + 9,
    )
    grad_hidden_one = back_product(grad_hidden_one.reshape(2 * BLK, WIDE).astype(LOW), to_wide)
    grad_ln_one, grad_gain_one, grad_shift_one = ln1_pull(grad_hidden_one)
    grad_in = (grad_resid + grad_ln_one).astype(LOW)
    grad_proj = grad_proj[:50].reshape(-1)

    terms = terms.reshape(3, HW)
    mine = (jnp.arange(4) == rank).astype(F32)[:, None, None]
    grad_bq = head_join(mine * terms[0][None, None])[0]
    grad_bv = head_join(mine * terms[2][None, None])[0]
    fc_terms = fc_terms.reshape(YN, 1, HN, 1, XN, PIECE)[..., :200]
    spot = (jnp.arange(CN) == c)[:, None, None] & (jnp.arange(LN) == l)
    spot = spot[None, ..., None, None]
    grad_fc_bias = jnp.where(spot, fc_terms, 0.0).reshape(-1)
    front = jnp.concatenate([grad_gain_one, grad_shift_one, grad_bq, grad_bv])
    tail = jnp.concatenate(
        [
            ones_row(grad_branch), grad_gain_two, grad_shift_two, grad_fc_bias,
            jnp.sum(grad_full, axis=0),
        ]
    )
    small = jnp.concatenate([front.reshape(32, 200), tail.reshape(32, 400)], axis=1)
    small = pad_to(small, 1, 1024).reshape(YN, CN, HN, LN, XN, 8, 128).transpose(0, 2, 4, 1, 3, 5, 6)
    units_qkv = pad_to(grad_qkv[:200].reshape(4, 50, QW), 1, 64)
    units_fc = pad_to(grad_fc[:200].reshape(4, 50, WIDE), 1, 64)
    grad_in, got_qkv, got_fc, total = call(
        epilogue, "epilogue", 8,
        (grad_in.reshape(2, BLK, D), units_qkv, units_fc, small.reshape(8, 4, 8, 128)),
        [((MICRO, BLK, D), LOW), ((4, 64, QW), LOW), ((4, 64, WIDE), LOW), ((8, 128), F32)],
        [VM] * 4, [ANY, ANY, ANY, VM],
        [
            pltpu.VMEM((7, 4, 8, 128), F32), pltpu.VMEM((4, 8, 128), F32),
            pltpu.VMEM((3, 8, 128), F32),
        ],
        2 * TEAM_SWAP_SEMS + TOKENS_SEMS + 20,
    )
    parts = got_qkv[:, :50].reshape(4, 50, 3, HW)
    grad_qkv = jnp.stack([head_join(parts[:, :, i]) for i in range(3)], axis=1)
    grad_qkv = grad_qkv.astype(F32).reshape(-1)
    grad_fc = got_fc[:, :50].reshape(CN, LN, 50, YN, HN, XN, PIECE)[..., :200]
    grad_fc = grad_fc.transpose(2, 3, 0, 4, 1, 5, 6).astype(F32).reshape(-1)
    total = total.reshape(-1)
    return (
        outputs[:, None],
        grad_in.astype(F32)[:, None],
        grad_qkv,
        grad_proj,
        grad_fc,
        grad_out_w,
        total[:200],
        total[200:600],
    )


def solution(mesh):
    placed = (
        P(None, "dp", "ctx", None),
        P(None, "dp", "ctx", None),
        P(("dp", "ctx")),
        P(("dp", "ctx")),
        P(("dp", "ctx")),
        P(("dp", "ctx")),
        P(("dp", "ctx")),
    )
    fast = dict(mesh.shape) == {"dp": DP, "ctx": CTX}
    return jax.shard_map(
        fast_shards if fast else shards,
        mesh=mesh,
        in_specs=placed,
        out_specs=(
            P(None, "dp", "ctx", None),
            P(None, "dp", "ctx", None),
            P(("dp", "ctx")),
            P(("dp", "ctx")),
            P(("dp", "ctx")),
            P(("dp", "ctx")),
            P(("dp", "ctx")),
            P(("dp", "ctx")),
        ),
        check_vma=False,
    )
```

```python
import functools

import jax
import jax.numpy as jnp
import numpy as np
from jax import lax
from jax.experimental import pallas as pl
from jax.experimental.pallas import tpu as pltpu
from jax.sharding import PartitionSpec as P

D = 1600
HEADS = 25
HEAD = 64
FF = 6400
MICRO = 2


EPS = 1e-05


def layer_norm(values, gain, shift):
    center = values - jnp.mean(values, axis=-1, keepdims=True)
    spread = jnp.mean(center * center, axis=-1, keepdims=True)
    return center * lax.rsqrt(spread + EPS) * gain + shift


def gelu_tanh(values):
    return jax.nn.gelu(values, approximate=True)


def unpack(gathered):
    packed_qkv, packed_proj, packed_fc, packed_out, packed_small = gathered
    return (
        packed_qkv.reshape(D, 3 * D),
        packed_proj.reshape(D, D),
        packed_fc.reshape(D, FF),
        packed_out.reshape(FF, D),
        packed_small.astype(jnp.float32),
    )


def fetch(w_qkv, w_proj, w_fc, w_out, smalls):
    return unpack(
        (
            lax.all_gather(w_qkv, ("dp", "ctx"), axis=0, tiled=True),
            lax.all_gather(w_proj, ("dp", "ctx"), axis=0, tiled=True),
            lax.all_gather(w_fc, ("dp", "ctx"), axis=0, tiled=True),
            lax.all_gather(w_out, ("dp", "ctx"), axis=0, tiled=True),
            lax.all_gather(smalls, ("dp", "ctx"), axis=0, tiled=True),
        )
    )


def fetch_again(w_qkv, w_proj, w_fc, w_out, smalls):
    return unpack(
        (
            lax.all_gather(w_qkv, ("dp", "ctx"), axis=0, tiled=True),
            lax.all_gather(w_proj, ("dp", "ctx"), axis=0, tiled=True),
            lax.all_gather(w_fc, ("dp", "ctx"), axis=0, tiled=True),
            lax.all_gather(w_out, ("dp", "ctx"), axis=0, tiled=True),
            lax.all_gather(smalls, ("dp", "ctx"), axis=0, tiled=True),
        )
    )


def outer_sum(left, right):
    return lax.dot_general(
        left, right, (((0,), (0,)), ((), ())), preferred_element_type=jnp.float32
    )


def back_product(grad, weight):
    return lax.dot_general(
        grad, weight, (((1,), (1,)), ((), ())), preferred_element_type=jnp.float32
    )


def flat_term(left, right, start, count):
    width = right.shape[1]
    span = count // width + 2
    padded = jnp.pad(left, ((0, 0), (0, span)))
    first_row = start // width
    piece = lax.dynamic_slice_in_dim(padded, first_row, span, 1)
    block = outer_sum(piece, right).astype(jnp.bfloat16).reshape(-1)
    return lax.dynamic_slice_in_dim(block, start, count, 0)


def masked_scores(queries, keys, query_start, key_start):
    scores = (
        jnp.einsum("sqhe,skhe->shqk", queries, keys, preferred_element_type=jnp.float32) * 0.125
    )
    query_pos = query_start + jnp.arange(queries.shape[1])
    key_pos = key_start + jnp.arange(keys.shape[1])
    allowed = query_pos[:, None] >= key_pos[None, :]
    return jnp.where(allowed[None, None], scores, -1e30)


def segment(small_vals, which):
    return small_vals[which * D : (which + 1) * D]


def shards(inputs, grad_out, w_qkv, w_proj, w_fc, w_out, smalls):
    seqs = inputs.shape[1]
    local_len = inputs.shape[2]
    rows = seqs * local_len
    offset = lax.axis_index("ctx") * local_len
    acc_small = [jnp.zeros((D,), jnp.float32) for _ in range(7)]
    acc_fc_bias = jnp.zeros((FF,), jnp.float32)
    acc_out_bias = jnp.zeros((D,), jnp.float32)
    result_list = []
    grad_list = []
    kept_hidden_one = []
    kept_mixed_grad = []
    kept_context = []
    kept_branch_grad = []
    kept_hidden_two = []
    kept_pre_grad = []
    kept_activ = []
    kept_out_grad = []
    for batch_index in range(MICRO):
        params = fetch(w_qkv, w_proj, w_fc, w_out, smalls)
        mat_qkv, mat_proj, mat_fc, mat_out, small_vals = params
        tokens = inputs[batch_index].astype(jnp.float32).reshape(rows, D)
        hidden_one, ln1_pull = jax.vjp(
            layer_norm, tokens, segment(small_vals, 0), segment(small_vals, 1)
        )
        hidden_one = hidden_one.astype(jnp.bfloat16)
        qkv_bias = jnp.concatenate(
            [segment(small_vals, 2), jnp.zeros((D,), jnp.float32), segment(small_vals, 3)]
        )
        mixed = (
            jnp.dot(hidden_one, mat_qkv, preferred_element_type=jnp.float32) + qkv_bias
        ).astype(jnp.bfloat16)
        queries = mixed[:, :D].reshape(seqs, local_len, HEADS, HEAD)
        keys_local = mixed[:, D : 2 * D].reshape(seqs, local_len, D)
        values_local = mixed[:, 2 * D :].reshape(seqs, local_len, D)
        keys_all, values_all = (
            lax.all_gather(keys_local, "ctx", axis=1, tiled=True),
            lax.all_gather(values_local, "ctx", axis=1, tiled=True),
        )
        keys_all = keys_all.reshape(seqs, -1, HEADS, HEAD)
        values_all = values_all.reshape(seqs, -1, HEADS, HEAD)
        scores = masked_scores(queries, keys_all, offset, 0)
        row_peak = jnp.max(scores, axis=-1, keepdims=True)
        log_total = row_peak + jnp.log(jnp.sum(jnp.exp(scores - row_peak), axis=-1, keepdims=True))
        attn_low = jnp.exp(scores - log_total).astype(jnp.bfloat16)
        context = jnp.einsum(
            "shqk,skhe->sqhe", attn_low, values_all, preferred_element_type=jnp.float32
        )
        context = context.reshape(rows, D).astype(jnp.bfloat16)
        resid = (
            tokens
            + jnp.dot(context, mat_proj, preferred_element_type=jnp.float32)
            + segment(small_vals, 4)
        )
        hidden_two, ln2_pull = jax.vjp(
            layer_norm, resid, segment(small_vals, 5), segment(small_vals, 6)
        )
        hidden_two = hidden_two.astype(jnp.bfloat16)
        pre_act = (
            jnp.dot(hidden_two, mat_fc, preferred_element_type=jnp.float32)
            + small_vals[7 * D : 7 * D + FF]
        )
        activ, gelu_pull = jax.vjp(gelu_tanh, pre_act)
        activ = activ.astype(jnp.bfloat16)
        result = (
            resid
            + jnp.dot(activ, mat_out, preferred_element_type=jnp.float32)
            + small_vals[7 * D + FF :]
        )
        result_list.append(result.astype(jnp.bfloat16).reshape(seqs, local_len, D))
        back_params = fetch_again(w_qkv, w_proj, w_fc, w_out, smalls)
        mat_qkv, mat_proj, mat_fc, mat_out, small_vals = back_params
        grad_low = grad_out[batch_index].reshape(rows, D)
        grad_full = grad_low.astype(jnp.float32)
        acc_out_bias = acc_out_bias + jnp.sum(grad_full, axis=0)
        grad_act = back_product(grad_low, mat_out)
        (grad_pre,) = gelu_pull(grad_act)
        grad_pre = grad_pre.astype(jnp.bfloat16)
        acc_fc_bias = acc_fc_bias + jnp.sum(grad_pre.astype(jnp.float32), axis=0)
        grad_hidden_two = back_product(grad_pre, mat_fc)
        grad_ln_two, grad_gain_two, grad_shift_two = ln2_pull(grad_hidden_two)
        acc_small[5] = acc_small[5] + grad_gain_two
        acc_small[6] = acc_small[6] + grad_shift_two
        grad_resid = grad_full + grad_ln_two
        grad_branch = grad_resid.astype(jnp.bfloat16)
        acc_small[4] = acc_small[4] + jnp.sum(grad_branch.astype(jnp.float32), axis=0)
        grad_context = (
            back_product(grad_branch, mat_proj)
            .astype(jnp.bfloat16)
            .reshape(seqs, local_len, HEADS, HEAD)
        )
        scores = masked_scores(queries, keys_all, offset, 0)
        attn_prob = jnp.exp(scores - log_total)
        grad_attn = jnp.einsum(
            "sqhe,skhe->shqk", grad_context, values_all, preferred_element_type=jnp.float32
        )
        row_delta = jnp.sum(attn_prob * grad_attn, axis=-1, keepdims=True)
        grad_scores = (attn_prob * (grad_attn - row_delta)).astype(jnp.bfloat16)
        grad_queries = (
            jnp.einsum("shqk,skhe->sqhe", grad_scores, keys_all, preferred_element_type=jnp.float32)
            * 0.125
        )
        query_all, dctx_all = (
            lax.all_gather(queries.reshape(seqs, local_len, D), "ctx", axis=1, tiled=True),
            lax.all_gather(grad_context.reshape(seqs, local_len, D), "ctx", axis=1, tiled=True),
        )
        lse_all, delta_all = (
            lax.all_gather(jnp.transpose(log_total[..., 0], (0, 2, 1)), "ctx", axis=1, tiled=True),
            lax.all_gather(jnp.transpose(row_delta[..., 0], (0, 2, 1)), "ctx", axis=1, tiled=True),
        )
        query_all = query_all.reshape(seqs, -1, HEADS, HEAD)
        dctx_all = dctx_all.reshape(seqs, -1, HEADS, HEAD)
        lse_all = jnp.transpose(lse_all, (0, 2, 1))[..., None]
        delta_all = jnp.transpose(delta_all, (0, 2, 1))[..., None]
        own_keys = keys_local.reshape(seqs, local_len, HEADS, HEAD)
        own_values = values_local.reshape(seqs, local_len, HEADS, HEAD)
        col_scores = masked_scores(query_all, own_keys, 0, offset)
        col_prob = jnp.exp(col_scores - lse_all)
        col_dattn = jnp.einsum(
            "sqhe,skhe->shqk", dctx_all, own_values, preferred_element_type=jnp.float32
        )
        col_ds = (col_prob * (col_dattn - delta_all)).astype(jnp.bfloat16)
        grad_keys = (
            jnp.einsum("shqk,sqhe->skhe", col_ds, query_all, preferred_element_type=jnp.float32)
            * 0.125
        )
        grad_values = jnp.einsum(
            "shqk,sqhe->skhe",
            col_prob.astype(jnp.bfloat16),
            dctx_all,
            preferred_element_type=jnp.float32,
        )
        grad_mixed = jnp.concatenate(
            [
                grad_queries.reshape(rows, D),
                grad_keys.reshape(rows, D),
                grad_values.reshape(rows, D),
            ],
            axis=1,
        ).astype(jnp.bfloat16)
        bias_terms = jnp.sum(grad_mixed.astype(jnp.float32), axis=0)
        acc_small[2] = acc_small[2] + bias_terms[:D]
        acc_small[3] = acc_small[3] + bias_terms[2 * D :]
        grad_hidden_one = back_product(grad_mixed, mat_qkv)
        grad_ln_one, grad_gain_one, grad_shift_one = ln1_pull(grad_hidden_one)
        acc_small[0] = acc_small[0] + grad_gain_one
        acc_small[1] = acc_small[1] + grad_shift_one
        grad_list.append((grad_resid + grad_ln_one).reshape(seqs, local_len, D))
        kept_hidden_one.append(hidden_one)
        kept_mixed_grad.append(grad_mixed)
        kept_context.append(context)
        kept_branch_grad.append(grad_branch)
        kept_hidden_two.append(hidden_two)
        kept_pre_grad.append(grad_pre)
        kept_activ.append(activ)
        kept_out_grad.append(grad_low)
    front_grads = jnp.concatenate(acc_small[0:4])
    tail_grads = jnp.concatenate(acc_small[4:7] + [acc_fc_bias, acc_out_bias])
    grad_qkv = lax.psum_scatter(
        flat_term(
            jnp.concatenate(kept_hidden_one),
            jnp.concatenate(kept_mixed_grad),
            jnp.int32(0),
            lax.axis_size(("dp", "ctx")) * w_qkv.shape[0],
        ),
        ("dp", "ctx"),
        scatter_dimension=0,
        tiled=True,
    ).astype(jnp.float32)
    grad_proj = lax.psum_scatter(
        flat_term(
            jnp.concatenate(kept_context),
            jnp.concatenate(kept_branch_grad),
            jnp.int32(0),
            lax.axis_size(("dp", "ctx")) * w_proj.shape[0],
        ),
        ("dp", "ctx"),
        scatter_dimension=0,
        tiled=True,
    ).astype(jnp.float32)
    grad_fc = lax.psum_scatter(
        flat_term(
            jnp.concatenate(kept_hidden_two),
            jnp.concatenate(kept_pre_grad),
            jnp.int32(0),
            lax.axis_size(("dp", "ctx")) * w_fc.shape[0],
        ),
        ("dp", "ctx"),
        scatter_dimension=0,
        tiled=True,
    ).astype(jnp.float32)
    grad_out_w = lax.psum_scatter(
        flat_term(
            jnp.concatenate(kept_activ),
            jnp.concatenate(kept_out_grad),
            jnp.int32(0),
            lax.axis_size(("dp", "ctx")) * w_out.shape[0],
        ),
        ("dp", "ctx"),
        scatter_dimension=0,
        tiled=True,
    ).astype(jnp.float32)
    grad_front, grad_tail = (
        lax.psum_scatter(front_grads, ("dp", "ctx"), scatter_dimension=0, tiled=True),
        lax.psum_scatter(tail_grads, ("dp", "ctx"), scatter_dimension=0, tiled=True),
    )
    return (
        jnp.stack(result_list),
        jnp.stack(grad_list),
        grad_qkv,
        grad_proj,
        grad_fc,
        grad_out_w,
        grad_front,
        grad_tail,
    )


DP, CTX = 4, 8
YN, CN, HN, LN, XN = 2, 2, 2, 2, 2
SLOTS = 7
HW = SLOTS * HEAD
QW = 3 * HW
STARTS = (0, 7, 13, 19)
COUNTS = (7, 6, 6, 6)
BLK = 128
SEQ = 8 * BLK
PIECE = 208
WIDE = 8 * PIECE
PB = 64
PROJ = 32 * PB
LOW = jnp.bfloat16
F32 = jnp.float32
VMEM_BYTES = 60 * 1024 * 1024
ANY = pl.BlockSpec(memory_space=pl.ANY)
VM = pl.BlockSpec(memory_space=pltpu.VMEM)


def here():
    dp, ctx = lax.axis_index("dp"), lax.axis_index("ctx")
    return dp // CN, dp % CN, ctx // 4, (ctx // XN) % LN, ctx % XN


def device(y, c, h, l, x):
    return (y * CN + c, (h * LN + l) * XN + x)


def team_number(y, h, x):
    return y * 4 + h * 2 + x


class Wires:
    def __init__(self, sems):
        self.sems, self.used = sems, 0

    def one(self):
        self.used += 1
        assert self.used <= self.sems.shape[0]
        return self.sems.at[self.used - 1]

    def far(self, source, target, where):
        return pltpu.make_async_remote_copy(
            src_ref=source,
            dst_ref=target,
            send_sem=self.one(),
            recv_sem=self.one(),
            device_id=where,
            device_id_type=pl.DeviceIdType.MESH,
        )

    def near(self, source, target):
        return pltpu.make_async_copy(source, target, self.one())


def signal(where):
    pl.semaphore_signal(
        pltpu.get_barrier_semaphore(), inc=1, device_id=where, device_id_type=pl.DeviceIdType.MESH
    )


def team_peers(y, c, h, l, x):
    return [
        device(y, 1 - c, h, l, x), device(y, c, h, 1 - l, x), device(y, 1 - c, h, 1 - l, x)
    ]


def grid_peers(y, c, h, l, x):
    return [
        device(1 - y, c, h, l, x), device(y, c, 1 - h, l, x), device(y, c, h, l, 1 - x)
    ]


def meet(peers):
    for peer in peers:
        signal(peer)
    pl.semaphore_wait(pltpu.get_barrier_semaphore(), len(peers))


def call(body, name, ident, ins, outs, in_specs, out_specs, scratch, sems, cost=None):
    return pl.pallas_call(
        body,
        out_shape=[jax.ShapeDtypeStruct(s, d) for s, d in outs],
        in_specs=in_specs,
        out_specs=out_specs,
        scratch_shapes=list(scratch) + [pltpu.SemaphoreType.DMA((sems,))],
        compiler_params=pltpu.CompilerParams(
            collective_id=ident, has_side_effects=True, vmem_limit_bytes=VMEM_BYTES
        ),
        name=name,
    )(*ins)


class Routes:
    def __init__(self, spot):
        y, c, h, l, x = spot
        self.place = (y, h, x)
        self.peers = {
            "y": device(1 - y, c, h, l, x),
            "h": device(y, c, 1 - h, l, x),
            "x": device(y, c, h, l, 1 - x),
        }

    def flipped(self, ways):
        y, h, x = self.place
        return team_number(
            1 - y if "y" in ways else y, 1 - h if "h" in ways else h, 1 - x if "x" in ways else x
        )


def halves(rows):
    cut = (rows // 2 + 15) // 16 * 16
    return ((0, cut, "hxy"), (cut, rows - cut, "hyx"))


class Gather:
    def __init__(self, wires, piece, whole, spot):
        routes = Routes(spot)
        self.local = wires.near(piece, whole.at[routes.flipped("")])
        self.parts = []
        for start, size, order in halves(piece.shape[0]):
            at = pl.ds(start, size)
            first, second, third = order

            def copy(ways, way):
                spot = whole.at[routes.flipped(ways), at]
                source = piece.at[at] if not ways else spot
                return wires.far(source, spot, routes.peers[way])

            self.parts.append(
                {
                    "first": copy("", first),
                    "second": [copy("", second), copy(first, second)],
                    "third": [
                        copy("", third), copy(second, third), copy(first, third),
                        copy(first + second, third),
                    ],
                }
            )

    def start(self):
        self.local.start()
        for part in self.parts:
            part["first"].start()
            part["second"][0].start()
            part["third"][0].start()

    def step(self, turn):
        for part in self.parts:
            if turn == 1:
                part["second"][0].wait_recv()
                part["third"][1].start()
            elif turn == 2:
                part["first"].wait_recv()
                part["second"][1].start()
                part["third"][2].start()
            else:
                part["second"][1].wait_recv()
                part["third"][3].start()

    def finish(self):
        self.local.wait()
        for part in self.parts:
            for copy in [part["first"]] + part["second"]:
                copy.wait_send()
            for copy in part["third"]:
                copy.wait()


GATHER_SEMS = 1 + 2 * 2 * 7


class Scatter:
    def __init__(self, wires, parts, landed, spot):
        routes = Routes(spot)
        self.rows = landed.shape[1]
        self.parts, self.landed = parts, landed
        self.jobs = []
        for start, size, order in halves(self.rows):
            first, second, third = order
            at = pl.ds(start, size)

            def term(ways):
                base = routes.flipped(ways) * self.rows + start
                return parts.at[pl.ds(pl.multiple_of(base, 16), size)]

            stay = [second + first, second, first, ""]
            job = {
                "terms": [term(ways) for ways in stay],
                "spots": [landed.at[k, at] for k in range(7)],
                "over": [
                    wires.far(term(third + ways), landed.at[k, at], routes.peers[third])
                    for k, ways in enumerate(stay)
                ],
                "along": [
                    wires.far(landed.at[k, at], landed.at[4 + k, at], routes.peers[second])
                    for k in range(2)
                ],
                "last": wires.far(landed.at[2, at], landed.at[6, at], routes.peers[first]),
                "at": slice(start, start + size),
            }
            self.jobs.append(job)

    def start(self):
        for k in (0, 2):
            for job in self.jobs:
                job["over"][k].start()

    def step(self, turn):
        k = (0, 2, 1)[turn - 1]
        for job in self.jobs:
            job["over"][k].wait_recv()
            if turn < 3:
                job["over"][2 * turn - 1].start()
            total = job["spots"][k][...].astype(F32) + job["terms"][k][...].astype(F32)
            if turn == 2:
                job["along"][0].wait_recv()
                total = total + job["spots"][4][...].astype(F32)
            job["spots"][k][...] = total.astype(LOW)
            (job["along"] + [job["last"]])[k].start()

    def finish(self, total):
        for job in self.jobs:
            job["over"][3].wait_recv()
            job["along"][1].wait_recv()
            job["last"].wait_recv()
            summed = job["terms"][3][...].astype(F32)
            for k in (3, 5, 6):
                summed = summed + job["spots"][k][...].astype(F32)
            total[job["at"], :] = summed.astype(total.dtype)
            for copy in job["over"] + job["along"] + [job["last"]]:
                copy.wait_send()


SCATTER_SEMS = 2 * 2 * 7


class TeamGather:
    def __init__(self, wires, block, whole, spot):
        y, c, h, l, x = spot
        mate, beside = device(y, 1 - c, h, l, x), device(y, c, h, 1 - l, x)

        def at(l, s):
            return whole.at[c * 4 + l * 2 + s]

        self.local = [wires.near(block.at[s], at(l, s)) for s in range(2)]
        self.to_mate = [wires.far(block.at[s], at(l, s), mate) for s in range(2)]
        self.to_side = [wires.far(block.at[s], at(l, s), beside) for s in range(2)]
        self.relay = [wires.far(at(1 - l, s), at(1 - l, s), mate) for s in range(2)]

    def start(self):
        for copy in self.to_side + self.to_mate + self.local:
            copy.start()

    def step(self, s):
        self.to_side[s].wait_recv()
        self.relay[s].start()

    def finish(self):
        for copy in self.local + self.to_mate + self.relay:
            copy.wait()
        for copy in self.to_side:
            copy.wait_send()


TEAM_GATHER_SEMS = 2 + 2 * 6


class TeamSwap:
    def __init__(self, wires, source, target, spot):
        y, c, h, l, x = spot
        self.local = wires.near(source(c, l), target(c, l))
        self.copies = [
            wires.far(source(p, q), target(c, l), device(y, p, h, q, x))
            for p, q in ((c, 1 - l), (1 - c, 1 - l), (1 - c, l))
        ]

    def start(self):
        for copy in self.copies + [self.local]:
            copy.start()

    def finish(self):
        for copy in self.copies + [self.local]:
            copy.wait()


TEAM_SWAP_SEMS = 1 + 2 * 3


def pair_rows(c, l):
    return pl.ds(pl.multiple_of((c * 2 + l) * 2 * BLK, 2 * BLK), 2 * BLK)


def block_rows(c, l, s):
    return pl.ds(pl.multiple_of((c * 4 + l * 2 + s) * BLK, BLK), BLK)


class TeamScatter:
    def __init__(self, wires, parts, landed, leaving, arrived, spot):
        y, c, h, l, x = spot
        self.c, self.l = c, l
        self.parts, self.landed, self.leaving, self.arrived = parts, landed, leaving, arrived
        mate, beside = device(y, 1 - c, h, l, x), device(y, c, h, 1 - l, x)
        self.to_mate = [
            wires.far(parts.at[pair_rows(1 - c, q)], landed.at[k], mate)
            for k, q in enumerate((1 - l, l))
        ]
        self.to_side = [wires.far(leaving.at[s], arrived.at[s], beside) for s in range(2)]

    def start(self):
        for copy in self.to_mate:
            copy.start()

    def step(self, s):
        if s == 0:
            self.to_mate[0].wait_recv()
        rows = slice(s * BLK, (s + 1) * BLK)
        self.leaving[s] = (
            self.landed[0, rows, :].astype(F32)
            + self.parts[block_rows(self.c, 1 - self.l, s), :].astype(F32)
        ).astype(LOW)
        self.to_side[s].start()

    def finish(self, total):
        self.to_mate[1].wait_recv()
        for s in range(2):
            self.to_side[s].wait_recv()
            total[s] = (
                self.landed[1, s * BLK : (s + 1) * BLK, :].astype(F32)
                + self.parts[block_rows(self.c, self.l, s), :].astype(F32)
                + self.arrived[s].astype(F32)
            )
        for copy in self.to_mate + self.to_side:
            copy.wait_send()


TEAM_SCATTER_SEMS = 2 * 4


def team_scatter_scratch(width):
    return [
        pltpu.VMEM((2, 2 * BLK, width), LOW),
        pltpu.VMEM((2, BLK, width), LOW),
        pltpu.VMEM((2, BLK, width), LOW),
    ]


def scatter_scratch(rows, width):
    return [pltpu.VMEM((7, rows, width), LOW)]


class Tokens:
    def __init__(self, wires, source, target, spot):
        y, c, h, l, x = spot
        self.stays = h == c
        goals = token_goals(spot)
        pairs = []
        for k in range(2):
            other = lax.rem(x + k, 2)
            pairs.append((source.at[other], target.at[x]))
        self.local = wires.near(*pairs[0])
        self.copies = [wires.far(*pair, goal) for pair, goal in zip(pairs, goals)]

    def start(self):
        pl.when(self.stays)(self.local.start)
        pl.when(jnp.logical_not(self.stays))(self.copies[0].start)
        self.copies[1].start()

    def finish(self):
        pl.when(self.stays)(self.local.wait)
        pl.when(jnp.logical_not(self.stays))(self.copies[0].wait)
        self.copies[1].wait()


TOKENS_SEMS = 1 + 2 * 2


def token_goals(spot):
    y, c, h, l, x = spot
    return [device(y, h, c, l, x), device(y, h, c, l, 1 - x)]


def meet_tokens(peers, spot):
    y, c, h, l, x = spot
    same, other = token_goals(spot)
    for peer in peers + [other]:
        signal(peer)
    pl.when(h != c)(functools.partial(signal, same))
    count = len(peers) + 1 + jnp.where(h == c, 0, 1)
    pl.semaphore_wait(pltpu.get_barrier_semaphore(), count)


class Smalls:
    def __init__(self, wires, small, smalls, spot):
        y, c, h, l, x = spot
        own = team_number(y, h, x)
        self.first = TeamSwap(
            wires, lambda p, q: small, lambda p, q: smalls.at[own, p * LN + q], spot
        )
        self.second = [
            wires.far(smalls.at[own], smalls.at[own], where) for where in team_twins(*spot)
        ]

    def start(self):
        self.first.start()

    def step(self):
        self.first.finish()
        for copy in self.second:
            copy.start()

    def finish(self):
        for copy in self.second:
            copy.wait()


SMALLS_SEMS = TEAM_SWAP_SEMS + 2 * 7


def team_twins(y, c, h, l, x):
    ways = ((0, 0, 1), (1, 0, 0), (0, 1, 0), (1, 0, 1), (0, 1, 1), (1, 1, 0), (1, 1, 1))
    return [
        device(1 - y if a else y, c, 1 - h if b else h, l, 1 - x if d else x) for a, b, d in ways
    ]


def join_units(units, wide, piece):
    for k in range(4):
        wide[k * 50 : (k + 1) * 50, :] = units[k, :50, :].astype(F32)
    wide[200:, :] = jnp.zeros((PIECE - 200, wide.shape[1]), F32)
    piece[...] = wide[...].astype(LOW)


def prologue(
    inputs, units_qkv, units_fc, small, piece_proj,
    tokens, smalls, all_qkv, all_proj, piece_fc,
    got_qkv, got_fc, wide_qkv, wide_fc, piece_qkv, beside_proj, sems,
):
    spot = y, c, h, l, x = here()
    wires = Wires(sems)
    rank = c * LN + l
    meet_tokens(team_peers(*spot) + team_twins(*spot), spot)
    values = Smalls(wires, small, smalls, spot)
    qkv_units = TeamSwap(
        wires, lambda p, q: units_qkv.at[p * LN + q], lambda p, q: got_qkv.at[p * LN + q], spot
    )
    fc_units = TeamSwap(
        wires, lambda p, q: units_fc.at[p * LN + q], lambda p, q: got_fc.at[p * LN + q], spot
    )
    move = Tokens(wires, inputs, tokens, spot)
    qkv = Gather(wires, piece_qkv, all_qkv, spot)
    other = c * LN + 1 - l
    proj = Gather(wires, piece_proj, all_proj.at[rank], spot)
    side = wires.far(piece_proj, beside_proj, device(y, c, h, 1 - l, x))
    beside = Gather(wires, beside_proj, all_proj.at[other], spot)
    mate = device(y, 1 - c, h, l, x)
    relay = [
        wires.far(all_proj.at[r], all_proj.at[r], mate) for r in (rank, other)
    ]
    values.start()
    qkv_units.start()
    values.step()
    side.start()
    proj.start()
    qkv_units.finish()
    join_units(got_qkv, wide_qkv, piece_qkv)
    qkv.start()
    fc_units.start()
    move.start()
    side.wait()
    beside.start()
    proj.step(1)
    proj.step(2)
    proj.step(3)
    values.finish()
    qkv.step(1)
    proj.finish()
    relay[0].start()
    beside.step(1)
    qkv.step(2)
    beside.step(2)
    fc_units.finish()
    join_units(got_fc, wide_fc, piece_fc)
    qkv.step(3)
    beside.step(3)
    beside.finish()
    relay[1].start()
    move.finish()
    qkv.finish()
    for copy in relay:
        copy.wait()


def forward(
    hidden, grads, piece_fc, piece_out, mat_qkv, mat_proj, to_proj, to_wide,
    tokens, bias_qkv, bias_proj, gain2, shift2,
    hidden_all, cotangent, grad_all, all_fc, all_out, second_all, mixed, totals, context_out, resid,
    mat_in, proj_in, to_proj_in, to_wide_in, context, got, second, sems,
):
    spot = y, c, h, l, x = here()
    wires = Wires(sems)
    load = [
        wires.near(*both)
        for both in (
            (mat_qkv, mat_in), (mat_proj, proj_in), (to_proj, to_proj_in), (to_wide, to_wide_in)
        )
    ]
    for copy in load:
        copy.start()
    meet_tokens(team_peers(*spot) + grid_peers(*spot), spot)
    team = TeamGather(wires, hidden, hidden_all, spot)
    fc = Gather(wires, piece_fc, all_fc, spot)
    out = Gather(wires, piece_out, all_out, spot)
    bring = Tokens(wires, grads, cotangent, spot)
    team_two = TeamGather(wires, cotangent, grad_all, spot)
    team_three = TeamGather(wires, second, second_all, spot)
    swaps = [
        TeamSwap(
            wires,
            lambda p, q, s=s: context.at[block_rows(p, q, s)],
            lambda p, q, s=s: got.at[p * LN + q, s],
            spot,
        )
        for s in range(2)
    ]
    team.start()
    fc.start()
    team.step(0)
    team.step(1)
    load[0].wait()
    team.finish()
    bring.start()
    fc.step(1)

    @pl.loop(0, SEQ // QB)
    def _(i):
        rows = pl.ds(pl.multiple_of(i * QB, QB), QB)
        flat = hidden_all[pl.ds(pl.multiple_of(i * 2, 2), 2)].reshape(QB, WIDE)
        mixed[rows, :] = (dot(flat, mat_in[...]) + bias_qkv[...]).astype(LOW)

    fc.step(2)
    for head in range(SLOTS):
        attend(mixed, context, totals, head)
        if head == 0:
            fc.step(3)
            out.start()
            bring.finish()
            team_two.start()
        if head == 3:
            team_two.step(0)
        if head == 4:
            out.step(1)
    team_two.step(1)
    for copy in swaps:
        copy.start()
    for copy in load[1:]:
        copy.wait()
    for copy in swaps:
        copy.finish()
    out.step(2)
    placed = 0.0
    for r in range(4):
        placed = placed + dot(
            got[r].reshape(2 * BLK, HW), to_proj_in[r * HW : (r + 1) * HW, :]
        )
    placed = placed.astype(LOW)
    context_out[...] = placed
    found = tokens[...].astype(F32) + dot(placed, proj_in[...]) + bias_proj[...]
    resid[...] = found
    normed = layer_norm(found, gain2[...], shift2[...]).astype(LOW)
    second[...] = dot(normed, to_wide_in[...]).astype(LOW).reshape(2, BLK, WIDE)
    team_three.start()
    fc.finish()
    team_three.step(0)
    out.step(3)
    team_three.step(1)
    team_two.finish()
    team_three.finish()
    out.finish()


def gelu_both(f):
    square = f * f
    t = jnp.tanh(0.7978845608028654 * f * (1.0 + 0.044715 * square))
    half = 0.5 * (1.0 + t)
    slope = half + f * (0.5 * 0.7978845608028654) * (1.0 - t * t) * (1.0 + 3 * 0.044715 * square)
    return f * half, slope


def chunks(total, step):
    return [(start, min(step, total - start)) for start in range(0, total, step)]


def outer_into(target, left, right):
    count = left.shape[1] // 256

    @pl.loop(0, count)
    def _(i):
        at = pl.ds(pl.multiple_of(i * 256, 256), 256)
        target[at, :] = outer_sum(left[:, at], right()).astype(LOW)

    rest = left.shape[1] - count * 256
    if rest:
        target[count * 256 :, :] = outer_sum(left[:, count * 256 :], right()).astype(LOW)


def feed_forward(
    hidden_two, grad_all, mat_fc, mat_out, bias_fc,
    result, hidden, grad_out_w, grad_pre, terms,
    h2, dy, wf, wo, activ, part_r, part_h, part_o, l1, s1, a1, l2, s2, a2, l3, sems,
):
    spot = y, c, h, l, x = here()
    wires = Wires(sems)
    load = [
        wires.near(*both) for both in ((hidden_two, h2), (mat_fc, wf), (grad_all, dy), (mat_out, wo))
    ]
    for copy in load:
        copy.start()
    meet(team_peers(*spot) + grid_peers(*spot))
    second = TeamScatter(wires, part_h, l2, s2, a2, spot)
    first = TeamScatter(wires, part_r, l1, s1, a1, spot)
    out = Scatter(wires, part_o, l3, spot)
    load[0].wait()
    load[1].wait()

    @pl.loop(0, SEQ // QB)
    def _(i):
        rows = pl.ds(pl.multiple_of(i * QB, QB), QB)
        f = dot(h2[rows, :], wf[...]) + bias_fc[...]
        value, slope = gelu_both(f)
        activ[rows, :] = value.astype(LOW)
        grad_pre[rows, :] = slope.astype(LOW)

    load[2].wait()
    outer_into(part_o, activ, lambda: dy[...].reshape(SEQ, D))
    out.start()
    load[3].wait()
    terms[...] = jnp.zeros_like(terms)

    @pl.loop(0, SEQ // QB)
    def _(i):
        rows = pl.ds(pl.multiple_of(i * QB, QB), QB)
        here_dy = dy[pl.ds(pl.multiple_of(i * 2, 2), 2)].reshape(QB, D)
        df = (back_product(here_dy, wo[...]) * grad_pre[rows, :].astype(F32)).astype(LOW)
        grad_pre[rows, :] = df
        terms[...] += jnp.sum(df.astype(F32), axis=0, keepdims=True)

    def into(target, make):
        def half(which):
            @pl.loop(0, 2)
            def _(s):
                rows = pair_rows(which, s)
                target[rows, :] = make(rows).astype(LOW)

        return half

    half = into(part_h, lambda rows: back_product(grad_pre[rows, :], wf[...]))
    half(1 - c)
    second.start()
    half(c)
    out.step(1)
    second.step(0)
    second.step(1)
    half = into(part_r, lambda rows: dot(activ[rows, :], wo[...]))
    half(1 - c)
    first.start()
    half(c)
    out.step(2)
    first.step(0)
    first.step(1)
    second.finish(hidden)
    out.step(3)
    first.finish(result)
    out.finish(grad_out_w)


def backward(
    hidden_one, hidden_two, grad_pre, mat_qkv, mixed_all, totals, swap_parts, context, branch, result,
    tokens, grad_resid, gain1, to_wide,
    units_qkv, got_fc, grad_proj, outputs, grad_in, terms, norms,
    ha, hb, wq, part_f, part_h, grads, mixed, acc_k, acc_v,
    l1, s1, a1, l2, l3, l4, pm, px, hidden, grad_low, wide_fc, wide_qkv, units_fc, sems,
):
    spot = y, c, h, l, x = here()
    wires = Wires(sems)
    load = [wires.near(*both) for both in ((hidden_two, ha), (grad_pre, hb), (mixed_all, mixed), (mat_qkv, wq))]
    again = wires.near(hidden_one, ha)
    for copy in load:
        copy.start()
    meet_tokens(team_peers(*spot) + grid_peers(*spot), spot)
    swaps = [
        TeamSwap(
            wires,
            lambda p, q, s=s: swap_parts.at[p * LN + q, s],
            lambda p, q, s=s: grads.at[block_rows(p, q, s)],
            spot,
        )
        for s in range(2)
    ]
    for copy in swaps:
        copy.start()
    fc = Scatter(wires, part_f, l2, spot)
    first = TeamScatter(wires, part_h, l1, s1, a1, spot)
    qkv = Scatter(wires, wq, l3, spot)
    quarter = PROJ // 4
    to_mate = wires.far(hb, pm, device(y, 1 - c, h, l, x))

    def side(q):
        return pl.ds(pl.multiple_of(q * quarter, 16), quarter)

    def term(p, q):
        at = pl.ds(pl.multiple_of((p * 2 + q) * quarter, quarter), quarter)
        return outer_sum(context[:, at], branch[...])

    to_side = wires.far(pm.at[side(1 - l)], px, device(y, c, h, 1 - l, x))
    proj = Scatter(wires, px, l4, spot)
    move = Tokens(wires, result, outputs, spot)
    back = Tokens(wires, grad_low, grad_in, spot)
    swap_fc = TeamSwap(
        wires, lambda p, q: units_fc.at[p * LN + q], lambda p, q: got_fc.at[p * LN + q], spot
    )
    spread = part_f.at[pl.ds(0, D)]
    load_wide = wires.near(to_wide, spread)
    load[0].wait()
    load[1].wait()
    outer_into(part_f, ha, lambda: hb[...])
    fc.start()
    again.start()
    for q in range(2):
        hb[side(q), :D] = term(1 - c, q).astype(LOW)
    to_mate.start()
    load[2].wait()
    for copy in swaps:
        copy.finish()
    for head in range(SLOTS):
        attend_back(mixed, totals, grads, acc_k, acc_v, head)
        if head == 0:
            fc.step(1)
            to_mate.wait_recv()
            pm[side(1 - l), :D] = (pm[side(1 - l), :D].astype(F32) + term(c, 1 - l)).astype(LOW)
        if head == 1:
            to_side.start()
        if head == 2:
            fc.step(2)
        if head == 4:
            fc.step(3)
            move.start()
    load[3].wait()

    def half(which):
        @pl.loop(0, 2)
        def _(s):
            rows = pair_rows(which, s)
            part_h[rows, :] = back_product(mixed[rows, :], wq[...]).astype(LOW)

    half(1 - c)
    first.start()
    half(c)
    again.wait()
    outer_into(wq, ha, lambda: mixed[...])
    qkv.start()
    first.step(0)
    first.step(1)
    fc.finish(wide_fc)
    load_wide.start()
    split_units(wide_fc, units_fc)
    swap_fc.start()
    to_side.wait_recv()
    px[:, :D] = (pm[side(l), :D].astype(F32) + term(c, l) + px[:, :D].astype(F32)).astype(LOW)
    proj.start()
    qkv.step(1)
    terms[...] = jnp.sum(mixed[...].astype(F32), axis=0, keepdims=True)
    load_wide.wait()
    qkv.step(2)
    proj.step(1)
    first.finish(hidden)
    grad = back_product(hidden[...].reshape(2 * BLK, WIDE).astype(LOW), spread[...])
    grad, norms[0:1, :], norms[1:2, :] = norm_back(tokens[...].astype(F32), gain1[...], grad)
    grad_low[...] = (grad_resid[...] + grad).astype(LOW).reshape(2, BLK, D)
    back.start()
    qkv.step(3)
    proj.step(2)
    proj.step(3)
    qkv.finish(wide_qkv)
    split_units(wide_qkv, units_qkv)
    proj.finish(grad_proj)
    swap_fc.finish()
    move.finish()
    back.finish()
    to_mate.wait_send()
    to_side.wait_send()


def split_units(wide, units):
    wide[PIECE:, :] = jnp.zeros((224 - PIECE, wide.shape[1]), F32)
    for k in range(4):
        units[k] = wide[k * 50 : k * 50 + 64, :].astype(LOW)


def norm_back(values, gain, grad):
    center = values - jnp.mean(values, axis=1, keepdims=True)
    scale = lax.rsqrt(jnp.mean(center * center, axis=1, keepdims=True) + EPS)
    unit = center * scale
    grad_gain = jnp.sum(grad * unit, axis=0, keepdims=True)
    grad_shift = jnp.sum(grad, axis=0, keepdims=True)
    grad = grad * gain
    inner = jnp.mean(grad * unit, axis=1, keepdims=True)
    return scale * (grad - jnp.mean(grad, axis=1, keepdims=True) - unit * inner), grad_gain, grad_shift


def epilogue(units_qkv, small, got_qkv, total, by_team, own, by_rank, sems):
    spot = y, c, h, l, x = here()
    wires = Wires(sems)
    meet(team_peers(*spot) + team_twins(*spot))
    qkv = TeamSwap(
        wires, lambda p, q: units_qkv.at[p * LN + q], lambda p, q: got_qkv.at[p * LN + q], spot
    )
    here_team = team_number(y, h, x)
    ways = ((0, 0, 1), (1, 0, 0), (0, 1, 0), (1, 0, 1), (0, 1, 1), (1, 1, 0), (1, 1, 1))
    twins = [
        wires.far(
            small.at[team_number(1 - y if a else y, 1 - h if b else h, 1 - x if d else x)],
            by_team.at[i],
            where,
        )
        for i, ((a, b, d), where) in enumerate(zip(ways, team_twins(*spot)))
    ]
    for copy in twins:
        copy.start()
    qkv.start()
    for copy in twins:
        copy.wait()
    summed = small[here_team]
    for i in range(7):
        summed = summed + by_team[i]
    own[...] = summed
    team = [
        wires.far(own.at[p * LN + q], by_rank.at[i], device(y, p, h, q, x))
        for i, (p, q) in enumerate(((c, 1 - l), (1 - c, 1 - l), (1 - c, l)))
    ]
    for copy in team:
        copy.start()
    for copy in team:
        copy.wait()
    total[...] = own[c * LN + l] + by_rank[0] + by_rank[1] + by_rank[2]
    qkv.finish()


QB = 256


def attend(mixed, context, totals, head):
    lanes = slice(head * HEAD, (head + 1) * HEAD)
    keys = mixed[:, HW + head * HEAD : HW + (head + 1) * HEAD]
    values = mixed[:, 2 * HW + head * HEAD : 2 * HW + (head + 1) * HEAD]
    for block in range(SEQ // QB):
        rows = slice(block * QB, (block + 1) * QB)
        upto = (block + 1) * QB
        scores = (
            lax.dot_general(
                mixed[rows, lanes], keys[:upto], (((1,), (1,)), ((), ())), preferred_element_type=F32
            )
            * 0.125
        )
        row = lax.broadcasted_iota(jnp.int32, (QB, upto), 0) + block * QB
        col = lax.broadcasted_iota(jnp.int32, (QB, upto), 1)
        scores = jnp.where(row >= col, scores, -1e30)
        peak = jnp.max(scores, axis=1, keepdims=True)
        weights = jnp.exp(scores - peak)
        total = jnp.sum(weights, axis=1, keepdims=True)
        prob = (weights * (1.0 / total)).astype(LOW)
        found = jnp.dot(prob, values[:upto], preferred_element_type=F32).astype(LOW)
        context[rows, lanes] = found
        totals[rows, head : head + 1] = peak + jnp.log(total)


def attend_back(mixed, totals, grads, acc_k, acc_v, head):
    lanes = slice(head * HEAD, (head + 1) * HEAD)
    lanes_k = slice(HW + head * HEAD, HW + (head + 1) * HEAD)
    lanes_v = slice(2 * HW + head * HEAD, 2 * HW + (head + 1) * HEAD)
    keys = mixed[:, lanes_k]
    values = mixed[:, lanes_v]
    acc_k[...] = jnp.zeros_like(acc_k)
    acc_v[...] = jnp.zeros_like(acc_v)
    for block in range(SEQ // QB):
        rows = slice(block * QB, (block + 1) * QB)
        upto = (block + 1) * QB
        queries = mixed[rows, lanes]
        outer = grads[rows, lanes]
        scores = (
            lax.dot_general(
                queries, keys[:upto], (((1,), (1,)), ((), ())), preferred_element_type=F32
            )
            * 0.125
        )
        row = lax.broadcasted_iota(jnp.int32, (QB, upto), 0) + block * QB
        col = lax.broadcasted_iota(jnp.int32, (QB, upto), 1)
        scores = jnp.where(row >= col, scores, -1e30)
        prob = jnp.exp(scores - totals[rows, head : head + 1])
        dprob = lax.dot_general(
            outer, values[:upto], (((1,), (1,)), ((), ())), preferred_element_type=F32
        )
        delta = jnp.sum(prob * dprob, axis=1, keepdims=True)
        ds = (prob * (dprob - delta)).astype(LOW)
        mixed[rows, lanes] = (
            jnp.dot(ds, keys[:upto], preferred_element_type=F32) * 0.125
        ).astype(LOW)
        acc_k[:upto] += outer_sum(ds, queries)
        acc_v[:upto] += outer_sum(prob.astype(LOW), outer)
    mixed[:, lanes_k] = (acc_k[...] * 0.125).astype(LOW)
    mixed[:, lanes_v] = acc_v[...].astype(LOW)


def plain(body, name, ins, outs, scratch=()):
    return pl.pallas_call(
        body,
        out_shape=[jax.ShapeDtypeStruct(s, d) for s, d in outs],
        in_specs=[VM] * len(ins),
        out_specs=[VM] * len(outs),
        scratch_shapes=list(scratch),
        compiler_params=pltpu.CompilerParams(vmem_limit_bytes=VMEM_BYTES),
        name=name,
    )(*ins)


def pick(values, index):
    return lax.dynamic_index_in_dim(values, index, 0, keepdims=False)


def pad_to(values, axis, size):
    widths = [(0, 0)] * values.ndim
    widths[axis] = (0, size - values.shape[axis])
    return jnp.pad(values, widths)


def head_parts(columns):
    return jnp.stack(
        [
            pad_to(columns[:, start * HEAD : (start + count) * HEAD], 1, HW)
            for start, count in zip(STARTS, COUNTS)
        ]
    )


def head_join(parts):
    return jnp.concatenate([parts[r][:, : COUNTS[r] * HEAD] for r in range(4)], axis=1)


def feature_order():
    order = -np.ones((8, PIECE), np.int32)
    grid = np.arange(D).reshape(YN, CN, HN, LN, XN, 50).transpose(0, 2, 4, 1, 3, 5)
    order[:, :200] = grid.reshape(8, 200)
    return order.reshape(-1)


def context_order():
    natural = -np.ones(D, np.int32)
    grid = np.arange(D).reshape(YN, CN, HN, LN, XN, 50).transpose(1, 3, 0, 2, 4, 5).reshape(32, 50)
    for block in range(32):
        natural[grid[block]] = block * PB + np.arange(50)
    order = -np.ones((4, HW), np.int32)
    for r in range(4):
        width = COUNTS[r] * HEAD
        order[r, :width] = natural[STARTS[r] * HEAD : STARTS[r] * HEAD + width]
    return order.reshape(-1)


def one_hot(order, size):
    return (np.arange(size)[:, None] == order[None, :]).astype(LOW)


def dot(left, right):
    return jnp.dot(left, right, preferred_element_type=F32)


def ones_row(values):
    return jnp.sum(values.astype(F32), axis=0)


def fast_shards(inputs, grad_out, w_qkv, w_proj, w_fc, w_out, smalls):
    y, c, h, l, x = here()
    rank = c * LN + l
    to_wide = jnp.asarray(one_hot(feature_order(), D))
    to_proj = jnp.asarray(one_hot(context_order(), PROJ).T.copy())

    rows = w_qkv.reshape(50, 3, D)
    units_qkv = jnp.stack([head_parts(rows[:, i]) for i in range(3)], axis=2).reshape(4, 50, QW)
    units_qkv = pad_to(units_qkv, 1, 64)
    units_fc = w_fc.reshape(50, YN, CN, HN, LN, XN, 200).transpose(2, 4, 0, 1, 3, 5, 6)
    units_fc = pad_to(pad_to(units_fc, 6, PIECE).reshape(4, 50, WIDE), 1, 64)
    small = pad_to(smalls, 0, 2048).reshape(16, 128)
    piece_out = pad_to(w_out.reshape(200, D), 0, PIECE)
    piece_proj = pad_to(w_proj.reshape(50, D), 0, PB)
    tokens, smalls_all, mat_qkv, mat_proj, piece_fc = call(
        prologue, "prologue", 1,
        (inputs.reshape(MICRO, BLK, D), units_qkv, units_fc, small, piece_proj),
        [
            ((2, BLK, D), LOW), ((8, 4, 16, 128), LOW), ((8, PIECE, QW), LOW), ((4, 8, PB, D), LOW),
            ((PIECE, WIDE), LOW),
        ],
        [VM] * 5, [ANY] * 4 + [VM],
        [
            pltpu.VMEM((4, 64, QW), LOW), pltpu.VMEM((4, 64, WIDE), LOW),
            pltpu.VMEM((PIECE, QW), F32), pltpu.VMEM((PIECE, WIDE), F32), pltpu.VMEM((PIECE, QW), LOW),
            pltpu.VMEM((PB, D), LOW),
        ],
        SMALLS_SEMS + 2 * TEAM_SWAP_SEMS + TOKENS_SEMS + 3 * GATHER_SEMS + 6,
    )
    mat_qkv = mat_qkv.reshape(WIDE, QW)
    mat_proj = mat_proj.reshape(PROJ, D)
    small = smalls_all.reshape(YN, HN, XN, CN, LN, 2048)[..., :600].transpose(0, 3, 1, 4, 2, 5)
    small = small.reshape(-1).astype(F32)
    gain1, shift1, bias_q, bias_v, bias_proj, gain2, shift2 = [segment(small, i) for i in range(7)]
    bias_fc = small[7 * D : 7 * D + FF].reshape(YN, CN, HN, LN, XN, 200)
    bias_fc = lax.dynamic_index_in_dim(bias_fc, c, 1, keepdims=False)
    bias_fc = lax.dynamic_index_in_dim(bias_fc, l, 2, keepdims=False)
    bias_fc = pad_to(bias_fc, 3, PIECE).reshape(WIDE)
    bias_out = small[7 * D + FF :]
    bias_qkv = jnp.stack(
        [head_parts(bias_q[None]), jnp.zeros((4, 1, HW)), head_parts(bias_v[None])], axis=1
    )
    bias_qkv = pick(bias_qkv, rank).reshape(QW)

    tokens_low = tokens.reshape(2 * BLK, D)
    tokens = tokens_low.astype(F32)
    hidden_one = layer_norm(tokens, gain1, shift1)
    hidden_one = dot(hidden_one.astype(LOW), to_wide).astype(LOW)
    (
        hidden_one, cotangent, grad_all, mat_fc, mat_out, hidden_two, mixed, totals, context, resid,
    ) = call(
        forward, "forward", 2,
        (
            hidden_one.reshape(2, BLK, WIDE), grad_out.reshape(MICRO, BLK, D), piece_fc, piece_out,
            mat_qkv, mat_proj, to_proj, to_wide, tokens_low, bias_qkv.reshape(1, QW),
            bias_proj.reshape(1, D), gain2.reshape(1, D), shift2.reshape(1, D),
        ),
        [
            ((8, BLK, WIDE), LOW), ((2, BLK, D), LOW), ((8, BLK, D), LOW),
            ((8, PIECE, WIDE), LOW), ((8, PIECE, D), LOW),
            ((8, BLK, WIDE), LOW), ((SEQ, QW), LOW), ((SEQ, SLOTS), F32), ((2 * BLK, PROJ), LOW),
            ((2 * BLK, D), F32),
        ],
        [VM] * 4 + [ANY] * 4 + [VM] * 5, [VM, VM] + [ANY] * 4 + [VM] * 4,
        [
            pltpu.VMEM((WIDE, QW), LOW), pltpu.VMEM((PROJ, D), LOW), pltpu.VMEM((4 * HW, PROJ), LOW),
            pltpu.VMEM((D, WIDE), LOW), pltpu.VMEM((SEQ, HW), LOW), pltpu.VMEM((4, 2, BLK, HW), LOW),
            pltpu.VMEM((2, BLK, WIDE), LOW),
        ],
        3 * TEAM_GATHER_SEMS + TOKENS_SEMS + 2 * GATHER_SEMS + 2 * TEAM_SWAP_SEMS + 4,
    )
    hidden_one = hidden_one.reshape(SEQ, WIDE)
    hidden_two = hidden_two.reshape(SEQ, WIDE)
    mat_out = mat_out.reshape(WIDE, D)
    mat_fc = mat_fc.reshape(WIDE, WIDE)
    _, ln2_pull = jax.vjp(layer_norm, resid, gain2, shift2)
    result, grad_hidden_two, grad_out_w, grad_pre, fc_terms = call(
        feed_forward, "feed_forward", 5,
        (hidden_two, grad_all, mat_fc, mat_out, bias_fc.reshape(1, WIDE)),
        [
            ((2, BLK, D), F32), ((2, BLK, WIDE), F32), ((PIECE, D), F32), ((SEQ, WIDE), LOW),
            ((1, WIDE), F32),
        ],
        [ANY] * 4 + [VM], [VM] * 5,
        [
            pltpu.VMEM((SEQ, WIDE), LOW), pltpu.VMEM((8, BLK, D), LOW), pltpu.VMEM((WIDE, WIDE), LOW),
            pltpu.VMEM((WIDE, D), LOW), pltpu.VMEM((SEQ, WIDE), LOW), pltpu.VMEM((SEQ, D), LOW),
            pltpu.VMEM((SEQ, WIDE), LOW), pltpu.VMEM((WIDE, D), LOW),
        ]
        + team_scatter_scratch(D) + team_scatter_scratch(WIDE) + scatter_scratch(PIECE, D),
        2 * TEAM_SCATTER_SEMS + SCATTER_SEMS + 4,
    )
    result = (resid + result.reshape(2 * BLK, D) + bias_out).astype(LOW)
    grad_out_w = grad_out_w[:200].reshape(-1)

    grad_full = cotangent.reshape(2 * BLK, D).astype(F32)
    grad_hidden_two = back_product(grad_hidden_two.reshape(2 * BLK, WIDE).astype(LOW), to_wide)
    grad_ln_two, grad_gain_two, grad_shift_two = ln2_pull(grad_hidden_two)
    grad_resid = grad_full + grad_ln_two
    grad_branch = grad_resid.astype(LOW)
    grad_context = back_product(grad_branch, mat_proj).astype(LOW)
    grad_context = back_product(grad_context, to_proj).astype(LOW)
    grad_context = jnp.stack(
        [grad_context[:, r * HW : (r + 1) * HW] for r in range(4)]
    ).reshape(4, 2, BLK, HW)
    units_qkv, got_fc, grad_proj, outputs, grad_in, terms, norms = call(
        backward, "backward", 7,
        (
            hidden_one, hidden_two, grad_pre, mat_qkv, mixed, totals, grad_context, context,
            grad_branch, result.reshape(2, BLK, D), tokens_low, grad_resid, gain1.reshape(1, D),
            to_wide,
        ),
        [
            ((4, 64, QW), LOW), ((4, 64, WIDE), LOW), ((PB, WIDE), F32), ((2, BLK, D), LOW),
            ((2, BLK, D), LOW), ((1, QW), F32), ((2, D), F32),
        ],
        [ANY] * 5 + [VM, ANY] + [VM] * 6 + [ANY], [VM, ANY, VM, ANY, ANY, VM, VM],
        [
            pltpu.VMEM((SEQ, WIDE), LOW), pltpu.VMEM((SEQ, WIDE), LOW), pltpu.VMEM((WIDE, QW), LOW),
            pltpu.VMEM((WIDE, WIDE), LOW), pltpu.VMEM((SEQ, WIDE), LOW),
            pltpu.VMEM((SEQ, HW), LOW), pltpu.VMEM((SEQ, QW), LOW),
            pltpu.VMEM((SEQ, HEAD), F32), pltpu.VMEM((SEQ, HEAD), F32),
        ]
        + team_scatter_scratch(WIDE) + scatter_scratch(PIECE, WIDE) + scatter_scratch(PIECE, QW)
        + scatter_scratch(PB, WIDE)
        + [
            pltpu.VMEM((PROJ // 2, WIDE), LOW), pltpu.VMEM((PROJ // 4, WIDE), LOW),
            pltpu.VMEM((2, BLK, WIDE), F32), pltpu.VMEM((2, BLK, D), LOW),
            pltpu.VMEM((224, WIDE), F32), pltpu.VMEM((224, QW), F32), pltpu.VMEM((4, 64, WIDE), LOW),
        ],
        TEAM_SCATTER_SEMS + 3 * SCATTER_SEMS + 2 * TOKENS_SEMS + 3 * TEAM_SWAP_SEMS + 10,
    )
    grad_proj = grad_proj[:50, :D].reshape(-1)

    terms = terms.reshape(3, HW)
    mine = (jnp.arange(4) == rank).astype(F32)[:, None, None]
    grad_bq = head_join(mine * terms[0][None, None])[0]
    grad_bv = head_join(mine * terms[2][None, None])[0]
    fc_terms = fc_terms.reshape(YN, 1, HN, 1, XN, PIECE)[..., :200]
    spot = (jnp.arange(CN) == c)[:, None, None] & (jnp.arange(LN) == l)
    spot = spot[None, ..., None, None]
    grad_fc_bias = jnp.where(spot, fc_terms, 0.0).reshape(-1)
    front = jnp.concatenate([norms.reshape(-1), grad_bq, grad_bv])
    tail = jnp.concatenate(
        [
            ones_row(grad_branch), grad_gain_two, grad_shift_two, grad_fc_bias,
            jnp.sum(grad_full, axis=0),
        ]
    )
    small = jnp.concatenate([front.reshape(32, 200), tail.reshape(32, 400)], axis=1)
    small = pad_to(small, 1, 1024).reshape(YN, CN, HN, LN, XN, 8, 128).transpose(0, 2, 4, 1, 3, 5, 6)
    got_qkv, total = call(
        epilogue, "epilogue", 8, (units_qkv, small.reshape(8, 4, 8, 128)),
        [((4, 64, QW), LOW), ((8, 128), F32)],
        [VM] * 2, [ANY, VM],
        [
            pltpu.VMEM((7, 4, 8, 128), F32), pltpu.VMEM((4, 8, 128), F32),
            pltpu.VMEM((3, 8, 128), F32),
        ],
        TEAM_SWAP_SEMS + 20,
    )
    parts = got_qkv[:, :50].reshape(4, 50, 3, HW)
    grad_qkv = jnp.stack([head_join(parts[:, :, i]) for i in range(3)], axis=1)
    grad_qkv = grad_qkv.astype(F32).reshape(-1)
    grad_fc = got_fc[:, :50].reshape(CN, LN, 50, YN, HN, XN, PIECE)[..., :200]
    grad_fc = grad_fc.transpose(2, 3, 0, 4, 1, 5, 6).astype(F32).reshape(-1)
    total = total.reshape(-1)
    return (
        outputs[:, None],
        grad_in.astype(F32)[:, None],
        grad_qkv,
        grad_proj,
        grad_fc,
        grad_out_w,
        total[:200],
        total[200:600],
    )


def solution(mesh):
    placed = (
        P(None, "dp", "ctx", None),
        P(None, "dp", "ctx", None),
        P(("dp", "ctx")),
        P(("dp", "ctx")),
        P(("dp", "ctx")),
        P(("dp", "ctx")),
        P(("dp", "ctx")),
    )
    fast = dict(mesh.shape) == {"dp": DP, "ctx": CTX}
    return jax.shard_map(
        fast_shards if fast else shards,
        mesh=mesh,
        in_specs=placed,
        out_specs=(
            P(None, "dp", "ctx", None),
            P(None, "dp", "ctx", None),
            P(("dp", "ctx")),
            P(("dp", "ctx")),
            P(("dp", "ctx")),
            P(("dp", "ctx")),
            P(("dp", "ctx")),
            P(("dp", "ctx")),
        ),
        check_vma=False,
    )
```

```python
import functools

import jax
import jax.numpy as jnp
import numpy as np
from jax import lax
from jax.experimental import pallas as pl
from jax.experimental.pallas import tpu as pltpu
from jax.sharding import PartitionSpec as P

D = 1600
HEADS = 25
HEAD = 64
FF = 6400
MICRO = 2


EPS = 1e-05


def layer_norm(values, gain, shift):
    center = values - jnp.mean(values, axis=-1, keepdims=True)
    spread = jnp.mean(center * center, axis=-1, keepdims=True)
    return center * lax.rsqrt(spread + EPS) * gain + shift


def gelu_tanh(values):
    return jax.nn.gelu(values, approximate=True)


def unpack(gathered):
    packed_qkv, packed_proj, packed_fc, packed_out, packed_small = gathered
    return (
        packed_qkv.reshape(D, 3 * D),
        packed_proj.reshape(D, D),
        packed_fc.reshape(D, FF),
        packed_out.reshape(FF, D),
        packed_small.astype(jnp.float32),
    )


def fetch(w_qkv, w_proj, w_fc, w_out, smalls):
    return unpack(
        (
            lax.all_gather(w_qkv, ("dp", "ctx"), axis=0, tiled=True),
            lax.all_gather(w_proj, ("dp", "ctx"), axis=0, tiled=True),
            lax.all_gather(w_fc, ("dp", "ctx"), axis=0, tiled=True),
            lax.all_gather(w_out, ("dp", "ctx"), axis=0, tiled=True),
            lax.all_gather(smalls, ("dp", "ctx"), axis=0, tiled=True),
        )
    )


def fetch_again(w_qkv, w_proj, w_fc, w_out, smalls):
    return unpack(
        (
            lax.all_gather(w_qkv, ("dp", "ctx"), axis=0, tiled=True),
            lax.all_gather(w_proj, ("dp", "ctx"), axis=0, tiled=True),
            lax.all_gather(w_fc, ("dp", "ctx"), axis=0, tiled=True),
            lax.all_gather(w_out, ("dp", "ctx"), axis=0, tiled=True),
            lax.all_gather(smalls, ("dp", "ctx"), axis=0, tiled=True),
        )
    )


def outer_sum(left, right):
    return lax.dot_general(
        left, right, (((0,), (0,)), ((), ())), preferred_element_type=jnp.float32
    )


def back_product(grad, weight):
    return lax.dot_general(
        grad, weight, (((1,), (1,)), ((), ())), preferred_element_type=jnp.float32
    )


def flat_term(left, right, start, count):
    width = right.shape[1]
    span = count // width + 2
    padded = jnp.pad(left, ((0, 0), (0, span)))
    first_row = start // width
    piece = lax.dynamic_slice_in_dim(padded, first_row, span, 1)
    block = outer_sum(piece, right).astype(jnp.bfloat16).reshape(-1)
    return lax.dynamic_slice_in_dim(block, start, count, 0)


def masked_scores(queries, keys, query_start, key_start):
    scores = (
        jnp.einsum("sqhe,skhe->shqk", queries, keys, preferred_element_type=jnp.float32) * 0.125
    )
    query_pos = query_start + jnp.arange(queries.shape[1])
    key_pos = key_start + jnp.arange(keys.shape[1])
    allowed = query_pos[:, None] >= key_pos[None, :]
    return jnp.where(allowed[None, None], scores, -1e30)


def segment(small_vals, which):
    return small_vals[which * D : (which + 1) * D]


def shards(inputs, grad_out, w_qkv, w_proj, w_fc, w_out, smalls):
    seqs = inputs.shape[1]
    local_len = inputs.shape[2]
    rows = seqs * local_len
    offset = lax.axis_index("ctx") * local_len
    acc_small = [jnp.zeros((D,), jnp.float32) for _ in range(7)]
    acc_fc_bias = jnp.zeros((FF,), jnp.float32)
    acc_out_bias = jnp.zeros((D,), jnp.float32)
    result_list = []
    grad_list = []
    kept_hidden_one = []
    kept_mixed_grad = []
    kept_context = []
    kept_branch_grad = []
    kept_hidden_two = []
    kept_pre_grad = []
    kept_activ = []
    kept_out_grad = []
    for batch_index in range(MICRO):
        params = fetch(w_qkv, w_proj, w_fc, w_out, smalls)
        mat_qkv, mat_proj, mat_fc, mat_out, small_vals = params
        tokens = inputs[batch_index].astype(jnp.float32).reshape(rows, D)
        hidden_one, ln1_pull = jax.vjp(
            layer_norm, tokens, segment(small_vals, 0), segment(small_vals, 1)
        )
        hidden_one = hidden_one.astype(jnp.bfloat16)
        qkv_bias = jnp.concatenate(
            [segment(small_vals, 2), jnp.zeros((D,), jnp.float32), segment(small_vals, 3)]
        )
        mixed = (
            jnp.dot(hidden_one, mat_qkv, preferred_element_type=jnp.float32) + qkv_bias
        ).astype(jnp.bfloat16)
        queries = mixed[:, :D].reshape(seqs, local_len, HEADS, HEAD)
        keys_local = mixed[:, D : 2 * D].reshape(seqs, local_len, D)
        values_local = mixed[:, 2 * D :].reshape(seqs, local_len, D)
        keys_all, values_all = (
            lax.all_gather(keys_local, "ctx", axis=1, tiled=True),
            lax.all_gather(values_local, "ctx", axis=1, tiled=True),
        )
        keys_all = keys_all.reshape(seqs, -1, HEADS, HEAD)
        values_all = values_all.reshape(seqs, -1, HEADS, HEAD)
        scores = masked_scores(queries, keys_all, offset, 0)
        row_peak = jnp.max(scores, axis=-1, keepdims=True)
        log_total = row_peak + jnp.log(jnp.sum(jnp.exp(scores - row_peak), axis=-1, keepdims=True))
        attn_low = jnp.exp(scores - log_total).astype(jnp.bfloat16)
        context = jnp.einsum(
            "shqk,skhe->sqhe", attn_low, values_all, preferred_element_type=jnp.float32
        )
        context = context.reshape(rows, D).astype(jnp.bfloat16)
        resid = (
            tokens
            + jnp.dot(context, mat_proj, preferred_element_type=jnp.float32)
            + segment(small_vals, 4)
        )
        hidden_two, ln2_pull = jax.vjp(
            layer_norm, resid, segment(small_vals, 5), segment(small_vals, 6)
        )
        hidden_two = hidden_two.astype(jnp.bfloat16)
        pre_act = (
            jnp.dot(hidden_two, mat_fc, preferred_element_type=jnp.float32)
            + small_vals[7 * D : 7 * D + FF]
        )
        activ, gelu_pull = jax.vjp(gelu_tanh, pre_act)
        activ = activ.astype(jnp.bfloat16)
        result = (
            resid
            + jnp.dot(activ, mat_out, preferred_element_type=jnp.float32)
            + small_vals[7 * D + FF :]
        )
        result_list.append(result.astype(jnp.bfloat16).reshape(seqs, local_len, D))
        back_params = fetch_again(w_qkv, w_proj, w_fc, w_out, smalls)
        mat_qkv, mat_proj, mat_fc, mat_out, small_vals = back_params
        grad_low = grad_out[batch_index].reshape(rows, D)
        grad_full = grad_low.astype(jnp.float32)
        acc_out_bias = acc_out_bias + jnp.sum(grad_full, axis=0)
        grad_act = back_product(grad_low, mat_out)
        (grad_pre,) = gelu_pull(grad_act)
        grad_pre = grad_pre.astype(jnp.bfloat16)
        acc_fc_bias = acc_fc_bias + jnp.sum(grad_pre.astype(jnp.float32), axis=0)
        grad_hidden_two = back_product(grad_pre, mat_fc)
        grad_ln_two, grad_gain_two, grad_shift_two = ln2_pull(grad_hidden_two)
        acc_small[5] = acc_small[5] + grad_gain_two
        acc_small[6] = acc_small[6] + grad_shift_two
        grad_resid = grad_full + grad_ln_two
        grad_branch = grad_resid.astype(jnp.bfloat16)
        acc_small[4] = acc_small[4] + jnp.sum(grad_branch.astype(jnp.float32), axis=0)
        grad_context = (
            back_product(grad_branch, mat_proj)
            .astype(jnp.bfloat16)
            .reshape(seqs, local_len, HEADS, HEAD)
        )
        scores = masked_scores(queries, keys_all, offset, 0)
        attn_prob = jnp.exp(scores - log_total)
        grad_attn = jnp.einsum(
            "sqhe,skhe->shqk", grad_context, values_all, preferred_element_type=jnp.float32
        )
        row_delta = jnp.sum(attn_prob * grad_attn, axis=-1, keepdims=True)
        grad_scores = (attn_prob * (grad_attn - row_delta)).astype(jnp.bfloat16)
        grad_queries = (
            jnp.einsum("shqk,skhe->sqhe", grad_scores, keys_all, preferred_element_type=jnp.float32)
            * 0.125
        )
        query_all, dctx_all = (
            lax.all_gather(queries.reshape(seqs, local_len, D), "ctx", axis=1, tiled=True),
            lax.all_gather(grad_context.reshape(seqs, local_len, D), "ctx", axis=1, tiled=True),
        )
        lse_all, delta_all = (
            lax.all_gather(jnp.transpose(log_total[..., 0], (0, 2, 1)), "ctx", axis=1, tiled=True),
            lax.all_gather(jnp.transpose(row_delta[..., 0], (0, 2, 1)), "ctx", axis=1, tiled=True),
        )
        query_all = query_all.reshape(seqs, -1, HEADS, HEAD)
        dctx_all = dctx_all.reshape(seqs, -1, HEADS, HEAD)
        lse_all = jnp.transpose(lse_all, (0, 2, 1))[..., None]
        delta_all = jnp.transpose(delta_all, (0, 2, 1))[..., None]
        own_keys = keys_local.reshape(seqs, local_len, HEADS, HEAD)
        own_values = values_local.reshape(seqs, local_len, HEADS, HEAD)
        col_scores = masked_scores(query_all, own_keys, 0, offset)
        col_prob = jnp.exp(col_scores - lse_all)
        col_dattn = jnp.einsum(
            "sqhe,skhe->shqk", dctx_all, own_values, preferred_element_type=jnp.float32
        )
        col_ds = (col_prob * (col_dattn - delta_all)).astype(jnp.bfloat16)
        grad_keys = (
            jnp.einsum("shqk,sqhe->skhe", col_ds, query_all, preferred_element_type=jnp.float32)
            * 0.125
        )
        grad_values = jnp.einsum(
            "shqk,sqhe->skhe",
            col_prob.astype(jnp.bfloat16),
            dctx_all,
            preferred_element_type=jnp.float32,
        )
        grad_mixed = jnp.concatenate(
            [
                grad_queries.reshape(rows, D),
                grad_keys.reshape(rows, D),
                grad_values.reshape(rows, D),
            ],
            axis=1,
        ).astype(jnp.bfloat16)
        bias_terms = jnp.sum(grad_mixed.astype(jnp.float32), axis=0)
        acc_small[2] = acc_small[2] + bias_terms[:D]
        acc_small[3] = acc_small[3] + bias_terms[2 * D :]
        grad_hidden_one = back_product(grad_mixed, mat_qkv)
        grad_ln_one, grad_gain_one, grad_shift_one = ln1_pull(grad_hidden_one)
        acc_small[0] = acc_small[0] + grad_gain_one
        acc_small[1] = acc_small[1] + grad_shift_one
        grad_list.append((grad_resid + grad_ln_one).reshape(seqs, local_len, D))
        kept_hidden_one.append(hidden_one)
        kept_mixed_grad.append(grad_mixed)
        kept_context.append(context)
        kept_branch_grad.append(grad_branch)
        kept_hidden_two.append(hidden_two)
        kept_pre_grad.append(grad_pre)
        kept_activ.append(activ)
        kept_out_grad.append(grad_low)
    front_grads = jnp.concatenate(acc_small[0:4])
    tail_grads = jnp.concatenate(acc_small[4:7] + [acc_fc_bias, acc_out_bias])
    grad_qkv = lax.psum_scatter(
        flat_term(
            jnp.concatenate(kept_hidden_one),
            jnp.concatenate(kept_mixed_grad),
            jnp.int32(0),
            lax.axis_size(("dp", "ctx")) * w_qkv.shape[0],
        ),
        ("dp", "ctx"),
        scatter_dimension=0,
        tiled=True,
    ).astype(jnp.float32)
    grad_proj = lax.psum_scatter(
        flat_term(
            jnp.concatenate(kept_context),
            jnp.concatenate(kept_branch_grad),
            jnp.int32(0),
            lax.axis_size(("dp", "ctx")) * w_proj.shape[0],
        ),
        ("dp", "ctx"),
        scatter_dimension=0,
        tiled=True,
    ).astype(jnp.float32)
    grad_fc = lax.psum_scatter(
        flat_term(
            jnp.concatenate(kept_hidden_two),
            jnp.concatenate(kept_pre_grad),
            jnp.int32(0),
            lax.axis_size(("dp", "ctx")) * w_fc.shape[0],
        ),
        ("dp", "ctx"),
        scatter_dimension=0,
        tiled=True,
    ).astype(jnp.float32)
    grad_out_w = lax.psum_scatter(
        flat_term(
            jnp.concatenate(kept_activ),
            jnp.concatenate(kept_out_grad),
            jnp.int32(0),
            lax.axis_size(("dp", "ctx")) * w_out.shape[0],
        ),
        ("dp", "ctx"),
        scatter_dimension=0,
        tiled=True,
    ).astype(jnp.float32)
    grad_front, grad_tail = (
        lax.psum_scatter(front_grads, ("dp", "ctx"), scatter_dimension=0, tiled=True),
        lax.psum_scatter(tail_grads, ("dp", "ctx"), scatter_dimension=0, tiled=True),
    )
    return (
        jnp.stack(result_list),
        jnp.stack(grad_list),
        grad_qkv,
        grad_proj,
        grad_fc,
        grad_out_w,
        grad_front,
        grad_tail,
    )


DP, CTX = 4, 8
YN, CN, HN, LN, XN = 2, 2, 2, 2, 2
SLOTS = 7
HW = SLOTS * HEAD
QW = 3 * HW
STARTS = (0, 7, 13, 19)
COUNTS = (7, 6, 6, 6)
BLK = 128
SEQ = 8 * BLK
PIECE = 208
WIDE = 8 * PIECE
PB = 64
PROJ = 32 * PB
LOW = jnp.bfloat16
F32 = jnp.float32
VMEM_BYTES = 60 * 1024 * 1024
ANY = pl.BlockSpec(memory_space=pl.ANY)
VM = pl.BlockSpec(memory_space=pltpu.VMEM)


def here():
    dp, ctx = lax.axis_index("dp"), lax.axis_index("ctx")
    return dp // CN, dp % CN, ctx // 4, (ctx // XN) % LN, ctx % XN


def device(y, c, h, l, x):
    return (y * CN + c, (h * LN + l) * XN + x)


def team_number(y, h, x):
    return y * 4 + h * 2 + x


class Wires:
    def __init__(self, sems):
        self.sems, self.used = sems, 0

    def one(self):
        self.used += 1
        assert self.used <= self.sems.shape[0]
        return self.sems.at[self.used - 1]

    def far(self, source, target, where):
        return pltpu.make_async_remote_copy(
            src_ref=source,
            dst_ref=target,
            send_sem=self.one(),
            recv_sem=self.one(),
            device_id=where,
            device_id_type=pl.DeviceIdType.MESH,
        )

    def near(self, source, target):
        return pltpu.make_async_copy(source, target, self.one())


def signal(where):
    pl.semaphore_signal(
        pltpu.get_barrier_semaphore(), inc=1, device_id=where, device_id_type=pl.DeviceIdType.MESH
    )


def team_peers(y, c, h, l, x):
    return [
        device(y, 1 - c, h, l, x), device(y, c, h, 1 - l, x), device(y, 1 - c, h, 1 - l, x)
    ]


def grid_peers(y, c, h, l, x):
    return [
        device(1 - y, c, h, l, x), device(y, c, 1 - h, l, x), device(y, c, h, l, 1 - x)
    ]


def meet(peers):
    for peer in peers:
        signal(peer)
    pl.semaphore_wait(pltpu.get_barrier_semaphore(), len(peers))


def call(body, name, ident, ins, outs, in_specs, out_specs, scratch, sems, cost=None):
    return pl.pallas_call(
        body,
        out_shape=[jax.ShapeDtypeStruct(s, d) for s, d in outs],
        in_specs=in_specs,
        out_specs=out_specs,
        scratch_shapes=list(scratch) + [pltpu.SemaphoreType.DMA((sems,))],
        compiler_params=pltpu.CompilerParams(
            collective_id=ident, has_side_effects=True, vmem_limit_bytes=VMEM_BYTES
        ),
        name=name,
    )(*ins)


class Routes:
    def __init__(self, spot):
        y, c, h, l, x = spot
        self.place = (y, h, x)
        self.peers = {
            "y": device(1 - y, c, h, l, x),
            "h": device(y, c, 1 - h, l, x),
            "x": device(y, c, h, l, 1 - x),
        }

    def flipped(self, ways):
        y, h, x = self.place
        return team_number(
            1 - y if "y" in ways else y, 1 - h if "h" in ways else h, 1 - x if "x" in ways else x
        )


def halves(rows):
    cut = (rows // 2 + 15) // 16 * 16
    return ((0, cut, "hxy"), (cut, rows - cut, "hyx"))


class Gather:
    def __init__(self, wires, piece, whole, spot):
        routes = Routes(spot)
        self.local = wires.near(piece, whole.at[routes.flipped("")])
        self.parts = []
        for start, size, order in halves(piece.shape[0]):
            at = pl.ds(start, size)
            first, second, third = order

            def copy(ways, way):
                spot = whole.at[routes.flipped(ways), at]
                source = piece.at[at] if not ways else spot
                return wires.far(source, spot, routes.peers[way])

            self.parts.append(
                {
                    "first": copy("", first),
                    "second": [copy("", second), copy(first, second)],
                    "third": [
                        copy("", third), copy(second, third), copy(first, third),
                        copy(first + second, third),
                    ],
                }
            )

    def start(self):
        self.local.start()
        for part in self.parts:
            part["first"].start()
            part["second"][0].start()
            part["third"][0].start()

    def step(self, turn):
        for part in self.parts:
            if turn == 1:
                part["second"][0].wait_recv()
                part["third"][1].start()
            elif turn == 2:
                part["first"].wait_recv()
                part["second"][1].start()
                part["third"][2].start()
            else:
                part["second"][1].wait_recv()
                part["third"][3].start()

    def finish(self):
        self.local.wait()
        for part in self.parts:
            for copy in [part["first"]] + part["second"]:
                copy.wait_send()
            for copy in part["third"]:
                copy.wait()


GATHER_SEMS = 1 + 2 * 2 * 7


class Scatter:
    def __init__(self, wires, parts, landed, spot):
        routes = Routes(spot)
        self.rows = landed.shape[1]
        self.parts, self.landed = parts, landed
        self.jobs = []
        for start, size, order in halves(self.rows):
            first, second, third = order
            at = pl.ds(start, size)

            def term(ways):
                base = routes.flipped(ways) * self.rows + start
                return parts.at[pl.ds(pl.multiple_of(base, 16), size)]

            stay = [second + first, second, first, ""]
            job = {
                "terms": [term(ways) for ways in stay],
                "spots": [landed.at[k, at] for k in range(7)],
                "over": [
                    wires.far(term(third + ways), landed.at[k, at], routes.peers[third])
                    for k, ways in enumerate(stay)
                ],
                "along": [
                    wires.far(landed.at[k, at], landed.at[4 + k, at], routes.peers[second])
                    for k in range(2)
                ],
                "last": wires.far(landed.at[2, at], landed.at[6, at], routes.peers[first]),
                "at": slice(start, start + size),
            }
            self.jobs.append(job)

    def start(self):
        for k in (0, 2):
            for job in self.jobs:
                job["over"][k].start()

    def step(self, turn):
        k = (0, 2, 1)[turn - 1]
        for job in self.jobs:
            job["over"][k].wait_recv()
            if turn < 3:
                job["over"][2 * turn - 1].start()
            total = job["spots"][k][...].astype(F32) + job["terms"][k][...].astype(F32)
            if turn == 2:
                job["along"][0].wait_recv()
                total = total + job["spots"][4][...].astype(F32)
            job["spots"][k][...] = total.astype(LOW)
            (job["along"] + [job["last"]])[k].start()

    def finish(self, total):
        for job in self.jobs:
            job["over"][3].wait_recv()
            job["along"][1].wait_recv()
            job["last"].wait_recv()
            summed = job["terms"][3][...].astype(F32)
            for k in (3, 5, 6):
                summed = summed + job["spots"][k][...].astype(F32)
            total[job["at"], :] = summed.astype(total.dtype)
            for copy in job["over"] + job["along"] + [job["last"]]:
                copy.wait_send()


SCATTER_SEMS = 2 * 2 * 7


class TeamGather:
    def __init__(self, wires, block, whole, spot):
        y, c, h, l, x = spot
        mate, beside = device(y, 1 - c, h, l, x), device(y, c, h, 1 - l, x)

        def at(l, s):
            return whole.at[c * 4 + l * 2 + s]

        self.local = [wires.near(block.at[s], at(l, s)) for s in range(2)]
        self.to_mate = [wires.far(block.at[s], at(l, s), mate) for s in range(2)]
        self.to_side = [wires.far(block.at[s], at(l, s), beside) for s in range(2)]
        self.relay = [wires.far(at(1 - l, s), at(1 - l, s), mate) for s in range(2)]

    def start(self):
        for copy in self.to_side + self.to_mate + self.local:
            copy.start()

    def step(self, s):
        self.to_side[s].wait_recv()
        self.relay[s].start()

    def finish(self):
        for copy in self.local + self.to_mate + self.relay:
            copy.wait()
        for copy in self.to_side:
            copy.wait_send()


TEAM_GATHER_SEMS = 2 + 2 * 6


class TeamSwap:
    def __init__(self, wires, source, target, spot):
        y, c, h, l, x = spot
        self.local = wires.near(source(c, l), target(c, l))
        self.copies = [
            wires.far(source(p, q), target(c, l), device(y, p, h, q, x))
            for p, q in ((c, 1 - l), (1 - c, 1 - l), (1 - c, l))
        ]

    def start(self):
        for copy in self.copies + [self.local]:
            copy.start()

    def finish(self):
        for copy in self.copies + [self.local]:
            copy.wait()


TEAM_SWAP_SEMS = 1 + 2 * 3


def pair_rows(c, l):
    return pl.ds(pl.multiple_of((c * 2 + l) * 2 * BLK, 2 * BLK), 2 * BLK)


def block_rows(c, l, s):
    return pl.ds(pl.multiple_of((c * 4 + l * 2 + s) * BLK, BLK), BLK)


class TeamScatter:
    def __init__(self, wires, parts, landed, leaving, arrived, spot):
        y, c, h, l, x = spot
        self.c, self.l = c, l
        self.parts, self.landed, self.leaving, self.arrived = parts, landed, leaving, arrived
        mate, beside = device(y, 1 - c, h, l, x), device(y, c, h, 1 - l, x)
        self.to_mate = [
            wires.far(parts.at[pair_rows(1 - c, q)], landed.at[k], mate)
            for k, q in enumerate((1 - l, l))
        ]
        self.to_side = [wires.far(leaving.at[s], arrived.at[s], beside) for s in range(2)]

    def start(self):
        for copy in self.to_mate:
            copy.start()

    def step(self, s):
        if s == 0:
            self.to_mate[0].wait_recv()
        rows = slice(s * BLK, (s + 1) * BLK)
        self.leaving[s] = (
            self.landed[0, rows, :].astype(F32)
            + self.parts[block_rows(self.c, 1 - self.l, s), :].astype(F32)
        ).astype(LOW)
        self.to_side[s].start()

    def finish(self, total):
        self.to_mate[1].wait_recv()
        for s in range(2):
            self.to_side[s].wait_recv()
            total[s] = (
                self.landed[1, s * BLK : (s + 1) * BLK, :].astype(F32)
                + self.parts[block_rows(self.c, self.l, s), :].astype(F32)
                + self.arrived[s].astype(F32)
            )
        for copy in self.to_mate + self.to_side:
            copy.wait_send()


TEAM_SCATTER_SEMS = 2 * 4


def team_scatter_scratch(width):
    return [
        pltpu.VMEM((2, 2 * BLK, width), LOW),
        pltpu.VMEM((2, BLK, width), LOW),
        pltpu.VMEM((2, BLK, width), LOW),
    ]


def scatter_scratch(rows, width):
    return [pltpu.VMEM((7, rows, width), LOW)]


class Tokens:
    def __init__(self, wires, source, target, spot):
        y, c, h, l, x = spot
        self.stays = h == c
        goals = token_goals(spot)
        pairs = []
        for k in range(2):
            other = lax.rem(x + k, 2)
            pairs.append((source.at[other], target.at[x]))
        self.local = wires.near(*pairs[0])
        self.copies = [wires.far(*pair, goal) for pair, goal in zip(pairs, goals)]

    def start(self):
        pl.when(self.stays)(self.local.start)
        pl.when(jnp.logical_not(self.stays))(self.copies[0].start)
        self.copies[1].start()

    def finish(self):
        pl.when(self.stays)(self.local.wait)
        pl.when(jnp.logical_not(self.stays))(self.copies[0].wait)
        self.copies[1].wait()


TOKENS_SEMS = 1 + 2 * 2


def token_goals(spot):
    y, c, h, l, x = spot
    return [device(y, h, c, l, x), device(y, h, c, l, 1 - x)]


def meet_tokens(peers, spot):
    y, c, h, l, x = spot
    same, other = token_goals(spot)
    for peer in peers + [other]:
        signal(peer)
    pl.when(h != c)(functools.partial(signal, same))
    count = len(peers) + 1 + jnp.where(h == c, 0, 1)
    pl.semaphore_wait(pltpu.get_barrier_semaphore(), count)


class Smalls:
    def __init__(self, wires, small, smalls, spot):
        y, c, h, l, x = spot
        own = team_number(y, h, x)
        self.first = TeamSwap(
            wires, lambda p, q: small, lambda p, q: smalls.at[own, p * LN + q], spot
        )
        self.second = [
            wires.far(smalls.at[own], smalls.at[own], where) for where in team_twins(*spot)
        ]

    def start(self):
        self.first.start()

    def step(self):
        self.first.finish()
        for copy in self.second:
            copy.start()

    def finish(self):
        for copy in self.second:
            copy.wait()


SMALLS_SEMS = TEAM_SWAP_SEMS + 2 * 7


def team_twins(y, c, h, l, x):
    ways = ((0, 0, 1), (1, 0, 0), (0, 1, 0), (1, 0, 1), (0, 1, 1), (1, 1, 0), (1, 1, 1))
    return [
        device(1 - y if a else y, c, 1 - h if b else h, l, 1 - x if d else x) for a, b, d in ways
    ]


def join_units(units, wide, piece):
    for k in range(4):
        wide[k * 50 : (k + 1) * 50, :] = units[k, :50, :].astype(F32)
    wide[200:, :] = jnp.zeros((PIECE - 200, wide.shape[1]), F32)
    piece[...] = wide[...].astype(LOW)


def prologue(
    inputs, units_qkv, units_fc, small, piece_proj,
    tokens, smalls, all_qkv, all_proj, piece_fc,
    got_qkv, got_fc, wide_qkv, wide_fc, piece_qkv, beside_proj, sems,
):
    spot = y, c, h, l, x = here()
    wires = Wires(sems)
    rank = c * LN + l
    meet_tokens(team_peers(*spot) + team_twins(*spot), spot)
    values = Smalls(wires, small, smalls, spot)
    qkv_units = TeamSwap(
        wires, lambda p, q: units_qkv.at[p * LN + q], lambda p, q: got_qkv.at[p * LN + q], spot
    )
    fc_units = TeamSwap(
        wires, lambda p, q: units_fc.at[p * LN + q], lambda p, q: got_fc.at[p * LN + q], spot
    )
    move = Tokens(wires, inputs, tokens, spot)
    qkv = Gather(wires, piece_qkv, all_qkv, spot)
    other = c * LN + 1 - l
    proj = Gather(wires, piece_proj, all_proj.at[rank], spot)
    side = wires.far(piece_proj, beside_proj, device(y, c, h, 1 - l, x))
    beside = Gather(wires, beside_proj, all_proj.at[other], spot)
    mate = device(y, 1 - c, h, l, x)
    relay = [
        wires.far(all_proj.at[r], all_proj.at[r], mate) for r in (rank, other)
    ]
    values.start()
    qkv_units.start()
    values.step()
    side.start()
    proj.start()
    qkv_units.finish()
    join_units(got_qkv, wide_qkv, piece_qkv)
    qkv.start()
    fc_units.start()
    move.start()
    side.wait()
    beside.start()
    proj.step(1)
    proj.step(2)
    proj.step(3)
    values.finish()
    qkv.step(1)
    proj.finish()
    relay[0].start()
    beside.step(1)
    qkv.step(2)
    beside.step(2)
    fc_units.finish()
    join_units(got_fc, wide_fc, piece_fc)
    qkv.step(3)
    beside.step(3)
    beside.finish()
    relay[1].start()
    move.finish()
    qkv.finish()
    for copy in relay:
        copy.wait()


def forward(
    hidden, grads, piece_fc, piece_out, mat_qkv, mat_proj, to_proj, to_wide,
    tokens, bias_qkv, bias_proj, gain2, shift2,
    hidden_all, cotangent, grad_all, all_fc, all_out, second_all, mixed, totals, context_out, resid,
    mat_in, proj_in, to_proj_in, to_wide_in, context, got, second, sems,
):
    spot = y, c, h, l, x = here()
    wires = Wires(sems)
    load = [
        wires.near(*both)
        for both in (
            (mat_qkv, mat_in), (mat_proj, proj_in), (to_proj, to_proj_in), (to_wide, to_wide_in)
        )
    ]
    for copy in load:
        copy.start()
    meet_tokens(team_peers(*spot) + grid_peers(*spot), spot)
    team = TeamGather(wires, hidden, hidden_all, spot)
    fc = Gather(wires, piece_fc, all_fc, spot)
    out = Gather(wires, piece_out, all_out, spot)
    bring = Tokens(wires, grads, cotangent, spot)
    team_two = TeamGather(wires, cotangent, grad_all, spot)
    team_three = TeamGather(wires, second, second_all, spot)
    swaps = [
        TeamSwap(
            wires,
            lambda p, q, s=s: context.at[block_rows(p, q, s)],
            lambda p, q, s=s: got.at[p * LN + q, s],
            spot,
        )
        for s in range(2)
    ]
    team.start()
    fc.start()
    team.step(0)
    team.step(1)
    load[0].wait()
    team.finish()
    bring.start()
    fc.step(1)

    @pl.loop(0, SEQ // QB)
    def _(i):
        rows = pl.ds(pl.multiple_of(i * QB, QB), QB)
        flat = hidden_all[pl.ds(pl.multiple_of(i * 2, 2), 2)].reshape(QB, WIDE)
        mixed[rows, :] = (dot(flat, mat_in[...]) + bias_qkv[...]).astype(LOW)

    fc.step(2)
    for head in range(SLOTS):
        attend(mixed, context, totals, head)
        if head == 0:
            fc.step(3)
            out.start()
            bring.finish()
            team_two.start()
        if head == 3:
            team_two.step(0)
        if head == 4:
            out.step(1)
    team_two.step(1)
    for copy in swaps:
        copy.start()
    for copy in load[1:]:
        copy.wait()
    for copy in swaps:
        copy.finish()
    out.step(2)
    placed = 0.0
    for r in range(4):
        placed = placed + dot(
            got[r].reshape(2 * BLK, HW), to_proj_in[r * HW : (r + 1) * HW, :]
        )
    placed = placed.astype(LOW)
    context_out[...] = placed
    found = tokens[...].astype(F32) + dot(placed, proj_in[...]) + bias_proj[...]
    resid[...] = found
    normed = layer_norm(found, gain2[...], shift2[...]).astype(LOW)
    second[...] = dot(normed, to_wide_in[...]).astype(LOW).reshape(2, BLK, WIDE)
    team_three.start()
    fc.finish()
    team_three.step(0)
    out.step(3)
    team_three.step(1)
    team_two.finish()
    team_three.finish()
    out.finish()


def gelu_both(f):
    square = f * f
    t = jnp.tanh(0.7978845608028654 * f * (1.0 + 0.044715 * square))
    half = 0.5 * (1.0 + t)
    slope = half + f * (0.5 * 0.7978845608028654) * (1.0 - t * t) * (1.0 + 3 * 0.044715 * square)
    return f * half, slope


def chunks(total, step):
    return [(start, min(step, total - start)) for start in range(0, total, step)]


def outer_into(target, left, right):
    count = left.shape[1] // 256

    @pl.loop(0, count)
    def _(i):
        at = pl.ds(pl.multiple_of(i * 256, 256), 256)
        target[at, :] = outer_sum(left[:, at], right()).astype(LOW)

    rest = left.shape[1] - count * 256
    if rest:
        target[count * 256 :, :] = outer_sum(left[:, count * 256 :], right()).astype(LOW)


def feed_forward(
    hidden_two, grad_all, mat_fc, mat_out, mat_proj, to_proj, to_wide,
    bias_fc, bias_out, gain2, resid, cotangent,
    result, grad_out_w, grad_pre, terms, grad_resid, branch, swap_parts, norms,
    h2, dy, wf, wo, activ, part_r, part_o, l1, s1, a1, l2, s2, a2, l3,
    hidden, total_r, spread, sems,
):
    spot = y, c, h, l, x = here()
    wires = Wires(sems)
    load = [
        wires.near(*both) for both in ((hidden_two, h2), (mat_fc, wf), (grad_all, dy), (mat_out, wo))
    ]
    for copy in load:
        copy.start()
    load_wide = wires.near(to_wide, wf.at[pl.ds(0, D)])
    load_proj = [wires.near(mat_proj.at[pl.ds(0, WIDE)], wo)] + [
        wires.near(mat_proj.at[pl.ds(WIDE + k * BLK, BLK)], dy.at[k]) for k in range(3)
    ]
    load_spread = [wires.near(to_proj.at[pl.ds(r * HW, HW)], spread) for r in range(4)]
    load_spread[0].start()
    meet(team_peers(*spot) + grid_peers(*spot))
    second = TeamScatter(wires, h2, l2, s2, a2, spot)
    first = TeamScatter(wires, part_r, l1, s1, a1, spot)
    out = Scatter(wires, part_o, l3, spot)
    load[0].wait()
    load[1].wait()

    @pl.loop(0, SEQ // QB)
    def _(i):
        rows = pl.ds(pl.multiple_of(i * QB, QB), QB)
        f = dot(h2[rows, :], wf[...]) + bias_fc[...]
        value, slope = gelu_both(f)
        activ[rows, :] = value.astype(LOW)
        grad_pre[rows, :] = slope.astype(LOW)

    load[2].wait()
    outer_into(part_o, activ, lambda: dy[...].reshape(SEQ, D))
    out.start()
    load[3].wait()
    terms[...] = jnp.zeros_like(terms)

    @pl.loop(0, SEQ // QB)
    def _(i):
        rows = pl.ds(pl.multiple_of(i * QB, QB), QB)
        here_dy = dy[pl.ds(pl.multiple_of(i * 2, 2), 2)].reshape(QB, D)
        df = (back_product(here_dy, wo[...]) * grad_pre[rows, :].astype(F32)).astype(LOW)
        grad_pre[rows, :] = df
        terms[...] += jnp.sum(df.astype(F32), axis=0, keepdims=True)

    def into(target, make):
        def half(which):
            @pl.loop(0, 2)
            def _(s):
                rows = pair_rows(which, s)
                target[rows, :] = make(rows).astype(LOW)

        return half

    half = into(h2, lambda rows: back_product(grad_pre[rows, :], wf[...]))
    half(1 - c)
    second.start()
    half(c)
    load_wide.start()
    out.step(1)
    second.step(0)
    second.step(1)
    half = into(part_r, lambda rows: dot(activ[rows, :], wo[...]))
    half(1 - c)
    first.start()
    half(c)
    for copy in load_proj:
        copy.start()
    out.step(2)
    first.step(0)
    first.step(1)
    load_wide.wait()
    second.finish(hidden)
    out.step(3)
    grad = back_product(hidden[...].reshape(2 * BLK, WIDE).astype(LOW), wf[:D, :])
    grad, norms[0:1, :], norms[1:2, :] = norm_back(resid[...], gain2[...], grad)
    own = cotangent[...].reshape(2 * BLK, D).astype(F32)
    norms[3:4, :] = jnp.sum(own, axis=0, keepdims=True)
    grad = own + grad
    grad_resid[...] = grad
    branch[...] = grad.astype(LOW)
    norms[2:3, :] = jnp.sum(branch[...].astype(F32), axis=0, keepdims=True)
    for copy in load_proj:
        copy.wait()
    low = back_product(branch[...], wo[...]).astype(LOW)
    high = back_product(branch[...], dy[0:3].reshape(3 * BLK, D)).astype(LOW)
    for r in range(4):
        load_spread[r].wait()
        part = back_product(low, spread[:, :WIDE]) + back_product(high, spread[:, WIDE:])
        swap_parts[r] = part.astype(LOW).reshape(2, BLK, HW)
        if r < 3:
            load_spread[r + 1].start()
    first.finish(total_r)
    result[...] = (
        resid[...].reshape(2, BLK, D) + total_r[...] + bias_out[...].reshape(1, 1, D)
    ).astype(LOW)
    out.finish(grad_out_w)


def backward(
    hidden_one, hidden_two, grad_pre, mat_qkv, mixed_all, totals, swap_parts, context, branch, result,
    tokens, grad_resid, gain1, to_wide,
    units_qkv, got_fc, grad_proj, outputs, grad_in, terms, norms,
    ha, hb, wq, part_f, part_h, grads, mixed, acc_k, acc_v,
    l1, s1, a1, l2, l3, l4, pm, px, hidden, grad_low, wide_fc, wide_qkv, units_fc, sems,
):
    spot = y, c, h, l, x = here()
    wires = Wires(sems)
    load = [wires.near(*both) for both in ((hidden_two, ha), (grad_pre, hb), (mixed_all, mixed), (mat_qkv, wq))]
    again = wires.near(hidden_one, ha)
    for copy in load:
        copy.start()
    meet_tokens(team_peers(*spot) + grid_peers(*spot), spot)
    swaps = [
        TeamSwap(
            wires,
            lambda p, q, s=s: swap_parts.at[p * LN + q, s],
            lambda p, q, s=s: grads.at[block_rows(p, q, s)],
            spot,
        )
        for s in range(2)
    ]
    for copy in swaps:
        copy.start()
    fc = Scatter(wires, part_f, l2, spot)
    first = TeamScatter(wires, part_h, l1, s1, a1, spot)
    qkv = Scatter(wires, wq, l3, spot)
    quarter = PROJ // 4
    to_mate = wires.far(hb, pm, device(y, 1 - c, h, l, x))

    def side(q):
        return pl.ds(pl.multiple_of(q * quarter, 16), quarter)

    def term(p, q):
        at = pl.ds(pl.multiple_of((p * 2 + q) * quarter, quarter), quarter)
        return outer_sum(context[:, at], branch[...])

    to_side = wires.far(pm.at[side(1 - l)], px, device(y, c, h, 1 - l, x))
    proj = Scatter(wires, px, l4, spot)
    move = Tokens(wires, result, outputs, spot)
    back = Tokens(wires, grad_low, grad_in, spot)
    swap_fc = TeamSwap(
        wires, lambda p, q: units_fc.at[p * LN + q], lambda p, q: got_fc.at[p * LN + q], spot
    )
    spread = part_f.at[pl.ds(0, D)]
    load_wide = wires.near(to_wide, spread)
    load[0].wait()
    load[1].wait()
    outer_into(part_f, ha, lambda: hb[...])
    fc.start()
    again.start()
    for q in range(2):
        hb[side(q), :D] = term(1 - c, q).astype(LOW)
    to_mate.start()
    load[2].wait()
    for copy in swaps:
        copy.finish()
    for head in range(SLOTS):
        attend_back(mixed, totals, grads, acc_k, acc_v, head)
        if head == 0:
            fc.step(1)
            to_mate.wait_recv()
            pm[side(1 - l), :D] = (pm[side(1 - l), :D].astype(F32) + term(c, 1 - l)).astype(LOW)
        if head == 1:
            to_side.start()
        if head == 2:
            fc.step(2)
        if head == 4:
            fc.step(3)
            move.start()
    load[3].wait()

    def half(which):
        @pl.loop(0, 2)
        def _(s):
            rows = pair_rows(which, s)
            part_h[rows, :] = back_product(mixed[rows, :], wq[...]).astype(LOW)

    half(1 - c)
    first.start()
    half(c)
    again.wait()
    outer_into(wq, ha, lambda: mixed[...])
    qkv.start()
    first.step(0)
    first.step(1)
    fc.finish(wide_fc)
    load_wide.start()
    split_units(wide_fc, units_fc)
    swap_fc.start()
    to_side.wait_recv()
    px[:, :D] = (pm[side(l), :D].astype(F32) + term(c, l) + px[:, :D].astype(F32)).astype(LOW)
    proj.start()
    qkv.step(1)
    terms[...] = jnp.sum(mixed[...].astype(F32), axis=0, keepdims=True)
    load_wide.wait()
    qkv.step(2)
    proj.step(1)
    first.finish(hidden)
    grad = back_product(hidden[...].reshape(2 * BLK, WIDE).astype(LOW), spread[...])
    grad, norms[0:1, :], norms[1:2, :] = norm_back(tokens[...].astype(F32), gain1[...], grad)
    grad_low[...] = (grad_resid[...] + grad).astype(LOW).reshape(2, BLK, D)
    back.start()
    qkv.step(3)
    proj.step(2)
    proj.step(3)
    qkv.finish(wide_qkv)
    split_units(wide_qkv, units_qkv)
    proj.finish(grad_proj)
    swap_fc.finish()
    move.finish()
    back.finish()
    to_mate.wait_send()
    to_side.wait_send()


def split_units(wide, units):
    wide[PIECE:, :] = jnp.zeros((224 - PIECE, wide.shape[1]), F32)
    for k in range(4):
        units[k] = wide[k * 50 : k * 50 + 64, :].astype(LOW)


def norm_back(values, gain, grad):
    center = values - jnp.mean(values, axis=1, keepdims=True)
    scale = lax.rsqrt(jnp.mean(center * center, axis=1, keepdims=True) + EPS)
    unit = center * scale
    grad_gain = jnp.sum(grad * unit, axis=0, keepdims=True)
    grad_shift = jnp.sum(grad, axis=0, keepdims=True)
    grad = grad * gain
    inner = jnp.mean(grad * unit, axis=1, keepdims=True)
    return scale * (grad - jnp.mean(grad, axis=1, keepdims=True) - unit * inner), grad_gain, grad_shift


def epilogue(units_qkv, small, got_qkv, total, by_team, own, by_rank, sems):
    spot = y, c, h, l, x = here()
    wires = Wires(sems)
    meet(team_peers(*spot) + team_twins(*spot))
    qkv = TeamSwap(
        wires, lambda p, q: units_qkv.at[p * LN + q], lambda p, q: got_qkv.at[p * LN + q], spot
    )
    here_team = team_number(y, h, x)
    ways = ((0, 0, 1), (1, 0, 0), (0, 1, 0), (1, 0, 1), (0, 1, 1), (1, 1, 0), (1, 1, 1))
    twins = [
        wires.far(
            small.at[team_number(1 - y if a else y, 1 - h if b else h, 1 - x if d else x)],
            by_team.at[i],
            where,
        )
        for i, ((a, b, d), where) in enumerate(zip(ways, team_twins(*spot)))
    ]
    for copy in twins:
        copy.start()
    qkv.start()
    for copy in twins:
        copy.wait()
    summed = small[here_team]
    for i in range(7):
        summed = summed + by_team[i]
    own[...] = summed
    team = [
        wires.far(own.at[p * LN + q], by_rank.at[i], device(y, p, h, q, x))
        for i, (p, q) in enumerate(((c, 1 - l), (1 - c, 1 - l), (1 - c, l)))
    ]
    for copy in team:
        copy.start()
    for copy in team:
        copy.wait()
    total[...] = own[c * LN + l] + by_rank[0] + by_rank[1] + by_rank[2]
    qkv.finish()


QB = 256


def attend(mixed, context, totals, head):
    lanes = slice(head * HEAD, (head + 1) * HEAD)
    keys = mixed[:, HW + head * HEAD : HW + (head + 1) * HEAD]
    values = mixed[:, 2 * HW + head * HEAD : 2 * HW + (head + 1) * HEAD]
    for block in range(SEQ // QB):
        rows = slice(block * QB, (block + 1) * QB)
        upto = (block + 1) * QB
        scores = (
            lax.dot_general(
                mixed[rows, lanes], keys[:upto], (((1,), (1,)), ((), ())), preferred_element_type=F32
            )
            * 0.125
        )
        row = lax.broadcasted_iota(jnp.int32, (QB, upto), 0) + block * QB
        col = lax.broadcasted_iota(jnp.int32, (QB, upto), 1)
        scores = jnp.where(row >= col, scores, -1e30)
        peak = jnp.max(scores, axis=1, keepdims=True)
        weights = jnp.exp(scores - peak)
        total = jnp.sum(weights, axis=1, keepdims=True)
        prob = (weights * (1.0 / total)).astype(LOW)
        found = jnp.dot(prob, values[:upto], preferred_element_type=F32).astype(LOW)
        context[rows, lanes] = found
        totals[rows, head : head + 1] = peak + jnp.log(total)


def attend_back(mixed, totals, grads, acc_k, acc_v, head):
    lanes = slice(head * HEAD, (head + 1) * HEAD)
    lanes_k = slice(HW + head * HEAD, HW + (head + 1) * HEAD)
    lanes_v = slice(2 * HW + head * HEAD, 2 * HW + (head + 1) * HEAD)
    keys = mixed[:, lanes_k]
    values = mixed[:, lanes_v]
    acc_k[...] = jnp.zeros_like(acc_k)
    acc_v[...] = jnp.zeros_like(acc_v)
    for block in range(SEQ // QB):
        rows = slice(block * QB, (block + 1) * QB)
        upto = (block + 1) * QB
        queries = mixed[rows, lanes]
        outer = grads[rows, lanes]
        scores = (
            lax.dot_general(
                queries, keys[:upto], (((1,), (1,)), ((), ())), preferred_element_type=F32
            )
            * 0.125
        )
        row = lax.broadcasted_iota(jnp.int32, (QB, upto), 0) + block * QB
        col = lax.broadcasted_iota(jnp.int32, (QB, upto), 1)
        scores = jnp.where(row >= col, scores, -1e30)
        prob = jnp.exp(scores - totals[rows, head : head + 1])
        dprob = lax.dot_general(
            outer, values[:upto], (((1,), (1,)), ((), ())), preferred_element_type=F32
        )
        delta = jnp.sum(prob * dprob, axis=1, keepdims=True)
        ds = (prob * (dprob - delta)).astype(LOW)
        mixed[rows, lanes] = (
            jnp.dot(ds, keys[:upto], preferred_element_type=F32) * 0.125
        ).astype(LOW)
        acc_k[:upto] += outer_sum(ds, queries)
        acc_v[:upto] += outer_sum(prob.astype(LOW), outer)
    mixed[:, lanes_k] = (acc_k[...] * 0.125).astype(LOW)
    mixed[:, lanes_v] = acc_v[...].astype(LOW)


def plain(body, name, ins, outs, scratch=()):
    return pl.pallas_call(
        body,
        out_shape=[jax.ShapeDtypeStruct(s, d) for s, d in outs],
        in_specs=[VM] * len(ins),
        out_specs=[VM] * len(outs),
        scratch_shapes=list(scratch),
        compiler_params=pltpu.CompilerParams(vmem_limit_bytes=VMEM_BYTES),
        name=name,
    )(*ins)


def pick(values, index):
    return lax.dynamic_index_in_dim(values, index, 0, keepdims=False)


def pad_to(values, axis, size):
    widths = [(0, 0)] * values.ndim
    widths[axis] = (0, size - values.shape[axis])
    return jnp.pad(values, widths)


def head_parts(columns):
    return jnp.stack(
        [
            pad_to(columns[:, start * HEAD : (start + count) * HEAD], 1, HW)
            for start, count in zip(STARTS, COUNTS)
        ]
    )


def head_join(parts):
    return jnp.concatenate([parts[r][:, : COUNTS[r] * HEAD] for r in range(4)], axis=1)


def feature_order():
    order = -np.ones((8, PIECE), np.int32)
    grid = np.arange(D).reshape(YN, CN, HN, LN, XN, 50).transpose(0, 2, 4, 1, 3, 5)
    order[:, :200] = grid.reshape(8, 200)
    return order.reshape(-1)


def context_order():
    natural = -np.ones(D, np.int32)
    grid = np.arange(D).reshape(YN, CN, HN, LN, XN, 50).transpose(1, 3, 0, 2, 4, 5).reshape(32, 50)
    for block in range(32):
        natural[grid[block]] = block * PB + np.arange(50)
    order = -np.ones((4, HW), np.int32)
    for r in range(4):
        width = COUNTS[r] * HEAD
        order[r, :width] = natural[STARTS[r] * HEAD : STARTS[r] * HEAD + width]
    return order.reshape(-1)


def one_hot(order, size):
    return (np.arange(size)[:, None] == order[None, :]).astype(LOW)


def dot(left, right):
    return jnp.dot(left, right, preferred_element_type=F32)


def ones_row(values):
    return jnp.sum(values.astype(F32), axis=0)


def fast_shards(inputs, grad_out, w_qkv, w_proj, w_fc, w_out, smalls):
    y, c, h, l, x = here()
    rank = c * LN + l
    to_wide = jnp.asarray(one_hot(feature_order(), D))
    to_proj = jnp.asarray(one_hot(context_order(), PROJ).T.copy())

    rows = w_qkv.reshape(50, 3, D)
    units_qkv = jnp.stack([head_parts(rows[:, i]) for i in range(3)], axis=2).reshape(4, 50, QW)
    units_qkv = pad_to(units_qkv, 1, 64)
    units_fc = w_fc.reshape(50, YN, CN, HN, LN, XN, 200).transpose(2, 4, 0, 1, 3, 5, 6)
    units_fc = pad_to(pad_to(units_fc, 6, PIECE).reshape(4, 50, WIDE), 1, 64)
    small = pad_to(smalls, 0, 2048).reshape(16, 128)
    piece_out = pad_to(w_out.reshape(200, D), 0, PIECE)
    piece_proj = pad_to(w_proj.reshape(50, D), 0, PB)
    tokens, smalls_all, mat_qkv, mat_proj, piece_fc = call(
        prologue, "prologue", 1,
        (inputs.reshape(MICRO, BLK, D), units_qkv, units_fc, small, piece_proj),
        [
            ((2, BLK, D), LOW), ((8, 4, 16, 128), LOW), ((8, PIECE, QW), LOW), ((4, 8, PB, D), LOW),
            ((PIECE, WIDE), LOW),
        ],
        [VM] * 5, [ANY] * 4 + [VM],
        [
            pltpu.VMEM((4, 64, QW), LOW), pltpu.VMEM((4, 64, WIDE), LOW),
            pltpu.VMEM((PIECE, QW), F32), pltpu.VMEM((PIECE, WIDE), F32), pltpu.VMEM((PIECE, QW), LOW),
            pltpu.VMEM((PB, D), LOW),
        ],
        SMALLS_SEMS + 2 * TEAM_SWAP_SEMS + TOKENS_SEMS + 3 * GATHER_SEMS + 6,
    )
    mat_qkv = mat_qkv.reshape(WIDE, QW)
    mat_proj = mat_proj.reshape(PROJ, D)
    small = smalls_all.reshape(YN, HN, XN, CN, LN, 2048)[..., :600].transpose(0, 3, 1, 4, 2, 5)
    small = small.reshape(-1).astype(F32)
    gain1, shift1, bias_q, bias_v, bias_proj, gain2, shift2 = [segment(small, i) for i in range(7)]
    bias_fc = small[7 * D : 7 * D + FF].reshape(YN, CN, HN, LN, XN, 200)
    bias_fc = lax.dynamic_index_in_dim(bias_fc, c, 1, keepdims=False)
    bias_fc = lax.dynamic_index_in_dim(bias_fc, l, 2, keepdims=False)
    bias_fc = pad_to(bias_fc, 3, PIECE).reshape(WIDE)
    bias_out = small[7 * D + FF :]
    bias_qkv = jnp.stack(
        [head_parts(bias_q[None]), jnp.zeros((4, 1, HW)), head_parts(bias_v[None])], axis=1
    )
    bias_qkv = pick(bias_qkv, rank).reshape(QW)

    tokens_low = tokens.reshape(2 * BLK, D)
    tokens = tokens_low.astype(F32)
    hidden_one = layer_norm(tokens, gain1, shift1)
    hidden_one = dot(hidden_one.astype(LOW), to_wide).astype(LOW)
    (
        hidden_one, cotangent, grad_all, mat_fc, mat_out, hidden_two, mixed, totals, context, resid,
    ) = call(
        forward, "forward", 2,
        (
            hidden_one.reshape(2, BLK, WIDE), grad_out.reshape(MICRO, BLK, D), piece_fc, piece_out,
            mat_qkv, mat_proj, to_proj, to_wide, tokens_low, bias_qkv.reshape(1, QW),
            bias_proj.reshape(1, D), gain2.reshape(1, D), shift2.reshape(1, D),
        ),
        [
            ((8, BLK, WIDE), LOW), ((2, BLK, D), LOW), ((8, BLK, D), LOW),
            ((8, PIECE, WIDE), LOW), ((8, PIECE, D), LOW),
            ((8, BLK, WIDE), LOW), ((SEQ, QW), LOW), ((SEQ, SLOTS), F32), ((2 * BLK, PROJ), LOW),
            ((2 * BLK, D), F32),
        ],
        [VM] * 4 + [ANY] * 4 + [VM] * 5, [VM, VM] + [ANY] * 4 + [VM] * 4,
        [
            pltpu.VMEM((WIDE, QW), LOW), pltpu.VMEM((PROJ, D), LOW), pltpu.VMEM((4 * HW, PROJ), LOW),
            pltpu.VMEM((D, WIDE), LOW), pltpu.VMEM((SEQ, HW), LOW), pltpu.VMEM((4, 2, BLK, HW), LOW),
            pltpu.VMEM((2, BLK, WIDE), LOW),
        ],
        3 * TEAM_GATHER_SEMS + TOKENS_SEMS + 2 * GATHER_SEMS + 2 * TEAM_SWAP_SEMS + 4,
    )
    hidden_one = hidden_one.reshape(SEQ, WIDE)
    hidden_two = hidden_two.reshape(SEQ, WIDE)
    mat_out = mat_out.reshape(WIDE, D)
    mat_fc = mat_fc.reshape(WIDE, WIDE)
    (
        result, grad_out_w, grad_pre, fc_terms, grad_resid, grad_branch, swap_parts, norms_two,
    ) = call(
        feed_forward, "feed_forward", 5,
        (
            hidden_two, grad_all, mat_fc, mat_out, mat_proj, to_proj, to_wide,
            bias_fc.reshape(1, WIDE), bias_out.reshape(1, D), gain2.reshape(1, D), resid, cotangent,
        ),
        [
            ((2, BLK, D), LOW), ((PIECE, D), F32), ((SEQ, WIDE), LOW), ((1, WIDE), F32),
            ((2 * BLK, D), F32), ((2 * BLK, D), LOW), ((4, 2, BLK, HW), LOW), ((4, D), F32),
        ],
        [ANY] * 7 + [VM] * 5, [VM] * 8,
        [
            pltpu.VMEM((SEQ, WIDE), LOW), pltpu.VMEM((8, BLK, D), LOW), pltpu.VMEM((WIDE, WIDE), LOW),
            pltpu.VMEM((WIDE, D), LOW), pltpu.VMEM((SEQ, WIDE), LOW), pltpu.VMEM((SEQ, D), LOW),
            pltpu.VMEM((WIDE, D), LOW),
        ]
        + team_scatter_scratch(D) + team_scatter_scratch(WIDE) + scatter_scratch(PIECE, D)
        + [
            pltpu.VMEM((2, BLK, WIDE), F32), pltpu.VMEM((2, BLK, D), F32),
            pltpu.VMEM((HW, PROJ), LOW),
        ],
        2 * TEAM_SCATTER_SEMS + SCATTER_SEMS + 13,
    )
    grad_out_w = grad_out_w[:200].reshape(-1)

    units_qkv, got_fc, grad_proj, outputs, grad_in, terms, norms = call(
        backward, "backward", 7,
        (
            hidden_one, hidden_two, grad_pre, mat_qkv, mixed, totals, swap_parts, context,
            grad_branch, result, tokens_low, grad_resid, gain1.reshape(1, D),
            to_wide,
        ),
        [
            ((4, 64, QW), LOW), ((4, 64, WIDE), LOW), ((PB, WIDE), F32), ((2, BLK, D), LOW),
            ((2, BLK, D), LOW), ((1, QW), F32), ((2, D), F32),
        ],
        [ANY] * 5 + [VM, ANY] + [VM] * 6 + [ANY], [VM, ANY, VM, ANY, ANY, VM, VM],
        [
            pltpu.VMEM((SEQ, WIDE), LOW), pltpu.VMEM((SEQ, WIDE), LOW), pltpu.VMEM((WIDE, QW), LOW),
            pltpu.VMEM((WIDE, WIDE), LOW), pltpu.VMEM((SEQ, WIDE), LOW),
            pltpu.VMEM((SEQ, HW), LOW), pltpu.VMEM((SEQ, QW), LOW),
            pltpu.VMEM((SEQ, HEAD), F32), pltpu.VMEM((SEQ, HEAD), F32),
        ]
        + team_scatter_scratch(WIDE) + scatter_scratch(PIECE, WIDE) + scatter_scratch(PIECE, QW)
        + scatter_scratch(PB, WIDE)
        + [
            pltpu.VMEM((PROJ // 2, WIDE), LOW), pltpu.VMEM((PROJ // 4, WIDE), LOW),
            pltpu.VMEM((2, BLK, WIDE), F32), pltpu.VMEM((2, BLK, D), LOW),
            pltpu.VMEM((224, WIDE), F32), pltpu.VMEM((224, QW), F32), pltpu.VMEM((4, 64, WIDE), LOW),
        ],
        TEAM_SCATTER_SEMS + 3 * SCATTER_SEMS + 2 * TOKENS_SEMS + 3 * TEAM_SWAP_SEMS + 10,
    )
    grad_proj = grad_proj[:50, :D].reshape(-1)

    terms = terms.reshape(3, HW)
    mine = (jnp.arange(4) == rank).astype(F32)[:, None, None]
    grad_bq = head_join(mine * terms[0][None, None])[0]
    grad_bv = head_join(mine * terms[2][None, None])[0]
    fc_terms = fc_terms.reshape(YN, 1, HN, 1, XN, PIECE)[..., :200]
    spot = (jnp.arange(CN) == c)[:, None, None] & (jnp.arange(LN) == l)
    spot = spot[None, ..., None, None]
    grad_fc_bias = jnp.where(spot, fc_terms, 0.0).reshape(-1)
    front = jnp.concatenate([norms.reshape(-1), grad_bq, grad_bv])
    tail = jnp.concatenate(
        [
            norms_two[2], norms_two[0], norms_two[1], grad_fc_bias, norms_two[3],
        ]
    )
    small = jnp.concatenate([front.reshape(32, 200), tail.reshape(32, 400)], axis=1)
    small = pad_to(small, 1, 1024).reshape(YN, CN, HN, LN, XN, 8, 128).transpose(0, 2, 4, 1, 3, 5, 6)
    got_qkv, total = call(
        epilogue, "epilogue", 8, (units_qkv, small.reshape(8, 4, 8, 128)),
        [((4, 64, QW), LOW), ((8, 128), F32)],
        [VM] * 2, [ANY, VM],
        [
            pltpu.VMEM((7, 4, 8, 128), F32), pltpu.VMEM((4, 8, 128), F32),
            pltpu.VMEM((3, 8, 128), F32),
        ],
        TEAM_SWAP_SEMS + 20,
    )
    parts = got_qkv[:, :50].reshape(4, 50, 3, HW)
    grad_qkv = jnp.stack([head_join(parts[:, :, i]) for i in range(3)], axis=1)
    grad_qkv = grad_qkv.astype(F32).reshape(-1)
    grad_fc = got_fc[:, :50].reshape(CN, LN, 50, YN, HN, XN, PIECE)[..., :200]
    grad_fc = grad_fc.transpose(2, 3, 0, 4, 1, 5, 6).astype(F32).reshape(-1)
    total = total.reshape(-1)
    return (
        outputs[:, None],
        grad_in.astype(F32)[:, None],
        grad_qkv,
        grad_proj,
        grad_fc,
        grad_out_w,
        total[:200],
        total[200:600],
    )


def solution(mesh):
    placed = (
        P(None, "dp", "ctx", None),
        P(None, "dp", "ctx", None),
        P(("dp", "ctx")),
        P(("dp", "ctx")),
        P(("dp", "ctx")),
        P(("dp", "ctx")),
        P(("dp", "ctx")),
    )
    fast = dict(mesh.shape) == {"dp": DP, "ctx": CTX}
    return jax.shard_map(
        fast_shards if fast else shards,
        mesh=mesh,
        in_specs=placed,
        out_specs=(
            P(None, "dp", "ctx", None),
            P(None, "dp", "ctx", None),
            P(("dp", "ctx")),
            P(("dp", "ctx")),
            P(("dp", "ctx")),
            P(("dp", "ctx")),
            P(("dp", "ctx")),
            P(("dp", "ctx")),
        ),
        check_vma=False,
    )
```

```python
import functools

import jax
import jax.numpy as jnp
import numpy as np
from jax import lax
from jax.experimental import pallas as pl
from jax.experimental.pallas import tpu as pltpu
from jax.sharding import PartitionSpec as P

D = 1600
HEADS = 25
HEAD = 64
FF = 6400
MICRO = 2


EPS = 1e-05


def layer_norm(values, gain, shift):
    center = values - jnp.mean(values, axis=-1, keepdims=True)
    spread = jnp.mean(center * center, axis=-1, keepdims=True)
    return center * lax.rsqrt(spread + EPS) * gain + shift


def gelu_tanh(values):
    return jax.nn.gelu(values, approximate=True)


def unpack(gathered):
    packed_qkv, packed_proj, packed_fc, packed_out, packed_small = gathered
    return (
        packed_qkv.reshape(D, 3 * D),
        packed_proj.reshape(D, D),
        packed_fc.reshape(D, FF),
        packed_out.reshape(FF, D),
        packed_small.astype(jnp.float32),
    )


def fetch(w_qkv, w_proj, w_fc, w_out, smalls):
    return unpack(
        (
            lax.all_gather(w_qkv, ("dp", "ctx"), axis=0, tiled=True),
            lax.all_gather(w_proj, ("dp", "ctx"), axis=0, tiled=True),
            lax.all_gather(w_fc, ("dp", "ctx"), axis=0, tiled=True),
            lax.all_gather(w_out, ("dp", "ctx"), axis=0, tiled=True),
            lax.all_gather(smalls, ("dp", "ctx"), axis=0, tiled=True),
        )
    )


def fetch_again(w_qkv, w_proj, w_fc, w_out, smalls):
    return unpack(
        (
            lax.all_gather(w_qkv, ("dp", "ctx"), axis=0, tiled=True),
            lax.all_gather(w_proj, ("dp", "ctx"), axis=0, tiled=True),
            lax.all_gather(w_fc, ("dp", "ctx"), axis=0, tiled=True),
            lax.all_gather(w_out, ("dp", "ctx"), axis=0, tiled=True),
            lax.all_gather(smalls, ("dp", "ctx"), axis=0, tiled=True),
        )
    )


def outer_sum(left, right):
    return lax.dot_general(
        left, right, (((0,), (0,)), ((), ())), preferred_element_type=jnp.float32
    )


def back_product(grad, weight):
    return lax.dot_general(
        grad, weight, (((1,), (1,)), ((), ())), preferred_element_type=jnp.float32
    )


def flat_term(left, right, start, count):
    width = right.shape[1]
    span = count // width + 2
    padded = jnp.pad(left, ((0, 0), (0, span)))
    first_row = start // width
    piece = lax.dynamic_slice_in_dim(padded, first_row, span, 1)
    block = outer_sum(piece, right).astype(jnp.bfloat16).reshape(-1)
    return lax.dynamic_slice_in_dim(block, start, count, 0)


def masked_scores(queries, keys, query_start, key_start):
    scores = (
        jnp.einsum("sqhe,skhe->shqk", queries, keys, preferred_element_type=jnp.float32) * 0.125
    )
    query_pos = query_start + jnp.arange(queries.shape[1])
    key_pos = key_start + jnp.arange(keys.shape[1])
    allowed = query_pos[:, None] >= key_pos[None, :]
    return jnp.where(allowed[None, None], scores, -1e30)


def segment(small_vals, which):
    return small_vals[which * D : (which + 1) * D]


def shards(inputs, grad_out, w_qkv, w_proj, w_fc, w_out, smalls):
    seqs = inputs.shape[1]
    local_len = inputs.shape[2]
    rows = seqs * local_len
    offset = lax.axis_index("ctx") * local_len
    acc_small = [jnp.zeros((D,), jnp.float32) for _ in range(7)]
    acc_fc_bias = jnp.zeros((FF,), jnp.float32)
    acc_out_bias = jnp.zeros((D,), jnp.float32)
    result_list = []
    grad_list = []
    kept_hidden_one = []
    kept_mixed_grad = []
    kept_context = []
    kept_branch_grad = []
    kept_hidden_two = []
    kept_pre_grad = []
    kept_activ = []
    kept_out_grad = []
    for batch_index in range(MICRO):
        params = fetch(w_qkv, w_proj, w_fc, w_out, smalls)
        mat_qkv, mat_proj, mat_fc, mat_out, small_vals = params
        tokens = inputs[batch_index].astype(jnp.float32).reshape(rows, D)
        hidden_one, ln1_pull = jax.vjp(
            layer_norm, tokens, segment(small_vals, 0), segment(small_vals, 1)
        )
        hidden_one = hidden_one.astype(jnp.bfloat16)
        qkv_bias = jnp.concatenate(
            [segment(small_vals, 2), jnp.zeros((D,), jnp.float32), segment(small_vals, 3)]
        )
        mixed = (
            jnp.dot(hidden_one, mat_qkv, preferred_element_type=jnp.float32) + qkv_bias
        ).astype(jnp.bfloat16)
        queries = mixed[:, :D].reshape(seqs, local_len, HEADS, HEAD)
        keys_local = mixed[:, D : 2 * D].reshape(seqs, local_len, D)
        values_local = mixed[:, 2 * D :].reshape(seqs, local_len, D)
        keys_all, values_all = (
            lax.all_gather(keys_local, "ctx", axis=1, tiled=True),
            lax.all_gather(values_local, "ctx", axis=1, tiled=True),
        )
        keys_all = keys_all.reshape(seqs, -1, HEADS, HEAD)
        values_all = values_all.reshape(seqs, -1, HEADS, HEAD)
        scores = masked_scores(queries, keys_all, offset, 0)
        row_peak = jnp.max(scores, axis=-1, keepdims=True)
        log_total = row_peak + jnp.log(jnp.sum(jnp.exp(scores - row_peak), axis=-1, keepdims=True))
        attn_low = jnp.exp(scores - log_total).astype(jnp.bfloat16)
        context = jnp.einsum(
            "shqk,skhe->sqhe", attn_low, values_all, preferred_element_type=jnp.float32
        )
        context = context.reshape(rows, D).astype(jnp.bfloat16)
        resid = (
            tokens
            + jnp.dot(context, mat_proj, preferred_element_type=jnp.float32)
            + segment(small_vals, 4)
        )
        hidden_two, ln2_pull = jax.vjp(
            layer_norm, resid, segment(small_vals, 5), segment(small_vals, 6)
        )
        hidden_two = hidden_two.astype(jnp.bfloat16)
        pre_act = (
            jnp.dot(hidden_two, mat_fc, preferred_element_type=jnp.float32)
            + small_vals[7 * D : 7 * D + FF]
        )
        activ, gelu_pull = jax.vjp(gelu_tanh, pre_act)
        activ = activ.astype(jnp.bfloat16)
        result = (
            resid
            + jnp.dot(activ, mat_out, preferred_element_type=jnp.float32)
            + small_vals[7 * D + FF :]
        )
        result_list.append(result.astype(jnp.bfloat16).reshape(seqs, local_len, D))
        back_params = fetch_again(w_qkv, w_proj, w_fc, w_out, smalls)
        mat_qkv, mat_proj, mat_fc, mat_out, small_vals = back_params
        grad_low = grad_out[batch_index].reshape(rows, D)
        grad_full = grad_low.astype(jnp.float32)
        acc_out_bias = acc_out_bias + jnp.sum(grad_full, axis=0)
        grad_act = back_product(grad_low, mat_out)
        (grad_pre,) = gelu_pull(grad_act)
        grad_pre = grad_pre.astype(jnp.bfloat16)
        acc_fc_bias = acc_fc_bias + jnp.sum(grad_pre.astype(jnp.float32), axis=0)
        grad_hidden_two = back_product(grad_pre, mat_fc)
        grad_ln_two, grad_gain_two, grad_shift_two = ln2_pull(grad_hidden_two)
        acc_small[5] = acc_small[5] + grad_gain_two
        acc_small[6] = acc_small[6] + grad_shift_two
        grad_resid = grad_full + grad_ln_two
        grad_branch = grad_resid.astype(jnp.bfloat16)
        acc_small[4] = acc_small[4] + jnp.sum(grad_branch.astype(jnp.float32), axis=0)
        grad_context = (
            back_product(grad_branch, mat_proj)
            .astype(jnp.bfloat16)
            .reshape(seqs, local_len, HEADS, HEAD)
        )
        scores = masked_scores(queries, keys_all, offset, 0)
        attn_prob = jnp.exp(scores - log_total)
        grad_attn = jnp.einsum(
            "sqhe,skhe->shqk", grad_context, values_all, preferred_element_type=jnp.float32
        )
        row_delta = jnp.sum(attn_prob * grad_attn, axis=-1, keepdims=True)
        grad_scores = (attn_prob * (grad_attn - row_delta)).astype(jnp.bfloat16)
        grad_queries = (
            jnp.einsum("shqk,skhe->sqhe", grad_scores, keys_all, preferred_element_type=jnp.float32)
            * 0.125
        )
        query_all, dctx_all = (
            lax.all_gather(queries.reshape(seqs, local_len, D), "ctx", axis=1, tiled=True),
            lax.all_gather(grad_context.reshape(seqs, local_len, D), "ctx", axis=1, tiled=True),
        )
        lse_all, delta_all = (
            lax.all_gather(jnp.transpose(log_total[..., 0], (0, 2, 1)), "ctx", axis=1, tiled=True),
            lax.all_gather(jnp.transpose(row_delta[..., 0], (0, 2, 1)), "ctx", axis=1, tiled=True),
        )
        query_all = query_all.reshape(seqs, -1, HEADS, HEAD)
        dctx_all = dctx_all.reshape(seqs, -1, HEADS, HEAD)
        lse_all = jnp.transpose(lse_all, (0, 2, 1))[..., None]
        delta_all = jnp.transpose(delta_all, (0, 2, 1))[..., None]
        own_keys = keys_local.reshape(seqs, local_len, HEADS, HEAD)
        own_values = values_local.reshape(seqs, local_len, HEADS, HEAD)
        col_scores = masked_scores(query_all, own_keys, 0, offset)
        col_prob = jnp.exp(col_scores - lse_all)
        col_dattn = jnp.einsum(
            "sqhe,skhe->shqk", dctx_all, own_values, preferred_element_type=jnp.float32
        )
        col_ds = (col_prob * (col_dattn - delta_all)).astype(jnp.bfloat16)
        grad_keys = (
            jnp.einsum("shqk,sqhe->skhe", col_ds, query_all, preferred_element_type=jnp.float32)
            * 0.125
        )
        grad_values = jnp.einsum(
            "shqk,sqhe->skhe",
            col_prob.astype(jnp.bfloat16),
            dctx_all,
            preferred_element_type=jnp.float32,
        )
        grad_mixed = jnp.concatenate(
            [
                grad_queries.reshape(rows, D),
                grad_keys.reshape(rows, D),
                grad_values.reshape(rows, D),
            ],
            axis=1,
        ).astype(jnp.bfloat16)
        bias_terms = jnp.sum(grad_mixed.astype(jnp.float32), axis=0)
        acc_small[2] = acc_small[2] + bias_terms[:D]
        acc_small[3] = acc_small[3] + bias_terms[2 * D :]
        grad_hidden_one = back_product(grad_mixed, mat_qkv)
        grad_ln_one, grad_gain_one, grad_shift_one = ln1_pull(grad_hidden_one)
        acc_small[0] = acc_small[0] + grad_gain_one
        acc_small[1] = acc_small[1] + grad_shift_one
        grad_list.append((grad_resid + grad_ln_one).reshape(seqs, local_len, D))
        kept_hidden_one.append(hidden_one)
        kept_mixed_grad.append(grad_mixed)
        kept_context.append(context)
        kept_branch_grad.append(grad_branch)
        kept_hidden_two.append(hidden_two)
        kept_pre_grad.append(grad_pre)
        kept_activ.append(activ)
        kept_out_grad.append(grad_low)
    front_grads = jnp.concatenate(acc_small[0:4])
    tail_grads = jnp.concatenate(acc_small[4:7] + [acc_fc_bias, acc_out_bias])
    grad_qkv = lax.psum_scatter(
        flat_term(
            jnp.concatenate(kept_hidden_one),
            jnp.concatenate(kept_mixed_grad),
            jnp.int32(0),
            lax.axis_size(("dp", "ctx")) * w_qkv.shape[0],
        ),
        ("dp", "ctx"),
        scatter_dimension=0,
        tiled=True,
    ).astype(jnp.float32)
    grad_proj = lax.psum_scatter(
        flat_term(
            jnp.concatenate(kept_context),
            jnp.concatenate(kept_branch_grad),
            jnp.int32(0),
            lax.axis_size(("dp", "ctx")) * w_proj.shape[0],
        ),
        ("dp", "ctx"),
        scatter_dimension=0,
        tiled=True,
    ).astype(jnp.float32)
    grad_fc = lax.psum_scatter(
        flat_term(
            jnp.concatenate(kept_hidden_two),
            jnp.concatenate(kept_pre_grad),
            jnp.int32(0),
            lax.axis_size(("dp", "ctx")) * w_fc.shape[0],
        ),
        ("dp", "ctx"),
        scatter_dimension=0,
        tiled=True,
    ).astype(jnp.float32)
    grad_out_w = lax.psum_scatter(
        flat_term(
            jnp.concatenate(kept_activ),
            jnp.concatenate(kept_out_grad),
            jnp.int32(0),
            lax.axis_size(("dp", "ctx")) * w_out.shape[0],
        ),
        ("dp", "ctx"),
        scatter_dimension=0,
        tiled=True,
    ).astype(jnp.float32)
    grad_front, grad_tail = (
        lax.psum_scatter(front_grads, ("dp", "ctx"), scatter_dimension=0, tiled=True),
        lax.psum_scatter(tail_grads, ("dp", "ctx"), scatter_dimension=0, tiled=True),
    )
    return (
        jnp.stack(result_list),
        jnp.stack(grad_list),
        grad_qkv,
        grad_proj,
        grad_fc,
        grad_out_w,
        grad_front,
        grad_tail,
    )


DP, CTX = 4, 8
YN, CN, HN, LN, XN = 2, 2, 2, 2, 2
SLOTS = 7
HW = SLOTS * HEAD
QW = 3 * HW
STARTS = (0, 7, 13, 19)
COUNTS = (7, 6, 6, 6)
BLK = 128
SEQ = 8 * BLK
PIECE = 208
WIDE = 8 * PIECE
PB = 64
PROJ = 32 * PB
LOW = jnp.bfloat16
F32 = jnp.float32
VMEM_BYTES = 60 * 1024 * 1024
ANY = pl.BlockSpec(memory_space=pl.ANY)
VM = pl.BlockSpec(memory_space=pltpu.VMEM)


def here():
    dp, ctx = lax.axis_index("dp"), lax.axis_index("ctx")
    return dp // CN, dp % CN, ctx // 4, (ctx // XN) % LN, ctx % XN


def device(y, c, h, l, x):
    return (y * CN + c, (h * LN + l) * XN + x)


def team_number(y, h, x):
    return y * 4 + h * 2 + x


class Wires:
    def __init__(self, sems):
        self.sems, self.used = sems, 0

    def one(self):
        self.used += 1
        assert self.used <= self.sems.shape[0]
        return self.sems.at[self.used - 1]

    def far(self, source, target, where):
        return pltpu.make_async_remote_copy(
            src_ref=source,
            dst_ref=target,
            send_sem=self.one(),
            recv_sem=self.one(),
            device_id=where,
            device_id_type=pl.DeviceIdType.MESH,
        )

    def near(self, source, target):
        return pltpu.make_async_copy(source, target, self.one())


def signal(where):
    pl.semaphore_signal(
        pltpu.get_barrier_semaphore(), inc=1, device_id=where, device_id_type=pl.DeviceIdType.MESH
    )


def team_peers(y, c, h, l, x):
    return [
        device(y, 1 - c, h, l, x), device(y, c, h, 1 - l, x), device(y, 1 - c, h, 1 - l, x)
    ]


def grid_peers(y, c, h, l, x):
    return [
        device(1 - y, c, h, l, x), device(y, c, 1 - h, l, x), device(y, c, h, l, 1 - x)
    ]


def meet(peers):
    for peer in peers:
        signal(peer)
    pl.semaphore_wait(pltpu.get_barrier_semaphore(), len(peers))


def call(body, name, ident, ins, outs, in_specs, out_specs, scratch, sems, cost=None):
    return pl.pallas_call(
        body,
        out_shape=[jax.ShapeDtypeStruct(s, d) for s, d in outs],
        in_specs=in_specs,
        out_specs=out_specs,
        scratch_shapes=list(scratch) + [pltpu.SemaphoreType.DMA((sems,))],
        compiler_params=pltpu.CompilerParams(
            collective_id=ident, has_side_effects=True, vmem_limit_bytes=VMEM_BYTES
        ),
        name=name,
    )(*ins)


class Routes:
    def __init__(self, spot):
        y, c, h, l, x = spot
        self.place = (y, h, x)
        self.peers = {
            "y": device(1 - y, c, h, l, x),
            "h": device(y, c, 1 - h, l, x),
            "x": device(y, c, h, l, 1 - x),
        }

    def flipped(self, ways):
        y, h, x = self.place
        return team_number(
            1 - y if "y" in ways else y, 1 - h if "h" in ways else h, 1 - x if "x" in ways else x
        )


def halves(rows):
    cut = (rows // 2 + 15) // 16 * 16
    return ((0, cut, "hxy"), (cut, rows - cut, "hyx"))


class Gather:
    def __init__(self, wires, piece, whole, spot):
        routes = Routes(spot)
        self.local = wires.near(piece, whole.at[routes.flipped("")])
        self.parts = []
        for start, size, order in halves(piece.shape[0]):
            at = pl.ds(start, size)
            first, second, third = order

            def copy(ways, way):
                spot = whole.at[routes.flipped(ways), at]
                source = piece.at[at] if not ways else spot
                return wires.far(source, spot, routes.peers[way])

            self.parts.append(
                {
                    "first": copy("", first),
                    "second": [copy("", second), copy(first, second)],
                    "third": [
                        copy("", third), copy(second, third), copy(first, third),
                        copy(first + second, third),
                    ],
                }
            )

    def start(self):
        self.local.start()
        for part in self.parts:
            part["first"].start()
            part["second"][0].start()
            part["third"][0].start()

    def step(self, turn):
        for part in self.parts:
            if turn == 1:
                part["second"][0].wait_recv()
                part["third"][1].start()
            elif turn == 2:
                part["first"].wait_recv()
                part["second"][1].start()
                part["third"][2].start()
            else:
                part["second"][1].wait_recv()
                part["third"][3].start()

    def finish(self):
        self.local.wait()
        for part in self.parts:
            for copy in [part["first"]] + part["second"]:
                copy.wait_send()
            for copy in part["third"]:
                copy.wait()


GATHER_SEMS = 1 + 2 * 2 * 7


class Scatter:
    def __init__(self, wires, parts, landed, spot):
        routes = Routes(spot)
        self.rows = landed.shape[1]
        self.parts, self.landed = parts, landed
        self.jobs = []
        for start, size, order in halves(self.rows):
            first, second, third = order
            at = pl.ds(start, size)

            def term(ways):
                base = routes.flipped(ways) * self.rows + start
                return parts.at[pl.ds(pl.multiple_of(base, 16), size)]

            stay = [second + first, second, first, ""]
            job = {
                "terms": [term(ways) for ways in stay],
                "spots": [landed.at[k, at] for k in range(7)],
                "over": [
                    wires.far(term(third + ways), landed.at[k, at], routes.peers[third])
                    for k, ways in enumerate(stay)
                ],
                "along": [
                    wires.far(landed.at[k, at], landed.at[4 + k, at], routes.peers[second])
                    for k in range(2)
                ],
                "last": wires.far(landed.at[2, at], landed.at[6, at], routes.peers[first]),
                "at": slice(start, start + size),
            }
            self.jobs.append(job)

    def start(self):
        for k in (0, 2):
            for job in self.jobs:
                job["over"][k].start()

    def step(self, turn):
        k = (0, 2, 1)[turn - 1]
        for job in self.jobs:
            job["over"][k].wait_recv()
            if turn < 3:
                job["over"][2 * turn - 1].start()
            total = job["spots"][k][...].astype(F32) + job["terms"][k][...].astype(F32)
            if turn == 2:
                job["along"][0].wait_recv()
                total = total + job["spots"][4][...].astype(F32)
            job["spots"][k][...] = total.astype(LOW)
            (job["along"] + [job["last"]])[k].start()

    def finish(self, total):
        for job in self.jobs:
            job["over"][3].wait_recv()
            job["along"][1].wait_recv()
            job["last"].wait_recv()
            summed = job["terms"][3][...].astype(F32)
            for k in (3, 5, 6):
                summed = summed + job["spots"][k][...].astype(F32)
            total[job["at"], :] = summed.astype(total.dtype)
            for copy in job["over"] + job["along"] + [job["last"]]:
                copy.wait_send()


SCATTER_SEMS = 2 * 2 * 7


class TeamGather:
    def __init__(self, wires, block, whole, spot):
        y, c, h, l, x = spot
        mate, beside = device(y, 1 - c, h, l, x), device(y, c, h, 1 - l, x)

        def at(l, s):
            return whole.at[c * 4 + l * 2 + s]

        self.local = [wires.near(block.at[s], at(l, s)) for s in range(2)]
        self.to_mate = [wires.far(block.at[s], at(l, s), mate) for s in range(2)]
        self.to_side = [wires.far(block.at[s], at(l, s), beside) for s in range(2)]
        self.relay = [wires.far(at(1 - l, s), at(1 - l, s), mate) for s in range(2)]

    def start(self):
        for copy in self.to_side + self.to_mate + self.local:
            copy.start()

    def step(self, s):
        self.to_side[s].wait_recv()
        self.relay[s].start()

    def finish(self):
        for copy in self.local + self.to_mate + self.relay:
            copy.wait()
        for copy in self.to_side:
            copy.wait_send()


TEAM_GATHER_SEMS = 2 + 2 * 6


class TeamSwap:
    def __init__(self, wires, source, target, spot):
        y, c, h, l, x = spot
        self.local = wires.near(source(c, l), target(c, l))
        self.copies = [
            wires.far(source(p, q), target(c, l), device(y, p, h, q, x))
            for p, q in ((c, 1 - l), (1 - c, 1 - l), (1 - c, l))
        ]

    def start(self):
        for copy in self.copies + [self.local]:
            copy.start()

    def finish(self):
        for copy in self.copies + [self.local]:
            copy.wait()


TEAM_SWAP_SEMS = 1 + 2 * 3


def pair_rows(c, l):
    return pl.ds(pl.multiple_of((c * 2 + l) * 2 * BLK, 2 * BLK), 2 * BLK)


def block_rows(c, l, s):
    return pl.ds(pl.multiple_of((c * 4 + l * 2 + s) * BLK, BLK), BLK)


class TeamScatter:
    def __init__(self, wires, parts, landed, leaving, arrived, spot):
        y, c, h, l, x = spot
        self.c, self.l = c, l
        self.parts, self.landed, self.leaving, self.arrived = parts, landed, leaving, arrived
        mate, beside = device(y, 1 - c, h, l, x), device(y, c, h, 1 - l, x)
        self.to_mate = [
            wires.far(parts.at[pair_rows(1 - c, q)], landed.at[k], mate)
            for k, q in enumerate((1 - l, l))
        ]
        self.to_side = [wires.far(leaving.at[s], arrived.at[s], beside) for s in range(2)]

    def start(self):
        for copy in self.to_mate:
            copy.start()

    def step(self, s):
        if s == 0:
            self.to_mate[0].wait_recv()
        rows = slice(s * BLK, (s + 1) * BLK)
        self.leaving[s] = (
            self.landed[0, rows, :].astype(F32)
            + self.parts[block_rows(self.c, 1 - self.l, s), :].astype(F32)
        ).astype(LOW)
        self.to_side[s].start()

    def finish(self, total):
        self.to_mate[1].wait_recv()
        for s in range(2):
            self.to_side[s].wait_recv()
            total[s] = (
                self.landed[1, s * BLK : (s + 1) * BLK, :].astype(F32)
                + self.parts[block_rows(self.c, self.l, s), :].astype(F32)
                + self.arrived[s].astype(F32)
            )
        for copy in self.to_mate + self.to_side:
            copy.wait_send()


TEAM_SCATTER_SEMS = 2 * 4


def team_scatter_scratch(width):
    return [
        pltpu.VMEM((2, 2 * BLK, width), LOW),
        pltpu.VMEM((2, BLK, width), LOW),
        pltpu.VMEM((2, BLK, width), LOW),
    ]


def scatter_scratch(rows, width):
    return [pltpu.VMEM((7, rows, width), LOW)]


class Tokens:
    def __init__(self, wires, source, target, spot):
        y, c, h, l, x = spot
        self.stays = h == c
        goals = token_goals(spot)
        pairs = []
        for k in range(2):
            other = lax.rem(x + k, 2)
            pairs.append((source.at[other], target.at[x]))
        self.local = wires.near(*pairs[0])
        self.copies = [wires.far(*pair, goal) for pair, goal in zip(pairs, goals)]

    def start(self):
        pl.when(self.stays)(self.local.start)
        pl.when(jnp.logical_not(self.stays))(self.copies[0].start)
        self.copies[1].start()

    def finish(self):
        pl.when(self.stays)(self.local.wait)
        pl.when(jnp.logical_not(self.stays))(self.copies[0].wait)
        self.copies[1].wait()


TOKENS_SEMS = 1 + 2 * 2


def token_goals(spot):
    y, c, h, l, x = spot
    return [device(y, h, c, l, x), device(y, h, c, l, 1 - x)]


def meet_tokens(peers, spot):
    y, c, h, l, x = spot
    same, other = token_goals(spot)
    for peer in peers + [other]:
        signal(peer)
    pl.when(h != c)(functools.partial(signal, same))
    count = len(peers) + 1 + jnp.where(h == c, 0, 1)
    pl.semaphore_wait(pltpu.get_barrier_semaphore(), count)


class Smalls:
    def __init__(self, wires, small, smalls, spot):
        y, c, h, l, x = spot
        own = team_number(y, h, x)
        self.first = TeamSwap(
            wires, lambda p, q: small, lambda p, q: smalls.at[own, p * LN + q], spot
        )
        self.second = [
            wires.far(smalls.at[own], smalls.at[own], where) for where in team_twins(*spot)
        ]

    def start(self):
        self.first.start()

    def step(self):
        self.first.finish()
        for copy in self.second:
            copy.start()

    def finish(self):
        for copy in self.second:
            copy.wait()


SMALLS_SEMS = TEAM_SWAP_SEMS + 2 * 7


def team_twins(y, c, h, l, x):
    ways = ((0, 0, 1), (1, 0, 0), (0, 1, 0), (1, 0, 1), (0, 1, 1), (1, 1, 0), (1, 1, 1))
    return [
        device(1 - y if a else y, c, 1 - h if b else h, l, 1 - x if d else x) for a, b, d in ways
    ]


def join_units(units, wide, piece):
    for k in range(4):
        wide[k * 50 : (k + 1) * 50, :] = units[k, :50, :].astype(F32)
    wide[200:, :] = jnp.zeros((PIECE - 200, wide.shape[1]), F32)
    piece[...] = wide[...].astype(LOW)


def prologue(
    inputs, units_qkv, units_fc, small, piece_proj,
    tokens, smalls, all_qkv, all_proj, piece_fc,
    got_qkv, got_fc, wide_qkv, wide_fc, piece_qkv, beside_proj, sems,
):
    spot = y, c, h, l, x = here()
    wires = Wires(sems)
    rank = c * LN + l
    meet_tokens(team_peers(*spot) + team_twins(*spot), spot)
    values = Smalls(wires, small, smalls, spot)
    qkv_units = TeamSwap(
        wires, lambda p, q: units_qkv.at[p * LN + q], lambda p, q: got_qkv.at[p * LN + q], spot
    )
    fc_units = TeamSwap(
        wires, lambda p, q: units_fc.at[p * LN + q], lambda p, q: got_fc.at[p * LN + q], spot
    )
    move = Tokens(wires, inputs, tokens, spot)
    qkv = Gather(wires, piece_qkv, all_qkv, spot)
    other = c * LN + 1 - l
    proj = Gather(wires, piece_proj, all_proj.at[rank], spot)
    side = wires.far(piece_proj, beside_proj, device(y, c, h, 1 - l, x))
    beside = Gather(wires, beside_proj, all_proj.at[other], spot)
    mate = device(y, 1 - c, h, l, x)
    relay = [
        wires.far(all_proj.at[r], all_proj.at[r], mate) for r in (rank, other)
    ]
    values.start()
    qkv_units.start()
    values.step()
    side.start()
    proj.start()
    qkv_units.finish()
    join_units(got_qkv, wide_qkv, piece_qkv)
    qkv.start()
    fc_units.start()
    move.start()
    side.wait()
    beside.start()
    proj.step(1)
    proj.step(2)
    proj.step(3)
    values.finish()
    qkv.step(1)
    proj.finish()
    relay[0].start()
    beside.step(1)
    qkv.step(2)
    beside.step(2)
    fc_units.finish()
    join_units(got_fc, wide_fc, piece_fc)
    qkv.step(3)
    beside.step(3)
    beside.finish()
    relay[1].start()
    move.finish()
    qkv.finish()
    for copy in relay:
        copy.wait()


def forward(
    hidden, grads, piece_fc, piece_out, mat_qkv, mat_proj, to_proj, to_wide,
    tokens, bias_qkv, bias_proj, gain2, shift2,
    hidden_out, cotangent, grad_all, all_fc, all_out, second_all, mixed_out, totals, context_out, resid,
    hidden_all, mixed,
    mat_in, proj_in, to_proj_in, to_wide_in, context, got, second, sems,
):
    spot = y, c, h, l, x = here()
    wires = Wires(sems)
    load = [
        wires.near(*both)
        for both in (
            (mat_qkv, mat_in), (mat_proj, proj_in), (to_proj, to_proj_in), (to_wide, to_wide_in)
        )
    ]
    for copy in load:
        copy.start()
    meet_tokens(team_peers(*spot) + grid_peers(*spot), spot)
    keep = [wires.near(hidden_all, hidden_out), wires.near(mixed, mixed_out)]
    team = TeamGather(wires, hidden, hidden_all, spot)
    fc = Gather(wires, piece_fc, all_fc, spot)
    out = Gather(wires, piece_out, all_out, spot)
    bring = Tokens(wires, grads, cotangent, spot)
    team_two = TeamGather(wires, cotangent, grad_all, spot)
    team_three = TeamGather(wires, second, second_all, spot)
    swaps = [
        TeamSwap(
            wires,
            lambda p, q, s=s: context.at[block_rows(p, q, s)],
            lambda p, q, s=s: got.at[p * LN + q, s],
            spot,
        )
        for s in range(2)
    ]
    team.start()
    fc.start()
    team.step(0)
    team.step(1)
    load[0].wait()
    team.finish()
    keep[0].start()
    bring.start()
    fc.step(1)

    @pl.loop(0, SEQ // QB)
    def _(i):
        rows = pl.ds(pl.multiple_of(i * QB, QB), QB)
        flat = hidden_all[pl.ds(pl.multiple_of(i * 2, 2), 2)].reshape(QB, WIDE)
        mixed[rows, :] = (dot(flat, mat_in[...]) + bias_qkv[...]).astype(LOW)

    keep[1].start()
    fc.step(2)
    for head in range(SLOTS):
        attend(mixed, context, totals, head)
        if head == 0:
            fc.step(3)
            out.start()
            bring.finish()
            team_two.start()
        if head == 3:
            team_two.step(0)
        if head == 4:
            out.step(1)
    team_two.step(1)
    for copy in swaps:
        copy.start()
    for copy in load[1:]:
        copy.wait()
    for copy in swaps:
        copy.finish()
    out.step(2)
    placed = 0.0
    for r in range(4):
        placed = placed + dot(
            got[r].reshape(2 * BLK, HW), to_proj_in[r * HW : (r + 1) * HW, :]
        )
    placed = placed.astype(LOW)
    context_out[...] = placed
    found = tokens[...].astype(F32) + dot(placed, proj_in[...]) + bias_proj[...]
    resid[...] = found
    normed = layer_norm(found, gain2[...], shift2[...]).astype(LOW)
    second[...] = dot(normed, to_wide_in[...]).astype(LOW).reshape(2, BLK, WIDE)
    team_three.start()
    fc.finish()
    team_three.step(0)
    out.step(3)
    team_three.step(1)
    team_two.finish()
    team_three.finish()
    out.finish()
    for copy in keep:
        copy.wait()


def gelu_both(f):
    square = f * f
    t = jnp.tanh(0.7978845608028654 * f * (1.0 + 0.044715 * square))
    half = 0.5 * (1.0 + t)
    slope = half + f * (0.5 * 0.7978845608028654) * (1.0 - t * t) * (1.0 + 3 * 0.044715 * square)
    return f * half, slope


def chunks(total, step):
    return [(start, min(step, total - start)) for start in range(0, total, step)]


def outer_into(target, left, right):
    count = left.shape[1] // 256

    @pl.loop(0, count)
    def _(i):
        at = pl.ds(pl.multiple_of(i * 256, 256), 256)
        target[at, :] = outer_sum(left[:, at], right()).astype(LOW)

    rest = left.shape[1] - count * 256
    if rest:
        target[count * 256 :, :] = outer_sum(left[:, count * 256 :], right()).astype(LOW)


def feed_forward(
    hidden_two, grad_all, mat_fc, mat_out, mat_proj, to_proj, to_wide,
    bias_fc, bias_out, gain2, resid, cotangent,
    result, grad_out_w, grad_pre_out, terms, grad_resid, branch, swap_parts, norms,
    h2, dy, wf, wo, activ, part_r, part_o, l1, s1, a1, l2, s2, a2, l3,
    hidden, total_r, spread, grad_pre, sems,
):
    spot = y, c, h, l, x = here()
    wires = Wires(sems)
    load = [
        wires.near(*both) for both in ((hidden_two, h2), (mat_fc, wf), (grad_all, dy), (mat_out, wo))
    ]
    for copy in load[:2]:
        copy.start()
    keep = wires.near(grad_pre, grad_pre_out)
    load_wide = wires.near(to_wide, wf.at[pl.ds(0, D)])
    load_proj = [wires.near(mat_proj.at[pl.ds(0, WIDE)], wo)] + [
        wires.near(mat_proj.at[pl.ds(WIDE + k * BLK, BLK)], dy.at[k]) for k in range(3)
    ]
    load_spread = [wires.near(to_proj.at[pl.ds(r * HW, HW)], spread) for r in range(4)]
    meet(team_peers(*spot) + grid_peers(*spot))
    second = TeamScatter(wires, h2, l2, s2, a2, spot)
    first = TeamScatter(wires, part_r, l1, s1, a1, spot)
    out = Scatter(wires, part_o, l3, spot)
    load[0].wait()
    load[1].wait()
    for copy in load[2:] + load_spread[:1]:
        copy.start()

    @pl.loop(0, SEQ // QB)
    def _(i):
        rows = pl.ds(pl.multiple_of(i * QB, QB), QB)
        f = dot(h2[rows, :], wf[...]) + bias_fc[...]
        value, slope = gelu_both(f)
        activ[rows, :] = value.astype(LOW)
        grad_pre[rows, :] = slope.astype(LOW)

    load[2].wait()
    outer_into(part_o, activ, lambda: dy[...].reshape(SEQ, D))
    out.start()
    load[3].wait()
    terms[...] = jnp.zeros_like(terms)

    @pl.loop(0, SEQ // QB)
    def _(i):
        rows = pl.ds(pl.multiple_of(i * QB, QB), QB)
        here_dy = dy[pl.ds(pl.multiple_of(i * 2, 2), 2)].reshape(QB, D)
        df = (back_product(here_dy, wo[...]) * grad_pre[rows, :].astype(F32)).astype(LOW)
        grad_pre[rows, :] = df
        terms[...] += jnp.sum(df.astype(F32), axis=0, keepdims=True)

    keep.start()

    def into(target, make):
        def half(which):
            @pl.loop(0, 2)
            def _(s):
                rows = pair_rows(which, s)
                target[rows, :] = make(rows).astype(LOW)

        return half

    half = into(h2, lambda rows: back_product(grad_pre[rows, :], wf[...]))
    half(1 - c)
    second.start()
    half(c)
    load_wide.start()
    out.step(1)
    second.step(0)
    second.step(1)
    half = into(part_r, lambda rows: dot(activ[rows, :], wo[...]))
    half(1 - c)
    first.start()
    half(c)
    for copy in load_proj:
        copy.start()
    out.step(2)
    first.step(0)
    first.step(1)
    load_wide.wait()
    second.finish(hidden)
    out.step(3)
    grad = back_product(hidden[...].reshape(2 * BLK, WIDE).astype(LOW), wf[:D, :])
    grad, norms[0:1, :], norms[1:2, :] = norm_back(resid[...], gain2[...], grad)
    own = cotangent[...].reshape(2 * BLK, D).astype(F32)
    norms[3:4, :] = jnp.sum(own, axis=0, keepdims=True)
    grad = own + grad
    grad_resid[...] = grad
    branch[...] = grad.astype(LOW)
    norms[2:3, :] = jnp.sum(branch[...].astype(F32), axis=0, keepdims=True)
    for copy in load_proj:
        copy.wait()
    low = back_product(branch[...], wo[...]).astype(LOW)
    high = back_product(branch[...], dy[0:3].reshape(3 * BLK, D)).astype(LOW)
    for r in range(4):
        load_spread[r].wait()
        part = back_product(low, spread[:, :WIDE]) + back_product(high, spread[:, WIDE:])
        swap_parts[r] = part.astype(LOW).reshape(2, BLK, HW)
        if r < 3:
            load_spread[r + 1].start()
    first.finish(total_r)
    result[...] = (
        resid[...].reshape(2, BLK, D) + total_r[...] + bias_out[...].reshape(1, 1, D)
    ).astype(LOW)
    out.finish(grad_out_w)
    keep.wait()


def backward(
    hidden_one, hidden_two, grad_pre, mat_qkv, mixed_all, totals, swap_parts, context, branch, result,
    tokens, grad_resid, gain1, to_wide,
    units_qkv, got_fc, grad_proj, outputs, grad_in, terms, norms,
    ha, hb, wq, part_f, part_h, grads, mixed, acc_k, acc_v,
    l1, s1, a1, l2, l3, l4, l5, pm, part_t, got_t, hidden, grad_low, wide_fc, wide_qkv, units_fc, sems,
):
    spot = y, c, h, l, x = here()
    wires = Wires(sems)
    load = [wires.near(*both) for both in ((hidden_two, ha), (grad_pre, hb), (mixed_all, mixed), (mat_qkv, wq))]
    again = wires.near(hidden_one, ha)
    for copy in load[:2]:
        copy.start()
    meet_tokens(team_peers(*spot) + grid_peers(*spot), spot)
    swaps = [
        TeamSwap(
            wires,
            lambda p, q, s=s: swap_parts.at[p * LN + q, s],
            lambda p, q, s=s: grads.at[block_rows(p, q, s)],
            spot,
        )
        for s in range(2)
    ]
    for copy in swaps:
        copy.start()
    fc = Scatter(wires, part_f, l2, spot)
    first = TeamScatter(wires, part_h, l1, s1, a1, spot)
    qkv = Scatter(wires, wq, l3, spot)
    quarter = PROJ // 4
    to_mate = wires.far(hb, pm, device(y, 1 - c, h, l, x))

    def side(q):
        return pl.ds(pl.multiple_of(q * quarter, 16), quarter)

    def term(p, q):
        at = pl.ds(pl.multiple_of((p * 2 + q) * quarter, quarter), quarter)
        return outer_sum(context[:, at], branch[...])

    to_side = wires.far(part_t, got_t, device(y, c, h, 1 - l, x))
    proj = Scatter(wires, pm.at[side(l)], l4, spot)
    beside = Scatter(wires, pm.at[side(1 - l)], l5, spot)
    move = Tokens(wires, result, outputs, spot)
    back = Tokens(wires, grad_low, grad_in, spot)
    swap_fc = TeamSwap(
        wires, lambda p, q: units_fc.at[p * LN + q], lambda p, q: got_fc.at[p * LN + q], spot
    )
    spread = part_f.at[pl.ds(0, D)]
    load_wide = wires.near(to_wide, spread)
    load[0].wait()
    load[1].wait()
    for copy in load[2:]:
        copy.start()
    outer_into(part_f, ha, lambda: hb[...])
    fc.start()
    again.start()
    for q in range(2):
        hb[side(q), :D] = term(1 - c, q).astype(LOW)
    to_mate.start()
    load[2].wait()
    for copy in swaps:
        copy.finish()
    for head in range(SLOTS):
        attend_back(mixed, totals, grads, acc_k, acc_v, head)
        if head == 0:
            fc.step(1)
            to_mate.wait_recv()
            for q in range(2):
                pm[side(q), :D] = (pm[side(q), :D].astype(F32) + term(c, q)).astype(LOW)
        if head == 2:
            fc.step(2)
            beside.start()
            proj.start()
        if head == 4:
            fc.step(3)
            move.start()
    load[3].wait()

    def half(which):
        @pl.loop(0, 2)
        def _(s):
            rows = pair_rows(which, s)
            part_h[rows, :] = back_product(mixed[rows, :], wq[...]).astype(LOW)

    half(1 - c)
    first.start()
    half(c)
    again.wait()
    beside.step(1)
    proj.step(1)
    outer_into(wq, ha, lambda: mixed[...])
    qkv.start()
    first.step(0)
    first.step(1)
    fc.finish(wide_fc)
    load_wide.start()
    split_units(wide_fc, units_fc)
    swap_fc.start()
    beside.step(2)
    proj.step(2)
    qkv.step(1)
    beside.step(3)
    proj.step(3)
    terms[...] = jnp.sum(mixed[...].astype(F32), axis=0, keepdims=True)
    load_wide.wait()
    qkv.step(2)
    first.finish(hidden)
    grad = back_product(hidden[...].reshape(2 * BLK, WIDE).astype(LOW), spread[...])
    grad, norms[0:1, :], norms[1:2, :] = norm_back(tokens[...].astype(F32), gain1[...], grad)
    grad_low[...] = (grad_resid[...] + grad).astype(LOW).reshape(2, BLK, D)
    back.start()
    beside.finish(part_t)
    to_side.start()
    qkv.step(3)
    proj.finish(grad_proj)
    to_side.wait_recv()
    grad_proj[...] = grad_proj[...] + got_t[...].astype(F32)
    qkv.finish(wide_qkv)
    split_units(wide_qkv, units_qkv)
    swap_fc.finish()
    move.finish()
    back.finish()
    to_mate.wait_send()
    to_side.wait_send()


def split_units(wide, units):
    wide[PIECE:, :] = jnp.zeros((224 - PIECE, wide.shape[1]), F32)
    for k in range(4):
        units[k] = wide[k * 50 : k * 50 + 64, :].astype(LOW)


def norm_back(values, gain, grad):
    center = values - jnp.mean(values, axis=1, keepdims=True)
    scale = lax.rsqrt(jnp.mean(center * center, axis=1, keepdims=True) + EPS)
    unit = center * scale
    grad_gain = jnp.sum(grad * unit, axis=0, keepdims=True)
    grad_shift = jnp.sum(grad, axis=0, keepdims=True)
    grad = grad * gain
    inner = jnp.mean(grad * unit, axis=1, keepdims=True)
    return scale * (grad - jnp.mean(grad, axis=1, keepdims=True) - unit * inner), grad_gain, grad_shift


def epilogue(units_qkv, small, got_qkv, total, by_team, own, by_rank, sems):
    spot = y, c, h, l, x = here()
    wires = Wires(sems)
    meet(team_peers(*spot) + team_twins(*spot))
    qkv = TeamSwap(
        wires, lambda p, q: units_qkv.at[p * LN + q], lambda p, q: got_qkv.at[p * LN + q], spot
    )
    here_team = team_number(y, h, x)
    ways = ((0, 0, 1), (1, 0, 0), (0, 1, 0), (1, 0, 1), (0, 1, 1), (1, 1, 0), (1, 1, 1))
    twins = [
        wires.far(
            small.at[team_number(1 - y if a else y, 1 - h if b else h, 1 - x if d else x)],
            by_team.at[i],
            where,
        )
        for i, ((a, b, d), where) in enumerate(zip(ways, team_twins(*spot)))
    ]
    for copy in twins:
        copy.start()
    qkv.start()
    for copy in twins:
        copy.wait()
    summed = small[here_team]
    for i in range(7):
        summed = summed + by_team[i]
    own[...] = summed
    team = [
        wires.far(own.at[p * LN + q], by_rank.at[i], device(y, p, h, q, x))
        for i, (p, q) in enumerate(((c, 1 - l), (1 - c, 1 - l), (1 - c, l)))
    ]
    for copy in team:
        copy.start()
    for copy in team:
        copy.wait()
    total[...] = own[c * LN + l] + by_rank[0] + by_rank[1] + by_rank[2]
    qkv.finish()


QB = 256


def attend(mixed, context, totals, head):
    lanes = slice(head * HEAD, (head + 1) * HEAD)
    keys = mixed[:, HW + head * HEAD : HW + (head + 1) * HEAD]
    values = mixed[:, 2 * HW + head * HEAD : 2 * HW + (head + 1) * HEAD]
    for block in range(SEQ // QB):
        rows = slice(block * QB, (block + 1) * QB)
        upto = (block + 1) * QB
        scores = (
            lax.dot_general(
                mixed[rows, lanes], keys[:upto], (((1,), (1,)), ((), ())), preferred_element_type=F32
            )
            * 0.125
        )
        row = lax.broadcasted_iota(jnp.int32, (QB, upto), 0) + block * QB
        col = lax.broadcasted_iota(jnp.int32, (QB, upto), 1)
        scores = jnp.where(row >= col, scores, -1e30)
        peak = jnp.max(scores, axis=1, keepdims=True)
        weights = jnp.exp(scores - peak)
        total = jnp.sum(weights, axis=1, keepdims=True)
        prob = (weights * (1.0 / total)).astype(LOW)
        found = jnp.dot(prob, values[:upto], preferred_element_type=F32).astype(LOW)
        context[rows, lanes] = found
        totals[rows, head : head + 1] = peak + jnp.log(total)


def attend_back(mixed, totals, grads, acc_k, acc_v, head):
    lanes = slice(head * HEAD, (head + 1) * HEAD)
    lanes_k = slice(HW + head * HEAD, HW + (head + 1) * HEAD)
    lanes_v = slice(2 * HW + head * HEAD, 2 * HW + (head + 1) * HEAD)
    keys = mixed[:, lanes_k]
    values = mixed[:, lanes_v]
    acc_k[...] = jnp.zeros_like(acc_k)
    acc_v[...] = jnp.zeros_like(acc_v)
    for block in range(SEQ // QB):
        rows = slice(block * QB, (block + 1) * QB)
        upto = (block + 1) * QB
        queries = mixed[rows, lanes]
        outer = grads[rows, lanes]
        scores = (
            lax.dot_general(
                queries, keys[:upto], (((1,), (1,)), ((), ())), preferred_element_type=F32
            )
            * 0.125
        )
        row = lax.broadcasted_iota(jnp.int32, (QB, upto), 0) + block * QB
        col = lax.broadcasted_iota(jnp.int32, (QB, upto), 1)
        scores = jnp.where(row >= col, scores, -1e30)
        prob = jnp.exp(scores - totals[rows, head : head + 1])
        dprob = lax.dot_general(
            outer, values[:upto], (((1,), (1,)), ((), ())), preferred_element_type=F32
        )
        delta = jnp.sum(prob * dprob, axis=1, keepdims=True)
        ds = (prob * (dprob - delta)).astype(LOW)
        mixed[rows, lanes] = (
            jnp.dot(ds, keys[:upto], preferred_element_type=F32) * 0.125
        ).astype(LOW)
        acc_k[:upto] += outer_sum(ds, queries)
        acc_v[:upto] += outer_sum(prob.astype(LOW), outer)
    mixed[:, lanes_k] = (acc_k[...] * 0.125).astype(LOW)
    mixed[:, lanes_v] = acc_v[...].astype(LOW)


def plain(body, name, ins, outs, scratch=()):
    return pl.pallas_call(
        body,
        out_shape=[jax.ShapeDtypeStruct(s, d) for s, d in outs],
        in_specs=[VM] * len(ins),
        out_specs=[VM] * len(outs),
        scratch_shapes=list(scratch),
        compiler_params=pltpu.CompilerParams(vmem_limit_bytes=VMEM_BYTES),
        name=name,
    )(*ins)


def pick(values, index):
    return lax.dynamic_index_in_dim(values, index, 0, keepdims=False)


def pad_to(values, axis, size):
    widths = [(0, 0)] * values.ndim
    widths[axis] = (0, size - values.shape[axis])
    return jnp.pad(values, widths)


def head_parts(columns):
    return jnp.stack(
        [
            pad_to(columns[:, start * HEAD : (start + count) * HEAD], 1, HW)
            for start, count in zip(STARTS, COUNTS)
        ]
    )


def head_join(parts):
    return jnp.concatenate([parts[r][:, : COUNTS[r] * HEAD] for r in range(4)], axis=1)


def feature_order():
    order = -np.ones((8, PIECE), np.int32)
    grid = np.arange(D).reshape(YN, CN, HN, LN, XN, 50).transpose(0, 2, 4, 1, 3, 5)
    order[:, :200] = grid.reshape(8, 200)
    return order.reshape(-1)


def context_order():
    natural = -np.ones(D, np.int32)
    grid = np.arange(D).reshape(YN, CN, HN, LN, XN, 50).transpose(1, 3, 0, 2, 4, 5).reshape(32, 50)
    for block in range(32):
        natural[grid[block]] = block * PB + np.arange(50)
    order = -np.ones((4, HW), np.int32)
    for r in range(4):
        width = COUNTS[r] * HEAD
        order[r, :width] = natural[STARTS[r] * HEAD : STARTS[r] * HEAD + width]
    return order.reshape(-1)


def one_hot(order, size):
    return (np.arange(size)[:, None] == order[None, :]).astype(LOW)


def dot(left, right):
    return jnp.dot(left, right, preferred_element_type=F32)


def ones_row(values):
    return jnp.sum(values.astype(F32), axis=0)


def fast_shards(inputs, grad_out, w_qkv, w_proj, w_fc, w_out, smalls):
    y, c, h, l, x = here()
    rank = c * LN + l
    to_wide = jnp.asarray(one_hot(feature_order(), D))
    to_proj = jnp.asarray(one_hot(context_order(), PROJ).T.copy())

    rows = w_qkv.reshape(50, 3, D)
    units_qkv = jnp.stack([head_parts(rows[:, i]) for i in range(3)], axis=2).reshape(4, 50, QW)
    units_qkv = pad_to(units_qkv, 1, 64)
    units_fc = w_fc.reshape(50, YN, CN, HN, LN, XN, 200).transpose(2, 4, 0, 1, 3, 5, 6)
    units_fc = pad_to(pad_to(units_fc, 6, PIECE).reshape(4, 50, WIDE), 1, 64)
    small = pad_to(smalls, 0, 2048).reshape(16, 128)
    piece_out = pad_to(w_out.reshape(200, D), 0, PIECE)
    piece_proj = pad_to(w_proj.reshape(50, D), 0, PB)
    tokens, smalls_all, mat_qkv, mat_proj, piece_fc = call(
        prologue, "prologue", 1,
        (inputs.reshape(MICRO, BLK, D), units_qkv, units_fc, small, piece_proj),
        [
            ((2, BLK, D), LOW), ((8, 4, 16, 128), LOW), ((8, PIECE, QW), LOW), ((4, 8, PB, D), LOW),
            ((PIECE, WIDE), LOW),
        ],
        [VM] * 5, [ANY] * 4 + [VM],
        [
            pltpu.VMEM((4, 64, QW), LOW), pltpu.VMEM((4, 64, WIDE), LOW),
            pltpu.VMEM((PIECE, QW), F32), pltpu.VMEM((PIECE, WIDE), F32), pltpu.VMEM((PIECE, QW), LOW),
            pltpu.VMEM((PB, D), LOW),
        ],
        SMALLS_SEMS + 2 * TEAM_SWAP_SEMS + TOKENS_SEMS + 3 * GATHER_SEMS + 6,
    )
    mat_qkv = mat_qkv.reshape(WIDE, QW)
    mat_proj = mat_proj.reshape(PROJ, D)
    small = smalls_all.reshape(YN, HN, XN, CN, LN, 2048)[..., :600].transpose(0, 3, 1, 4, 2, 5)
    small = small.reshape(-1).astype(F32)
    gain1, shift1, bias_q, bias_v, bias_proj, gain2, shift2 = [segment(small, i) for i in range(7)]
    bias_fc = small[7 * D : 7 * D + FF].reshape(YN, CN, HN, LN, XN, 200)
    bias_fc = lax.dynamic_index_in_dim(bias_fc, c, 1, keepdims=False)
    bias_fc = lax.dynamic_index_in_dim(bias_fc, l, 2, keepdims=False)
    bias_fc = pad_to(bias_fc, 3, PIECE).reshape(WIDE)
    bias_out = small[7 * D + FF :]
    bias_qkv = jnp.stack(
        [head_parts(bias_q[None]), jnp.zeros((4, 1, HW)), head_parts(bias_v[None])], axis=1
    )
    bias_qkv = pick(bias_qkv, rank).reshape(QW)

    tokens_low = tokens.reshape(2 * BLK, D)
    tokens = tokens_low.astype(F32)
    hidden_one = layer_norm(tokens, gain1, shift1)
    hidden_one = dot(hidden_one.astype(LOW), to_wide).astype(LOW)
    (
        hidden_one, cotangent, grad_all, mat_fc, mat_out, hidden_two, mixed, totals, context, resid,
    ) = call(
        forward, "forward", 2,
        (
            hidden_one.reshape(2, BLK, WIDE), grad_out.reshape(MICRO, BLK, D), piece_fc, piece_out,
            mat_qkv, mat_proj, to_proj, to_wide, tokens_low, bias_qkv.reshape(1, QW),
            bias_proj.reshape(1, D), gain2.reshape(1, D), shift2.reshape(1, D),
        ),
        [
            ((8, BLK, WIDE), LOW), ((2, BLK, D), LOW), ((8, BLK, D), LOW),
            ((8, PIECE, WIDE), LOW), ((8, PIECE, D), LOW),
            ((8, BLK, WIDE), LOW), ((SEQ, QW), LOW), ((SEQ, SLOTS), F32), ((2 * BLK, PROJ), LOW),
            ((2 * BLK, D), F32),
        ],
        [VM] * 4 + [ANY] * 4 + [VM] * 5, [ANY, VM] + [ANY] * 5 + [VM] * 3,
        [
            pltpu.VMEM((8, BLK, WIDE), LOW), pltpu.VMEM((SEQ, QW), LOW),
            pltpu.VMEM((WIDE, QW), LOW), pltpu.VMEM((PROJ, D), LOW), pltpu.VMEM((4 * HW, PROJ), LOW),
            pltpu.VMEM((D, WIDE), LOW), pltpu.VMEM((SEQ, HW), LOW), pltpu.VMEM((4, 2, BLK, HW), LOW),
            pltpu.VMEM((2, BLK, WIDE), LOW),
        ],
        3 * TEAM_GATHER_SEMS + TOKENS_SEMS + 2 * GATHER_SEMS + 2 * TEAM_SWAP_SEMS + 6,
    )
    hidden_one = hidden_one.reshape(SEQ, WIDE)
    hidden_two = hidden_two.reshape(SEQ, WIDE)
    mat_out = mat_out.reshape(WIDE, D)
    mat_fc = mat_fc.reshape(WIDE, WIDE)
    (
        result, grad_out_w, grad_pre, fc_terms, grad_resid, grad_branch, swap_parts, norms_two,
    ) = call(
        feed_forward, "feed_forward", 5,
        (
            hidden_two, grad_all, mat_fc, mat_out, mat_proj, to_proj, to_wide,
            bias_fc.reshape(1, WIDE), bias_out.reshape(1, D), gain2.reshape(1, D), resid, cotangent,
        ),
        [
            ((2, BLK, D), LOW), ((PIECE, D), F32), ((SEQ, WIDE), LOW), ((1, WIDE), F32),
            ((2 * BLK, D), F32), ((2 * BLK, D), LOW), ((4, 2, BLK, HW), LOW), ((4, D), F32),
        ],
        [ANY] * 7 + [VM] * 5, [VM, VM, ANY] + [VM] * 5,
        [
            pltpu.VMEM((SEQ, WIDE), LOW), pltpu.VMEM((8, BLK, D), LOW), pltpu.VMEM((WIDE, WIDE), LOW),
            pltpu.VMEM((WIDE, D), LOW), pltpu.VMEM((SEQ, WIDE), LOW), pltpu.VMEM((SEQ, D), LOW),
            pltpu.VMEM((WIDE, D), LOW),
        ]
        + team_scatter_scratch(D) + team_scatter_scratch(WIDE) + scatter_scratch(PIECE, D)
        + [
            pltpu.VMEM((2, BLK, WIDE), F32), pltpu.VMEM((2, BLK, D), F32),
            pltpu.VMEM((HW, PROJ), LOW), pltpu.VMEM((SEQ, WIDE), LOW),
        ],
        2 * TEAM_SCATTER_SEMS + SCATTER_SEMS + 14,
    )
    grad_out_w = grad_out_w[:200].reshape(-1)

    units_qkv, got_fc, grad_proj, outputs, grad_in, terms, norms = call(
        backward, "backward", 7,
        (
            hidden_one, hidden_two, grad_pre, mat_qkv, mixed, totals, swap_parts, context,
            grad_branch, result, tokens_low, grad_resid, gain1.reshape(1, D),
            to_wide,
        ),
        [
            ((4, 64, QW), LOW), ((4, 64, WIDE), LOW), ((PB, WIDE), F32), ((2, BLK, D), LOW),
            ((2, BLK, D), LOW), ((1, QW), F32), ((2, D), F32),
        ],
        [ANY] * 5 + [VM, ANY] + [VM] * 6 + [ANY], [VM, ANY, VM, ANY, ANY, VM, VM],
        [
            pltpu.VMEM((SEQ, WIDE), LOW), pltpu.VMEM((SEQ, WIDE), LOW), pltpu.VMEM((WIDE, QW), LOW),
            pltpu.VMEM((WIDE, WIDE), LOW), pltpu.VMEM((SEQ, WIDE), LOW),
            pltpu.VMEM((SEQ, HW), LOW), pltpu.VMEM((SEQ, QW), LOW),
            pltpu.VMEM((SEQ, HEAD), F32), pltpu.VMEM((SEQ, HEAD), F32),
        ]
        + team_scatter_scratch(WIDE) + scatter_scratch(PIECE, WIDE) + scatter_scratch(PIECE, QW)
        + scatter_scratch(PB, WIDE) + scatter_scratch(PB, WIDE)
        + [
            pltpu.VMEM((PROJ // 2, WIDE), LOW), pltpu.VMEM((PB, WIDE), LOW), pltpu.VMEM((PB, WIDE), LOW),
            pltpu.VMEM((2, BLK, WIDE), F32), pltpu.VMEM((2, BLK, D), LOW),
            pltpu.VMEM((224, WIDE), F32), pltpu.VMEM((224, QW), F32), pltpu.VMEM((4, 64, WIDE), LOW),
        ],
        TEAM_SCATTER_SEMS + 4 * SCATTER_SEMS + 2 * TOKENS_SEMS + 3 * TEAM_SWAP_SEMS + 10,
    )
    grad_proj = grad_proj[:50, :D].reshape(-1)

    terms = terms.reshape(3, HW)
    mine = (jnp.arange(4) == rank).astype(F32)[:, None, None]
    grad_bq = head_join(mine * terms[0][None, None])[0]
    grad_bv = head_join(mine * terms[2][None, None])[0]
    fc_terms = fc_terms.reshape(YN, 1, HN, 1, XN, PIECE)[..., :200]
    spot = (jnp.arange(CN) == c)[:, None, None] & (jnp.arange(LN) == l)
    spot = spot[None, ..., None, None]
    grad_fc_bias = jnp.where(spot, fc_terms, 0.0).reshape(-1)
    front = jnp.concatenate([norms.reshape(-1), grad_bq, grad_bv])
    tail = jnp.concatenate(
        [
            norms_two[2], norms_two[0], norms_two[1], grad_fc_bias, norms_two[3],
        ]
    )
    small = jnp.concatenate([front.reshape(32, 200), tail.reshape(32, 400)], axis=1)
    small = pad_to(small, 1, 1024).reshape(YN, CN, HN, LN, XN, 8, 128).transpose(0, 2, 4, 1, 3, 5, 6)
    got_qkv, total = call(
        epilogue, "epilogue", 8, (units_qkv, small.reshape(8, 4, 8, 128)),
        [((4, 64, QW), LOW), ((8, 128), F32)],
        [VM] * 2, [ANY, VM],
        [
            pltpu.VMEM((7, 4, 8, 128), F32), pltpu.VMEM((4, 8, 128), F32),
            pltpu.VMEM((3, 8, 128), F32),
        ],
        TEAM_SWAP_SEMS + 20,
    )
    parts = got_qkv[:, :50].reshape(4, 50, 3, HW)
    grad_qkv = jnp.stack([head_join(parts[:, :, i]) for i in range(3)], axis=1)
    grad_qkv = grad_qkv.astype(F32).reshape(-1)
    grad_fc = got_fc[:, :50].reshape(CN, LN, 50, YN, HN, XN, PIECE)[..., :200]
    grad_fc = grad_fc.transpose(2, 3, 0, 4, 1, 5, 6).astype(F32).reshape(-1)
    total = total.reshape(-1)
    return (
        outputs[:, None],
        grad_in.astype(F32)[:, None],
        grad_qkv,
        grad_proj,
        grad_fc,
        grad_out_w,
        total[:200],
        total[200:600],
    )


def solution(mesh):
    placed = (
        P(None, "dp", "ctx", None),
        P(None, "dp", "ctx", None),
        P(("dp", "ctx")),
        P(("dp", "ctx")),
        P(("dp", "ctx")),
        P(("dp", "ctx")),
        P(("dp", "ctx")),
    )
    fast = dict(mesh.shape) == {"dp": DP, "ctx": CTX}
    return jax.shard_map(
        fast_shards if fast else shards,
        mesh=mesh,
        in_specs=placed,
        out_specs=(
            P(None, "dp", "ctx", None),
            P(None, "dp", "ctx", None),
            P(("dp", "ctx")),
            P(("dp", "ctx")),
            P(("dp", "ctx")),
            P(("dp", "ctx")),
            P(("dp", "ctx")),
            P(("dp", "ctx")),
        ),
        check_vma=False,
    )
```
